128 devices in a mesh: ctx: 64 (over x, y, z_hi, core), wa: 2 (over z_lo).
Axes of the slice: x: 4, y: 4, z: 4 (z_hi: 2, z_lo: 2; z = z_hi * 2 + z_lo), core: 2. Of those that a mesh axis runs over, the one named last changes fastest.
Arguments:
- tokens: bfloat16 [8192, 768], P('ctx'), may hold values from -6 to 6
- doc_start: int32 [8192], P('ctx'), may hold values from 0 to 8191, as said below
- exit_layer: int32 [8192], P('ctx'), may hold values from 1 to 12, as said below
- cotangent: bfloat16 [8192, 768], P('ctx'), may hold values from -6 to 6
- ln1_gain: float32 [768], replicated, may hold values from 0.25 to 1.75
- ln1_shift: float32 [768], replicated, may hold values from -1.5 to 1.5
- q_weight: bfloat16 [768, 768], P(None, 'wa'), may hold values from -0.3125 to 0.3125
- q_bias: float32 [768], P('wa'), may hold values from -1.5 to 1.5
- k_weight: bfloat16 [768, 768], P(None, 'wa'), may hold values from -0.3125 to 0.3125
- v_weight: bfloat16 [768, 768], P(None, 'wa'), may hold values from -0.21875 to 0.21875
- v_bias: float32 [768], P('wa'), may hold values from -1.5 to 1.5
- o_weight: bfloat16 [768, 768], P('wa'), may hold values from -1.75 to 1.75
- o_bias: float32 [768], replicated, may hold values from -1.5 to 1.5
- ln2_gain: float32 [768], replicated, may hold values from 0.25 to 1.75
- ln2_shift: float32 [768], replicated, may hold values from -1.5 to 1.5
- up_weight: bfloat16 [768, 3072], P(None, 'wa'), may hold values from -0.21875 to 0.21875
- up_bias: float32 [3072], P('wa'), may hold values from -1.5 to 1.5
- down_weight: bfloat16 [3072, 768], P('wa'), may hold values from -0.15625 to 0.15625
- down_bias: float32 [768], replicated, may hold values from -1.5 to 1.5
Outputs:
- output: bfloat16 [8192, 768], P('ctx')
- input_grad: float32 [8192, 768], P('ctx')
- ln1_gain_grad: float32 [768], replicated
- ln1_shift_grad: float32 [768], replicated
- q_weight_grad: float32 [768, 768], P('ctx', 'wa')
- q_bias_grad: float32 [768], P('wa')
- k_weight_grad: float32 [768, 768], P('ctx', 'wa')
- v_weight_grad: float32 [768, 768], P('ctx', 'wa')
- v_bias_grad: float32 [768], P('wa')
- o_weight_grad_t: float32 [768, 768], P('ctx', 'wa')
- o_bias_grad: float32 [768], replicated
- ln2_gain_grad: float32 [768], replicated
- ln2_shift_grad: float32 [768], replicated
- up_weight_grad: float32 [768, 3072], P('ctx', 'wa')
- up_bias_grad: float32 [3072], P('wa')
- down_weight_grad_t: float32 [768, 3072], P('ctx', 'wa')
- down_bias_grad: float32 [768], replicated
The draws below stay inside these ranges and needn't reach their ends.
Inputs may be any that keep to these rules, and one draw needn't show every extreme that they name: doc_start(k) is the stream position at which the document holding place(k) begins; documents are contiguous runs of the stream of 1 to 4096 positions; one of exactly 4096 positions begins among the first 64 positions of the stream, and the stream's last position is a document of its own. `exit_layer`: within a document, exit layers never increase along the stream, and a document's first position has exit layer 12, so the active positions of each document form a non-empty prefix of it; every position of the document of 4096 positions that begins among the first 64 is active.
All inputs are finite; a program needn't handle non-finite values.
Results may differ from the reference program's by a relative error of at most 0.014.
The reference program's roundings to bfloat16 on the way count: a program that leaves them out, or rounds other values in their place, can miss the bound.
Values may be sent and summed in bfloat16 or wider, within the bound.
No kernel may reach another device: no remote copies, remote signals or barrier semaphores. Data moves between devices by JAX's collectives and lax.ppermute only.
A program may use at most 192 MiB of HBM per device.

```python
import math
import jax
import jax.numpy as jnp
from jax import lax

D = 768
HEADS = 12
HEAD_DIM = 64
FF = 3072
NLAYERS = 12
LAYER = 6
TOK_DEV = 128
HH = 768
HALF = 64
TOKENS = 8192
DOC_MOST = 4096


def stream_place_drawn(row_ids, per_device, stream_len):
    half_rows = per_device // 2
    device = row_ids // per_device
    within = row_ids % per_device
    return jnp.where(within < half_rows, device * half_rows + within, stream_len - (device + 1) * half_rows + within - half_rows)


def stream_layout(key):
    layout_key = jax.random.fold_in(key, 7)
    planted_key, cut_key, pick_key = jax.random.split(layout_key, 3)
    positions = jnp.arange(TOKENS, dtype=jnp.int32)
    planted = jax.random.randint(planted_key, (), 0, min(HALF, TOKENS - DOC_MOST + 1), dtype=jnp.int32)
    random_cuts = jax.random.randint(cut_key, (TOKENS,), 0, DOC_MOST // 4, dtype=jnp.int32) == 0
    inside = (positions > planted) & (positions < planted + DOC_MOST)
    grid_cuts = (positions - planted) % DOC_MOST == 0
    opening = random_cuts & jnp.logical_not(inside) | grid_cuts | (positions == 0) | (positions == TOKENS - 1)
    begins = lax.cummax(jnp.where(opening, positions, 0), axis=0)
    next_open = lax.cummin(jnp.where(opening, positions, TOKENS), axis=0, reverse=True)
    following = jnp.concatenate([next_open[1:], jnp.full((1,), TOKENS, jnp.int32)])
    length = following - begins
    within = positions - begins
    draw_picks = jax.random.randint(pick_key, (TOKENS,), 0, 1 << 20, dtype=jnp.int32)
    active_len = jnp.where(begins == planted, length, 1 + draw_picks[begins] % length)
    upper_exit = LAYER + 1 + (NLAYERS - LAYER - 1) * (active_len - within) // active_len
    lower_exit = 1 + (LAYER - 1) * (length - 1 - within) // jnp.maximum(length - active_len, 1)
    exit_layers = jnp.where(within < active_len, upper_exit, lower_exit)
    return (begins, exit_layers)


def draw_doc_start(key, part):
    begins, exit_layers = stream_layout(key)
    position = stream_place_drawn(jnp.arange(TOKENS, dtype=jnp.int32), TOK_DEV, TOKENS)
    return begins[position].astype(jnp.int32)


def draw_exit_layer(key, part):
    begins, exit_layers = stream_layout(key)
    position = stream_place_drawn(jnp.arange(TOKENS, dtype=jnp.int32), TOK_DEV, TOKENS)
    return exit_layers[position].astype(jnp.int32)


def block_scale(rng, dims, shards, smallest, largest):
    gain, own = 1.0, jax.random.fold_in(rng, 6)
    for dim, parts in shards:
        heights = jnp.exp(jax.random.uniform(jax.random.fold_in(own, dim), (parts,), jnp.float32, smallest / len(shards), largest / len(shards)))
        gain = gain * jnp.repeat(heights, dims[dim] // parts).reshape([-1 if axis == dim else 1 for axis in range(len(dims))])
    return gain


def noise(rng, dims, deviation, most, shards=(), held_as=jnp.bfloat16):
    entries = jax.random.normal(rng, dims, jnp.float32) * deviation
    if len(shards) > 0:
        entries = block_scale(rng, dims, shards, -0.22, 0.18) * entries
    return jnp.clip(entries, min=-most, max=most).astype(held_as)


def setup_inputs(seed: int = 0) -> dict:
    splits = jax.random.split(jax.random.key(seed), 20)
    tokens = noise(splits[0], (TOKENS, D), 1.0, 6.0, ((0, 64),))
    doc_start = draw_doc_start(jax.random.fold_in(splits[19], 71), 0)
    exit_layer = draw_exit_layer(jax.random.fold_in(splits[19], 71), 0)
    cotangent = noise(splits[3], (TOKENS, D), 1.0, 6.0, ((0, 64),))
    ln1_gain = jnp.clip(1.0 + 0.15 * jax.random.normal(splits[4], (D,), jnp.float32), 0.25, 1.75)
    ln1_shift = noise(splits[5], (D,), 0.3, 1.5, (), jnp.float32)
    q_weight = noise(splits[6], (D, HH), (D // 2) ** -0.5, 0.3125, ((1, 2),))
    q_bias = noise(splits[7], (HH,), 0.3, 1.5, ((0, 2),), jnp.float32)
    k_weight = noise(splits[8], (D, HH), (D // 2) ** -0.5, 0.3125, ((1, 2),))
    v_weight = noise(splits[9], (D, HH), D ** -0.5, 0.21875, ((1, 2),))
    v_bias = noise(splits[10], (HH,), 0.3, 1.5, ((0, 2),), jnp.float32)
    o_weight = noise(splits[11], (HH, D), (HH // 64) ** -0.5, 1.75, ((0, 2),))
    o_bias = noise(splits[12], (D,), 0.3, 1.5, (), jnp.float32)
    ln2_gain = jnp.clip(1.0 + 0.15 * jax.random.normal(splits[13], (D,), jnp.float32), 0.25, 1.75)
    ln2_shift = noise(splits[14], (D,), 0.3, 1.5, (), jnp.float32)
    up_weight = noise(splits[15], (D, FF), D ** -0.5, 0.21875, ((1, 2),))
    up_bias = noise(splits[16], (FF,), 0.3, 1.5, ((0, 2),), jnp.float32)
    down_weight = noise(splits[17], (FF, D), (FF // 2) ** -0.5, 0.15625, ((0, 2),))
    down_bias = noise(splits[18], (D,), 0.3, 1.5, (), jnp.float32)
    return dict(tokens=tokens, doc_start=doc_start, exit_layer=exit_layer, cotangent=cotangent, ln1_gain=ln1_gain, ln1_shift=ln1_shift, q_weight=q_weight, q_bias=q_bias, k_weight=k_weight, v_weight=v_weight, v_bias=v_bias, o_weight=o_weight, o_bias=o_bias, ln2_gain=ln2_gain, ln2_shift=ln2_shift, up_weight=up_weight, up_bias=up_bias, down_weight=down_weight, down_bias=down_bias)


@jax.custom_vjp
def low(v):
    return lax.optimization_barrier(v.astype(jnp.bfloat16)).astype(jnp.float32)

@jax.custom_vjp
def low_back(v):
    return v

def low_keep(v):
    return (low(v), None)

def low_pass(kept, grad):
    return (grad,)

def back_keep(v):
    return (v, None)

def back_low(kept, grad):
    return (low(grad),)
low.defvjp(low_keep, low_pass)
low_back.defvjp(back_keep, back_low)

def layer_norm(values, gain_vec, shift_vec):
    average = lax.optimization_barrier(jnp.mean(values, axis=-1, keepdims=True))
    centred = values - average
    variance = lax.optimization_barrier(jnp.mean(centred * centred, axis=-1, keepdims=True))
    return centred * lax.rsqrt(variance + 1e-05) * gain_vec + shift_vec

def product(left_op, right_op):
    return jnp.dot(left_op, right_op, precision=lax.Precision.HIGHEST, preferred_element_type=jnp.float32)

def stream_place(row_ids, per_device, stream_len):
    half_rows = per_device // 2
    device = row_ids // per_device
    within = row_ids % per_device
    return jnp.where(within < half_rows, device * half_rows + within, stream_len - (device + 1) * half_rows + within - half_rows)

def attention(queries, keyset, values, starts):
    scaling = 1.0 / math.sqrt(HEAD_DIM)
    block_rows = math.gcd(512, TOKENS)
    query_heads = queries.reshape(TOKENS, HEADS, HEAD_DIM)
    padding = jnp.zeros((DOC_MOST, HEADS, HEAD_DIM), jnp.float32)
    keys_pad = jnp.concatenate([padding, keyset.reshape(TOKENS, HEADS, HEAD_DIM)], axis=0)
    values_pad = jnp.concatenate([padding, values.reshape(TOKENS, HEADS, HEAD_DIM)], axis=0)

    def one_block(first_row):
        query_rows = lax.dynamic_slice_in_dim(query_heads, first_row, block_rows, 0)
        key_rows = lax.dynamic_slice_in_dim(keys_pad, first_row, DOC_MOST + block_rows, 0)
        value_rows = lax.dynamic_slice_in_dim(values_pad, first_row, DOC_MOST + block_rows, 0)
        doc_begin = lax.dynamic_slice_in_dim(starts, first_row, block_rows, 0)
        query_place = first_row + jnp.arange(block_rows, dtype=jnp.int32)
        key_place = first_row - DOC_MOST + jnp.arange(DOC_MOST + block_rows, dtype=jnp.int32)
        visible = (key_place[None, :] >= doc_begin[:, None]) & (key_place[None, :] <= query_place[:, None])
        scores = low_back(jnp.einsum('qhd,khd->hqk', query_rows, key_rows, precision=lax.Precision.HIGHEST) * scaling)
        expweights = jnp.where(visible[None], jnp.exp(scores), 0.0)
        denominator = lax.optimization_barrier(jnp.sum(expweights, axis=-1))
        numerator = jnp.einsum('hqk,khd->qhd', low(expweights), value_rows, precision=lax.Precision.HIGHEST)
        return numerator / denominator.T[:, :, None]
    firsts = jnp.arange(0, TOKENS, block_rows, dtype=jnp.int32)
    blocks = lax.map(jax.checkpoint(one_block), firsts)
    return blocks.reshape(TOKENS, HEADS * HEAD_DIM)

def layer(stream_in, starts, active, weights):
    ln1_gain, ln1_shift, q_weight, q_bias, k_weight, v_weight, v_bias, o_weight, o_bias, ln2_gain, ln2_shift, up_weight, up_bias, down_weight, down_bias = weights
    normed_one = low(layer_norm(stream_in, ln1_gain, ln1_shift))
    queries = low(low_back(product(normed_one, q_weight) + q_bias))
    keyset = low(low_back(product(normed_one, k_weight)))
    values = low(low_back(product(normed_one, v_weight) + v_bias))
    head_out = low(low_back(attention(queries, keyset, values, starts)))
    middle = stream_in + low_back(product(head_out, o_weight) + o_bias)
    normed_two = low(layer_norm(middle, ln2_gain, ln2_shift))
    pre_act = low_back(product(normed_two, up_weight) + up_bias)
    hidden = low(jax.nn.gelu(pre_act, approximate=True))
    branch = low_back(product(hidden, down_weight) + down_bias)
    return jnp.where(active[:, None], middle + branch, stream_in)

def reference(tokens, doc_start, exit_layer, cotangent, ln1_gain, ln1_shift, q_weight, q_bias, k_weight, v_weight, v_bias, o_weight, o_bias, ln2_gain, ln2_shift, up_weight, up_bias, down_weight, down_bias):
    position = stream_place(jnp.arange(TOKENS, dtype=jnp.int32), TOK_DEV, TOKENS)
    holder = jnp.zeros((TOKENS,), jnp.int32).at[position].set(jnp.arange(TOKENS, dtype=jnp.int32))
    stream_in = tokens.astype(jnp.float32)[holder]
    starts = doc_start[holder]
    active = exit_layer[holder] > LAYER
    cot_stream = cotangent.astype(jnp.float32)[holder]
    params = tuple((array_in.astype(jnp.float32) for array_in in (ln1_gain, ln1_shift, q_weight, q_bias, k_weight, v_weight, v_bias, o_weight, o_bias, ln2_gain, ln2_shift, up_weight, up_bias, down_weight, down_bias)))

    def forward(stream_arg, *weights):
        return layer(stream_arg, starts, active, weights)
    result, pullback = jax.vjp(forward, stream_in, *params)
    gradients = pullback(cot_stream)
    return (result[position].astype(jnp.bfloat16), gradients[0][position], gradients[1], gradients[2], gradients[3], gradients[4], gradients[5], gradients[6], gradients[7], gradients[8].T, gradients[9], gradients[10], gradients[11], gradients[12], gradients[13], gradients[14].T, gradients[15])
```

```python
import math

import jax
import jax.numpy as jnp
from jax import lax
from jax.sharding import Mesh, PartitionSpec as P

HEAD_DIM = 64
LAYER = 6
CTX = ("x", "y", "zh", "core")
CHIPS = ("x", "y", "zh")
PLANE = ("x", "y")


epsilon = 1e-05
trans_right = (((1,), (1,)), ((), ()))
trans_left = (((0,), (0,)), ((), ()))
sub_rows = 2048
cubic_coef = 0.044715


def gelu_pair(values):
    outer = math.sqrt(2.0 / math.pi)
    inner = outer * (values + cubic_coef * values * values * values)
    tangent = jnp.tanh(inner)
    result = 0.5 * values * (1.0 + tangent)
    gelu_slope = 0.5 * (1.0 + tangent) + 0.5 * values * (1.0 - tangent * tangent) * outer * (
        1.0 + 3.0 * cubic_coef * values * values
    )
    return (result, gelu_slope)


def stream_place(row_ids, per_device, stream_len):
    half_rows = per_device // 2
    device = row_ids // per_device
    within = row_ids % per_device
    return jnp.where(
        within < half_rows,
        device * half_rows + within,
        stream_len - (device + 1) * half_rows + within - half_rows,
    )


def norm_forward(values, gain_vec, shift_vec):
    average = jnp.mean(values, axis=-1, keepdims=True)
    centred = values - average
    inverse_std = lax.rsqrt(jnp.mean(centred * centred, axis=-1, keepdims=True) + epsilon)
    normed = centred * inverse_std
    return (normed * gain_vec + shift_vec, normed, inverse_std)


def norm_backward(grad_out, normed, inverse_std, gain_vec):
    scaled = grad_out * gain_vec
    return inverse_std * (
        scaled
        - jnp.mean(scaled, axis=-1, keepdims=True)
        - normed * jnp.mean(scaled * normed, axis=-1, keepdims=True)
    )


def swap_add(part, axis):
    other = lax.ppermute(part, axis, ((0, 1), (1, 0)))
    return part.astype(jnp.float32) + other.astype(jnp.float32)


def sum_vectors(vectors):
    sizes = [vector.shape[0] for vector in vectors]
    rows = jnp.concatenate(vectors).reshape(-1, 128)
    rows = swap_add(rows, "core")
    plane = lax.axis_size(PLANE)
    copies = jnp.broadcast_to(rows[None], (plane,) + rows.shape)
    rows = jnp.sum(lax.all_to_all(copies, PLANE, 0, 0, tiled=True), axis=0)
    rows = swap_add(rows, "zh").reshape(-1)
    ends = [sum(sizes[: i + 1]) for i in range(len(sizes))]
    return [rows[end - size : end] for end, size in zip(ends, sizes, strict=True)]


def sum_products(pairs):
    parts = []
    for left, right in pairs:
        half = right.shape[1] // 2
        left_chip = lax.all_gather(left, "core", axis=0, tiled=True)
        right_chip = lax.all_to_all(right, "core", 1, 0, tiled=True)
        parts.append(
            lax.dot_general(
                left_chip, right_chip, trans_left, preferred_element_type=jnp.float32
            ).astype(jnp.bfloat16)
        )
    chips = lax.axis_size(CHIPS)
    joined = jnp.concatenate(parts, axis=1)
    joined = joined.reshape(chips, joined.shape[0] // chips, joined.shape[1])
    received = lax.all_to_all(joined, CHIPS, 0, 0, tiled=True)
    summed = jnp.sum(received.astype(jnp.float32), axis=0)
    outs = []
    begin = 0
    for left, right in pairs:
        half = right.shape[1] // 2
        outs.append(
            lax.all_to_all(summed[:, begin : begin + half], "core", 0, 1, tiled=True)
        )
        begin += half
    return outs


def by_blocks(step_fn, running, row_total):

    def one_step(index, state):
        return step_fn(state, index * sub_rows, sub_rows)

    return lax.fori_loop(0, row_total // sub_rows, one_step, running)


def attend_block(query_rows, key_rows, visible, scaling):
    scores = (
        jnp.einsum("qhd,khd->hqk", query_rows, key_rows, preferred_element_type=jnp.float32)
        * scaling
    )
    return jnp.where(visible[None], jnp.exp(scores), 0.0)


def block_grads(query_rows, dhead_rows, denoms, row_dot, key_rows, value_rows, visible, scaling):
    expweights = attend_block(query_rows, key_rows, visible, scaling)
    reciprocal = 1.0 / denoms
    dprob = jnp.einsum("qhd,khd->hqk", dhead_rows, value_rows, preferred_element_type=jnp.float32)
    dscore = (expweights * (dprob - row_dot.T[:, :, None]) * reciprocal.T[:, :, None]).astype(
        jnp.bfloat16
    )
    query_grad = (
        jnp.einsum("hqk,khd->qhd", dscore, key_rows, preferred_element_type=jnp.float32) * scaling
    )
    key_grad = (
        jnp.einsum("hqk,qhd->khd", dscore, query_rows, preferred_element_type=jnp.float32) * scaling
    )
    dnumer = dhead_rows.astype(jnp.float32) * reciprocal[:, :, None]
    upper_part = dnumer.astype(jnp.bfloat16)
    lower_part = (dnumer - upper_part.astype(jnp.float32)).astype(jnp.bfloat16)
    rounded = expweights.astype(jnp.bfloat16)
    value_grad = jnp.einsum(
        "hqk,qhd->khd", rounded, upper_part, preferred_element_type=jnp.float32
    ) + jnp.einsum("hqk,qhd->khd", rounded, lower_part, preferred_element_type=jnp.float32)
    return (query_grad, key_grad, value_grad)


def on_device(
    tokens,
    doc_start,
    exit_layer,
    cotangent,
    ln1_gain,
    ln1_shift,
    q_weight,
    q_bias,
    k_weight,
    v_weight,
    v_bias,
    o_weight,
    o_bias,
    ln2_gain,
    ln2_shift,
    up_weight,
    up_bias,
    down_weight,
    down_bias,
):
    per_device, model_width = tokens.shape
    cycle_size = lax.axis_size(CTX)
    stream_len = per_device * cycle_size
    local_width = q_weight.shape[1]
    local_heads = local_width // HEAD_DIM
    local_hidden = up_weight.shape[1]
    scaling = 1.0 / math.sqrt(HEAD_DIM)
    cycle_index = lax.axis_index(CTX)
    own_rows = cycle_index * per_device + jnp.arange(per_device, dtype=jnp.int32)
    query_place = stream_place(own_rows, per_device, stream_len)
    active = exit_layer > LAYER
    stream_in = tokens.astype(jnp.float32)
    normed_one, unit_one, inv_one = norm_forward(stream_in, ln1_gain, ln1_shift)
    lowered_one = normed_one.astype(jnp.bfloat16)
    queries = (jnp.dot(lowered_one, q_weight, preferred_element_type=jnp.float32) + q_bias).astype(
        jnp.bfloat16
    )
    keyset = jnp.dot(lowered_one, k_weight, preferred_element_type=jnp.float32).astype(jnp.bfloat16)
    valueset = (jnp.dot(lowered_one, v_weight, preferred_element_type=jnp.float32) + v_bias).astype(
        jnp.bfloat16
    )
    query_heads = queries.reshape(per_device, local_heads, HEAD_DIM)
    key_value = jnp.concatenate([keyset, valueset], axis=1)

    def split_pairs(rows_kv):
        row_total = rows_kv.shape[0]
        return (
            rows_kv[:, :local_width].reshape(row_total, local_heads, HEAD_DIM),
            rows_kv[:, local_width:].reshape(row_total, local_heads, HEAD_DIM),
        )

    def key_visible(begin_row, row_total):
        key_place = stream_place(
            begin_row + jnp.arange(row_total, dtype=jnp.int32), per_device, stream_len
        )
        return (key_place[None, :] >= doc_start[:, None]) & (
            key_place[None, :] <= query_place[:, None]
        )

    start_state = (
        jnp.zeros((per_device, local_heads, HEAD_DIM), jnp.float32),
        jnp.zeros((per_device, local_heads), jnp.float32),
    )
    shard_rows = lax.all_gather(key_value, CTX, axis=0, tiled=True)

    def step_fn(state, offset, size_rows):
        block_kv = lax.dynamic_slice_in_dim(shard_rows, offset, size_rows, 0)
        key_rows, value_rows = split_pairs(block_kv)
        visible = key_visible(offset, size_rows)

        def accumulate(inner):
            numer_acc, denom_acc = inner
            expweights = attend_block(query_heads, key_rows, visible, scaling)
            numer_acc = numer_acc + jnp.einsum(
                "hqk,khd->qhd",
                expweights.astype(jnp.bfloat16),
                value_rows,
                preferred_element_type=jnp.float32,
            )
            return (numer_acc, denom_acc + jnp.sum(expweights, axis=-1).T)

        return accumulate(state)

    numerator, denominators = by_blocks(step_fn, start_state, shard_rows.shape[0])
    attn_full = numerator / denominators[:, :, None]
    attn_low = attn_full.reshape(per_device, local_width).astype(jnp.bfloat16)
    attn_out = (
        swap_add(jnp.dot(attn_low, o_weight, preferred_element_type=jnp.float32), "wa") + o_bias
    )
    middle = stream_in + attn_out
    normed_two, unit_two, inv_two = norm_forward(middle, ln2_gain, ln2_shift)
    lowered_two = normed_two.astype(jnp.bfloat16)
    pre_act = jnp.dot(lowered_two, up_weight, preferred_element_type=jnp.float32) + up_bias
    hidden_full, gelu_slope = gelu_pair(pre_act)
    hidden = hidden_full.astype(jnp.bfloat16)
    ffn_out = (
        swap_add(
            jnp.dot(hidden, down_weight, preferred_element_type=jnp.float32).astype(jnp.bfloat16),
            "wa",
        )
        + down_bias
    )
    output = jnp.where(active[:, None], middle + ffn_out, stream_in).astype(jnp.bfloat16)
    cot_stream = cotangent.astype(jnp.float32)
    branch_grad = jnp.where(active[:, None], cot_stream, 0.0)
    branch_low = branch_grad.astype(jnp.bfloat16)
    dhidden = lax.dot_general(
        branch_low, down_weight, trans_right, preferred_element_type=jnp.float32
    )
    dpre_low = (dhidden * gelu_slope).astype(jnp.bfloat16)
    dnormed_two = swap_add(
        lax.dot_general(dpre_low, up_weight, trans_right, preferred_element_type=jnp.float32), "wa"
    )
    dmiddle = branch_grad + norm_backward(dnormed_two, unit_two, inv_two, ln2_gain)
    dattn_low = dmiddle.astype(jnp.bfloat16)
    dheads_low = lax.dot_general(
        dattn_low, o_weight, trans_right, preferred_element_type=jnp.float32
    ).astype(jnp.bfloat16)
    dhead_heads = dheads_low.reshape(per_device, local_heads, HEAD_DIM)
    row_dot = jnp.sum(dhead_heads.astype(jnp.float32) * attn_full, axis=-1)
    back_state = (
        jnp.zeros((per_device, local_heads, HEAD_DIM), jnp.float32),
        jnp.zeros((stream_len, 2 * local_width), jnp.float32),
    )
    key_shard_rows = lax.all_gather(key_value, CTX, axis=0, tiled=True)

    def step_fn(state, offset, size_rows):
        block_kv = lax.dynamic_slice_in_dim(key_shard_rows, offset, size_rows, 0)
        key_rows, value_rows = split_pairs(block_kv)
        target = offset
        visible = key_visible(target, size_rows)

        def accumulate(inner):
            query_acc, pair_all = inner
            query_grad, key_grad, value_grad = block_grads(
                query_heads,
                dhead_heads,
                denominators,
                row_dot,
                key_rows,
                value_rows,
                visible,
                scaling,
            )
            addend = jnp.concatenate(
                [
                    key_grad.reshape(size_rows, local_width),
                    value_grad.reshape(size_rows, local_width),
                ],
                axis=1,
            )
            previous = lax.dynamic_slice_in_dim(pair_all, target, size_rows, 0)
            return (
                query_acc + query_grad,
                lax.dynamic_update_slice_in_dim(pair_all, previous + addend, target, 0),
            )

        return accumulate(state)

    query_acc, pair_all = by_blocks(step_fn, back_state, key_shard_rows.shape[0])
    pair_sum = lax.psum_scatter(pair_all, CTX, scatter_dimension=0, tiled=True)
    query_sum = query_acc.reshape(per_device, local_width)
    query_low = query_sum.astype(jnp.bfloat16)
    key_low = pair_sum[:, :local_width].astype(jnp.bfloat16)
    value_low = pair_sum[:, local_width:].astype(jnp.bfloat16)
    dnormed_part = (
        lax.dot_general(query_low, q_weight, trans_right, preferred_element_type=jnp.float32)
        + lax.dot_general(key_low, k_weight, trans_right, preferred_element_type=jnp.float32)
        + lax.dot_general(value_low, v_weight, trans_right, preferred_element_type=jnp.float32)
    )
    dnormed_one = swap_add(dnormed_part.astype(jnp.bfloat16), "wa")
    input_grad = (
        dmiddle
        + norm_backward(dnormed_one, unit_one, inv_one, ln1_gain)
        + jnp.where(active[:, None], 0.0, cot_stream)
    )
    small_terms = (
        jnp.sum(query_low.astype(jnp.float32), axis=0),
        jnp.sum(value_low.astype(jnp.float32), axis=0),
        jnp.sum(dpre_low.astype(jnp.float32), axis=0),
        jnp.sum(dattn_low.astype(jnp.float32), axis=0),
        jnp.sum(branch_grad, axis=0),
        jnp.sum(dnormed_one * unit_one, axis=0),
        jnp.sum(dnormed_one, axis=0),
        jnp.sum(dnormed_two * unit_two, axis=0),
        jnp.sum(dnormed_two, axis=0),
    )
    (
        q_bias_grad,
        v_bias_grad,
        up_bias_grad,
        o_bias_grad,
        down_bias_grad,
        ln1_gain_grad,
        ln1_shift_grad,
        ln2_gain_grad,
        ln2_shift_grad,
    ) = sum_vectors(small_terms)
    (
        q_weight_grad,
        k_weight_grad,
        v_weight_grad,
        o_weight_grad_t,
        up_weight_grad,
        down_weight_grad_t,
    ) = sum_products(
        (
            (lowered_one, query_low),
            (lowered_one, key_low),
            (lowered_one, value_low),
            (dattn_low, attn_low),
            (lowered_two, dpre_low),
            (branch_low, hidden),
        )
    )
    return (
        output,
        input_grad,
        ln1_gain_grad,
        ln1_shift_grad,
        q_weight_grad,
        q_bias_grad,
        k_weight_grad,
        v_weight_grad,
        v_bias_grad,
        o_weight_grad_t,
        o_bias_grad,
        ln2_gain_grad,
        ln2_shift_grad,
        up_weight_grad,
        up_bias_grad,
        down_weight_grad_t,
        down_bias_grad,
    )


def solution(mesh):
    fine = Mesh(mesh.devices.reshape(4, 4, 2, 2, 2), CTX + ("wa",))
    return jax.shard_map(
        on_device,
        mesh=fine,
        in_specs=(
            P(CTX, None),
            P(CTX),
            P(CTX),
            P(CTX, None),
            P(),
            P(),
            P(None, "wa"),
            P("wa"),
            P(None, "wa"),
            P(None, "wa"),
            P("wa"),
            P("wa", None),
            P(),
            P(),
            P(),
            P(None, "wa"),
            P("wa"),
            P("wa", None),
            P(),
        ),
        out_specs=(
            P(CTX, None),
            P(CTX, None),
            P(),
            P(),
            P(CTX, "wa"),
            P("wa"),
            P(CTX, "wa"),
            P(CTX, "wa"),
            P("wa"),
            P(CTX, "wa"),
            P(),
            P(),
            P(),
            P(CTX, "wa"),
            P("wa"),
            P(CTX, "wa"),
            P(),
        ),
        check_vma=False,
    )
```

```python
import math

import jax
import jax.numpy as jnp
from jax import lax
from jax.experimental import pallas as pl
from jax.experimental.pallas import tpu as pltpu
from jax.sharding import Mesh, PartitionSpec as P

HEAD_DIM = 64
LAYER = 6
CTX = ("x", "y", "zh", "core")
CHIPS = ("x", "y", "zh")
PLANE = ("x", "y")
HALF = 64
BLOCKS = 16
GROUP = 256
STREAM = 8192
ROWS = (BLOCKS + 1) * HALF
TILE = 256
FAR = 1e9
SCALING = 1.0 / math.sqrt(HEAD_DIM)
EXP2_SCALE = SCALING / math.log(2.0)
VMEM_BYTES = 48 * 2**20


epsilon = 1e-05
trans_right = (((1,), (1,)), ((), ()))
trans_left = (((0,), (0,)), ((), ()))
cubic_coef = 0.044715


def gelu_pair(values):
    outer = math.sqrt(2.0 / math.pi)
    inner = outer * (values + cubic_coef * values * values * values)
    tangent = jnp.tanh(inner)
    result = 0.5 * values * (1.0 + tangent)
    gelu_slope = 0.5 * (1.0 + tangent) + 0.5 * values * (1.0 - tangent * tangent) * outer * (
        1.0 + 3.0 * cubic_coef * values * values
    )
    return (result, gelu_slope)


def norm_forward(values, gain_vec, shift_vec):
    average = jnp.mean(values, axis=-1, keepdims=True)
    centred = values - average
    inverse_std = lax.rsqrt(jnp.mean(centred * centred, axis=-1, keepdims=True) + epsilon)
    normed = centred * inverse_std
    return (normed * gain_vec + shift_vec, normed, inverse_std)


def norm_backward(grad_out, normed, inverse_std, gain_vec):
    scaled = grad_out * gain_vec
    return inverse_std * (
        scaled
        - jnp.mean(scaled, axis=-1, keepdims=True)
        - normed * jnp.mean(scaled * normed, axis=-1, keepdims=True)
    )


def swap_add(part, axis):
    other = lax.ppermute(part, axis, ((0, 1), (1, 0)))
    return part.astype(jnp.float32) + other.astype(jnp.float32)


def sum_vectors(vectors):
    sizes = [vector.shape[0] for vector in vectors]
    rows = jnp.concatenate(vectors).reshape(-1, 128)
    rows = swap_add(rows, "core")
    plane = lax.axis_size(PLANE)
    copies = jnp.broadcast_to(rows[None], (plane,) + rows.shape)
    rows = jnp.sum(lax.all_to_all(copies, PLANE, 0, 0, tiled=True), axis=0)
    rows = swap_add(rows, "zh").reshape(-1)
    ends = [sum(sizes[: i + 1]) for i in range(len(sizes))]
    return [rows[end - size : end] for end, size in zip(ends, sizes, strict=True)]


def sum_products(pairs):
    parts = []
    for left, right in pairs:
        half = right.shape[1] // 2
        left_chip = lax.all_gather(left, "core", axis=0, tiled=True)
        right_chip = lax.all_to_all(right, "core", 1, 0, tiled=True)
        parts.append(
            lax.dot_general(
                left_chip, right_chip, trans_left, preferred_element_type=jnp.float32
            ).astype(jnp.bfloat16)
        )
    chips = lax.axis_size(CHIPS)
    joined = jnp.concatenate(parts, axis=1)
    joined = joined.reshape(chips, joined.shape[0] // chips, joined.shape[1])
    received = lax.all_to_all(joined, CHIPS, 0, 0, tiled=True)
    summed = jnp.sum(received.astype(jnp.float32), axis=0)
    outs = []
    begin = 0
    for left, right in pairs:
        half = right.shape[1] // 2
        outs.append(
            lax.all_to_all(summed[:, begin : begin + half], "core", 0, 1, tiled=True)
        )
        begin += half
    return outs


def lane_ids(rows, cols):
    return lax.broadcasted_iota(jnp.int32, (rows, cols), 1)


def row_ids_of(rows, cols):
    return lax.broadcasted_iota(jnp.int32, (rows, cols), 0)


def turn(values):
    return pltpu.roll(values, HALF, 1)


def unpack_low(packed):
    wide = packed.astype(jnp.float32)
    left = lane_ids(32, 128) < HALF
    both = jnp.concatenate([wide, turn(wide)], axis=0)
    return jnp.where(jnp.concatenate([left, left], axis=0), both, 0.0)


def unpack_high(packed):
    wide = packed.astype(jnp.float32)
    right = lane_ids(32, 128) >= HALF
    both = jnp.concatenate([turn(wide), wide], axis=0)
    return jnp.where(jnp.concatenate([right, right], axis=0), both, 0.0)


def pack_from_low(block):
    return jnp.where(lane_ids(32, 128) < HALF, block[:32], turn(block[32:]))


def pack_from_high(block):
    return jnp.where(lane_ids(32, 128) < HALF, turn(block[:32]), block[32:])


def key_places(scal_ref, group):
    lane = lane_ids(8, GROUP)
    sub = (lane >> 6) ^ scal_ref[1]
    return (scal_ref[0] * (STREAM // 2) + GROUP * group + (sub << 6) + (lane & 63)).astype(
        jnp.float32
    )


def edge_places():
    return (STREAM // 2 + lane_ids(8, 128)).astype(jnp.float32)


def query_places(scal_ref, block):
    row = row_ids_of(HALF, 128)
    return (
        scal_ref[0] * (STREAM // 2) + GROUP * block + (scal_ref[1] << 6) + row
    ).astype(jnp.float32)


def spread(rows, width):
    return jnp.concatenate([rows] * (width // 128), axis=1) if width > 128 else rows


def tiles_of(group):
    first = group * HALF
    ranges = [(first, HALF, True)]
    begin = first + HALF
    while begin < ROWS:
        count = min(TILE, ROWS - begin)
        ranges.append((begin, count, False))
        begin += count
    return ranges


def weights_of(scal_ref, q_ref, start_ref, keys, places, begin, count, diagonal, group):
    scores = lax.dot_general(
        q_ref[begin : begin + count], keys, trans_right, preferred_element_type=jnp.float32
    )
    width = keys.shape[0]
    seen = spread(start_ref[begin : begin + count], width) <= places[:1]
    if diagonal:
        seen = seen & (places[:1] <= spread(query_places(scal_ref, group), width))
    return jnp.where(seen, jnp.exp2(scores * EXP2_SCALE), 0.0)


def attend_kernel(
    scal_ref, own_ref, one_ref, two_ref, three_ref, edge_ref,
    back_ref, kv_ref, q_ref, start_ref, full_ref, recip_ref,
    num_ref, den_ref,
):
    upper = scal_ref[0]
    diag = jnp.where(
        lane_ids(HALF, 128) == row_ids_of(HALF, 128),
        64.0,
        jnp.where(lane_ids(HALF, 128) == row_ids_of(HALF, 128) + HALF, 1.0, 0.0),
    )

    def starts(line, off):
        found = jnp.sum(line.astype(jnp.float32) * diag, axis=1, keepdims=True)
        return jnp.broadcast_to(jnp.where(off, FAR, found), (HALF, 128))

    for block in range(BLOCKS):
        place = jnp.where(upper == 1, BLOCKS - 1 - block, block)
        rows = slice(block * HALF, (block + 1) * HALF)
        mine = own_ref[pl.ds(place, 1)][0]
        kv_ref[block, 0:HALF] = mine[:HALF]
        kv_ref[block, HALF : 2 * HALF] = one_ref[pl.ds(place, 1)][0]
        kv_ref[block, 2 * HALF : 3 * HALF] = two_ref[pl.ds(place, 1)][0]
        kv_ref[block, 3 * HALF :] = three_ref[pl.ds(place, 1)][0]
        q_ref[rows] = unpack_low(mine[HALF : HALF + 32]).astype(jnp.bfloat16)
        off = (scal_ref[3] == 1) if block == 0 else False
        start_ref[rows] = starts(mine[HALF + 32 : HALF + 33], off)
    kv_ref[BLOCKS] = jnp.zeros((GROUP, 128), jnp.bfloat16)
    kv_ref[BLOCKS, :HALF] = edge_ref[:HALF]
    q_ref[BLOCKS * HALF :] = unpack_low(edge_ref[HALF : HALF + 32]).astype(jnp.bfloat16)
    start_ref[BLOCKS * HALF :] = starts(edge_ref[HALF + 32 : HALF + 33], scal_ref[2] == 0)

    for group in range(BLOCKS + 1):
        if group < BLOCKS:
            keys = kv_ref[group]
            places = key_places(scal_ref, group)
            ranges = tiles_of(group)
        else:
            keys = kv_ref[group, :128]
            places = edge_places()
            ranges = [(BLOCKS * HALF, HALF, False)]
        for begin, count, diagonal in ranges:
            rows = slice(begin, begin + count)
            if group == BLOCKS:
                scores = lax.dot_general(
                    q_ref[rows], keys, trans_right, preferred_element_type=jnp.float32
                )
                seen = (start_ref[rows] <= places[:1]) & (
                    places[:1] <= (STREAM // 2 + row_ids_of(HALF, 128)).astype(jnp.float32)
                )
                weights = jnp.where(seen, jnp.exp2(scores * EXP2_SCALE), 0.0)
                total = weights
            else:
                weights = weights_of(
                    scal_ref, q_ref, start_ref, keys, places, begin, count, diagonal, group
                )
                total = weights[:, :128] + weights[:, 128:]
            product = jnp.dot(
                weights.astype(jnp.bfloat16), keys, preferred_element_type=jnp.float32
            )
            if group == 0:
                num_ref[rows] = product
                den_ref[rows] = total
            else:
                num_ref[rows] += product
                den_ref[rows] += total

    for block in range(BLOCKS + 1):
        rows = slice(block * HALF, (block + 1) * HALF)
        den = jnp.sum(den_ref[rows], axis=1, keepdims=True)
        recip = jnp.broadcast_to(1.0 / jnp.where(den == 0.0, 1.0, den), (HALF, 128))
        recip_ref[rows] = recip
        full = jnp.where(lane_ids(HALF, 128) < HALF, 0.0, num_ref[rows] * recip)
        full_ref[rows] = full
        packed = pack_from_high(full).astype(jnp.bfloat16)
        if block < BLOCKS:
            place = jnp.where(upper == 1, BLOCKS - 1 - block, block)
            back_ref[pl.ds(place, 1), :32] = packed[None]
            back_ref[pl.ds(place, 1), 32:] = jnp.zeros((1, 32, 128), jnp.bfloat16)
        else:
            back_ref[BLOCKS - 1, 32:] = packed


def attend_grad_kernel(
    scal_ref, kv_ref, q_ref, start_ref, full_ref, recip_ref, dh_in_ref,
    mine_ref, one_ref, two_ref, three_ref, dq_ref, edge_ref,
    dh_ref, dhn_ref, dot_ref, dq_acc,
):
    upper = scal_ref[0]
    for block in range(BLOCKS + 1):
        rows = slice(block * HALF, (block + 1) * HALF)
        if block < BLOCKS:
            place = jnp.where(upper == 1, BLOCKS - 1 - block, block)
            packed = dh_in_ref[pl.ds(place, 1), :32][0]
        else:
            packed = dh_in_ref[BLOCKS - 1, 32:]
        dheads = unpack_high(packed)
        dh_ref[rows] = dheads.astype(jnp.bfloat16)
        dhn_ref[rows] = (dheads * recip_ref[rows]).astype(jnp.bfloat16)
        dot_ref[rows] = jnp.broadcast_to(
            jnp.sum(dheads * full_ref[rows], axis=1, keepdims=True), (HALF, 128)
        )

    for group in range(BLOCKS + 1):
        if group < BLOCKS:
            keys = kv_ref[group]
            places = key_places(scal_ref, group)
            ranges = tiles_of(group)
        else:
            keys = kv_ref[group, :128]
            places = edge_places()
            ranges = [(BLOCKS * HALF, HALF, False)]
        width = keys.shape[0]
        grads = None
        for begin, count, diagonal in ranges:
            rows = slice(begin, begin + count)
            scores = lax.dot_general(
                q_ref[rows], keys, trans_right, preferred_element_type=jnp.float32
            )
            seen = spread(start_ref[rows], width) <= places[:1]
            if diagonal:
                seen = seen & (places[:1] <= spread(query_places(scal_ref, group), width))
            if group == BLOCKS:
                seen = seen & (
                    places[:1] <= (STREAM // 2 + row_ids_of(HALF, 128)).astype(jnp.float32)
                )
            weights = jnp.where(seen, jnp.exp2(scores * EXP2_SCALE), 0.0)
            dprob = lax.dot_general(
                dh_ref[rows], keys, trans_right, preferred_element_type=jnp.float32
            )
            dscore = (
                weights
                * (dprob - spread(dot_ref[rows], width))
                * spread(recip_ref[rows], width)
            ).astype(jnp.bfloat16)
            dquery = jnp.dot(dscore, keys, preferred_element_type=jnp.float32)
            if group == 0:
                dq_acc[rows] = dquery
            else:
                dq_acc[rows] += dquery
            term = lax.dot_general(
                dscore, q_ref[rows], trans_left, preferred_element_type=jnp.float32
            ) * SCALING + lax.dot_general(
                weights.astype(jnp.bfloat16),
                dhn_ref[rows],
                trans_left,
                preferred_element_type=jnp.float32,
            )
            grads = term if grads is None else grads + term
        low = grads.astype(jnp.bfloat16)
        if group < BLOCKS:
            place = jnp.where(upper == 1, BLOCKS - 1 - group, group)
            for quarter, out in enumerate((mine_ref, one_ref, two_ref, three_ref)):
                out[pl.ds(place, 1)] = low[None, quarter * HALF : (quarter + 1) * HALF]
        else:
            edge_ref[:HALF] = low[:HALF]

    for block in range(BLOCKS + 1):
        rows = slice(block * HALF, (block + 1) * HALF)
        packed = pack_from_low(dq_acc[rows] * SCALING).astype(jnp.bfloat16)
        if block < BLOCKS:
            place = jnp.where(upper == 1, BLOCKS - 1 - block, block)
            dq_ref[pl.ds(place, 1)] = packed[None]
        else:
            edge_ref[HALF:] = packed


def whole(*shape, dtype=jnp.bfloat16):
    return jax.ShapeDtypeStruct(shape, dtype)


def attend(scal, own, one, two, three, edge):
    vmem = pl.BlockSpec(memory_space=pltpu.VMEM)
    return pl.pallas_call(
        attend_kernel,
        out_shape=(
            whole(BLOCKS, 64, 128),
            whole(BLOCKS + 1, GROUP, 128),
            whole(ROWS, 128),
            whole(ROWS, 128, dtype=jnp.float32),
            whole(ROWS, 128, dtype=jnp.float32),
            whole(ROWS, 128, dtype=jnp.float32),
        ),
        in_specs=[pl.BlockSpec(memory_space=pltpu.SMEM)] + [vmem] * 5,
        out_specs=[vmem] * 6,
        scratch_shapes=[
            pltpu.VMEM((ROWS, 128), jnp.float32),
            pltpu.VMEM((ROWS, 128), jnp.float32),
        ],
        compiler_params=pltpu.CompilerParams(vmem_limit_bytes=VMEM_BYTES),
        name="attend",
    )(scal, own, one, two, three, edge)


def attend_grad(scal, kv, q, start, full, recip, dh):
    vmem = pl.BlockSpec(memory_space=pltpu.VMEM)
    return pl.pallas_call(
        attend_grad_kernel,
        out_shape=(
            whole(BLOCKS, HALF, 128),
            whole(BLOCKS, HALF, 128),
            whole(BLOCKS, HALF, 128),
            whole(BLOCKS, HALF, 128),
            whole(BLOCKS, 32, 128),
            whole(96, 128),
        ),
        in_specs=[pl.BlockSpec(memory_space=pltpu.SMEM)] + [vmem] * 6,
        out_specs=[vmem] * 6,
        scratch_shapes=[
            pltpu.VMEM((ROWS, 128), jnp.bfloat16),
            pltpu.VMEM((ROWS, 128), jnp.bfloat16),
            pltpu.VMEM((ROWS, 128), jnp.float32),
            pltpu.VMEM((ROWS, 128), jnp.float32),
        ],
        compiler_params=pltpu.CompilerParams(vmem_limit_bytes=VMEM_BYTES),
        name="attend_grad",
    )(scal, kv, q, start, full, recip, dh)


def pack_rows(block):
    return jnp.concatenate([block[..., :32, :], block[..., 32:, :]], axis=-1)


def unpack_rows(packed):
    return jnp.concatenate([packed[..., :HEAD_DIM], packed[..., HEAD_DIM:]], axis=-2)


def by_heads(rows):
    return rows.reshape(2, HALF, -1, HEAD_DIM).transpose(2, 0, 1, 3)


def by_rows(blocks):
    return blocks.transpose(1, 2, 0, 3).reshape(2 * HALF, -1)


def to_plane(blocks):
    spare = jnp.zeros((4,) + blocks.shape[1:], blocks.dtype)
    return lax.all_to_all(jnp.concatenate([blocks, spare]), PLANE, 0, 0, tiled=True)


def to_rows(blocks):
    return lax.all_to_all(blocks, PLANE, 0, 0, tiled=True)[:12]


def on_device(
    tokens,
    doc_start,
    exit_layer,
    cotangent,
    ln1_gain,
    ln1_shift,
    q_weight,
    q_bias,
    k_weight,
    v_weight,
    v_bias,
    o_weight,
    o_bias,
    ln2_gain,
    ln2_shift,
    up_weight,
    up_bias,
    down_weight,
    down_bias,
):
    swap = ((0, 1), (1, 0))
    cross = ((0, 3), (1, 2), (2, 1), (3, 0))
    plane_index = lax.axis_index(PLANE)
    sub_index = lax.axis_index(("zh", "core"))
    upper = plane_index % 2
    scal = jnp.stack(
        [
            upper,
            jnp.bitwise_xor(sub_index, 3 * upper),
            jnp.where((upper == 0) & (sub_index == 3), 1, 0),
            jnp.where((upper == 1) & (sub_index == 3), 1, 0),
        ]
    ).astype(jnp.int32)
    active = exit_layer > LAYER
    stream_in = tokens.astype(jnp.float32)
    normed_one, unit_one, inv_one = norm_forward(stream_in, ln1_gain, ln1_shift)
    lowered_one = normed_one.astype(jnp.bfloat16)
    queries = (jnp.dot(lowered_one, q_weight, preferred_element_type=jnp.float32) + q_bias).astype(
        jnp.bfloat16
    )
    keyset = jnp.dot(lowered_one, k_weight, preferred_element_type=jnp.float32).astype(jnp.bfloat16)
    valueset = (jnp.dot(lowered_one, v_weight, preferred_element_type=jnp.float32) + v_bias).astype(
        jnp.bfloat16
    )
    heads = queries.shape[1] // HEAD_DIM
    starts = jnp.concatenate([doc_start // 64, doc_start % 64]).astype(jnp.bfloat16)
    starts = starts.reshape(2, 2, HALF).transpose(1, 0, 2).reshape(1, 2, 1, 128)
    starts = jnp.broadcast_to(starts, (heads, 2, 16, 128))
    payload = jnp.concatenate(
        [
            jnp.concatenate([by_heads(keyset), by_heads(valueset)], axis=-1),
            pack_rows(by_heads(queries)),
            starts,
        ],
        axis=2,
    ).reshape(2 * heads, HALF + 48, 128)
    own = to_plane(payload)
    pairs = own[:, :HALF]
    one = lax.ppermute(pairs, "core", swap)
    two = lax.ppermute(pairs, "zh", swap)
    three = lax.ppermute(pairs, ("zh", "core"), cross)
    edge = lax.ppermute(own[BLOCKS - 1], "y", ((1, 0), (3, 2)))
    back, kv, q_rows, start_rows, full_rows, recip_rows = attend(scal, own, one, two, three, edge)
    got = to_rows(back).reshape(heads, 2, 2, 32, 128)
    attn_blocks = jnp.stack([got[:, 0, 0], got[:, 1, 0] + got[:, 0, 1]], axis=1)
    attn_low = by_rows(unpack_rows(attn_blocks))
    attn_out = (
        swap_add(jnp.dot(attn_low, o_weight, preferred_element_type=jnp.float32), "wa") + o_bias
    )
    middle = stream_in + attn_out
    normed_two, unit_two, inv_two = norm_forward(middle, ln2_gain, ln2_shift)
    lowered_two = normed_two.astype(jnp.bfloat16)
    pre_act = jnp.dot(lowered_two, up_weight, preferred_element_type=jnp.float32) + up_bias
    hidden_full, gelu_slope = gelu_pair(pre_act)
    hidden = hidden_full.astype(jnp.bfloat16)
    ffn_out = (
        swap_add(
            jnp.dot(hidden, down_weight, preferred_element_type=jnp.float32).astype(jnp.bfloat16),
            "wa",
        )
        + down_bias
    )
    output = jnp.where(active[:, None], middle + ffn_out, stream_in).astype(jnp.bfloat16)
    cot_stream = cotangent.astype(jnp.float32)
    branch_grad = jnp.where(active[:, None], cot_stream, 0.0)
    branch_low = branch_grad.astype(jnp.bfloat16)
    dhidden = lax.dot_general(
        branch_low, down_weight, trans_right, preferred_element_type=jnp.float32
    )
    dpre_low = (dhidden * gelu_slope).astype(jnp.bfloat16)
    dnormed_two = swap_add(
        lax.dot_general(dpre_low, up_weight, trans_right, preferred_element_type=jnp.float32), "wa"
    )
    dmiddle = branch_grad + norm_backward(dnormed_two, unit_two, inv_two, ln2_gain)
    dattn_low = dmiddle.astype(jnp.bfloat16)
    dheads_low = lax.dot_general(
        dattn_low, o_weight, trans_right, preferred_element_type=jnp.float32
    ).astype(jnp.bfloat16)
    dhead_blocks = pack_rows(by_heads(dheads_low))
    dh = to_plane(
        jnp.concatenate(
            [dhead_blocks, jnp.broadcast_to(dhead_blocks[:, 1:], dhead_blocks.shape)], axis=2
        ).reshape(2 * heads, HALF, 128)
    )
    mine, give_one, give_two, give_three, dq, edge_grad = attend_grad(
        scal, kv, q_rows, start_rows, full_rows, recip_rows, dh
    )
    pair_sum = (
        mine.astype(jnp.float32)
        + lax.ppermute(give_one, "core", swap).astype(jnp.float32)
        + lax.ppermute(give_two, "zh", swap).astype(jnp.float32)
        + lax.ppermute(give_three, ("zh", "core"), cross).astype(jnp.float32)
    )
    edge_got = lax.ppermute(edge_grad, "y", ((0, 1), (2, 3)))
    last = jnp.concatenate([pair_sum[BLOCKS - 1], dq[BLOCKS - 1].astype(jnp.float32)])
    last = (last + edge_got.astype(jnp.float32)).astype(jnp.bfloat16)
    grads = jnp.concatenate([pair_sum.astype(jnp.bfloat16), dq], axis=1)
    grads = jnp.concatenate([grads[: BLOCKS - 1], last[None]])
    grads = to_rows(grads).reshape(heads, 2, 96, 128)
    key_low = by_rows(grads[:, :, :HALF, :HEAD_DIM])
    value_low = by_rows(grads[:, :, :HALF, HEAD_DIM:])
    query_low = by_rows(unpack_rows(grads[:, :, HALF:]))
    dnormed_part = (
        lax.dot_general(query_low, q_weight, trans_right, preferred_element_type=jnp.float32)
        + lax.dot_general(key_low, k_weight, trans_right, preferred_element_type=jnp.float32)
        + lax.dot_general(value_low, v_weight, trans_right, preferred_element_type=jnp.float32)
    )
    dnormed_one = swap_add(dnormed_part.astype(jnp.bfloat16), "wa")
    input_grad = (
        dmiddle
        + norm_backward(dnormed_one, unit_one, inv_one, ln1_gain)
        + jnp.where(active[:, None], 0.0, cot_stream)
    )
    small_terms = (
        jnp.sum(query_low.astype(jnp.float32), axis=0),
        jnp.sum(value_low.astype(jnp.float32), axis=0),
        jnp.sum(dpre_low.astype(jnp.float32), axis=0),
        jnp.sum(dattn_low.astype(jnp.float32), axis=0),
        jnp.sum(branch_grad, axis=0),
        jnp.sum(dnormed_one * unit_one, axis=0),
        jnp.sum(dnormed_one, axis=0),
        jnp.sum(dnormed_two * unit_two, axis=0),
        jnp.sum(dnormed_two, axis=0),
    )
    (
        q_bias_grad,
        v_bias_grad,
        up_bias_grad,
        o_bias_grad,
        down_bias_grad,
        ln1_gain_grad,
        ln1_shift_grad,
        ln2_gain_grad,
        ln2_shift_grad,
    ) = sum_vectors(small_terms)
    (
        q_weight_grad,
        k_weight_grad,
        v_weight_grad,
        o_weight_grad_t,
        up_weight_grad,
        down_weight_grad_t,
    ) = sum_products(
        (
            (lowered_one, query_low),
            (lowered_one, key_low),
            (lowered_one, value_low),
            (dattn_low, attn_low),
            (lowered_two, dpre_low),
            (branch_low, hidden),
        )
    )
    return (
        output,
        input_grad,
        ln1_gain_grad,
        ln1_shift_grad,
        q_weight_grad,
        q_bias_grad,
        k_weight_grad,
        v_weight_grad,
        v_bias_grad,
        o_weight_grad_t,
        o_bias_grad,
        ln2_gain_grad,
        ln2_shift_grad,
        up_weight_grad,
        up_bias_grad,
        down_weight_grad_t,
        down_bias_grad,
    )


def solution(mesh):
    fine = Mesh(mesh.devices.reshape(4, 4, 2, 2, 2), CTX + ("wa",))
    return jax.shard_map(
        on_device,
        mesh=fine,
        in_specs=(
            P(CTX, None),
            P(CTX),
            P(CTX),
            P(CTX, None),
            P(),
            P(),
            P(None, "wa"),
            P("wa"),
            P(None, "wa"),
            P(None, "wa"),
            P("wa"),
            P("wa", None),
            P(),
            P(),
            P(),
            P(None, "wa"),
            P("wa"),
            P("wa", None),
            P(),
        ),
        out_specs=(
            P(CTX, None),
            P(CTX, None),
            P(),
            P(),
            P(CTX, "wa"),
            P("wa"),
            P(CTX, "wa"),
            P(CTX, "wa"),
            P("wa"),
            P(CTX, "wa"),
            P(),
            P(),
            P(),
            P(CTX, "wa"),
            P("wa"),
            P(CTX, "wa"),
            P(),
        ),
        check_vma=False,
    )
```

```python
import functools
import math

import jax
import jax.numpy as jnp
from jax import lax
from jax.experimental import pallas as pl
from jax.experimental.pallas import tpu as pltpu
from jax.sharding import Mesh, PartitionSpec as P

HEAD_DIM = 64
LAYER = 6
CTX = ("x", "y", "zh", "core")
CHIPS = ("x", "y", "zh")
PLANE = ("x", "y")
SWAP = ((0, 1), (1, 0))
CROSS = ((0, 3), (1, 2), (2, 1), (3, 0))
HALF = 64
BLOCKS = 16
GROUP = 256
STREAM = 8192
ROWS = (BLOCKS + 1) * HALF
TILE = 256
FF_TILE = 512
FAR = 1e9
SCALING = 1.0 / math.sqrt(HEAD_DIM)
EXP2_SCALE = SCALING / math.log(2.0)
VMEM_BYTES = 48 * 2**20


epsilon = 1e-05
trans_right = (((1,), (1,)), ((), ()))
trans_left = (((0,), (0,)), ((), ()))
cubic_coef = 0.044715


def gelu_pair(values):
    outer = math.sqrt(2.0 / math.pi)
    inner = outer * (values + cubic_coef * values * values * values)
    tangent = jnp.tanh(inner)
    result = 0.5 * values * (1.0 + tangent)
    gelu_slope = 0.5 * (1.0 + tangent) + 0.5 * values * (1.0 - tangent * tangent) * outer * (
        1.0 + 3.0 * cubic_coef * values * values
    )
    return (result, gelu_slope)


def norm_forward(values, gain_vec, shift_vec):
    average = jnp.mean(values, axis=-1, keepdims=True)
    centred = values - average
    inverse_std = lax.rsqrt(jnp.mean(centred * centred, axis=-1, keepdims=True) + epsilon)
    normed = centred * inverse_std
    return (normed * gain_vec + shift_vec, normed, inverse_std)


def norm_backward(grad_out, normed, inverse_std, gain_vec):
    scaled = grad_out * gain_vec
    return inverse_std * (
        scaled
        - jnp.mean(scaled, axis=-1, keepdims=True)
        - normed * jnp.mean(scaled * normed, axis=-1, keepdims=True)
    )


def swap_add(part, axis):
    other = lax.ppermute(part, axis, SWAP)
    return part.astype(jnp.float32) + other.astype(jnp.float32)


def lane_ids(rows, cols):
    return lax.broadcasted_iota(jnp.int32, (rows, cols), 1)


def row_ids_of(rows, cols):
    return lax.broadcasted_iota(jnp.int32, (rows, cols), 0)


def turn(values):
    return pltpu.roll(values, HALF, 1)


def unpack_low(packed):
    wide = packed.astype(jnp.float32)
    left = lane_ids(32, 128) < HALF
    both = jnp.concatenate([wide, turn(wide)], axis=0)
    return jnp.where(jnp.concatenate([left, left], axis=0), both, 0.0)


def unpack_high(packed):
    wide = packed.astype(jnp.float32)
    right = lane_ids(32, 128) >= HALF
    both = jnp.concatenate([turn(wide), wide], axis=0)
    return jnp.where(jnp.concatenate([right, right], axis=0), both, 0.0)


def pack_from_low(block):
    return jnp.where(lane_ids(32, 128) < HALF, block[:32], turn(block[32:]))


def pack_from_high(block):
    return jnp.where(lane_ids(32, 128) < HALF, turn(block[:32]), block[32:])


def key_places(scal_ref, group):
    lane = lane_ids(8, GROUP)
    sub = (lane >> 6) ^ scal_ref[1]
    return (scal_ref[0] * (STREAM // 2) + GROUP * group + (sub << 6) + (lane & 63)).astype(
        jnp.float32
    )


def edge_places():
    return (STREAM // 2 + lane_ids(8, 128)).astype(jnp.float32)


def query_places(scal_ref, block):
    row = row_ids_of(HALF, 128)
    return (
        scal_ref[0] * (STREAM // 2) + GROUP * block + (scal_ref[1] << 6) + row
    ).astype(jnp.float32)


def spread(rows, width):
    return jnp.concatenate([rows] * (width // 128), axis=1) if width > 128 else rows


def tiles_of(group):
    first = group * HALF
    ranges = [(first, HALF, True)]
    begin = first + HALF
    while begin < ROWS:
        count = min(TILE, ROWS - begin)
        ranges.append((begin, count, False))
        begin += count
    return ranges


def weights_of(scal_ref, q_ref, start_ref, keys, places, begin, count, diagonal, group):
    scores = lax.dot_general(
        q_ref[begin : begin + count], keys, trans_right, preferred_element_type=jnp.float32
    )
    width = keys.shape[0]
    seen = spread(start_ref[begin : begin + count], width) <= places[:1]
    if diagonal:
        seen = seen & (places[:1] <= spread(query_places(scal_ref, group), width))
    return jnp.where(seen, jnp.exp2(scores * EXP2_SCALE), 0.0)


def attend_kernel(
    scal_ref, own_ref, one_ref, two_ref, three_ref, edge_ref,
    back_ref, kv_ref, q_ref, start_ref, full_ref, recip_ref,
    num_ref, den_ref,
):
    upper = scal_ref[0]
    diag = jnp.where(
        lane_ids(HALF, 128) == row_ids_of(HALF, 128),
        64.0,
        jnp.where(lane_ids(HALF, 128) == row_ids_of(HALF, 128) + HALF, 1.0, 0.0),
    )

    def starts(line, off):
        found = jnp.sum(line.astype(jnp.float32) * diag, axis=1, keepdims=True)
        return jnp.broadcast_to(jnp.where(off, FAR, found), (HALF, 128))

    for block in range(BLOCKS):
        place = jnp.where(upper == 1, BLOCKS - 1 - block, block)
        rows = slice(block * HALF, (block + 1) * HALF)
        mine = own_ref[pl.ds(place, 1)][0]
        kv_ref[block, 0:HALF] = mine[:HALF]
        kv_ref[block, HALF : 2 * HALF] = one_ref[pl.ds(place, 1)][0]
        kv_ref[block, 2 * HALF : 3 * HALF] = two_ref[pl.ds(place, 1)][0]
        kv_ref[block, 3 * HALF :] = three_ref[pl.ds(place, 1)][0]
        q_ref[rows] = unpack_low(mine[HALF : HALF + 32]).astype(jnp.bfloat16)
        off = (scal_ref[3] == 1) if block == 0 else False
        start_ref[rows] = starts(mine[HALF + 32 : HALF + 33], off)
    kv_ref[BLOCKS] = jnp.zeros((GROUP, 128), jnp.bfloat16)
    kv_ref[BLOCKS, :HALF] = edge_ref[:HALF]
    q_ref[BLOCKS * HALF :] = unpack_low(edge_ref[HALF : HALF + 32]).astype(jnp.bfloat16)
    start_ref[BLOCKS * HALF :] = starts(edge_ref[HALF + 32 : HALF + 33], scal_ref[2] == 0)

    for group in range(BLOCKS + 1):
        if group < BLOCKS:
            keys = kv_ref[group]
            places = key_places(scal_ref, group)
            ranges = tiles_of(group)
        else:
            keys = kv_ref[group, :128]
            places = edge_places()
            ranges = [(BLOCKS * HALF, HALF, False)]
        for begin, count, diagonal in ranges:
            rows = slice(begin, begin + count)
            if group == BLOCKS:
                scores = lax.dot_general(
                    q_ref[rows], keys, trans_right, preferred_element_type=jnp.float32
                )
                seen = (start_ref[rows] <= places[:1]) & (
                    places[:1] <= (STREAM // 2 + row_ids_of(HALF, 128)).astype(jnp.float32)
                )
                weights = jnp.where(seen, jnp.exp2(scores * EXP2_SCALE), 0.0)
                total = weights
            else:
                weights = weights_of(
                    scal_ref, q_ref, start_ref, keys, places, begin, count, diagonal, group
                )
                total = weights[:, :128] + weights[:, 128:]
            product = jnp.dot(
                weights.astype(jnp.bfloat16), keys, preferred_element_type=jnp.float32
            )
            if group == 0:
                num_ref[rows] = product
                den_ref[rows] = total
            else:
                num_ref[rows] += product
                den_ref[rows] += total

    for block in range(BLOCKS + 1):
        rows = slice(block * HALF, (block + 1) * HALF)
        den = jnp.sum(den_ref[rows], axis=1, keepdims=True)
        recip = jnp.broadcast_to(1.0 / jnp.where(den == 0.0, 1.0, den), (HALF, 128))
        recip_ref[rows] = recip
        full = jnp.where(lane_ids(HALF, 128) < HALF, 0.0, num_ref[rows] * recip)
        full_ref[rows] = full
        packed = pack_from_high(full).astype(jnp.bfloat16)
        if block < BLOCKS:
            place = jnp.where(upper == 1, BLOCKS - 1 - block, block)
            back_ref[pl.ds(place, 1), :32] = packed[None]
            back_ref[pl.ds(place, 1), 32:] = jnp.zeros((1, 32, 128), jnp.bfloat16)
        else:
            back_ref[BLOCKS - 1, 32:] = packed


def attend_grad_kernel(
    scal_ref, kv_ref, q_ref, start_ref, full_ref, recip_ref, dh_in_ref,
    mine_ref, one_ref, two_ref, three_ref, dq_ref, edge_ref,
    dh_ref, dhn_ref, dot_ref, dq_acc,
):
    upper = scal_ref[0]
    for block in range(BLOCKS + 1):
        rows = slice(block * HALF, (block + 1) * HALF)
        if block < BLOCKS:
            place = jnp.where(upper == 1, BLOCKS - 1 - block, block)
            packed = dh_in_ref[pl.ds(place, 1), :32][0]
        else:
            packed = dh_in_ref[BLOCKS - 1, 32:]
        dheads = unpack_high(packed)
        dh_ref[rows] = dheads.astype(jnp.bfloat16)
        dhn_ref[rows] = (dheads * recip_ref[rows]).astype(jnp.bfloat16)
        dot_ref[rows] = jnp.broadcast_to(
            jnp.sum(dheads * full_ref[rows], axis=1, keepdims=True), (HALF, 128)
        )

    for group in range(BLOCKS + 1):
        if group < BLOCKS:
            keys = kv_ref[group]
            places = key_places(scal_ref, group)
            ranges = tiles_of(group)
        else:
            keys = kv_ref[group, :128]
            places = edge_places()
            ranges = [(BLOCKS * HALF, HALF, False)]
        width = keys.shape[0]
        grads = None
        for begin, count, diagonal in ranges:
            rows = slice(begin, begin + count)
            scores = lax.dot_general(
                q_ref[rows], keys, trans_right, preferred_element_type=jnp.float32
            )
            seen = spread(start_ref[rows], width) <= places[:1]
            if diagonal:
                seen = seen & (places[:1] <= spread(query_places(scal_ref, group), width))
            if group == BLOCKS:
                seen = seen & (
                    places[:1] <= (STREAM // 2 + row_ids_of(HALF, 128)).astype(jnp.float32)
                )
            weights = jnp.where(seen, jnp.exp2(scores * EXP2_SCALE), 0.0)
            dprob = lax.dot_general(
                dh_ref[rows], keys, trans_right, preferred_element_type=jnp.float32
            )
            dscore = (
                weights
                * (dprob - spread(dot_ref[rows], width))
                * spread(recip_ref[rows], width)
            ).astype(jnp.bfloat16)
            dquery = jnp.dot(dscore, keys, preferred_element_type=jnp.float32)
            if group == 0:
                dq_acc[rows] = dquery
            else:
                dq_acc[rows] += dquery
            term = lax.dot_general(
                dscore, q_ref[rows], trans_left, preferred_element_type=jnp.float32
            ) * SCALING + lax.dot_general(
                weights.astype(jnp.bfloat16),
                dhn_ref[rows],
                trans_left,
                preferred_element_type=jnp.float32,
            )
            grads = term if grads is None else grads + term
        low = grads.astype(jnp.bfloat16)
        if group < BLOCKS:
            place = jnp.where(upper == 1, BLOCKS - 1 - group, group)
            for quarter, out in enumerate((mine_ref, one_ref, two_ref, three_ref)):
                out[pl.ds(place, 1)] = low[None, quarter * HALF : (quarter + 1) * HALF]
        else:
            edge_ref[:HALF] = low[:HALF]

    for block in range(BLOCKS + 1):
        rows = slice(block * HALF, (block + 1) * HALF)
        packed = pack_from_low(dq_acc[rows] * SCALING).astype(jnp.bfloat16)
        if block < BLOCKS:
            place = jnp.where(upper == 1, BLOCKS - 1 - block, block)
            dq_ref[pl.ds(place, 1)] = packed[None]
        else:
            edge_ref[HALF:] = packed


def whole(*shape, dtype=jnp.bfloat16):
    return jax.ShapeDtypeStruct(shape, dtype)


def attend(scal, own, one, two, three, edge):
    vmem = pl.BlockSpec(memory_space=pltpu.VMEM)
    return pl.pallas_call(
        attend_kernel,
        out_shape=(
            whole(BLOCKS, 64, 128),
            whole(BLOCKS + 1, GROUP, 128),
            whole(ROWS, 128),
            whole(ROWS, 128, dtype=jnp.float32),
            whole(ROWS, 128, dtype=jnp.float32),
            whole(ROWS, 128, dtype=jnp.float32),
        ),
        in_specs=[pl.BlockSpec(memory_space=pltpu.SMEM)] + [vmem] * 5,
        out_specs=[vmem] * 6,
        scratch_shapes=[
            pltpu.VMEM((ROWS, 128), jnp.float32),
            pltpu.VMEM((ROWS, 128), jnp.float32),
        ],
        compiler_params=pltpu.CompilerParams(vmem_limit_bytes=VMEM_BYTES),
        name="attend",
    )(scal, own, one, two, three, edge)


def attend_grad(scal, kv, q, start, full, recip, dh):
    vmem = pl.BlockSpec(memory_space=pltpu.VMEM)
    return pl.pallas_call(
        attend_grad_kernel,
        out_shape=(
            whole(BLOCKS, HALF, 128),
            whole(BLOCKS, HALF, 128),
            whole(BLOCKS, HALF, 128),
            whole(BLOCKS, HALF, 128),
            whole(BLOCKS, 32, 128),
            whole(96, 128),
        ),
        in_specs=[pl.BlockSpec(memory_space=pltpu.SMEM)] + [vmem] * 6,
        out_specs=[vmem] * 6,
        scratch_shapes=[
            pltpu.VMEM((ROWS, 128), jnp.bfloat16),
            pltpu.VMEM((ROWS, 128), jnp.bfloat16),
            pltpu.VMEM((ROWS, 128), jnp.float32),
            pltpu.VMEM((ROWS, 128), jnp.float32),
        ],
        compiler_params=pltpu.CompilerParams(vmem_limit_bytes=VMEM_BYTES),
        name="attend_grad",
    )(scal, kv, q, start, full, recip, dh)


def column(line):
    return jnp.sum(
        jnp.where(lane_ids(128, 128) == row_ids_of(128, 128), line, 0.0), axis=1, keepdims=True
    )


def pairs_low(even, odd):
    left = lane_ids(32, 128) < HALF
    return jnp.concatenate(
        [jnp.where(left, even, turn(odd)), jnp.where(left, turn(even), odd)], axis=0
    )


def project_kernel(
    tokens_ref, start_ref, gain_ref, shift_ref, q_ref, k_ref, v_ref, q_bias_ref, v_bias_ref,
    pay_ref, low_ref,
):
    normed, _, _ = norm_forward(tokens_ref[...].astype(jnp.float32), gain_ref[...], shift_ref[...])
    low = normed.astype(jnp.bfloat16)
    low_ref[...] = low
    starts = start_ref[...]
    high_part = (starts >> 6).astype(jnp.float32)
    low_part = (starts & 63).astype(jnp.float32)
    left = lane_ids(1, 128) < HALF
    lines = (
        jnp.where(left, high_part, turn(low_part)),
        jnp.where(left, turn(high_part), low_part),
    )
    lines = [jnp.broadcast_to(line, (16, 128)).astype(jnp.bfloat16) for line in lines]
    wide = lane_ids(HALF, 128) < HALF
    for pair in range(3):
        columns = slice(pair * 128, (pair + 1) * 128)
        queries = (
            jnp.dot(low, q_ref[:, columns], preferred_element_type=jnp.float32)
            + q_bias_ref[:, columns]
        )
        keyset = jnp.dot(low, k_ref[:, columns], preferred_element_type=jnp.float32)
        values = (
            jnp.dot(low, v_ref[:, columns], preferred_element_type=jnp.float32)
            + v_bias_ref[:, columns]
        )
        for half in range(2):
            rows = slice(half * HALF, (half + 1) * HALF)
            for odd in range(2):
                if odd:
                    both = jnp.where(wide, turn(keyset[rows]), values[rows])
                    packed = pack_from_high(queries[rows])
                else:
                    both = jnp.where(wide, keyset[rows], turn(values[rows]))
                    packed = pack_from_low(queries[rows])
                index = 4 * pair + 2 * odd + half
                pay_ref[index, :HALF] = both.astype(jnp.bfloat16)
                pay_ref[index, HALF : HALF + 32] = packed.astype(jnp.bfloat16)
                pay_ref[index, HALF + 32 :] = lines[half]
    pay_ref[12:] = jnp.zeros((4, HALF + 48, 128), jnp.bfloat16)


def attn_tile(got_ref, pair):
    parts = []
    for half in range(2):
        heads = []
        for odd in range(2):
            index = 4 * pair + 2 * odd
            if half:
                packed = got_ref[index + 1, :32].astype(jnp.float32) + got_ref[
                    index, 32:
                ].astype(jnp.float32)
            else:
                packed = got_ref[index, :32].astype(jnp.float32)
            heads.append(packed)
        parts.append(pairs_low(*heads))
    return jnp.concatenate(parts, axis=0).astype(jnp.bfloat16)


def middle_kernel(
    core_ref, got_ref, other_ref, tokens_ref, cot_ref, exit_ref, o_own_ref, o_other_ref,
    o_bias_ref, gain_ref, shift_ref, up_ref, up_bias_ref, down_ref,
    mid_ref, dn_ref, ffn_ref, keep_ref, send_ref, attn_ref, vec_ref,
    acc_ref, dacc_ref,
):
    first = core_ref[0] == 0
    total = None
    for pair in range(3):
        rows = slice(pair * 128, (pair + 1) * 128)
        own = attn_tile(got_ref, pair)
        attn_ref[:, rows] = own
        acc_ref[:, rows] = own
        acc_ref[:, 384 + pair * 128 : 512 + pair * 128] = attn_tile(other_ref, pair)
    total = jnp.dot(
        acc_ref[:, :384], o_own_ref[...], preferred_element_type=jnp.float32
    ) + jnp.dot(acc_ref[:, 384:], o_other_ref[...], preferred_element_type=jnp.float32)
    middle = tokens_ref[...].astype(jnp.float32) + (total + o_bias_ref[...])
    mid_ref[...] = middle
    normed, _, _ = norm_forward(middle, gain_ref[...], shift_ref[...])
    low = normed.astype(jnp.bfloat16)
    active = column((exit_ref[...] > LAYER).astype(jnp.float32))
    branch = jnp.where(active > 0.0, cot_ref[...].astype(jnp.float32), 0.0)
    branch_low = branch.astype(jnp.bfloat16)
    keep_ref[:, :768] = jnp.where(first, low, branch_low)
    send_ref[:, :768] = jnp.where(first, branch_low, low)
    vec_ref[:, 1536:] = jnp.sum(branch, axis=0, keepdims=True)
    ffn = None
    dnormed = None
    for begin in range(0, 1536, FF_TILE):
        columns = slice(begin, begin + FF_TILE)
        outs = slice(768 + begin, 768 + begin + FF_TILE)
        pre_act = (
            jnp.dot(low, up_ref[:, columns], preferred_element_type=jnp.float32)
            + up_bias_ref[:, columns]
        )
        hidden_full, slope = gelu_pair(pre_act)
        hidden = hidden_full.astype(jnp.bfloat16)
        dhidden = lax.dot_general(
            branch_low, down_ref[columns], trans_right, preferred_element_type=jnp.float32
        )
        dpre = (dhidden * slope).astype(jnp.bfloat16)
        vec_ref[:, columns] = jnp.sum(dpre.astype(jnp.float32), axis=0, keepdims=True)
        keep_ref[:, outs] = jnp.where(first, dpre, hidden)
        send_ref[:, outs] = jnp.where(first, hidden, dpre)
        ffn_term = jnp.dot(hidden, down_ref[columns], preferred_element_type=jnp.float32)
        dn_term = lax.dot_general(
            dpre, up_ref[:, columns], trans_right, preferred_element_type=jnp.float32
        )
        ffn = ffn_term if ffn is None else ffn + ffn_term
        dnormed = dn_term if dnormed is None else dnormed + dn_term
    ffn_ref[...] = ffn.astype(jnp.bfloat16)
    dn_ref[...] = dnormed.astype(jnp.bfloat16)


def dheads_kernel(
    dn_ref, other_ref, mid_ref, cot_ref, exit_ref, gain_ref, o_ref,
    dmid_ref, low_ref, pay_ref, vec_ref,
):
    middle = mid_ref[...]
    _, unit, inverse = norm_forward(middle, gain_ref[...], 0.0)
    dnormed = dn_ref[...].astype(jnp.float32) + other_ref[...].astype(jnp.float32)
    active = column((exit_ref[...] > LAYER).astype(jnp.float32))
    branch = jnp.where(active > 0.0, cot_ref[...].astype(jnp.float32), 0.0)
    dmiddle = branch + norm_backward(dnormed, unit, inverse, gain_ref[...])
    dmid_ref[...] = dmiddle
    low = dmiddle.astype(jnp.bfloat16)
    low_ref[...] = low
    vec_ref[:, :768] = jnp.sum(dnormed * unit, axis=0, keepdims=True)
    vec_ref[:, 768:1536] = jnp.sum(dnormed, axis=0, keepdims=True)
    vec_ref[:, 1536:] = jnp.sum(low.astype(jnp.float32), axis=0, keepdims=True)
    for pair in range(3):
        dheads = lax.dot_general(
            low,
            o_ref[pair * 128 : (pair + 1) * 128],
            trans_right,
            preferred_element_type=jnp.float32,
        )
        for odd in range(2):
            pack = pack_from_high if odd else pack_from_low
            lower = pack(dheads[:HALF]).astype(jnp.bfloat16)
            higher = pack(dheads[HALF:]).astype(jnp.bfloat16)
            index = 4 * pair + 2 * odd
            pay_ref[index, :32] = lower
            pay_ref[index, 32:] = higher
            pay_ref[index + 1, :32] = higher
            pay_ref[index + 1, 32:] = higher
    pay_ref[12:] = jnp.zeros((4, HALF, 128), jnp.bfloat16)


def dnormed_kernel(
    core_ref, got_ref, tokens_ref, attn_ref, q_ref, k_ref, v_ref,
    dn_ref, keep_ref, send_ref, vec_ref,
    key_ref, value_ref, query_ref,
):
    first = core_ref[0] == 0
    wide = lane_ids(HALF, 128) < HALF
    for pair in range(3):
        columns = slice(pair * 128, (pair + 1) * 128)
        for half in range(2):
            rows = slice(half * HALF, (half + 1) * HALF)
            even = got_ref[4 * pair + half].astype(jnp.float32)
            odd = got_ref[4 * pair + 2 + half].astype(jnp.float32)
            key_ref[rows, columns] = jnp.where(wide, even[:HALF], turn(odd[:HALF])).astype(
                jnp.bfloat16
            )
            value_ref[rows, columns] = jnp.where(wide, turn(even[:HALF]), odd[:HALF]).astype(
                jnp.bfloat16
            )
            query_ref[rows, columns] = pairs_low(even[HALF:], odd[HALF:]).astype(jnp.bfloat16)
    queries, keyset, values = query_ref[...], key_ref[...], value_ref[...]
    attn = attn_ref[...]
    keep_ref[:, :384] = jnp.where(first, queries, values)
    keep_ref[:, 384:] = jnp.where(first, keyset, attn)
    send_ref[:, :384] = jnp.where(first, values, queries)
    send_ref[:, 384:] = jnp.where(first, attn, keyset)
    dnormed = (
        lax.dot_general(queries, q_ref[...], trans_right, preferred_element_type=jnp.float32)
        + lax.dot_general(keyset, k_ref[...], trans_right, preferred_element_type=jnp.float32)
        + lax.dot_general(values, v_ref[...], trans_right, preferred_element_type=jnp.float32)
    )
    dn_ref[...] = dnormed.astype(jnp.bfloat16)
    _, unit, _ = norm_forward(tokens_ref[...].astype(jnp.float32), 1.0, 0.0)
    vec_ref[:, :384] = jnp.sum(queries.astype(jnp.float32), axis=0, keepdims=True)
    vec_ref[:, 384:768] = jnp.sum(values.astype(jnp.float32), axis=0, keepdims=True)
    vec_ref[:, 768:1536] = jnp.sum(dnormed * unit, axis=0, keepdims=True)
    vec_ref[:, 1536:] = jnp.sum(dnormed, axis=0, keepdims=True)


def input_grad_kernel(dn_ref, other_ref, tokens_ref, cot_ref, exit_ref, gain_ref, dmid_ref, out_ref):
    _, unit, inverse = norm_forward(tokens_ref[...].astype(jnp.float32), 1.0, 0.0)
    dnormed = dn_ref[...].astype(jnp.float32) + other_ref[...].astype(jnp.float32)
    active = column((exit_ref[...] > LAYER).astype(jnp.float32))
    out_ref[...] = (
        dmid_ref[...]
        + norm_backward(dnormed, unit, inverse, gain_ref[...])
        + jnp.where(active > 0.0, 0.0, cot_ref[...].astype(jnp.float32))
    )


def products_kernel(count, *refs):
    out_ref = refs[-1]
    begin = 0
    for index in range(count):
        left, left_other, right, right_other = refs[4 * index : 4 * index + 4]
        lefts = jnp.concatenate([left[...], left_other[...]], axis=0)
        width = right.shape[1]
        for at in range(0, width, 384):
            columns = slice(at, at + 384)
            rights = jnp.concatenate([right[:, columns], right_other[:, columns]], axis=0)
            out_ref[:, begin + at : begin + at + 384] = lax.dot_general(
                lefts, rights, trans_left, preferred_element_type=jnp.float32
            ).astype(jnp.bfloat16)
        begin += width


def call(kernel, name, outs, scratch, *args):
    vmem = pl.BlockSpec(memory_space=pltpu.VMEM)
    smem = pl.BlockSpec(memory_space=pltpu.SMEM)
    return pl.pallas_call(
        kernel,
        out_shape=outs,
        in_specs=[
            smem if arg.ndim == 1 and arg.dtype == jnp.int32 else vmem for arg in args
        ],
        out_specs=jax.tree.map(lambda out: vmem, outs),
        scratch_shapes=scratch,
        compiler_params=pltpu.CompilerParams(vmem_limit_bytes=VMEM_BYTES),
        name=name,
    )(*args)


def sum_vector(rows):
    rows = swap_add(rows, "core")
    plane = lax.axis_size(PLANE)
    copies = jnp.broadcast_to(rows[None], (plane,) + rows.shape)
    rows = jnp.sum(lax.all_to_all(copies, PLANE, 0, 0, tiled=True), axis=0)
    return swap_add(rows, "zh").reshape(-1)


def scatter_sum(product):
    chips = lax.axis_size(CHIPS)
    blocks = product.reshape(chips, product.shape[0] // chips, product.shape[1])
    received = lax.all_to_all(blocks, CHIPS, 0, 0, tiled=True)
    summed = jnp.sum(received.astype(jnp.float32), axis=0)
    mine = summed.shape[0] // 2
    first = lax.axis_index("core") == 0
    keep = jnp.where(first, summed[:mine], summed[mine:])
    send = jnp.where(first, summed[mine:], summed[:mine])
    got = lax.ppermute(send, "core", SWAP)
    return jnp.where(first, keep, got), jnp.where(first, got, keep)


def on_device(
    tokens,
    doc_start,
    exit_layer,
    cotangent,
    ln1_gain,
    ln1_shift,
    q_weight,
    q_bias,
    k_weight,
    v_weight,
    v_bias,
    o_weight,
    o_bias,
    ln2_gain,
    ln2_shift,
    up_weight,
    up_bias,
    down_weight,
    down_bias,
):
    core = lax.axis_index("core").astype(jnp.int32).reshape(1)
    plane_index = lax.axis_index(PLANE)
    sub_index = lax.axis_index(("zh", "core"))
    upper = plane_index % 2
    scal = jnp.stack(
        [
            upper,
            jnp.bitwise_xor(sub_index, 3 * upper),
            jnp.where((upper == 0) & (sub_index == 3), 1, 0),
            jnp.where((upper == 1) & (sub_index == 3), 1, 0),
        ]
    ).astype(jnp.int32)
    ln1_gain, ln1_shift, ln2_gain, ln2_shift, q_bias, v_bias, o_bias, up_bias, down_bias = [
        vector.reshape(1, -1)
        for vector in (
            ln1_gain, ln1_shift, ln2_gain, ln2_shift, q_bias, v_bias, o_bias, up_bias, down_bias,
        )
    ]
    doc_start = doc_start.reshape(1, -1)
    exits = exit_layer.reshape(1, -1)
    o_other = lax.ppermute(o_weight, "wa", SWAP)
    f32 = jnp.float32
    payload, low_one = call(
        project_kernel, "project", (whole(16, HALF + 48, 128), whole(128, 768)), [],
        tokens, doc_start, ln1_gain, ln1_shift, q_weight, k_weight, v_weight, q_bias, v_bias,
    )
    own = lax.all_to_all(payload, PLANE, 0, 0, tiled=True)
    pairs = own[:, :HALF]
    one = lax.ppermute(pairs, "core", SWAP)
    two = lax.ppermute(pairs, "zh", SWAP)
    three = lax.ppermute(pairs, ("zh", "core"), CROSS)
    edge = lax.ppermute(own[BLOCKS - 1], "y", ((1, 0), (3, 2)))
    back, kv, q_rows, start_rows, full_rows, recip_rows = attend(scal, own, one, two, three, edge)
    got = lax.all_to_all(back, PLANE, 0, 0, tiled=True)
    got_other = lax.ppermute(got, "wa", SWAP)
    middle, dn_two, ffn, keep, send, attn_low, vec_ffn = call(
        middle_kernel, "middle",
        (
            whole(128, 768, dtype=f32),
            whole(128, 768),
            whole(128, 768),
            whole(128, 2304),
            whole(128, 2304),
            whole(128, 384),
            whole(1, 2304, dtype=f32),
        ),
        [pltpu.VMEM((128, 768), jnp.bfloat16), pltpu.VMEM((128, 768), f32)],
        core, got, got_other, tokens, cotangent, exits, o_weight, o_other, o_bias, ln2_gain,
        ln2_shift, up_weight, up_bias, down_weight,
    )
    dn_two_other = lax.ppermute(dn_two, "wa", SWAP)
    dmiddle, dattn_low, dh_payload, vec_two = call(
        dheads_kernel, "dheads",
        (
            whole(128, 768, dtype=f32),
            whole(128, 768),
            whole(16, HALF, 128),
            whole(1, 2304, dtype=f32),
        ),
        [],
        dn_two, dn_two_other, middle, cotangent, exits, ln2_gain, o_weight,
    )
    dh = lax.all_to_all(dh_payload, PLANE, 0, 0, tiled=True)
    sent = lax.ppermute(jnp.concatenate([send, low_one, dattn_low], axis=1), "core", SWAP)
    ffn_products = call(
        functools.partial(products_kernel, 1), "ffn_products", whole(768, 1536), [],
        keep[:, :768], sent[:, :768], keep[:, 768:], sent[:, 768:2304],
    )
    up_weight_grad, down_weight_grad_t = scatter_sum(ffn_products)
    ffn_out = ffn.astype(f32) + lax.ppermute(ffn, "wa", SWAP).astype(f32) + down_bias
    stream_in = tokens.astype(f32)
    output = jnp.where((exit_layer > LAYER)[:, None], middle + ffn_out, stream_in).astype(
        jnp.bfloat16
    )
    vec_early = sum_vector(jnp.concatenate([vec_ffn, vec_two], axis=1))
    mine, give_one, give_two, give_three, dq, edge_grad = attend_grad(
        scal, kv, q_rows, start_rows, full_rows, recip_rows, dh
    )
    pair_sum = (
        mine.astype(f32)
        + lax.ppermute(give_one, "core", SWAP).astype(f32)
        + lax.ppermute(give_two, "zh", SWAP).astype(f32)
        + lax.ppermute(give_three, ("zh", "core"), CROSS).astype(f32)
    )
    edge_got = lax.ppermute(edge_grad, "y", ((0, 1), (2, 3)))
    last = jnp.concatenate([pair_sum[BLOCKS - 1], dq[BLOCKS - 1].astype(f32)])
    last = (last + edge_got.astype(f32)).astype(jnp.bfloat16)
    grads = jnp.concatenate([pair_sum.astype(jnp.bfloat16), dq], axis=1)
    grads = jnp.concatenate([grads[: BLOCKS - 1], last[None]])
    grads = lax.all_to_all(grads, PLANE, 0, 0, tiled=True)
    dn_one, keep_qkv, send_qkv, vec_one = call(
        dnormed_kernel, "dnormed",
        (
            whole(128, 768),
            whole(128, 768),
            whole(128, 768),
            whole(1, 2304, dtype=f32),
        ),
        [pltpu.VMEM((128, 384), jnp.bfloat16)] * 3,
        core, grads, tokens, attn_low, q_weight, k_weight, v_weight,
    )
    sent_qkv = lax.ppermute(send_qkv, "core", SWAP)
    first = core[0] == 0
    left_two = jnp.where(first, low_one, dattn_low)
    left_two_other = jnp.where(first, sent[:, 2304:3072], sent[:, 3072:])
    qkv_products = call(
        functools.partial(products_kernel, 2), "qkv_products", whole(768, 768), [],
        low_one, sent[:, 2304:3072], keep_qkv[:, :384], sent_qkv[:, :384],
        left_two, left_two_other, keep_qkv[:, 384:], sent_qkv[:, 384:],
    )
    qk_grads, vo_grads = scatter_sum(qkv_products)
    dn_one_other = lax.ppermute(dn_one, "wa", SWAP)
    input_grad = call(
        input_grad_kernel, "input_grad", whole(128, 768, dtype=f32), [],
        dn_one, dn_one_other, tokens, cotangent, exits, ln1_gain, dmiddle,
    )
    vec_one = jnp.concatenate([vec_one[:, :768], swap_add(vec_one[:, 768:], "wa")], axis=1)
    vec_late = sum_vector(vec_one)
    return (
        output,
        input_grad,
        vec_late[768:1536],
        vec_late[1536:],
        qk_grads[:, :384],
        vec_late[:384],
        qk_grads[:, 384:],
        vo_grads[:, :384],
        vec_late[384:768],
        vo_grads[:, 384:],
        vec_early[3840:],
        vec_early[2304:3072],
        vec_early[3072:3840],
        up_weight_grad,
        vec_early[:1536],
        down_weight_grad_t,
        vec_early[1536:2304],
    )


def solution(mesh):
    fine = Mesh(mesh.devices.reshape(4, 4, 2, 2, 2), CTX + ("wa",))
    return jax.shard_map(
        on_device,
        mesh=fine,
        in_specs=(
            P(CTX, None),
            P(CTX),
            P(CTX),
            P(CTX, None),
            P(),
            P(),
            P(None, "wa"),
            P("wa"),
            P(None, "wa"),
            P(None, "wa"),
            P("wa"),
            P("wa", None),
            P(),
            P(),
            P(),
            P(None, "wa"),
            P("wa"),
            P("wa", None),
            P(),
        ),
        out_specs=(
            P(CTX, None),
            P(CTX, None),
            P(),
            P(),
            P(CTX, "wa"),
            P("wa"),
            P(CTX, "wa"),
            P(CTX, "wa"),
            P("wa"),
            P(CTX, "wa"),
            P(),
            P(),
            P(),
            P(CTX, "wa"),
            P("wa"),
            P(CTX, "wa"),
            P(),
        ),
        check_vma=False,
    )
```

```python
import math

import jax
import jax.numpy as jnp
from jax import lax
from jax.experimental import pallas as pl
from jax.experimental.pallas import tpu as pltpu
from jax.sharding import Mesh, PartitionSpec as P

HEAD_DIM = 64
LAYER = 6
CTX = ("x", "y", "zh", "core")
PLANE = ("x", "y")
SWAP = ((0, 1), (1, 0))
CROSS = ((0, 3), (1, 2), (2, 1), (3, 0))
HALF = 64
BLOCKS = 16
GROUP = 256
STREAM = 8192
ROWS = (BLOCKS + 1) * HALF
TILE = 256
FF_TILE = 512
FAR = 1e9
SCALING = 1.0 / math.sqrt(HEAD_DIM)
EXP2_SCALE = SCALING / math.log(2.0)
VEC_ROWS = 27
VMEM_BYTES = 64 * 2**20


epsilon = 1e-05
trans_right = (((1,), (1,)), ((), ()))
trans_left = (((0,), (0,)), ((), ()))
cubic_coef = 0.044715


def gelu_pair(values):
    outer = math.sqrt(2.0 / math.pi)
    inner = outer * (values + cubic_coef * values * values * values)
    tangent = jnp.tanh(inner)
    result = 0.5 * values * (1.0 + tangent)
    gelu_slope = 0.5 * (1.0 + tangent) + 0.5 * values * (1.0 - tangent * tangent) * outer * (
        1.0 + 3.0 * cubic_coef * values * values
    )
    return (result, gelu_slope)


def norm_forward(values, gain_vec, shift_vec):
    average = jnp.mean(values, axis=-1, keepdims=True)
    centred = values - average
    inverse_std = lax.rsqrt(jnp.mean(centred * centred, axis=-1, keepdims=True) + epsilon)
    normed = centred * inverse_std
    return (normed * gain_vec + shift_vec, normed, inverse_std)


def norm_backward(grad_out, normed, inverse_std, gain_vec):
    scaled = grad_out * gain_vec
    return inverse_std * (
        scaled
        - jnp.mean(scaled, axis=-1, keepdims=True)
        - normed * jnp.mean(scaled * normed, axis=-1, keepdims=True)
    )


def swap_add(part, axis):
    other = lax.ppermute(part, axis, SWAP)
    return part.astype(jnp.float32) + other.astype(jnp.float32)


def whole(*shape, dtype=jnp.bfloat16):
    return jax.ShapeDtypeStruct(shape, dtype)


def head_place():
    upper = lax.axis_index("y") % 2
    sub = 2 * lax.axis_index("zh") + lax.axis_index("core")
    last = sub == 3
    return (
        upper,
        jnp.where(upper == 1, 3 - sub, sub),
        jnp.where((upper == 0) & last, 1, 0),
        jnp.where((upper == 1) & last, 1, 0),
    )


def call(kernel, name, mebibytes, ins, outs, scratch=(), lazy=()):
    copied_in = [at for at, (mode, _) in enumerate(ins) if mode == "d"]
    copied_out = [at for at, (mode, _) in enumerate(outs) if mode == "d"]

    def buffer(array):
        shape = array.shape if len(array.shape) > 1 else (1,) + tuple(array.shape)
        return pltpu.VMEM(shape, array.dtype)

    def body(*refs):
        given, rest = list(refs[: len(ins)]), refs[len(ins) :]
        results, rest = list(rest[: len(outs)]), rest[len(outs) :]
        in_buffers, rest = rest[: len(copied_in)], rest[len(copied_in) :]
        out_buffers, rest = rest[: len(copied_out)], rest[len(copied_out) :]
        in_sems, out_sems, rest = rest[0], rest[1], rest[2:]
        pending, flushing = [], []
        for slot, at in enumerate(copied_in):
            there = in_buffers[slot]
            into = there if len(ins[at][1].shape) > 1 else there.at[0]
            copy = pltpu.make_async_copy(given[at], into, in_sems.at[slot])
            copy.start()
            given[at] = there
            pending.append((there, at, copy))
        targets = []
        for slot, at in enumerate(copied_out):
            made = out_buffers[slot] if len(outs[at][1].shape) > 1 else out_buffers[slot].at[0]
            copy = pltpu.make_async_copy(made, results[at], out_sems.at[slot])
            results[at] = out_buffers[slot]
            targets.append((out_buffers[slot], copy))

        def wait(ref):
            for entry in list(pending):
                if entry[0] is ref:
                    entry[2].wait()
                    pending[:] = [other for other in pending if other is not entry]

        def flush(ref):
            for entry in list(targets):
                if entry[0] is ref:
                    entry[1].start()
                    flushing.append(entry[1])
                    targets[:] = [other for other in targets if other is not entry]

        for entry in list(pending):
            if entry[1] not in lazy:
                wait(entry[0])
        kernel(wait, flush, *given, *results, *rest)
        for entry in list(pending):
            wait(entry[0])
        for entry in list(targets):
            flush(entry[0])
        for copy in flushing:
            copy.wait()

    vmem, anywhere = pl.BlockSpec(memory_space=pltpu.VMEM), pl.BlockSpec(memory_space=pltpu.HBM)
    result = pl.pallas_call(
        body,
        out_shape=tuple(out for _, out in outs),
        in_specs=[anywhere if mode == "d" else vmem for mode, _ in ins],
        out_specs=tuple(anywhere if mode == "d" else vmem for mode, _ in outs),
        scratch_shapes=[buffer(ins[at][1]) for at in copied_in]
        + [buffer(outs[at][1]) for at in copied_out]
        + [
            pltpu.SemaphoreType.DMA((max(1, len(copied_in)),)),
            pltpu.SemaphoreType.DMA((max(1, len(copied_out)),)),
        ]
        + list(scratch),
        compiler_params=pltpu.CompilerParams(vmem_limit_bytes=VMEM_BYTES),
        name=name,
    )(*[array for _, array in ins])
    return result[0] if len(outs) == 1 else result


def lane_ids(rows, cols):
    return lax.broadcasted_iota(jnp.int32, (rows, cols), 1)


def row_ids_of(rows, cols):
    return lax.broadcasted_iota(jnp.int32, (rows, cols), 0)


def turn(values):
    return pltpu.roll(values, HALF, 1)


def unpack_low(packed):
    wide = packed.astype(jnp.float32)
    left = lane_ids(32, 128) < HALF
    both = jnp.concatenate([wide, turn(wide)], axis=0)
    return jnp.where(jnp.concatenate([left, left], axis=0), both, 0.0)


def unpack_high(packed):
    wide = packed.astype(jnp.float32)
    right = lane_ids(32, 128) >= HALF
    both = jnp.concatenate([turn(wide), wide], axis=0)
    return jnp.where(jnp.concatenate([right, right], axis=0), both, 0.0)


def pack_from_low(block):
    return jnp.where(lane_ids(32, 128) < HALF, block[:32], turn(block[32:]))


def pack_from_high(block):
    return jnp.where(lane_ids(32, 128) < HALF, turn(block[:32]), block[32:])


def key_places(scal, group):
    lane = lane_ids(8, GROUP)
    sub = (lane >> 6) ^ scal[1]
    return (scal[0] * (STREAM // 2) + GROUP * group + (sub << 6) + (lane & 63)).astype(
        jnp.float32
    )


def edge_places():
    return (STREAM // 2 + lane_ids(8, 128)).astype(jnp.float32)


def query_places(scal, block):
    row = row_ids_of(HALF, 128)
    return (
        scal[0] * (STREAM // 2) + GROUP * block + (scal[1] << 6) + row
    ).astype(jnp.float32)


def spread(rows, width):
    return jnp.concatenate([rows] * (width // 128), axis=1) if width > 128 else rows


def tiles_of(group):
    first = group * HALF
    ranges = [(first, HALF, True)]
    begin = first + HALF
    while begin < ROWS:
        count = min(TILE, ROWS - begin)
        ranges.append((begin, count, False))
        begin += count
    return ranges


def weights_of(scal, q_ref, start_ref, keys, places, begin, count, diagonal, group):
    scores = lax.dot_general(
        q_ref[begin : begin + count], keys, trans_right, preferred_element_type=jnp.float32
    )
    width = keys.shape[0]
    seen = spread(start_ref[begin : begin + count], width) <= places[:1]
    if diagonal:
        seen = seen & (places[:1] <= spread(query_places(scal, group), width))
    return jnp.where(seen, jnp.exp2(scores * EXP2_SCALE), 0.0)


def attend_kernel(
    wait, flush, own_ref, one_ref, two_ref, three_ref, edge_ref,
    back_ref, kv_ref, q_ref, start_ref, full_ref,
    num_ref, den_ref,
):
    scal = head_place()
    upper = scal[0]
    diag = jnp.where(
        lane_ids(HALF, 128) == row_ids_of(HALF, 128),
        64.0,
        jnp.where(lane_ids(HALF, 128) == row_ids_of(HALF, 128) + HALF, 1.0, 0.0),
    )

    def starts(line, off):
        found = jnp.sum(line.astype(jnp.float32) * diag, axis=1, keepdims=True)
        return jnp.broadcast_to(jnp.where(off, FAR, found), (HALF, 128))

    for block in range(BLOCKS):
        place = jnp.where(upper == 1, BLOCKS - 1 - block, block)
        rows = slice(block * HALF, (block + 1) * HALF)
        mine = own_ref[pl.ds(place, 1)][0]
        kv_ref[block, 0:HALF] = mine[:HALF]
        kv_ref[block, HALF : 2 * HALF] = one_ref[pl.ds(place, 1)][0]
        kv_ref[block, 2 * HALF : 3 * HALF] = two_ref[pl.ds(place, 1)][0]
        kv_ref[block, 3 * HALF :] = three_ref[pl.ds(place, 1)][0]
        q_ref[rows] = unpack_low(mine[HALF : HALF + 32]).astype(jnp.bfloat16)
        off = (scal[3] == 1) if block == 0 else False
        start_ref[rows] = starts(mine[HALF + 32 : HALF + 33], off)
    kv_ref[BLOCKS] = jnp.zeros((GROUP, 128), jnp.bfloat16)
    kv_ref[BLOCKS, :HALF] = edge_ref[:HALF]
    q_ref[BLOCKS * HALF :] = unpack_low(edge_ref[HALF : HALF + 32]).astype(jnp.bfloat16)
    start_ref[BLOCKS * HALF :] = starts(edge_ref[HALF + 32 : HALF + 33], scal[2] == 0)
    flush(kv_ref)
    flush(q_ref)
    flush(start_ref)

    for group in range(BLOCKS + 1):
        if group < BLOCKS:
            keys = kv_ref[group]
            places = key_places(scal, group)
            ranges = tiles_of(group)
        else:
            keys = kv_ref[group, :128]
            places = edge_places()
            ranges = [(BLOCKS * HALF, HALF, False)]
        for begin, count, diagonal in ranges:
            rows = slice(begin, begin + count)
            if group == BLOCKS:
                scores = lax.dot_general(
                    q_ref[rows], keys, trans_right, preferred_element_type=jnp.float32
                )
                seen = (start_ref[rows] <= places[:1]) & (
                    places[:1] <= (STREAM // 2 + row_ids_of(HALF, 128)).astype(jnp.float32)
                )
                weights = jnp.where(seen, jnp.exp2(scores * EXP2_SCALE), 0.0)
                total = weights
            else:
                weights = weights_of(
                    scal, q_ref, start_ref, keys, places, begin, count, diagonal, group
                )
                total = weights[:, :128] + weights[:, 128:]
            product = jnp.dot(
                weights.astype(jnp.bfloat16), keys, preferred_element_type=jnp.float32
            )
            if group == 0:
                num_ref[rows] = product
                den_ref[rows] = total
            else:
                num_ref[rows] += product
                den_ref[rows] += total

    for block in range(BLOCKS + 1):
        rows = slice(block * HALF, (block + 1) * HALF)
        den = jnp.sum(den_ref[rows], axis=1, keepdims=True)
        recip = jnp.broadcast_to(1.0 / jnp.where(den == 0.0, 1.0, den), (HALF, 128))
        full = num_ref[rows] * recip
        full_ref[rows] = jnp.where(lane_ids(HALF, 128) < HALF, recip, full)
        packed = pack_from_high(full).astype(jnp.bfloat16)
        if block < BLOCKS:
            place = jnp.where(upper == 1, BLOCKS - 1 - block, block)
            for copy in range(2):
                back_ref[pl.ds(2 * place + copy, 1), :32] = packed[None]
                back_ref[pl.ds(2 * place + copy, 1), 32:] = jnp.zeros((1, 32, 128), jnp.bfloat16)
        else:
            for copy in range(2):
                back_ref[2 * BLOCKS - 2 + copy, 32:] = packed


def attend_grad_kernel(
    wait, flush, kv_ref, q_ref, start_ref, full_ref, dh_in_ref,
    keep_ref, send_ref, dq_ref, edge_ref,
    dh_ref, dhn_ref, dot_ref, dq_acc, recip_ref,
):
    scal = head_place()
    upper = scal[0]
    wait(full_ref)
    for block in range(BLOCKS + 1):
        rows = slice(block * HALF, (block + 1) * HALF)
        if block < BLOCKS:
            place = jnp.where(upper == 1, BLOCKS - 1 - block, block)
            packed = dh_in_ref[pl.ds(place, 1), :32][0]
        else:
            packed = dh_in_ref[BLOCKS - 1, 32:]
        dheads = unpack_high(packed)
        full = full_ref[rows]
        left = lane_ids(HALF, 128) < HALF
        recip_ref[rows] = jnp.where(left, full, turn(full))
        dh_ref[rows] = dheads.astype(jnp.bfloat16)
        dhn_ref[rows] = (dheads * recip_ref[rows]).astype(jnp.bfloat16)
        dot_ref[rows] = jnp.broadcast_to(
            jnp.sum(jnp.where(left, 0.0, dheads * full), axis=1, keepdims=True), (HALF, 128)
        )

    wait(kv_ref)
    wait(q_ref)
    wait(start_ref)
    for group in range(BLOCKS + 1):
        if group < BLOCKS:
            keys = kv_ref[group]
            places = key_places(scal, group)
            ranges = tiles_of(group)
        else:
            keys = kv_ref[group, :128]
            places = edge_places()
            ranges = [(BLOCKS * HALF, HALF, False)]
        width = keys.shape[0]
        grads = None
        for begin, count, diagonal in ranges:
            rows = slice(begin, begin + count)
            scores = lax.dot_general(
                q_ref[rows], keys, trans_right, preferred_element_type=jnp.float32
            )
            seen = spread(start_ref[rows], width) <= places[:1]
            if diagonal:
                seen = seen & (places[:1] <= spread(query_places(scal, group), width))
            if group == BLOCKS:
                seen = seen & (
                    places[:1] <= (STREAM // 2 + row_ids_of(HALF, 128)).astype(jnp.float32)
                )
            weights = jnp.where(seen, jnp.exp2(scores * EXP2_SCALE), 0.0)
            dprob = lax.dot_general(
                dh_ref[rows], keys, trans_right, preferred_element_type=jnp.float32
            )
            dscore = (
                weights
                * (dprob - spread(dot_ref[rows], width))
                * spread(recip_ref[rows], width)
            ).astype(jnp.bfloat16)
            dquery = jnp.dot(dscore, keys, preferred_element_type=jnp.float32)
            if group == 0:
                dq_acc[rows] = dquery
            else:
                dq_acc[rows] += dquery
            term = lax.dot_general(
                dscore, q_ref[rows], trans_left, preferred_element_type=jnp.float32
            ) * SCALING + lax.dot_general(
                weights.astype(jnp.bfloat16),
                dhn_ref[rows],
                trans_left,
                preferred_element_type=jnp.float32,
            )
            grads = term if grads is None else grads + term
        low = grads.astype(jnp.bfloat16)
        if group < BLOCKS:
            place = jnp.where(upper == 1, BLOCKS - 1 - group, group)
            for quarter in range(4):
                out = send_ref if quarter % 2 else keep_ref
                out[pl.ds(quarter // 2 * BLOCKS + place, 1)] = low[
                    None, quarter * HALF : (quarter + 1) * HALF
                ]
        else:
            edge_ref[:HALF] = low[:HALF]

    for block in range(BLOCKS + 1):
        rows = slice(block * HALF, (block + 1) * HALF)
        packed = pack_from_low(dq_acc[rows] * SCALING).astype(jnp.bfloat16)
        if block < BLOCKS:
            place = jnp.where(upper == 1, BLOCKS - 1 - block, block)
            dq_ref[pl.ds(place, 1)] = packed[None]
        else:
            edge_ref[HALF:] = packed


def attend(own, one, two, three, edge):
    f32 = jnp.float32
    return call(
        attend_kernel, "attend", 24,
        [("v", own), ("v", one), ("v", two), ("v", three), ("v", edge)],
        [
            ("d", whole(2 * BLOCKS, HALF, 128)),
            ("d", whole(BLOCKS + 1, GROUP, 128)),
            ("d", whole(ROWS, 128)),
            ("d", whole(ROWS, 128, dtype=f32)),
            ("d", whole(ROWS, 128, dtype=f32)),
        ],
        [pltpu.VMEM((ROWS, 128), f32), pltpu.VMEM((ROWS, 128), f32)],
    )


def attend_grad(kv, q, start, full, dh):
    f32 = jnp.float32
    return call(
        attend_grad_kernel, "attend_grad", 24,
        [("d", kv), ("d", q), ("d", start), ("d", full), ("v", dh)],
        [
            ("v", whole(2 * BLOCKS, HALF, 128)),
            ("v", whole(2 * BLOCKS, HALF, 128)),
            ("v", whole(BLOCKS, 32, 128)),
            ("v", whole(96, 128)),
        ],
        [
            pltpu.VMEM((ROWS, 128), jnp.bfloat16),
            pltpu.VMEM((ROWS, 128), jnp.bfloat16),
            pltpu.VMEM((ROWS, 128), f32),
            pltpu.VMEM((ROWS, 128), f32),
            pltpu.VMEM((ROWS, 128), f32),
        ],
        lazy=(0, 1, 2, 3),
    )


def column(line):
    return jnp.sum(
        jnp.where(lane_ids(128, 128) == row_ids_of(128, 128), line, 0.0), axis=1, keepdims=True
    )


def pairs_low(even, odd):
    left = lane_ids(32, 128) < HALF
    return jnp.concatenate(
        [jnp.where(left, even, turn(odd)), jnp.where(left, turn(even), odd)], axis=0
    )


def project_kernel(
    wait, flush,
    tokens_ref, start_ref, gain_ref, shift_ref, q_bias_ref, v_bias_ref, q_ref, k_ref, v_ref,
    pay_ref, unit_ref,
):
    normed, unit, _ = norm_forward(
        tokens_ref[...].astype(jnp.float32), gain_ref[...], shift_ref[...]
    )
    low = normed.astype(jnp.bfloat16)
    unit_ref[...] = unit.astype(jnp.bfloat16)
    flush(unit_ref)
    starts = start_ref[...]
    high_part = (starts >> 6).astype(jnp.float32)
    low_part = (starts & 63).astype(jnp.float32)
    left = lane_ids(1, 128) < HALF
    lines = (
        jnp.where(left, high_part, turn(low_part)),
        jnp.where(left, turn(high_part), low_part),
    )
    lines = [jnp.broadcast_to(line, (16, 128)).astype(jnp.bfloat16) for line in lines]
    wide = lane_ids(HALF, 128) < HALF
    for ref in (q_ref, k_ref, v_ref):
        wait(ref)
    for pair in range(3):
        columns = slice(pair * 128, (pair + 1) * 128)
        queries = (
            jnp.dot(low, q_ref[:, columns], preferred_element_type=jnp.float32)
            + q_bias_ref[:, columns]
        )
        keyset = jnp.dot(low, k_ref[:, columns], preferred_element_type=jnp.float32)
        values = (
            jnp.dot(low, v_ref[:, columns], preferred_element_type=jnp.float32)
            + v_bias_ref[:, columns]
        )
        for half in range(2):
            rows = slice(half * HALF, (half + 1) * HALF)
            for odd in range(2):
                if odd:
                    both = jnp.where(wide, turn(keyset[rows]), values[rows])
                    packed = pack_from_high(queries[rows])
                else:
                    both = jnp.where(wide, keyset[rows], turn(values[rows]))
                    packed = pack_from_low(queries[rows])
                index = 4 * pair + 2 * odd + half
                pay_ref[index, :HALF] = both.astype(jnp.bfloat16)
                pay_ref[index, HALF : HALF + 32] = packed.astype(jnp.bfloat16)
                pay_ref[index, HALF + 32 :] = lines[half]
    pay_ref[12:] = jnp.zeros((4, HALF + 48, 128), jnp.bfloat16)


def prepare_kernel(
    wait, flush, unit_ref, gain_ref, shift_ref, q_ref, k_ref, v_ref,
    order_ref, out_ref, weight_ref, affine_ref,
):
    lane = lane_ids(8, 768)
    core = (lane >= 384).astype(jnp.int32)
    rest = lane - 384 * core
    high = (rest >= 192).astype(jnp.int32)
    within = rest - 192 * high
    plane = (within * 171) >> 11
    source = (48 * plane + 12 * (2 * high + core) + (within - 12 * plane))[:1]
    order = jnp.where(row_ids_of(768, 768) == source, 1.0, 0.0).astype(jnp.bfloat16)
    order_ref[...] = order
    flush(order_ref)
    ordered = jnp.dot(unit_ref[...], order, preferred_element_type=jnp.float32).astype(
        jnp.bfloat16
    )
    for index in range(12):
        out_ref[index] = ordered[HALF * (index % 2) : HALF * (index % 2 + 1)]
    out_ref[12:] = jnp.zeros((4, HALF, 768), jnp.bfloat16)
    flush(out_ref)
    affine = exact_product(
        jnp.concatenate([gain_ref[...], shift_ref[...]], axis=0), order, (((1,), (0,)), ((), ()))
    )
    affine_ref[...] = jnp.concatenate([affine, jnp.zeros((6, 768), jnp.float32)], axis=0)
    pair, odd = head_of()
    begin = pl.multiple_of(pair * 128, 128)
    left = lane_ids(768, 128) < HALF
    for ref in (q_ref, k_ref, v_ref):
        wait(ref)

    def head_columns(ref):
        tile = ref[:, pl.ds(begin, 128)].astype(jnp.float32)
        turned = turn(tile)
        return jnp.where(odd == 1, turned, tile), jnp.where(odd == 1, tile, turned)

    first = jnp.where(left, head_columns(k_ref)[0], head_columns(v_ref)[1])
    second = jnp.where(left, head_columns(q_ref)[0], 0.0)
    columns = jnp.concatenate([first, second], axis=1).astype(jnp.bfloat16)
    weight_ref[...] = lax.dot_general(
        order, columns, trans_left, preferred_element_type=jnp.float32
    ).astype(jnp.bfloat16)


def exact_product(rows, order, dims):
    parts = []
    rest = rows
    for _ in range(3):
        low = rest.astype(jnp.bfloat16).astype(jnp.float32)
        parts.append(low)
        rest = rest - low
    stacked = jnp.concatenate(parts + [jnp.zeros((2, 768), jnp.float32)], axis=0)
    product = lax.dot_general(
        stacked.astype(jnp.bfloat16), order, dims, preferred_element_type=jnp.float32
    )
    return product[0:2] + product[2:4] + product[4:6]


def head_of():
    plane = 4 * lax.axis_index("x") + lax.axis_index("y")
    head = jnp.minimum(plane // 2, 5)
    return head // 2, head % 2


def attn_tile(got_ref, side, pair):
    parts = []
    for half in range(2):
        heads = []
        for odd in range(2):
            index = 4 * pair + 2 * odd
            lower = got_ref[pl.ds(2 * index + side, 1)][0].astype(jnp.float32)
            if half:
                higher = got_ref[pl.ds(2 * index + 2 + side, 1)][0].astype(jnp.float32)
                packed = higher[:32] + lower[32:]
            else:
                packed = lower[:32]
            heads.append(packed)
        parts.append(pairs_low(*heads))
    return jnp.concatenate(parts, axis=0).astype(jnp.bfloat16)


def middle_kernel(
    wait, flush, got_ref, tokens_ref, cot_ref, exit_ref, o_bias_ref, gain_ref, shift_ref,
    up_bias_ref, o_own_ref, o_other_ref, up_ref, down_ref,
    dn_ref, send_ref, keep_ref, mid_ref, ffn_ref, attn_ref, vec_ref,
    acc_ref,
):
    first = lax.axis_index("core") == 0
    side = lax.axis_index("wa")
    for pair in range(3):
        rows = slice(pair * 128, (pair + 1) * 128)
        attn_ref[:, rows] = attn_tile(got_ref, side, pair)
        acc_ref[:, rows] = attn_tile(got_ref, 1 - side, pair)
    flush(attn_ref)
    for ref in (o_own_ref, o_other_ref, up_ref, down_ref):
        wait(ref)
    total = jnp.dot(
        attn_ref[...], o_own_ref[...], preferred_element_type=jnp.float32
    ) + jnp.dot(acc_ref[...], o_other_ref[...], preferred_element_type=jnp.float32)
    middle = tokens_ref[...].astype(jnp.float32) + (total + o_bias_ref[...])
    mid_ref[...] = middle
    flush(mid_ref)
    normed, _, _ = norm_forward(middle, gain_ref[...], shift_ref[...])
    low = normed.astype(jnp.bfloat16)
    active = column((exit_ref[...] > LAYER).astype(jnp.float32))
    branch = jnp.where(active > 0.0, cot_ref[...].astype(jnp.float32), 0.0)
    branch_low = branch.astype(jnp.bfloat16)
    keep_ref[:, :768] = jnp.where(first, low, branch_low)
    send_ref[:, :768] = jnp.where(first, branch_low, low)
    vec_ref[:, 1536:] = jnp.sum(branch, axis=0, keepdims=True)
    ffn = None
    dnormed = None
    for begin in range(0, 1536, FF_TILE):
        columns = slice(begin, begin + FF_TILE)
        outs = slice(768 + begin, 768 + begin + FF_TILE)
        pre_act = (
            jnp.dot(low, up_ref[:, columns], preferred_element_type=jnp.float32)
            + up_bias_ref[:, columns]
        )
        hidden_full, slope = gelu_pair(pre_act)
        hidden = hidden_full.astype(jnp.bfloat16)
        dhidden = lax.dot_general(
            branch_low, down_ref[columns], trans_right, preferred_element_type=jnp.float32
        )
        dpre = (dhidden * slope).astype(jnp.bfloat16)
        vec_ref[:, columns] = jnp.sum(dpre.astype(jnp.float32), axis=0, keepdims=True)
        keep_ref[:, outs] = jnp.where(first, dpre, hidden)
        send_ref[:, outs] = jnp.where(first, hidden, dpre)
        ffn_term = jnp.dot(hidden, down_ref[columns], preferred_element_type=jnp.float32)
        dn_term = lax.dot_general(
            dpre, up_ref[:, columns], trans_right, preferred_element_type=jnp.float32
        )
        ffn = ffn_term if ffn is None else ffn + ffn_term
        dnormed = dn_term if dnormed is None else dnormed + dn_term
    ffn_ref[...] = ffn.astype(jnp.bfloat16)
    dn_ref[...] = dnormed.astype(jnp.bfloat16)


def dheads_kernel(
    wait, flush, dn_ref, other_ref, mid_ref, cot_ref, exit_ref, gain_ref, o_ref, attn_ref, order_ref,
    pay_ref, send_ref, keep_ref, dmid_ref, vec_ref,
):
    middle = mid_ref[...]
    _, unit, inverse = norm_forward(middle, gain_ref[...], 0.0)
    dnormed = dn_ref[...].astype(jnp.float32) + other_ref[...].astype(jnp.float32)
    active = column((exit_ref[...] > LAYER).astype(jnp.float32))
    branch = jnp.where(active > 0.0, cot_ref[...].astype(jnp.float32), 0.0)
    dmiddle = branch + norm_backward(dnormed, unit, inverse, gain_ref[...])
    dmid_ref[...] = dmiddle
    flush(dmid_ref)
    low = dmiddle.astype(jnp.bfloat16)
    vec_ref[:, :768] = jnp.sum(dnormed * unit, axis=0, keepdims=True)
    vec_ref[:, 768:1536] = jnp.sum(dnormed, axis=0, keepdims=True)
    vec_ref[:, 1536:] = jnp.sum(low.astype(jnp.float32), axis=0, keepdims=True)
    wait(o_ref)
    for pair in range(3):
        dheads = lax.dot_general(
            low,
            o_ref[pair * 128 : (pair + 1) * 128],
            trans_right,
            preferred_element_type=jnp.float32,
        )
        for odd in range(2):
            pack = pack_from_high if odd else pack_from_low
            lower = pack(dheads[:HALF]).astype(jnp.bfloat16)
            higher = pack(dheads[HALF:]).astype(jnp.bfloat16)
            index = 4 * pair + 2 * odd
            pay_ref[index, :32] = lower
            pay_ref[index, 32:] = higher
            pay_ref[index + 1, :32] = higher
            pay_ref[index + 1, 32:] = higher
    pay_ref[12:] = jnp.zeros((4, HALF, 128), jnp.bfloat16)
    flush(pay_ref)
    wait(order_ref)
    ordered = jnp.dot(low, order_ref[...], preferred_element_type=jnp.float32).astype(jnp.bfloat16)
    first = lax.axis_index("core") == 0
    keep_ref[:, :384] = jnp.where(first, ordered[:, :384], ordered[:, 384:])
    send_ref[:, :384] = jnp.where(first, ordered[:, 384:], ordered[:, :384])
    keep_ref[:, 384:] = attn_ref[...]
    send_ref[:, 384:] = attn_ref[...]


def o_products_kernel(wait, flush, keep_ref, sent_ref, near_ref, far_ref):
    both = jnp.concatenate([keep_ref[...], sent_ref[...]], axis=0)
    high = lax.axis_index("zh") == 0
    product = lax.dot_general(
        both[:, :384], both[:, 384:], trans_left, preferred_element_type=jnp.float32
    )
    near_ref[...] = jnp.where(high, product[:192], product[192:])
    far_ref[...] = jnp.where(high, product[192:], product[:192]).astype(jnp.bfloat16)


def ffn_products_kernel(wait, flush, keep_ref, sent_ref, out_ref):
    for at in range(768, 2304, 384):
        columns = slice(at, at + 384)
        lefts = jnp.concatenate([keep_ref[:, :768], sent_ref[:, :768]], axis=0)
        rights = jnp.concatenate([keep_ref[:, columns], sent_ref[:, columns]], axis=0)
        out_ref[:, at - 768 : at - 384] = lax.dot_general(
            lefts, rights, trans_left, preferred_element_type=jnp.float32
        ).astype(jnp.bfloat16)


def dnormed_kernel(
    wait, flush, got_ref, q_ref, k_ref, v_ref,
    dn_ref,
    key_ref, value_ref, query_ref,
):
    wide = lane_ids(HALF, 128) < HALF
    for pair in range(3):
        columns = slice(pair * 128, (pair + 1) * 128)
        for half in range(2):
            rows = slice(half * HALF, (half + 1) * HALF)
            even = got_ref[4 * pair + half].astype(jnp.float32)
            odd = got_ref[4 * pair + 2 + half].astype(jnp.float32)
            key_ref[rows, columns] = jnp.where(wide, even[:HALF], turn(odd[:HALF])).astype(
                jnp.bfloat16
            )
            value_ref[rows, columns] = jnp.where(wide, turn(even[:HALF]), odd[:HALF]).astype(
                jnp.bfloat16
            )
            query_ref[rows, columns] = pairs_low(even[HALF:], odd[HALF:]).astype(jnp.bfloat16)
    for ref in (q_ref, k_ref, v_ref):
        wait(ref)
    dn_ref[...] = (
        lax.dot_general(query_ref[...], q_ref[...], trans_right, preferred_element_type=jnp.float32)
        + lax.dot_general(key_ref[...], k_ref[...], trans_right, preferred_element_type=jnp.float32)
        + lax.dot_general(
            value_ref[...], v_ref[...], trans_right, preferred_element_type=jnp.float32
        )
    ).astype(jnp.bfloat16)


def input_grad_kernel(
    wait, flush, dn_ref, other_ref, tokens_ref, cot_ref, exit_ref, gain_ref, dmid_ref, out_ref
):
    _, unit, inverse = norm_forward(tokens_ref[...].astype(jnp.float32), 1.0, 0.0)
    dnormed = dn_ref[...].astype(jnp.float32) + other_ref[...].astype(jnp.float32)
    active = column((exit_ref[...] > LAYER).astype(jnp.float32))
    out_ref[...] = (
        dmid_ref[...]
        + norm_backward(dnormed, unit, inverse, gain_ref[...])
        + jnp.where(active > 0.0, 0.0, cot_ref[...].astype(jnp.float32))
    )


def far_kernel(wait, flush, kept_ref, taken_ref, far_ref):
    far_ref[...] = (
        kept_ref[BLOCKS:].astype(jnp.float32) + taken_ref[BLOCKS:].astype(jnp.float32)
    ).astype(jnp.bfloat16)


def merge_kernel(wait, flush, kept_ref, taken_ref, far_ref, dq_ref, edge_ref, out_ref):
    for block in range(BLOCKS):
        pair = (
            kept_ref[block].astype(jnp.float32)
            + taken_ref[block].astype(jnp.float32)
            + far_ref[block].astype(jnp.float32)
        )
        query = dq_ref[block]
        if block == BLOCKS - 1:
            pair = pair + edge_ref[:HALF].astype(jnp.float32)
            query = (query.astype(jnp.float32) + edge_ref[HALF:].astype(jnp.float32)).astype(
                jnp.bfloat16
            )
        out_ref[block, :HALF] = pair.astype(jnp.bfloat16)
        out_ref[block, HALF:] = query


def weigh_kernel(
    wait, flush, grads_ref, units_ref, affine_ref, weight_ref, ffn_ref, two_ref,
    given_ref, kept_ref,
    one_ref, grad_ref, sum_ref,
):
    pair, odd = head_of()
    odd = odd == 1
    core, high = lax.axis_index("core"), lax.axis_index("zh")
    gain_line, shift_line = affine_ref[0:1], affine_ref[1:2]
    for block in range(BLOCKS):
        rows = slice(block * HALF, (block + 1) * HALF)
        one_ref[rows] = (
            units_ref[block].astype(jnp.float32) * gain_line + shift_line
        ).astype(jnp.bfloat16)
        grad_ref[rows, :128] = grads_ref[block, :HALF]
        grad_ref[rows, 128:] = unpack_low(grads_ref[block, HALF:]).astype(jnp.bfloat16)
    grads = grad_ref[...]
    sum_ref[...] = lax.dot_general(
        one_ref[...], grads, trans_left, preferred_element_type=jnp.float32
    )
    for out, side in ((kept_ref, core), (given_ref, 1 - core)):
        for at in range(2):
            begin = pl.multiple_of(384 * side + 192 * (high if at == 0 else 1 - high), 64)
            out[192 * at : 192 * (at + 1)] = sum_ref[pl.ds(begin, 192)]
    shift = jnp.zeros((1, 768), jnp.float32)
    gain = jnp.zeros((1, 768), jnp.float32)
    for begin in range(0, BLOCKS * HALF, 128):
        rows = slice(begin, begin + 128)
        part = lax.dot_general(
            grad_ref[rows], weight_ref[...], trans_right, preferred_element_type=jnp.float32
        )
        shift = shift + jnp.sum(part, axis=0, keepdims=True)
        for block in (begin // HALF, begin // HALF + 1):
            unit = units_ref[block].astype(jnp.float32)
            at = HALF * block - begin
            gain = gain + jnp.sum(part[at : at + HALF] * unit, axis=0, keepdims=True)
    total = jnp.sum(grads.astype(jnp.float32), axis=0, keepdims=True)
    left = lane_ids(1, 128) < HALF
    query = total[:, 128:]
    query = jnp.where(odd, turn(query), query)
    value = jnp.where(left, 0.0, total[:, :128])
    value = jnp.where(odd, value, turn(value))
    line = jnp.concatenate(
        [shift, gain]
        + [jnp.where(pair == at, query, 0.0) for at in range(3)]
        + [jnp.where(pair == at, value, 0.0) for at in range(3)]
        + [ffn_ref[...], two_ref[...]],
        axis=1,
    )
    for out in (kept_ref, given_ref):
        out[384:] = jnp.zeros((32, 256), jnp.float32)
        for row in range(VEC_ROWS):
            out[384 + row : 385 + row] = line[:, 256 * row : 256 * (row + 1)]


def near_kernel(wait, flush, kept_ref, taken_ref, norm_ref, far_ref, near_ref):
    both = kept_ref[...] + taken_ref[...]
    near_ref[:192] = both[:192]
    near_ref[192:] = both[384:]
    far_ref[...] = both[192:]
    norm_ref[...] = both[384:392]


def tail_kernel(
    wait, flush, near_ref, far_ref, wa_ref, cross_ref, o_near_ref, o_far_ref, out_ref
):
    both = near_ref[...] + far_ref[...]
    norms = both[192:200] + (wa_ref[...] + cross_ref[...])
    sums = jnp.concatenate(
        [jnp.where(row_ids_of(8, 256) < 6, norms, both[192:200]), both[200:]], axis=0
    )
    sums = jnp.concatenate([sums[:, :128], sums[:, 128:]], axis=0).astype(jnp.bfloat16)
    o_both = o_near_ref[...] + o_far_ref[...].astype(jnp.float32)
    spare = jnp.zeros((4, 128), jnp.float32)
    for plane in range(16):
        rows = slice(12 * plane, 12 * plane + 12)
        tiles = [both[rows, :128], both[rows, 128:]]
        tiles += [o_both[rows, 128 * tile : 128 * tile + 128] for tile in range(3)]
        for at, tile in enumerate(tiles):
            out_ref[plane, 16 * at : 16 * at + 16] = jnp.concatenate([tile, spare], axis=0).astype(
                jnp.bfloat16
            )
        out_ref[plane, 80:] = sums


def finish_kernel(
    wait, flush, got_ref, order_ref,
    q_ref, k_ref, v_ref, o_ref, gain_out, shift_out, q_bias_out, v_bias_out,
    up_bias_out, down_bias_out, gain_two_out, shift_two_out, o_bias_out,
):
    left = lane_ids(16, 128) < HALF

    def rows_of(source, at):
        return got_ref[source, 16 * at : 16 * at + 16].astype(jnp.float32)

    for pair in range(3):
        columns = slice(128 * pair, 128 * (pair + 1))
        keys_values = [
            rows_of(4 * pair + 2 * odd, 0) + rows_of(4 * pair + 2 * odd + 1, 0) for odd in range(2)
        ]
        queries = [
            rows_of(4 * pair + 2 * odd, 1) + rows_of(4 * pair + 2 * odd + 1, 1) for odd in range(2)
        ]
        k_ref[:, columns] = jnp.where(left, keys_values[0], turn(keys_values[1]))[:12]
        v_ref[:, columns] = jnp.where(left, turn(keys_values[0]), keys_values[1])[:12]
        q_ref[:, columns] = jnp.where(left, queries[0], turn(queries[1]))[:12]
        total = rows_of(0, 2 + pair)
        for source in range(1, 16):
            total = total + rows_of(source, 2 + pair)
        o_ref[:, columns] = total[:12]
    sums = got_ref[0, 80:].astype(jnp.float32)
    for source in range(1, 16):
        sums = sums + got_ref[source, 80:].astype(jnp.float32)

    def line(begin, count):
        parts = []
        for row in range(begin, begin + count):
            parts += [sums[row : row + 1], sums[32 + row : 33 + row]]
        return jnp.concatenate(parts, axis=1)

    wait(order_ref)
    back = exact_product(
        jnp.concatenate([line(0, 3), line(3, 3)], axis=0), order_ref[...], trans_right
    )
    shift_out[...] = back[0:1]
    gain_out[...] = back[1:2]
    biases = line(6, 3)
    q_bias_out[...] = biases[:, :384]
    v_bias_out[...] = biases[:, 384:]
    up_bias_out[...] = line(9, 6)
    down_bias_out[...] = line(15, 3)
    gain_two_out[...] = line(18, 3)
    shift_two_out[...] = line(21, 3)
    o_bias_out[...] = line(24, 3)


def sub_sums(summed):
    mine = summed.shape[0] // 4
    parts = summed.reshape(4, mine, summed.shape[1])
    me = lax.axis_index(("zh", "core"))

    def part(index):
        return lax.dynamic_index_in_dim(parts, index, 0, keepdims=False)

    here = part(me)
    core_way = lax.ppermute(part(jnp.bitwise_xor(me, 1)), "core", SWAP)
    z_way = lax.ppermute(part(jnp.bitwise_xor(me, 2)), "zh", SWAP)
    cross_way = lax.ppermute(part(jnp.bitwise_xor(me, 3)), ("zh", "core"), CROSS)
    mine_sum, other_sum = here + z_way, core_way + cross_way
    first = lax.axis_index("core") == 0
    return jnp.where(first, mine_sum, other_sum), jnp.where(first, other_sum, mine_sum)


def on_device(
    tokens,
    doc_start,
    exit_layer,
    cotangent,
    ln1_gain,
    ln1_shift,
    q_weight,
    q_bias,
    k_weight,
    v_weight,
    v_bias,
    o_weight,
    o_bias,
    ln2_gain,
    ln2_shift,
    up_weight,
    up_bias,
    down_weight,
    down_bias,
):
    f32 = jnp.float32

    def copied(*arrays):
        return [("d", array) for array in arrays]

    o_other = lax.ppermute(o_weight, "wa", SWAP)
    payload, unit = call(
        project_kernel, "project", 16,
        copied(
            tokens, doc_start, ln1_gain, ln1_shift, q_bias, v_bias, q_weight, k_weight, v_weight
        ),
        [("d", whole(16, HALF + 48, 128)), ("d", whole(128, 768))],
        lazy=(6, 7, 8),
    )
    own = lax.all_to_all(payload, PLANE, 0, 0, tiled=True)
    order, units, head_weight, affine = call(
        prepare_kernel, "prepare", 24,
        copied(unit, ln1_gain, ln1_shift, q_weight, k_weight, v_weight),
        [
            ("d", whole(768, 768)),
            ("d", whole(16, HALF, 768)),
            ("d", whole(768, 256)),
            ("d", whole(8, 768, dtype=f32)),
        ],
        lazy=(3, 4, 5),
    )
    own, units, o_other = lax.optimization_barrier((own, units, o_other))
    pairs = own[:, :HALF]
    one = lax.ppermute(pairs, "core", SWAP)
    edge = lax.ppermute(own[BLOCKS - 1], "y", ((1, 0), (3, 2)))
    two = lax.ppermute(pairs, "zh", SWAP)
    units = lax.all_to_all(units, PLANE, 0, 0, tiled=True)
    two, edge = lax.optimization_barrier((two, edge))
    three = lax.ppermute(two, "core", SWAP)
    back, kv, q_rows, start_rows, full_rows = attend(own, one, two, three, edge)
    back, units = lax.optimization_barrier((back, units))
    got = lax.all_to_all(back, ("x", "y", "wa"), 0, 0, tiled=True)
    dn_two, send, keep, middle, ffn, attn_low, vec_ffn = call(
        middle_kernel, "middle", 32,
        [("v", got)]
        + copied(
            tokens, cotangent, exit_layer, o_bias, ln2_gain, ln2_shift, up_bias, o_weight, o_other,
            up_weight, down_weight,
        ),
        [
            ("v", whole(128, 768)),
            ("v", whole(128, 2304)),
            ("v", whole(128, 2304)),
            ("d", whole(128, 768, dtype=f32)),
            ("d", whole(128, 768)),
            ("d", whole(128, 384)),
            ("d", whole(1, 2304, dtype=f32)),
        ],
        [pltpu.VMEM((128, 384), jnp.bfloat16)],
        lazy=(8, 9, 10, 11),
    )
    dn_two_other = lax.ppermute(dn_two, "wa", SWAP)
    sent = lax.ppermute(send, "core", SWAP)
    ffn_products = call(
        ffn_products_kernel, "ffn_products", 24,
        [("v", keep), ("v", sent)],
        [("d", whole(768, 1536))],
    )
    dh_payload, o_send, o_keep, dmiddle, vec_two = call(
        dheads_kernel, "dheads", 16,
        [("v", dn_two), ("v", dn_two_other)]
        + copied(middle, cotangent, exit_layer, ln2_gain, o_weight, attn_low, order),
        [
            ("d", whole(16, HALF, 128)),
            ("v", whole(128, 768)),
            ("v", whole(128, 768)),
            ("d", whole(128, 768, dtype=f32)),
            ("d", whole(1, 2304, dtype=f32)),
        ],
        lazy=(6, 8),
    )
    dh = lax.all_to_all(dh_payload, PLANE, 0, 0, tiled=True)
    o_sent = lax.ppermute(o_send, "core", SWAP)
    o_near, o_far = call(
        o_products_kernel, "o_products", 8,
        [("v", o_keep), ("v", o_sent)],
        [("d", whole(192, 384, dtype=f32)), ("v", whole(192, 384))],
    )
    dh, ffn_products, o_far = lax.optimization_barrier((dh, ffn_products, o_far))
    o_got = lax.ppermute(o_far, "zh", SWAP)
    ffn_blocks = lax.all_to_all(
        ffn_products.reshape(16, 48, 1536), PLANE, 0, 0, tiled=True
    )
    kept, given, dq, edge_grad = attend_grad(kv, q_rows, start_rows, full_rows, dh)
    edge_got = lax.ppermute(edge_grad, "y", ((0, 1), (2, 3)))
    taken = lax.ppermute(given, "core", SWAP)
    far = call(
        far_kernel, "far", 8, [("v", kept), ("v", taken)], [("v", whole(BLOCKS, HALF, 128))]
    )
    far = lax.ppermute(far, "zh", SWAP)
    merged = call(
        merge_kernel, "merge", 8,
        [("v", kept), ("v", taken), ("v", far), ("v", dq), ("v", edge_got)],
        [("d", whole(BLOCKS, 96, 128))],
    )
    merged, ffn_blocks = lax.optimization_barrier((merged, ffn_blocks))
    grads = lax.all_to_all(merged, PLANE, 0, 0, tiled=True)
    given_sums, kept_sums = call(
        weigh_kernel, "weigh", 24,
        copied(
            merged, units, affine, head_weight, vec_ffn, vec_two
        ),
        [("v", whole(416, 256, dtype=f32)), ("v", whole(416, 256, dtype=f32))],
        [
            pltpu.VMEM((BLOCKS * HALF, 768), jnp.bfloat16),
            pltpu.VMEM((BLOCKS * HALF, 256), jnp.bfloat16),
            pltpu.VMEM((768, 256), f32),
        ],
    )
    taken_sums = lax.ppermute(given_sums, "core", SWAP)
    norm_sums, far_sums, near_sums = call(
        near_kernel, "near", 4,
        [("v", kept_sums), ("v", taken_sums)],
        [
            ("v", whole(8, 256, dtype=f32)),
            ("v", whole(224, 256, dtype=f32)),
            ("v", whole(224, 256, dtype=f32)),
        ],
    )
    far_sums = lax.ppermute(far_sums, "zh", SWAP)
    wa_sums = lax.ppermute(norm_sums, "wa", SWAP)
    cross_sums = lax.ppermute(norm_sums, ("zh", "wa"), CROSS)
    tail = call(
        tail_kernel, "tail", 8,
        [("v", near_sums), ("v", far_sums), ("v", wa_sums), ("v", cross_sums)]
        + copied(o_near, o_got),
        [("d", whole(16, 144, 128))],
    )
    dn_one = call(
        dnormed_kernel, "dnormed", 8,
        [("v", grads)] + copied(q_weight, k_weight, v_weight),
        [("v", whole(128, 768))],
        [pltpu.VMEM((128, 384), jnp.bfloat16)] * 3,
        lazy=(1, 2, 3),
    )
    dn_one_other = lax.ppermute(dn_one, "wa", SWAP)
    tail = lax.all_to_all(tail, PLANE, 0, 0, tiled=True)
    up_weight_grad, down_weight_grad_t = sub_sums(jnp.sum(ffn_blocks.astype(f32), axis=0))
    ffn_out = ffn.astype(f32) + lax.ppermute(ffn, "wa", SWAP).astype(f32) + down_bias
    output = jnp.where(
        (exit_layer > LAYER)[:, None], middle + ffn_out, tokens.astype(f32)
    ).astype(jnp.bfloat16)
    input_grad = call(
        input_grad_kernel, "input_grad", 8,
        [("v", dn_one), ("v", dn_one_other)]
        + copied(tokens, cotangent, exit_layer, ln1_gain, dmiddle),
        [("d", whole(128, 768, dtype=f32))],
    )
    (
        q_weight_grad, k_weight_grad, v_weight_grad, o_weight_grad_t,
        ln1_gain_grad, ln1_shift_grad, q_bias_grad, v_bias_grad,
        up_bias_grad, down_bias_grad, ln2_gain_grad, ln2_shift_grad, o_bias_grad,
    ) = call(
        finish_kernel, "finish", 8,
        [("v", tail), ("d", order)],
        [("d", whole(12, 384, dtype=f32)) for _ in range(4)]
        + [
            ("d", whole(count, dtype=f32))
            for count in (768, 768, 384, 384, 1536, 768, 768, 768, 768)
        ],
        lazy=(1,),
    )
    return (
        output,
        input_grad,
        ln1_gain_grad,
        ln1_shift_grad,
        q_weight_grad,
        q_bias_grad,
        k_weight_grad,
        v_weight_grad,
        v_bias_grad,
        o_weight_grad_t,
        o_bias_grad,
        ln2_gain_grad,
        ln2_shift_grad,
        up_weight_grad,
        up_bias_grad,
        down_weight_grad_t,
        down_bias_grad,
    )


def solution(mesh):
    fine = Mesh(mesh.devices.reshape(4, 4, 2, 2, 2), CTX + ("wa",))
    return jax.shard_map(
        on_device,
        mesh=fine,
        in_specs=(
            P(CTX, None),
            P(CTX),
            P(CTX),
            P(CTX, None),
            P(),
            P(),
            P(None, "wa"),
            P("wa"),
            P(None, "wa"),
            P(None, "wa"),
            P("wa"),
            P("wa", None),
            P(),
            P(),
            P(),
            P(None, "wa"),
            P("wa"),
            P("wa", None),
            P(),
        ),
        out_specs=(
            P(CTX, None),
            P(CTX, None),
            P(),
            P(),
            P(CTX, "wa"),
            P("wa"),
            P(CTX, "wa"),
            P(CTX, "wa"),
            P("wa"),
            P(CTX, "wa"),
            P(),
            P(),
            P(),
            P(CTX, "wa"),
            P("wa"),
            P(CTX, "wa"),
            P(),
        ),
        check_vma=False,
    )
```

```python
import math

import jax
import jax.numpy as jnp
from jax import lax
from jax.experimental import pallas as pl
from jax.experimental.pallas import tpu as pltpu
from jax.sharding import Mesh, PartitionSpec as P

HEAD_DIM = 64
LAYER = 6
CTX = ("x", "y", "zh", "core")
PLANE = ("x", "y")
SWAP = ((0, 1), (1, 0))
CROSS = ((0, 3), (1, 2), (2, 1), (3, 0))
HALF = 64
BLOCKS = 16
GROUP = 256
STREAM = 8192
ROWS = (BLOCKS + 1) * HALF
FF_TILE = 512
FAR = 1e9
SCALING = 1.0 / math.sqrt(HEAD_DIM)
EXP2_SCALE = SCALING / math.log(2.0)
VMEM_BYTES = 64 * 2**20


epsilon = 1e-05
trans_right = (((1,), (1,)), ((), ()))
trans_left = (((0,), (0,)), ((), ()))
cubic_coef = 0.044715


def gelu_pair(values):
    outer = math.sqrt(2.0 / math.pi)
    inner = outer * (values + cubic_coef * values * values * values)
    tangent = jnp.tanh(inner)
    result = 0.5 * values * (1.0 + tangent)
    gelu_slope = 0.5 * (1.0 + tangent) + 0.5 * values * (1.0 - tangent * tangent) * outer * (
        1.0 + 3.0 * cubic_coef * values * values
    )
    return (result, gelu_slope)


def norm_forward(values, gain_vec, shift_vec):
    average = jnp.mean(values, axis=-1, keepdims=True)
    centred = values - average
    inverse_std = lax.rsqrt(jnp.mean(centred * centred, axis=-1, keepdims=True) + epsilon)
    normed = centred * inverse_std
    return (normed * gain_vec + shift_vec, normed, inverse_std)


def norm_backward(grad_out, normed, inverse_std, gain_vec):
    scaled = grad_out * gain_vec
    return inverse_std * (
        scaled
        - jnp.mean(scaled, axis=-1, keepdims=True)
        - normed * jnp.mean(scaled * normed, axis=-1, keepdims=True)
    )


def swap_add(part, axis):
    other = lax.ppermute(part, axis, SWAP)
    return part.astype(jnp.float32) + other.astype(jnp.float32)


def whole(*shape, dtype=jnp.bfloat16):
    return jax.ShapeDtypeStruct(shape, dtype)


def head_place():
    upper = lax.axis_index("y") % 2
    sub = 2 * lax.axis_index("zh") + lax.axis_index("core")
    last = sub == 3
    return (
        upper,
        jnp.where(upper == 1, 3 - sub, sub),
        jnp.where((upper == 0) & last, 1, 0),
        jnp.where((upper == 1) & last, 1, 0),
    )


def call(kernel, name, ins, outs, scratch=(), lazy=()):
    copied_in = [at for at, (mode, _) in enumerate(ins) if mode == "d"]
    copied_out = [at for at, (mode, _) in enumerate(outs) if mode == "d"]

    def buffer(array):
        shape = array.shape if len(array.shape) > 1 else (1,) + tuple(array.shape)
        return pltpu.VMEM(shape, array.dtype)

    def body(*refs):
        given, rest = list(refs[: len(ins)]), refs[len(ins) :]
        results, rest = list(rest[: len(outs)]), rest[len(outs) :]
        in_buffers, rest = rest[: len(copied_in)], rest[len(copied_in) :]
        out_buffers, rest = rest[: len(copied_out)], rest[len(copied_out) :]
        in_sems, out_sems, rest = rest[0], rest[1], rest[2:]
        pending, flushing = [], []
        for slot, at in enumerate(copied_in):
            there = in_buffers[slot]
            into = there if len(ins[at][1].shape) > 1 else there.at[0]
            copy = pltpu.make_async_copy(given[at], into, in_sems.at[slot])
            copy.start()
            given[at] = there
            pending.append((there, at, copy))
        targets = []
        for slot, at in enumerate(copied_out):
            made = out_buffers[slot] if len(outs[at][1].shape) > 1 else out_buffers[slot].at[0]
            copy = pltpu.make_async_copy(made, results[at], out_sems.at[slot])
            results[at] = out_buffers[slot]
            targets.append((out_buffers[slot], copy))

        def wait(ref):
            for entry in list(pending):
                if entry[0] is ref:
                    entry[2].wait()
                    pending[:] = [other for other in pending if other is not entry]

        def flush(ref):
            for entry in list(targets):
                if entry[0] is ref:
                    entry[1].start()
                    flushing.append(entry[1])
                    targets[:] = [other for other in targets if other is not entry]

        for entry in list(pending):
            if entry[1] not in lazy:
                wait(entry[0])
        kernel(wait, flush, *given, *results, *rest)
        for entry in list(pending):
            wait(entry[0])
        for entry in list(targets):
            flush(entry[0])
        for copy in flushing:
            copy.wait()

    vmem, anywhere = pl.BlockSpec(memory_space=pltpu.VMEM), pl.BlockSpec(memory_space=pltpu.HBM)
    result = pl.pallas_call(
        body,
        out_shape=tuple(out for _, out in outs),
        in_specs=[anywhere if mode == "d" else vmem for mode, _ in ins],
        out_specs=tuple(anywhere if mode == "d" else vmem for mode, _ in outs),
        scratch_shapes=[buffer(ins[at][1]) for at in copied_in]
        + [buffer(outs[at][1]) for at in copied_out]
        + [
            pltpu.SemaphoreType.DMA((max(1, len(copied_in)),)),
            pltpu.SemaphoreType.DMA((max(1, len(copied_out)),)),
        ]
        + list(scratch),
        compiler_params=pltpu.CompilerParams(vmem_limit_bytes=VMEM_BYTES),
        name=name,
    )(*[array for _, array in ins])
    return result[0] if len(outs) == 1 else result


def lane_ids(rows, cols):
    return lax.broadcasted_iota(jnp.int32, (rows, cols), 1)


def row_ids_of(rows, cols):
    return lax.broadcasted_iota(jnp.int32, (rows, cols), 0)


def turn(values):
    return pltpu.roll(values, HALF, 1)


def unpack_low(packed):
    wide = packed.astype(jnp.float32)
    left = lane_ids(32, 128) < HALF
    both = jnp.concatenate([wide, turn(wide)], axis=0)
    return jnp.where(jnp.concatenate([left, left], axis=0), both, 0.0)


def unpack_high(packed):
    wide = packed.astype(jnp.float32)
    right = lane_ids(32, 128) >= HALF
    both = jnp.concatenate([turn(wide), wide], axis=0)
    return jnp.where(jnp.concatenate([right, right], axis=0), both, 0.0)


def pack_from_low(block):
    return jnp.where(lane_ids(32, 128) < HALF, block[:32], turn(block[32:]))


def pack_from_high(block):
    return jnp.where(lane_ids(32, 128) < HALF, turn(block[:32]), block[32:])


def key_places(scal, group):
    lane = lane_ids(8, GROUP)
    sub = (lane >> 6) ^ scal[1]
    return (scal[0] * (STREAM // 2) + GROUP * group + (sub << 6) + (lane & 63)).astype(
        jnp.float32
    )


def edge_places():
    return (STREAM // 2 + lane_ids(8, 128)).astype(jnp.float32)


def query_places(scal, block):
    row = row_ids_of(HALF, 128)
    return (
        scal[0] * (STREAM // 2) + GROUP * block + (scal[1] << 6) + row
    ).astype(jnp.float32)


def spread(rows, width):
    return jnp.concatenate([rows] * (width // 128), axis=1) if width > 128 else rows


def weights_of(scal, queries, starts, keys, places, group):
    scores = lax.dot_general(queries, keys, trans_right, preferred_element_type=jnp.float32)
    count = queries.shape[0]
    own = spread(query_places(scal, group), GROUP)
    limit = jnp.concatenate([own, jnp.full((count - HALF, GROUP), FAR, jnp.float32)], axis=0)
    seen = (spread(starts, GROUP) <= places[:1]) & (places[:1] <= limit)
    return jnp.where(seen, jnp.exp2(scores * EXP2_SCALE), 0.0)


def edge_weights(queries, starts, keys):
    scores = lax.dot_general(queries, keys, trans_right, preferred_element_type=jnp.float32)
    places = edge_places()[:1]
    limit = (STREAM // 2 + row_ids_of(HALF, 128)).astype(jnp.float32)
    return jnp.where(
        (starts <= places) & (places <= limit), jnp.exp2(scores * EXP2_SCALE), 0.0
    )


def attend_kernel(
    wait, flush, own_ref, one_ref, two_ref, three_ref, edge_ref,
    back_ref, kv_ref, q_ref, start_ref, full_ref,
    num_ref, den_ref,
):
    scal = head_place()
    upper = scal[0]
    diag = jnp.where(
        lane_ids(HALF, 128) == row_ids_of(HALF, 128),
        64.0,
        jnp.where(lane_ids(HALF, 128) == row_ids_of(HALF, 128) + HALF, 1.0, 0.0),
    )

    def starts(line, off):
        found = jnp.sum(line.astype(jnp.float32) * diag, axis=1, keepdims=True)
        return jnp.broadcast_to(jnp.where(off, FAR, found), (HALF, 128))

    for block in range(BLOCKS):
        place = jnp.where(upper == 1, BLOCKS - 1 - block, block)
        rows = slice(block * HALF, (block + 1) * HALF)
        mine = own_ref[pl.ds(place, 1)][0]
        kv_ref[block, 0:HALF] = mine[:HALF]
        kv_ref[block, HALF : 2 * HALF] = one_ref[pl.ds(place, 1)][0]
        kv_ref[block, 2 * HALF : 3 * HALF] = two_ref[pl.ds(place, 1)][0]
        kv_ref[block, 3 * HALF :] = three_ref[pl.ds(place, 1)][0]
        q_ref[rows] = unpack_low(mine[HALF : HALF + 32]).astype(jnp.bfloat16)
        off = (scal[3] == 1) if block == 0 else False
        start_ref[rows] = starts(mine[HALF + 32 : HALF + 33], off)
    kv_ref[BLOCKS] = jnp.zeros((GROUP, 128), jnp.bfloat16)
    kv_ref[BLOCKS, :HALF] = edge_ref[:HALF]
    q_ref[BLOCKS * HALF :] = unpack_low(edge_ref[HALF : HALF + 32]).astype(jnp.bfloat16)
    start_ref[BLOCKS * HALF :] = starts(edge_ref[HALF + 32 : HALF + 33], scal[2] == 0)
    flush(kv_ref)
    flush(q_ref)
    flush(start_ref)

    for group in range(BLOCKS + 1):
        rows = slice(group * HALF, ROWS)
        if group < BLOCKS:
            keys = kv_ref[group]
            weights = weights_of(
                scal, q_ref[rows], start_ref[rows], keys, key_places(scal, group), group
            )
            total = weights[:, :128] + weights[:, 128:]
        else:
            keys = kv_ref[group, :128]
            weights = total = edge_weights(q_ref[rows], start_ref[rows], keys)
        product = jnp.dot(weights.astype(jnp.bfloat16), keys, preferred_element_type=jnp.float32)
        if group == 0:
            num_ref[rows] = product
            den_ref[rows] = total
        else:
            num_ref[rows] += product
            den_ref[rows] += total

    for block in range(BLOCKS + 1):
        rows = slice(block * HALF, (block + 1) * HALF)
        den = jnp.sum(den_ref[rows], axis=1, keepdims=True)
        recip = jnp.broadcast_to(1.0 / jnp.where(den == 0.0, 1.0, den), (HALF, 128))
        full = num_ref[rows] * recip
        full_ref[rows] = jnp.where(lane_ids(HALF, 128) < HALF, recip, full)
        packed = pack_from_high(full).astype(jnp.bfloat16)
        if block < BLOCKS:
            place = jnp.where(upper == 1, BLOCKS - 1 - block, block)
            for copy in range(2):
                back_ref[pl.ds(2 * place + copy, 1), :32] = packed[None]
                back_ref[pl.ds(2 * place + copy, 1), 32:] = jnp.zeros((1, 32, 128), jnp.bfloat16)
        else:
            for copy in range(2):
                back_ref[2 * BLOCKS - 2 + copy, 32:] = packed


def attend_grad_kernel(
    wait, flush, kv_ref, q_ref, start_ref, full_ref, dh_in_ref,
    send_ref, keep_ref, dq_ref, edge_ref,
    dhn_ref, dot_ref, dq_acc,
):
    scal = head_place()
    upper = scal[0]
    left = lane_ids(HALF, 128) < HALF
    wait(full_ref)
    for block in range(BLOCKS + 1):
        rows = slice(block * HALF, (block + 1) * HALF)
        if block < BLOCKS:
            place = jnp.where(upper == 1, BLOCKS - 1 - block, block)
            packed = dh_in_ref[pl.ds(place, 1), :32][0]
        else:
            packed = dh_in_ref[BLOCKS - 1, 32:]
        full = full_ref[rows]
        scaled = unpack_high(packed) * jnp.where(left, full, turn(full))
        scaled = scaled.astype(jnp.bfloat16).astype(jnp.float32)
        dhn_ref[rows] = scaled.astype(jnp.bfloat16)
        dot_ref[rows] = jnp.broadcast_to(
            jnp.sum(jnp.where(left, 0.0, scaled * full), axis=1, keepdims=True), (HALF, 128)
        )
    wait(kv_ref)
    wait(q_ref)
    wait(start_ref)
    for group in range(BLOCKS + 1):
        rows = slice(group * HALF, ROWS)
        if group < BLOCKS:
            keys = kv_ref[group]
            weights = weights_of(
                scal, q_ref[rows], start_ref[rows], keys, key_places(scal, group), group
            )
        else:
            keys = kv_ref[group, :128]
            weights = edge_weights(q_ref[rows], start_ref[rows], keys)
        dprob = lax.dot_general(
            dhn_ref[rows], keys, trans_right, preferred_element_type=jnp.float32
        )
        dscore = (weights * (dprob - spread(dot_ref[rows], keys.shape[0]))).astype(jnp.bfloat16)
        dquery = jnp.dot(dscore, keys, preferred_element_type=jnp.float32)
        if group == 0:
            dq_acc[rows] = dquery
        else:
            dq_acc[rows] += dquery
        grads = lax.dot_general(
            dscore, q_ref[rows], trans_left, preferred_element_type=jnp.float32
        ) * SCALING + lax.dot_general(
            weights.astype(jnp.bfloat16),
            dhn_ref[rows],
            trans_left,
            preferred_element_type=jnp.float32,
        )
        low = grads.astype(jnp.bfloat16)
        if group < BLOCKS:
            place = jnp.where(upper == 1, BLOCKS - 1 - group, group)
            for quarter in range(4):
                out = send_ref if quarter % 2 else keep_ref
                out[pl.ds(quarter // 2 * BLOCKS + place, 1)] = low[
                    None, quarter * HALF : (quarter + 1) * HALF
                ]
        else:
            edge_ref[:HALF] = low[:HALF]

    for block in range(BLOCKS + 1):
        rows = slice(block * HALF, (block + 1) * HALF)
        packed = pack_from_low(dq_acc[rows] * SCALING).astype(jnp.bfloat16)
        if block < BLOCKS:
            place = jnp.where(upper == 1, BLOCKS - 1 - block, block)
            dq_ref[pl.ds(place, 1)] = packed[None]
        else:
            edge_ref[HALF:] = packed


def attend(own, one, two, three, edge):
    f32 = jnp.float32
    return call(
        attend_kernel, "attend",
        [("v", own), ("v", one), ("v", two), ("v", three), ("v", edge)],
        [
            ("d", whole(2 * BLOCKS, HALF, 128)),
            ("d", whole(BLOCKS + 1, GROUP, 128)),
            ("d", whole(ROWS, 128)),
            ("d", whole(ROWS, 128, dtype=f32)),
            ("d", whole(ROWS, 128, dtype=f32)),
        ],
        [pltpu.VMEM((ROWS, 128), f32), pltpu.VMEM((ROWS, 128), f32)],
    )


def attend_grad(kv, q, start, full, dh):
    f32 = jnp.float32
    return call(
        attend_grad_kernel, "attend_grad",
        [("d", kv), ("d", q), ("d", start), ("d", full), ("v", dh)],
        [
            ("v", whole(2 * BLOCKS, HALF, 128)),
            ("v", whole(2 * BLOCKS, HALF, 128)),
            ("v", whole(BLOCKS, 32, 128)),
            ("v", whole(96, 128)),
        ],
        [
            pltpu.VMEM((ROWS, 128), jnp.bfloat16),
            pltpu.VMEM((ROWS, 128), f32),
            pltpu.VMEM((ROWS, 128), f32),
        ],
        lazy=(0, 1, 2, 3),
    )


def column(line):
    return jnp.sum(
        jnp.where(lane_ids(128, 128) == row_ids_of(128, 128), line, 0.0), axis=1, keepdims=True
    )


def pairs_low(even, odd):
    left = lane_ids(32, 128) < HALF
    return jnp.concatenate(
        [jnp.where(left, even, turn(odd)), jnp.where(left, turn(even), odd)], axis=0
    )


def project_kernel(
    wait, flush,
    tokens_ref, start_ref, gain_ref, shift_ref, q_bias_ref, v_bias_ref, q_ref, k_ref, v_ref,
    pay_ref, low_ref,
):
    normed, _, _ = norm_forward(tokens_ref[...].astype(jnp.float32), gain_ref[...], shift_ref[...])
    low = normed.astype(jnp.bfloat16)
    low_ref[...] = low
    flush(low_ref)
    starts = start_ref[...]
    high_part = (starts >> 6).astype(jnp.float32)
    low_part = (starts & 63).astype(jnp.float32)
    left = lane_ids(1, 128) < HALF
    lines = (
        jnp.where(left, high_part, turn(low_part)),
        jnp.where(left, turn(high_part), low_part),
    )
    lines = [jnp.broadcast_to(line, (16, 128)).astype(jnp.bfloat16) for line in lines]
    wide = lane_ids(HALF, 128) < HALF
    for ref in (q_ref, k_ref, v_ref):
        wait(ref)
    for pair in range(3):
        columns = slice(pair * 128, (pair + 1) * 128)
        queries = (
            jnp.dot(low, q_ref[:, columns], preferred_element_type=jnp.float32)
            + q_bias_ref[:, columns]
        )
        keyset = jnp.dot(low, k_ref[:, columns], preferred_element_type=jnp.float32)
        values = (
            jnp.dot(low, v_ref[:, columns], preferred_element_type=jnp.float32)
            + v_bias_ref[:, columns]
        )
        for half in range(2):
            rows = slice(half * HALF, (half + 1) * HALF)
            for odd in range(2):
                if odd:
                    both = jnp.where(wide, turn(keyset[rows]), values[rows])
                    packed = pack_from_high(queries[rows])
                else:
                    both = jnp.where(wide, keyset[rows], turn(values[rows]))
                    packed = pack_from_low(queries[rows])
                index = 4 * pair + 2 * odd + half
                pay_ref[index, :HALF] = both.astype(jnp.bfloat16)
                pay_ref[index, HALF : HALF + 32] = packed.astype(jnp.bfloat16)
                pay_ref[index, HALF + 32 :] = lines[half]
    pay_ref[12:] = jnp.zeros((4, HALF + 48, 128), jnp.bfloat16)


def prepare_kernel(wait, flush, low_ref, send_ref, order_ref, keep_ref):
    lane = lane_ids(8, 768)
    core = (lane >= 384).astype(jnp.int32)
    rest = lane - 384 * core
    plane = (rest * 171) >> 12
    within = rest - 24 * plane
    high = (within >= 12).astype(jnp.int32)
    source = (48 * plane + 12 * (2 * high + core) + (within - 12 * high))[:1]
    order = jnp.where(row_ids_of(768, 768) == source, 1.0, 0.0).astype(jnp.bfloat16)
    order_ref[...] = order
    flush(order_ref)
    ordered = jnp.dot(low_ref[...], order, preferred_element_type=jnp.float32).astype(jnp.bfloat16)
    first = lax.axis_index("core") == 0
    keep_ref[...] = jnp.where(first, ordered[:, :384], ordered[:, 384:])
    send_ref[...] = jnp.where(first, ordered[:, 384:], ordered[:, :384])


def attn_tile(got_ref, side, pair):
    parts = []
    for half in range(2):
        heads = []
        for odd in range(2):
            index = 4 * pair + 2 * odd
            lower = got_ref[pl.ds(2 * index + side, 1)][0].astype(jnp.float32)
            if half:
                higher = got_ref[pl.ds(2 * index + 2 + side, 1)][0].astype(jnp.float32)
                packed = higher[:32] + lower[32:]
            else:
                packed = lower[:32]
            heads.append(packed)
        parts.append(pairs_low(*heads))
    return jnp.concatenate(parts, axis=0).astype(jnp.bfloat16)


def middle_kernel(
    wait, flush, got_ref, tokens_ref, cot_ref, exit_ref, o_bias_ref, gain_ref, shift_ref,
    up_bias_ref, o_own_ref, o_other_ref, up_ref, down_ref,
    dn_ref, send_ref, keep_ref, mid_ref, ffn_ref, attn_ref, vec_ref,
    acc_ref,
):
    first = lax.axis_index("core") == 0
    side = lax.axis_index("wa")
    for pair in range(3):
        rows = slice(pair * 128, (pair + 1) * 128)
        attn_ref[:, rows] = attn_tile(got_ref, side, pair)
        acc_ref[:, rows] = attn_tile(got_ref, 1 - side, pair)
    flush(attn_ref)
    wait(o_own_ref)
    wait(o_other_ref)
    total = jnp.dot(
        attn_ref[...], o_own_ref[...], preferred_element_type=jnp.float32
    ) + jnp.dot(acc_ref[...], o_other_ref[...], preferred_element_type=jnp.float32)
    middle = tokens_ref[...].astype(jnp.float32) + (total + o_bias_ref[...])
    mid_ref[...] = middle
    flush(mid_ref)
    normed, _, _ = norm_forward(middle, gain_ref[...], shift_ref[...])
    low = normed.astype(jnp.bfloat16)
    active = column((exit_ref[...] > LAYER).astype(jnp.float32))
    branch = jnp.where(active > 0.0, cot_ref[...].astype(jnp.float32), 0.0)
    branch_low = branch.astype(jnp.bfloat16)
    keep_ref[:, :768] = jnp.where(first, low, branch_low)
    send_ref[:, :768] = jnp.where(first, branch_low, low)
    vec_ref[:, 1536:] = jnp.sum(branch, axis=0, keepdims=True)
    ffn = None
    dnormed = None
    wait(up_ref)
    wait(down_ref)
    for begin in range(0, 1536, FF_TILE):
        columns = slice(begin, begin + FF_TILE)
        outs = slice(768 + begin, 768 + begin + FF_TILE)
        pre_act = (
            jnp.dot(low, up_ref[:, columns], preferred_element_type=jnp.float32)
            + up_bias_ref[:, columns]
        )
        hidden_full, slope = gelu_pair(pre_act)
        hidden = hidden_full.astype(jnp.bfloat16)
        dhidden = lax.dot_general(
            branch_low, down_ref[columns], trans_right, preferred_element_type=jnp.float32
        )
        dpre = (dhidden * slope).astype(jnp.bfloat16)
        vec_ref[:, columns] = jnp.sum(dpre.astype(jnp.float32), axis=0, keepdims=True)
        keep_ref[:, outs] = jnp.where(first, dpre, hidden)
        send_ref[:, outs] = jnp.where(first, hidden, dpre)
        ffn_term = jnp.dot(hidden, down_ref[columns], preferred_element_type=jnp.float32)
        dn_term = lax.dot_general(
            dpre, up_ref[:, columns], trans_right, preferred_element_type=jnp.float32
        )
        ffn = ffn_term if ffn is None else ffn + ffn_term
        dnormed = dn_term if dnormed is None else dnormed + dn_term
    ffn_ref[...] = ffn.astype(jnp.bfloat16)
    dn_ref[...] = dnormed.astype(jnp.bfloat16)


def dheads_kernel(
    wait, flush, dn_ref, other_ref, mid_ref, cot_ref, exit_ref, gain_ref, o_ref, attn_ref, order_ref,
    pay_ref, send_ref, keep_ref, dmid_ref, vec_ref,
):
    middle = mid_ref[...]
    _, unit, inverse = norm_forward(middle, gain_ref[...], 0.0)
    dnormed = dn_ref[...].astype(jnp.float32) + other_ref[...].astype(jnp.float32)
    active = column((exit_ref[...] > LAYER).astype(jnp.float32))
    branch = jnp.where(active > 0.0, cot_ref[...].astype(jnp.float32), 0.0)
    dmiddle = branch + norm_backward(dnormed, unit, inverse, gain_ref[...])
    dmid_ref[...] = dmiddle
    flush(dmid_ref)
    low = dmiddle.astype(jnp.bfloat16)
    vec_ref[:, :768] = jnp.sum(dnormed * unit, axis=0, keepdims=True)
    vec_ref[:, 768:1536] = jnp.sum(dnormed, axis=0, keepdims=True)
    vec_ref[:, 1536:] = jnp.sum(low.astype(jnp.float32), axis=0, keepdims=True)
    wait(o_ref)
    for pair in range(3):
        dheads = lax.dot_general(
            low,
            o_ref[pair * 128 : (pair + 1) * 128],
            trans_right,
            preferred_element_type=jnp.float32,
        )
        for odd in range(2):
            pack = pack_from_high if odd else pack_from_low
            lower = pack(dheads[:HALF]).astype(jnp.bfloat16)
            higher = pack(dheads[HALF:]).astype(jnp.bfloat16)
            index = 4 * pair + 2 * odd
            pay_ref[index, :32] = lower
            pay_ref[index, 32:] = higher
            pay_ref[index + 1, :32] = higher
            pay_ref[index + 1, 32:] = higher
    pay_ref[12:] = jnp.zeros((4, HALF, 128), jnp.bfloat16)
    flush(pay_ref)
    wait(order_ref)
    ordered = jnp.dot(low, order_ref[...], preferred_element_type=jnp.float32).astype(jnp.bfloat16)
    first = lax.axis_index("core") == 0
    keep_ref[:, :384] = jnp.where(first, ordered[:, :384], ordered[:, 384:])
    send_ref[:, :384] = jnp.where(first, ordered[:, 384:], ordered[:, :384])
    keep_ref[:, 384:] = attn_ref[...]
    send_ref[:, 384:] = attn_ref[...]


def o_products_kernel(wait, flush, keep_ref, sent_ref, far_ref, near_ref):
    both = jnp.concatenate([keep_ref[...], sent_ref[...]], axis=0)
    low = lax.axis_index("zh") == 0
    product = lax.dot_general(
        both[:, :384], both[:, 384:], trans_left, preferred_element_type=jnp.float32
    )
    spare = jnp.zeros((4, 384), jnp.float32)
    for plane in range(16):
        one = jnp.concatenate([product[24 * plane : 24 * plane + 12], spare], axis=0)
        two = jnp.concatenate([product[24 * plane + 12 : 24 * plane + 24], spare], axis=0)
        near_ref[plane] = jnp.where(low, one, two)
        far_ref[plane] = jnp.where(low, two, one).astype(jnp.bfloat16)


def ffn_products_kernel(wait, flush, keep_ref, sent_ref, out_ref):
    for at in range(768, 2304, 384):
        columns = slice(at, at + 384)
        lefts = jnp.concatenate([keep_ref[:, :768], sent_ref[:, :768]], axis=0)
        rights = jnp.concatenate([keep_ref[:, columns], sent_ref[:, columns]], axis=0)
        out_ref[:, at - 768 : at - 384] = lax.dot_general(
            lefts, rights, trans_left, preferred_element_type=jnp.float32
        ).astype(jnp.bfloat16)


def dnormed_kernel(
    wait, flush, got_ref, tokens_ref, ffn_ref, two_ref, q_ref, k_ref, v_ref,
    grads_ref, vec_ref, dn_ref,
):
    wide = lane_ids(HALF, 128) < HALF
    for pair in range(3):
        columns = slice(pair * 128, (pair + 1) * 128)
        key_columns = slice(384 + pair * 128, 512 + pair * 128)
        value_columns = slice(768 + pair * 128, 896 + pair * 128)
        for half in range(2):
            rows = slice(half * HALF, (half + 1) * HALF)
            even = got_ref[4 * pair + half, :96].astype(jnp.float32)
            odd = got_ref[4 * pair + 2 + half, :96].astype(jnp.float32)
            grads_ref[rows, key_columns] = jnp.where(wide, even[:HALF], turn(odd[:HALF])).astype(
                jnp.bfloat16
            )
            grads_ref[rows, value_columns] = jnp.where(
                wide, turn(even[:HALF]), odd[:HALF]
            ).astype(jnp.bfloat16)
            grads_ref[rows, columns] = pairs_low(even[HALF:], odd[HALF:]).astype(jnp.bfloat16)
    for ref in (q_ref, k_ref, v_ref):
        wait(ref)
    dnormed = (
        lax.dot_general(
            grads_ref[:, :384], q_ref[...], trans_right, preferred_element_type=jnp.float32
        )
        + lax.dot_general(
            grads_ref[:, 384:768], k_ref[...], trans_right, preferred_element_type=jnp.float32
        )
        + lax.dot_general(
            grads_ref[:, 768:], v_ref[...], trans_right, preferred_element_type=jnp.float32
        )
    )
    dn_ref[...] = dnormed.astype(jnp.bfloat16)
    _, unit, _ = norm_forward(tokens_ref[...].astype(jnp.float32), 1.0, 0.0)
    total = jnp.sum(grads_ref[...].astype(jnp.float32), axis=0, keepdims=True)
    vec_ref[:, :768] = jnp.sum(dnormed, axis=0, keepdims=True)
    vec_ref[:, 768:1536] = jnp.sum(dnormed * unit, axis=0, keepdims=True)
    vec_ref[:, 1536:1920] = total[:, :384]
    vec_ref[:, 1920:2304] = total[:, 768:]
    vec_ref[:, 2304:4608] = ffn_ref[...]
    vec_ref[:, 4608:] = two_ref[...]


def input_grad_kernel(
    wait, flush, dn_ref, other_ref, tokens_ref, cot_ref, exit_ref, gain_ref, dmid_ref, out_ref
):
    _, unit, inverse = norm_forward(tokens_ref[...].astype(jnp.float32), 1.0, 0.0)
    dnormed = dn_ref[...].astype(jnp.float32) + other_ref[...].astype(jnp.float32)
    active = column((exit_ref[...] > LAYER).astype(jnp.float32))
    out_ref[...] = (
        dmid_ref[...]
        + norm_backward(dnormed, unit, inverse, gain_ref[...])
        + jnp.where(active > 0.0, 0.0, cot_ref[...].astype(jnp.float32))
    )


def far_kernel(wait, flush, kept_ref, taken_ref, far_ref):
    far_ref[...] = (
        kept_ref[BLOCKS:].astype(jnp.float32) + taken_ref[BLOCKS:].astype(jnp.float32)
    ).astype(jnp.bfloat16)


def merge_kernel(
    wait, flush, kept_ref, taken_ref, far_ref, dq_ref, edge_ref, o_near_ref, o_far_ref, out_ref
):
    for block in range(BLOCKS):
        pair = (
            kept_ref[block].astype(jnp.float32)
            + taken_ref[block].astype(jnp.float32)
            + far_ref[block].astype(jnp.float32)
        )
        query = dq_ref[block]
        if block == BLOCKS - 1:
            pair = pair + edge_ref[:HALF].astype(jnp.float32)
            query = (query.astype(jnp.float32) + edge_ref[HALF:].astype(jnp.float32)).astype(
                jnp.bfloat16
            )
        out_ref[block, :HALF] = pair.astype(jnp.bfloat16)
        out_ref[block, HALF:96] = query
        product = o_near_ref[block] + o_far_ref[block].astype(jnp.float32)
        for tile in range(3):
            out_ref[block, 96 + 16 * tile : 112 + 16 * tile] = product[
                :, 128 * tile : 128 * tile + 128
            ].astype(jnp.bfloat16)


def o_sums_kernel(wait, flush, got_ref, out_ref):
    for tile in range(3):
        rows = slice(96 + 16 * tile, 112 + 16 * tile)
        total = got_ref[0, rows].astype(jnp.float32)
        for source in range(1, 16):
            total = total + got_ref[source, rows].astype(jnp.float32)
        out_ref[:, 128 * tile : 128 * tile + 128] = total[:12]


def qkv_products_kernel(
    wait, flush, keep_ref, sent_ref, grads_ref, grads_sent_ref, vec_ref, vec_sent_ref, out_ref
):
    lefts = jnp.concatenate([keep_ref[...], sent_ref[...]], axis=0)
    vec = vec_ref[...] + vec_sent_ref[...]
    lines = jnp.concatenate(
        [vec[:, 1152 * row : 1152 * (row + 1)] for row in range(6)]
        + [jnp.zeros((2, 1152), jnp.float32)],
        axis=0,
    )
    for at in range(0, 1152, 384):
        columns = slice(at, at + 384)
        rights = jnp.concatenate([grads_ref[:, columns], grads_sent_ref[:, columns]], axis=0)
        product = lax.dot_general(lefts, rights, trans_left, preferred_element_type=jnp.float32)
        for plane in range(16):
            out_ref[plane, :, columns] = jnp.concatenate(
                [product[24 * plane : 24 * plane + 24], lines[:, columns]], axis=0
            ).astype(jnp.bfloat16)


def plane_sums_kernel(wait, flush, got_ref, far_ref, norm_ref, near_ref):
    total = got_ref[0].astype(jnp.float32)
    for source in range(1, 16):
        total = total + got_ref[source].astype(jnp.float32)
    low = lax.axis_index("zh") == 0
    spare = jnp.zeros((4, 1152), jnp.float32)
    one, two, vec = total[:12], total[12:24], total[24:32]
    near_ref[...] = jnp.concatenate([jnp.where(low, one, two), spare, vec], axis=0)
    far_ref[...] = jnp.concatenate([jnp.where(low, two, one), spare, vec], axis=0)
    norm_ref[...] = vec


def finish_kernel(
    wait, flush, near_ref, far_ref, wa_ref, cross_ref,
    q_ref, k_ref, v_ref, shift_out, gain_out, q_bias_out, v_bias_out,
    up_bias_out, down_bias_out, gain_two_out, shift_two_out, o_bias_out,
):
    both = near_ref[...] + far_ref[...]
    q_ref[...] = both[:12, :384]
    k_ref[...] = both[:12, 384:768]
    v_ref[...] = both[:12, 768:]
    vec = both[16:24]
    norms = vec + (wa_ref[...] + cross_ref[...])
    shift_out[...] = norms[0:1, :768]
    gain_out[:, :384] = norms[0:1, 768:]
    gain_out[:, 384:] = norms[1:2, :384]
    q_bias_out[...] = vec[1:2, 384:768]
    v_bias_out[...] = vec[1:2, 768:]
    up_bias_out[:, :1152] = vec[2:3]
    up_bias_out[:, 1152:] = vec[3:4, :384]
    down_bias_out[...] = vec[3:4, 384:]
    gain_two_out[...] = vec[4:5, :768]
    shift_two_out[:, :384] = vec[4:5, 768:]
    shift_two_out[:, 384:] = vec[5:6, :384]
    o_bias_out[...] = vec[5:6, 384:]


def sub_sums(summed):
    mine = summed.shape[0] // 4
    parts = summed.reshape(4, mine, summed.shape[1])
    me = lax.axis_index(("zh", "core"))

    def part(index):
        return lax.dynamic_index_in_dim(parts, index, 0, keepdims=False)

    here = part(me)
    core_way = lax.ppermute(part(jnp.bitwise_xor(me, 1)), "core", SWAP)
    z_way = lax.ppermute(part(jnp.bitwise_xor(me, 2)), "zh", SWAP)
    cross_way = lax.ppermute(part(jnp.bitwise_xor(me, 3)), ("zh", "core"), CROSS)
    mine_sum, other_sum = here + z_way, core_way + cross_way
    first = lax.axis_index("core") == 0
    return jnp.where(first, mine_sum, other_sum), jnp.where(first, other_sum, mine_sum)


def on_device(
    tokens,
    doc_start,
    exit_layer,
    cotangent,
    ln1_gain,
    ln1_shift,
    q_weight,
    q_bias,
    k_weight,
    v_weight,
    v_bias,
    o_weight,
    o_bias,
    ln2_gain,
    ln2_shift,
    up_weight,
    up_bias,
    down_weight,
    down_bias,
):
    f32 = jnp.float32

    def copied(*arrays):
        return [("d", array) for array in arrays]

    payload, low_one = call(
        project_kernel, "project",
        copied(
            tokens, doc_start, ln1_gain, ln1_shift, q_bias, v_bias, q_weight, k_weight, v_weight
        ),
        [("d", whole(16, HALF + 48, 128)), ("d", whole(128, 768))],
        lazy=(6, 7, 8),
    )
    own = lax.all_to_all(payload, PLANE, 0, 0, tiled=True)
    low_one, o_given = lax.optimization_barrier((low_one, o_weight))
    o_other = lax.ppermute(o_given, "wa", SWAP)
    x_send, order, x_keep = call(
        prepare_kernel, "prepare",
        copied(low_one),
        [("v", whole(128, 384)), ("d", whole(768, 768)), ("d", whole(128, 384))],
    )
    own, x_send, o_other = lax.optimization_barrier((own, x_send, o_other))
    pairs = own[:, :HALF]
    one = lax.ppermute(pairs, "core", SWAP)
    edge = lax.ppermute(own[BLOCKS - 1], "y", ((1, 0), (3, 2)))
    two = lax.ppermute(pairs, "zh", SWAP)
    two, edge = lax.optimization_barrier((two, edge))
    three = lax.ppermute(two, "core", SWAP)
    x_sent = lax.ppermute(x_send, "core", SWAP)
    back, kv, q_rows, start_rows, full_rows = attend(own, one, two, three, edge)
    got = lax.all_to_all(back, ("x", "y", "wa"), 0, 0, tiled=True)
    dn_two, send, keep, middle, ffn, attn_low, vec_ffn = call(
        middle_kernel, "middle",
        [("v", got)]
        + copied(
            tokens, cotangent, exit_layer, o_bias, ln2_gain, ln2_shift, up_bias, o_weight, o_other,
            up_weight, down_weight,
        ),
        [
            ("v", whole(128, 768)),
            ("v", whole(128, 2304)),
            ("v", whole(128, 2304)),
            ("d", whole(128, 768, dtype=f32)),
            ("d", whole(128, 768)),
            ("d", whole(128, 384)),
            ("d", whole(1, 2304, dtype=f32)),
        ],
        [pltpu.VMEM((128, 384), jnp.bfloat16)],
        lazy=(8, 9, 10, 11),
    )
    dn_two_other = lax.ppermute(dn_two, "wa", SWAP)
    sent = lax.ppermute(send, "core", SWAP)
    ffn_products = call(
        ffn_products_kernel, "ffn_products",
        [("v", keep), ("v", sent)],
        [("d", whole(768, 1536))],
    )
    dh_payload, o_send, o_keep, dmiddle, vec_two = call(
        dheads_kernel, "dheads",
        [("v", dn_two), ("v", dn_two_other)]
        + copied(middle, cotangent, exit_layer, ln2_gain, o_weight, attn_low, order),
        [
            ("d", whole(16, HALF, 128)),
            ("v", whole(128, 768)),
            ("v", whole(128, 768)),
            ("d", whole(128, 768, dtype=f32)),
            ("d", whole(1, 2304, dtype=f32)),
        ],
        lazy=(6, 8),
    )
    dh = lax.all_to_all(dh_payload, PLANE, 0, 0, tiled=True)
    o_sent = lax.ppermute(o_send, "core", SWAP)
    o_far, o_near = call(
        o_products_kernel, "o_products",
        [("v", o_keep), ("v", o_sent)],
        [("v", whole(16, 16, 384)), ("d", whole(16, 16, 384, dtype=f32))],
    )
    o_got = lax.ppermute(o_far, "zh", SWAP)
    dh, ffn_products, o_got = lax.optimization_barrier((dh, ffn_products, o_got))
    ffn_blocks = lax.all_to_all(
        ffn_products.reshape(16, 48, 1536), PLANE, 0, 0, tiled=True
    )
    given, kept, dq, edge_grad = attend_grad(kv, q_rows, start_rows, full_rows, dh)
    edge_got = lax.ppermute(edge_grad, "y", ((0, 1), (2, 3)))
    taken = lax.ppermute(given, "core", SWAP)
    far = call(far_kernel, "far", [("v", kept), ("v", taken)], [("v", whole(BLOCKS, HALF, 128))])
    far = lax.ppermute(far, "zh", SWAP)
    merged = call(
        merge_kernel, "merge",
        [("v", kept), ("v", taken), ("v", far), ("v", dq), ("v", edge_got)] + copied(o_near, o_got),
        [("d", whole(BLOCKS, 144, 128))],
    )
    merged, ffn_blocks, ffn = lax.optimization_barrier((merged, ffn_blocks, ffn))
    grads = lax.all_to_all(merged, PLANE, 0, 0, tiled=True)
    grads_rows, vec, dn_one = call(
        dnormed_kernel, "dnormed",
        [("v", grads)] + copied(tokens, vec_ffn, vec_two, q_weight, k_weight, v_weight),
        [("v", whole(128, 1152)), ("v", whole(1, 6912, dtype=f32)), ("v", whole(128, 768))],
        lazy=(4, 5, 6),
    )
    o_weight_grad_t = call(
        o_sums_kernel, "o_sums", [("v", grads)], [("d", whole(12, 384, dtype=f32))]
    )
    grads_sent = lax.ppermute(grads_rows, "core", SWAP)
    vec_sent = lax.ppermute(vec, "core", SWAP)
    products = call(
        qkv_products_kernel, "qkv_products",
        copied(x_keep, x_sent)
        + [("v", grads_rows), ("v", grads_sent), ("v", vec), ("v", vec_sent)],
        [("d", whole(16, 32, 1152))],
    )
    products = lax.all_to_all(products, PLANE, 0, 0, tiled=True)
    far_sums, norm_sums, near_sums = call(
        plane_sums_kernel, "plane_sums",
        [("v", products)],
        [
            ("v", whole(24, 1152, dtype=f32)),
            ("v", whole(8, 1152, dtype=f32)),
            ("v", whole(24, 1152, dtype=f32)),
        ],
    )
    far_sums = lax.ppermute(far_sums, "zh", SWAP)
    wa_sums = lax.ppermute(norm_sums, "wa", SWAP)
    cross_sums = lax.ppermute(norm_sums, ("zh", "wa"), CROSS)
    dn_one_other = lax.ppermute(dn_one, "wa", SWAP)
    up_weight_grad, down_weight_grad_t = sub_sums(jnp.sum(ffn_blocks.astype(f32), axis=0))
    ffn_out = ffn.astype(f32) + lax.ppermute(ffn, "wa", SWAP).astype(f32) + down_bias
    output = jnp.where(
        (exit_layer > LAYER)[:, None], middle + ffn_out, tokens.astype(f32)
    ).astype(jnp.bfloat16)
    input_grad = call(
        input_grad_kernel, "input_grad",
        [("v", dn_one), ("v", dn_one_other)]
        + copied(tokens, cotangent, exit_layer, ln1_gain, dmiddle),
        [("d", whole(128, 768, dtype=f32))],
    )
    (
        q_weight_grad, k_weight_grad, v_weight_grad,
        ln1_shift_grad, ln1_gain_grad, q_bias_grad, v_bias_grad,
        up_bias_grad, down_bias_grad, ln2_gain_grad, ln2_shift_grad, o_bias_grad,
    ) = call(
        finish_kernel, "finish",
        [("v", near_sums), ("v", far_sums), ("v", wa_sums), ("v", cross_sums)],
        [("d", whole(12, 384, dtype=f32)) for _ in range(3)]
        + [
            ("d", whole(count, dtype=f32))
            for count in (768, 768, 384, 384, 1536, 768, 768, 768, 768)
        ],
    )
    return (
        output,
        input_grad,
        ln1_gain_grad,
        ln1_shift_grad,
        q_weight_grad,
        q_bias_grad,
        k_weight_grad,
        v_weight_grad,
        v_bias_grad,
        o_weight_grad_t,
        o_bias_grad,
        ln2_gain_grad,
        ln2_shift_grad,
        up_weight_grad,
        up_bias_grad,
        down_weight_grad_t,
        down_bias_grad,
    )


def solution(mesh):
    fine = Mesh(mesh.devices.reshape(4, 4, 2, 2, 2), CTX + ("wa",))
    return jax.shard_map(
        on_device,
        mesh=fine,
        in_specs=(
            P(CTX, None),
            P(CTX),
            P(CTX),
            P(CTX, None),
            P(),
            P(),
            P(None, "wa"),
            P("wa"),
            P(None, "wa"),
            P(None, "wa"),
            P("wa"),
            P("wa", None),
            P(),
            P(),
            P(),
            P(None, "wa"),
            P("wa"),
            P("wa", None),
            P(),
        ),
        out_specs=(
            P(CTX, None),
            P(CTX, None),
            P(),
            P(),
            P(CTX, "wa"),
            P("wa"),
            P(CTX, "wa"),
            P(CTX, "wa"),
            P("wa"),
            P(CTX, "wa"),
            P(),
            P(),
            P(),
            P(CTX, "wa"),
            P("wa"),
            P(CTX, "wa"),
            P(),
        ),
        check_vma=False,
    )
```

```python
import math

import jax
import jax.numpy as jnp
from jax import lax
from jax.experimental import pallas as pl
from jax.experimental.pallas import tpu as pltpu
from jax.sharding import Mesh, PartitionSpec as P

HEAD_DIM = 64
LAYER = 6
CTX = ("x", "y", "zh", "core")
CHIPS = ("x", "y", "zh")
PLANE = ("x", "y")
SWAP = ((0, 1), (1, 0))
CROSS = ((0, 3), (1, 2), (2, 1), (3, 0))
HALF = 64
BLOCKS = 16
GROUP = 256
STREAM = 8192
ROWS = (BLOCKS + 1) * HALF
FF_TILE = 512
FAR = 1e9
SCALING = 1.0 / math.sqrt(HEAD_DIM)
EXP2_SCALE = SCALING / math.log(2.0)
VMEM_BYTES = 64 * 2**20


epsilon = 1e-05
trans_right = (((1,), (1,)), ((), ()))
trans_left = (((0,), (0,)), ((), ()))
cubic_coef = 0.044715


def gelu_pair(values):
    outer = math.sqrt(2.0 / math.pi)
    inner = outer * (values + cubic_coef * values * values * values)
    tangent = jnp.tanh(inner)
    result = 0.5 * values * (1.0 + tangent)
    gelu_slope = 0.5 * (1.0 + tangent) + 0.5 * values * (1.0 - tangent * tangent) * outer * (
        1.0 + 3.0 * cubic_coef * values * values
    )
    return (result, gelu_slope)


def norm_forward(values, gain_vec, shift_vec):
    average = jnp.mean(values, axis=-1, keepdims=True)
    centred = values - average
    inverse_std = lax.rsqrt(jnp.mean(centred * centred, axis=-1, keepdims=True) + epsilon)
    normed = centred * inverse_std
    return (normed * gain_vec + shift_vec, normed, inverse_std)


def norm_backward(grad_out, normed, inverse_std, gain_vec):
    scaled = grad_out * gain_vec
    return inverse_std * (
        scaled
        - jnp.mean(scaled, axis=-1, keepdims=True)
        - normed * jnp.mean(scaled * normed, axis=-1, keepdims=True)
    )


def swap_add(part, axis):
    other = lax.ppermute(part, axis, SWAP)
    return part.astype(jnp.float32) + other.astype(jnp.float32)


def whole(*shape, dtype=jnp.bfloat16):
    return jax.ShapeDtypeStruct(shape, dtype)


def head_place():
    upper = lax.axis_index("y") % 2
    sub = 2 * lax.axis_index("zh") + lax.axis_index("core")
    last = sub == 3
    return (
        upper,
        jnp.where(upper == 1, 3 - sub, sub),
        jnp.where((upper == 0) & last, 1, 0),
        jnp.where((upper == 1) & last, 1, 0),
    )


def call(kernel, name, ins, outs, scratch=(), lazy=(), cost=2):
    copied_in = [at for at, (mode, _) in enumerate(ins) if mode == "d"]
    copied_out = [at for at, (mode, _) in enumerate(outs) if mode == "d"]

    def buffer(array):
        shape = array.shape if len(array.shape) > 1 else (1,) + tuple(array.shape)
        return pltpu.VMEM(shape, array.dtype)

    def body(*refs):
        given, rest = list(refs[: len(ins)]), refs[len(ins) :]
        results, rest = list(rest[: len(outs)]), rest[len(outs) :]
        in_buffers, rest = rest[: len(copied_in)], rest[len(copied_in) :]
        out_buffers, rest = rest[: len(copied_out)], rest[len(copied_out) :]
        in_sems, out_sems, rest = rest[0], rest[1], rest[2:]
        pending, flushing = [], []
        for slot, at in enumerate(copied_in):
            there = in_buffers[slot]
            into = there if len(ins[at][1].shape) > 1 else there.at[0]
            copy = pltpu.make_async_copy(given[at], into, in_sems.at[slot])
            copy.start()
            given[at] = there
            pending.append((there, at, copy))
        targets = []
        for slot, at in enumerate(copied_out):
            made = out_buffers[slot] if len(outs[at][1].shape) > 1 else out_buffers[slot].at[0]
            copy = pltpu.make_async_copy(made, results[at], out_sems.at[slot])
            results[at] = out_buffers[slot]
            targets.append((out_buffers[slot], copy))

        def wait(ref):
            for entry in list(pending):
                if entry[0] is ref:
                    entry[2].wait()
                    pending[:] = [other for other in pending if other is not entry]

        def flush(ref):
            for entry in list(targets):
                if entry[0] is ref:
                    entry[1].start()
                    flushing.append(entry[1])
                    targets[:] = [other for other in targets if other is not entry]

        for entry in list(pending):
            if entry[1] not in lazy:
                wait(entry[0])
        kernel(wait, flush, *given, *results, *rest)
        for entry in list(pending):
            wait(entry[0])
        for entry in list(targets):
            flush(entry[0])
        for copy in flushing:
            copy.wait()

    vmem, anywhere = pl.BlockSpec(memory_space=pltpu.VMEM), pl.BlockSpec(memory_space=pltpu.HBM)
    result = pl.pallas_call(
        body,
        out_shape=tuple(out for _, out in outs),
        in_specs=[anywhere if mode == "d" else vmem for mode, _ in ins],
        out_specs=tuple(anywhere if mode == "d" else vmem for mode, _ in outs),
        scratch_shapes=[buffer(ins[at][1]) for at in copied_in]
        + [buffer(outs[at][1]) for at in copied_out]
        + [
            pltpu.SemaphoreType.DMA((max(1, len(copied_in)),)),
            pltpu.SemaphoreType.DMA((max(1, len(copied_out)),)),
        ]
        + list(scratch),
        compiler_params=pltpu.CompilerParams(vmem_limit_bytes=VMEM_BYTES),
        cost_estimate=pl.CostEstimate(
            flops=cost * 10**9, transcendentals=0, bytes_accessed=0
        ),
        name=name,
    )(*[array for _, array in ins])
    return result[0] if len(outs) == 1 else result


def lane_ids(rows, cols):
    return lax.broadcasted_iota(jnp.int32, (rows, cols), 1)


def row_ids_of(rows, cols):
    return lax.broadcasted_iota(jnp.int32, (rows, cols), 0)


def turn(values):
    return pltpu.roll(values, HALF, 1)


def unpack_low(packed):
    wide = packed.astype(jnp.float32)
    left = lane_ids(32, 128) < HALF
    both = jnp.concatenate([wide, turn(wide)], axis=0)
    return jnp.where(jnp.concatenate([left, left], axis=0), both, 0.0)


def unpack_high(packed):
    wide = packed.astype(jnp.float32)
    right = lane_ids(32, 128) >= HALF
    both = jnp.concatenate([turn(wide), wide], axis=0)
    return jnp.where(jnp.concatenate([right, right], axis=0), both, 0.0)


def pack_from_low(block):
    return jnp.where(lane_ids(32, 128) < HALF, block[:32], turn(block[32:]))


def pack_from_high(block):
    return jnp.where(lane_ids(32, 128) < HALF, turn(block[:32]), block[32:])


def key_places(scal, group):
    lane = lane_ids(8, GROUP)
    sub = (lane >> 6) ^ scal[1]
    return (scal[0] * (STREAM // 2) + GROUP * group + (sub << 6) + (lane & 63)).astype(
        jnp.float32
    )


def edge_places():
    return (STREAM // 2 + lane_ids(8, 128)).astype(jnp.float32)


def query_places(scal, block):
    row = row_ids_of(HALF, 128)
    return (
        scal[0] * (STREAM // 2) + GROUP * block + (scal[1] << 6) + row
    ).astype(jnp.float32)


def spread(rows, width):
    return jnp.concatenate([rows] * (width // 128), axis=1) if width > 128 else rows


def weights_of(scal, queries, starts, keys, places, group):
    scores = lax.dot_general(queries, keys, trans_right, preferred_element_type=jnp.float32)
    count = queries.shape[0]
    own = spread(query_places(scal, group), GROUP)
    limit = jnp.concatenate([own, jnp.full((count - HALF, GROUP), FAR, jnp.float32)], axis=0)
    seen = (spread(starts, GROUP) <= places[:1]) & (places[:1] <= limit)
    return jnp.where(seen, jnp.exp2(scores * EXP2_SCALE), 0.0)


def edge_weights(queries, starts, keys):
    scores = lax.dot_general(queries, keys, trans_right, preferred_element_type=jnp.float32)
    places = edge_places()[:1]
    limit = (STREAM // 2 + row_ids_of(HALF, 128)).astype(jnp.float32)
    return jnp.where(
        (starts <= places) & (places <= limit), jnp.exp2(scores * EXP2_SCALE), 0.0
    )


def attend_kernel(
    wait, flush, own_ref, one_ref, two_ref, three_ref, edge_ref,
    back_ref, kv_ref, q_ref, start_ref, full_ref,
    num_ref, den_ref,
):
    scal = head_place()
    upper = scal[0]
    diag = jnp.where(
        lane_ids(HALF, 128) == row_ids_of(HALF, 128),
        64.0,
        jnp.where(lane_ids(HALF, 128) == row_ids_of(HALF, 128) + HALF, 1.0, 0.0),
    )

    def starts(line, off):
        found = jnp.sum(line.astype(jnp.float32) * diag, axis=1, keepdims=True)
        return jnp.broadcast_to(jnp.where(off, FAR, found), (HALF, 128))

    for block in range(BLOCKS):
        place = jnp.where(upper == 1, BLOCKS - 1 - block, block)
        rows = slice(block * HALF, (block + 1) * HALF)
        mine = own_ref[pl.ds(place, 1)][0]
        kv_ref[block, 0:HALF] = mine[:HALF]
        kv_ref[block, HALF : 2 * HALF] = one_ref[pl.ds(place, 1)][0]
        kv_ref[block, 2 * HALF : 3 * HALF] = two_ref[pl.ds(place, 1)][0]
        kv_ref[block, 3 * HALF :] = three_ref[pl.ds(place, 1)][0]
        q_ref[rows] = unpack_low(mine[HALF : HALF + 32]).astype(jnp.bfloat16)
        off = (scal[3] == 1) if block == 0 else False
        start_ref[rows] = starts(mine[HALF + 32 : HALF + 33], off)
    kv_ref[BLOCKS] = jnp.zeros((GROUP, 128), jnp.bfloat16)
    kv_ref[BLOCKS, :HALF] = edge_ref[:HALF]
    q_ref[BLOCKS * HALF :] = unpack_low(edge_ref[HALF : HALF + 32]).astype(jnp.bfloat16)
    start_ref[BLOCKS * HALF :] = starts(edge_ref[HALF + 32 : HALF + 33], scal[2] == 0)
    flush(kv_ref)
    flush(q_ref)
    flush(start_ref)

    for group in range(BLOCKS + 1):
        rows = slice(group * HALF, ROWS)
        if group < BLOCKS:
            keys = kv_ref[group]
            weights = weights_of(
                scal, q_ref[rows], start_ref[rows], keys, key_places(scal, group), group
            )
            total = weights[:, :128] + weights[:, 128:]
        else:
            keys = kv_ref[group, :128]
            weights = total = edge_weights(q_ref[rows], start_ref[rows], keys)
        product = jnp.dot(weights.astype(jnp.bfloat16), keys, preferred_element_type=jnp.float32)
        if group == 0:
            num_ref[rows] = product
            den_ref[rows] = total
        else:
            num_ref[rows] += product
            den_ref[rows] += total

    for block in range(BLOCKS + 1):
        rows = slice(block * HALF, (block + 1) * HALF)
        den = jnp.sum(den_ref[rows], axis=1, keepdims=True)
        recip = jnp.broadcast_to(1.0 / jnp.where(den == 0.0, 1.0, den), (HALF, 128))
        full = num_ref[rows] * recip
        full_ref[rows] = jnp.where(lane_ids(HALF, 128) < HALF, recip, full)
        packed = pack_from_high(full).astype(jnp.bfloat16)
        if block < BLOCKS:
            place = jnp.where(upper == 1, BLOCKS - 1 - block, block)
            for copy in range(2):
                back_ref[pl.ds(2 * place + copy, 1), :32] = packed[None]
                back_ref[pl.ds(2 * place + copy, 1), 32:] = jnp.zeros((1, 32, 128), jnp.bfloat16)
        else:
            for copy in range(2):
                back_ref[2 * BLOCKS - 2 + copy, 32:] = packed


def attend_grad_kernel(
    wait, flush, kv_ref, q_ref, start_ref, full_ref, dh_in_ref,
    send_ref, keep_ref, dq_ref, edge_ref,
    dhn_ref, dot_ref, dq_acc,
):
    scal = head_place()
    upper = scal[0]
    left = lane_ids(HALF, 128) < HALF
    wait(full_ref)
    for block in range(BLOCKS + 1):
        rows = slice(block * HALF, (block + 1) * HALF)
        if block < BLOCKS:
            place = jnp.where(upper == 1, BLOCKS - 1 - block, block)
            packed = dh_in_ref[pl.ds(place, 1), :32][0]
        else:
            packed = dh_in_ref[BLOCKS - 1, 32:]
        full = full_ref[rows]
        scaled = unpack_high(packed) * jnp.where(left, full, turn(full))
        scaled = scaled.astype(jnp.bfloat16).astype(jnp.float32)
        dhn_ref[rows] = scaled.astype(jnp.bfloat16)
        dot_ref[rows] = jnp.broadcast_to(
            jnp.sum(jnp.where(left, 0.0, scaled * full), axis=1, keepdims=True), (HALF, 128)
        )
    wait(kv_ref)
    wait(q_ref)
    wait(start_ref)
    for group in range(BLOCKS + 1):
        rows = slice(group * HALF, ROWS)
        if group < BLOCKS:
            keys = kv_ref[group]
            weights = weights_of(
                scal, q_ref[rows], start_ref[rows], keys, key_places(scal, group), group
            )
        else:
            keys = kv_ref[group, :128]
            weights = edge_weights(q_ref[rows], start_ref[rows], keys)
        dprob = lax.dot_general(
            dhn_ref[rows], keys, trans_right, preferred_element_type=jnp.float32
        )
        dscore = (weights * (dprob - spread(dot_ref[rows], keys.shape[0]))).astype(jnp.bfloat16)
        dquery = jnp.dot(dscore, keys, preferred_element_type=jnp.float32)
        if group == 0:
            dq_acc[rows] = dquery
        else:
            dq_acc[rows] += dquery
        grads = lax.dot_general(
            dscore, q_ref[rows], trans_left, preferred_element_type=jnp.float32
        ) * SCALING + lax.dot_general(
            weights.astype(jnp.bfloat16),
            dhn_ref[rows],
            trans_left,
            preferred_element_type=jnp.float32,
        )
        low = grads.astype(jnp.bfloat16)
        if group < BLOCKS:
            place = jnp.where(upper == 1, BLOCKS - 1 - group, group)
            for quarter in range(4):
                out = send_ref if quarter % 2 else keep_ref
                out[pl.ds(quarter // 2 * BLOCKS + place, 1)] = low[
                    None, quarter * HALF : (quarter + 1) * HALF
                ]
        else:
            edge_ref[:HALF] = low[:HALF]

    for block in range(BLOCKS + 1):
        rows = slice(block * HALF, (block + 1) * HALF)
        packed = pack_from_low(dq_acc[rows] * SCALING).astype(jnp.bfloat16)
        if block < BLOCKS:
            place = jnp.where(upper == 1, BLOCKS - 1 - block, block)
            dq_ref[pl.ds(place, 1)] = packed[None]
        else:
            edge_ref[HALF:] = packed


def attend(own, one, two, three, edge):
    f32 = jnp.float32
    return call(
        attend_kernel, "attend",
        [("v", own), ("v", one), ("v", two), ("v", three), ("v", edge)],
        [
            ("d", whole(2 * BLOCKS, HALF, 128)),
            ("d", whole(BLOCKS + 1, GROUP, 128)),
            ("d", whole(ROWS, 128)),
            ("d", whole(ROWS, 128, dtype=f32)),
            ("d", whole(ROWS, 128, dtype=f32)),
        ],
        [pltpu.VMEM((ROWS, 128), f32), pltpu.VMEM((ROWS, 128), f32)],
        cost=3,
    )


def attend_grad(kv, q, start, full, dh):
    f32 = jnp.float32
    return call(
        attend_grad_kernel, "attend_grad",
        [("d", kv), ("d", q), ("d", start), ("d", full), ("v", dh)],
        [
            ("v", whole(2 * BLOCKS, HALF, 128)),
            ("v", whole(2 * BLOCKS, HALF, 128)),
            ("v", whole(BLOCKS, 32, 128)),
            ("v", whole(96, 128)),
        ],
        [
            pltpu.VMEM((ROWS, 128), jnp.bfloat16),
            pltpu.VMEM((ROWS, 128), f32),
            pltpu.VMEM((ROWS, 128), f32),
        ],
        lazy=(0, 1, 2, 3),
        cost=40,
    )


def column(line):
    return jnp.sum(
        jnp.where(lane_ids(128, 128) == row_ids_of(128, 128), line, 0.0), axis=1, keepdims=True
    )


def pairs_low(even, odd):
    left = lane_ids(32, 128) < HALF
    return jnp.concatenate(
        [jnp.where(left, even, turn(odd)), jnp.where(left, turn(even), odd)], axis=0
    )


def project_kernel(
    wait, flush,
    tokens_ref, start_ref, gain_ref, shift_ref, q_bias_ref, v_bias_ref, q_ref, k_ref, v_ref,
    pay_ref, low_ref,
):
    normed, _, _ = norm_forward(tokens_ref[...].astype(jnp.float32), gain_ref[...], shift_ref[...])
    low = normed.astype(jnp.bfloat16)
    low_ref[...] = low
    flush(low_ref)
    starts = start_ref[...]
    high_part = (starts >> 6).astype(jnp.float32)
    low_part = (starts & 63).astype(jnp.float32)
    left = lane_ids(1, 128) < HALF
    lines = (
        jnp.where(left, high_part, turn(low_part)),
        jnp.where(left, turn(high_part), low_part),
    )
    lines = [jnp.broadcast_to(line, (16, 128)).astype(jnp.bfloat16) for line in lines]
    wide = lane_ids(HALF, 128) < HALF
    for ref in (q_ref, k_ref, v_ref):
        wait(ref)
    for pair in range(3):
        columns = slice(pair * 128, (pair + 1) * 128)
        queries = (
            jnp.dot(low, q_ref[:, columns], preferred_element_type=jnp.float32)
            + q_bias_ref[:, columns]
        )
        keyset = jnp.dot(low, k_ref[:, columns], preferred_element_type=jnp.float32)
        values = (
            jnp.dot(low, v_ref[:, columns], preferred_element_type=jnp.float32)
            + v_bias_ref[:, columns]
        )
        for half in range(2):
            rows = slice(half * HALF, (half + 1) * HALF)
            for odd in range(2):
                if odd:
                    both = jnp.where(wide, turn(keyset[rows]), values[rows])
                    packed = pack_from_high(queries[rows])
                else:
                    both = jnp.where(wide, keyset[rows], turn(values[rows]))
                    packed = pack_from_low(queries[rows])
                index = 4 * pair + 2 * odd + half
                pay_ref[index, :HALF] = both.astype(jnp.bfloat16)
                pay_ref[index, HALF : HALF + 32] = packed.astype(jnp.bfloat16)
                pay_ref[index, HALF + 32 :] = lines[half]
    pay_ref[12:] = jnp.zeros((4, HALF + 48, 128), jnp.bfloat16)


def prepare_kernel(wait, flush, low_ref, send_ref, keep_ref):
    lane = lane_ids(8, 1024)
    core = lane >> 9
    chip = (lane >> 4) & 31
    rest = lane & 15
    row = 48 * (chip >> 1) + 24 * (chip & 1) + 12 * core + rest
    source = jnp.where(rest < 12, row, -1)[:1]
    order = jnp.where(row_ids_of(768, 1024) == source, 1.0, 0.0).astype(jnp.bfloat16)
    ordered = jnp.dot(low_ref[...], order, preferred_element_type=jnp.float32).astype(jnp.bfloat16)
    first = lax.axis_index("core") == 0
    keep_ref[...] = jnp.where(first, ordered[:, :512], ordered[:, 512:])
    send_ref[...] = jnp.where(first, ordered[:, 512:], ordered[:, :512])


def attn_tile(got_ref, side, pair):
    parts = []
    for half in range(2):
        heads = []
        for odd in range(2):
            index = 4 * pair + 2 * odd
            lower = got_ref[pl.ds(2 * index + side, 1)][0].astype(jnp.float32)
            if half:
                higher = got_ref[pl.ds(2 * index + 2 + side, 1)][0].astype(jnp.float32)
                packed = higher[:32] + lower[32:]
            else:
                packed = lower[:32]
            heads.append(packed)
        parts.append(pairs_low(*heads))
    return jnp.concatenate(parts, axis=0).astype(jnp.bfloat16)


def branch_of(cot_ref, exit_ref):
    active = column((exit_ref[...] > LAYER).astype(jnp.float32))
    return jnp.where(active > 0.0, cot_ref[...].astype(jnp.float32), 0.0)


def dhidden_kernel(wait, flush, cot_ref, exit_ref, down_ref, out_ref, vec_ref):
    branch = branch_of(cot_ref, exit_ref)
    vec_ref[...] = jnp.sum(branch, axis=0, keepdims=True)
    out_ref[...] = lax.dot_general(
        branch.astype(jnp.bfloat16), down_ref[...], trans_right, preferred_element_type=jnp.float32
    )


def middle_kernel(
    wait, flush, got_ref, tokens_ref, cot_ref, exit_ref, o_bias_ref, gain_ref, shift_ref,
    up_bias_ref, o_own_ref, o_other_ref, up_ref, dhidden_ref,
    dn_ref, core_ref, high_ref, cross_ref, here_ref, mid_ref, hidden_ref, attn_ref, vec_ref,
    acc_ref, dpre_ref,
):
    side = lax.axis_index("wa")
    for pair in range(3):
        rows = slice(pair * 128, (pair + 1) * 128)
        attn_ref[:, rows] = attn_tile(got_ref, side, pair)
        acc_ref[:, rows] = attn_tile(got_ref, 1 - side, pair)
    flush(attn_ref)
    wait(o_own_ref)
    wait(o_other_ref)
    total = jnp.dot(
        attn_ref[...], o_own_ref[...], preferred_element_type=jnp.float32
    ) + jnp.dot(acc_ref[...], o_other_ref[...], preferred_element_type=jnp.float32)
    middle = tokens_ref[...].astype(jnp.float32) + (total + o_bias_ref[...])
    mid_ref[...] = middle
    flush(mid_ref)
    normed, _, _ = norm_forward(middle, gain_ref[...], shift_ref[...])
    low = normed.astype(jnp.bfloat16)
    branch_low = branch_of(cot_ref, exit_ref).astype(jnp.bfloat16)
    dnormed = None
    wait(up_ref)
    wait(dhidden_ref)
    for begin in range(0, 1536, FF_TILE):
        columns = slice(begin, begin + FF_TILE)
        pre_act = (
            jnp.dot(low, up_ref[:, columns], preferred_element_type=jnp.float32)
            + up_bias_ref[:, columns]
        )
        hidden_full, slope = gelu_pair(pre_act)
        hidden = hidden_full.astype(jnp.bfloat16)
        hidden_ref[:, columns] = hidden
        dpre = (dhidden_ref[:, columns] * slope).astype(jnp.bfloat16)
        vec_ref[:, columns] = jnp.sum(dpre.astype(jnp.float32), axis=0, keepdims=True)
        dpre_ref[:, columns] = dpre
        dn_term = lax.dot_general(
            dpre, up_ref[:, columns], trans_right, preferred_element_type=jnp.float32
        )
        dnormed = dn_term if dnormed is None else dnormed + dn_term
    dn_ref[...] = dnormed.astype(jnp.bfloat16)
    core, high = lax.axis_index("core"), lax.axis_index("zh")
    for ref, offset in ((core_ref, 1), (high_ref, 2), (cross_ref, 3), (here_ref, 0)):
        up_side = (core ^ (offset & 1)) == 0
        first_half = (high ^ (offset >> 1)) == 0
        ref[:, :768] = jnp.where(up_side, low, branch_low)
        ref[:, 768:] = jnp.where(
            up_side,
            jnp.where(first_half, dpre_ref[:, :768], dpre_ref[:, 768:]),
            jnp.where(first_half, hidden_ref[:, :768], hidden_ref[:, 768:]),
        )


def dheads_kernel(
    wait, flush, dn_ref, other_ref, mid_ref, cot_ref, exit_ref, gain_ref, attn_ref, o_ref,
    pay_ref, both_ref, dmid_ref, vec_ref,
):
    middle = mid_ref[...]
    _, unit, inverse = norm_forward(middle, gain_ref[...], 0.0)
    dnormed = dn_ref[...].astype(jnp.float32) + other_ref[...].astype(jnp.float32)
    branch = branch_of(cot_ref, exit_ref)
    dmiddle = branch + norm_backward(dnormed, unit, inverse, gain_ref[...])
    dmid_ref[...] = dmiddle
    flush(dmid_ref)
    low = dmiddle.astype(jnp.bfloat16)
    vec_ref[:, :768] = jnp.sum(dnormed * unit, axis=0, keepdims=True)
    vec_ref[:, 768:1536] = jnp.sum(dnormed, axis=0, keepdims=True)
    vec_ref[:, 1536:] = jnp.sum(low.astype(jnp.float32), axis=0, keepdims=True)
    wait(o_ref)
    for pair in range(3):
        dheads = lax.dot_general(
            low,
            o_ref[pair * 128 : (pair + 1) * 128],
            trans_right,
            preferred_element_type=jnp.float32,
        )
        for odd in range(2):
            pack = pack_from_high if odd else pack_from_low
            lower = pack(dheads[:HALF]).astype(jnp.bfloat16)
            higher = pack(dheads[HALF:]).astype(jnp.bfloat16)
            index = 4 * pair + 2 * odd
            pay_ref[index, :32] = lower
            pay_ref[index, 32:] = higher
            pay_ref[index + 1, :32] = higher
            pay_ref[index + 1, 32:] = higher
    pay_ref[12:] = jnp.zeros((4, HALF, 128), jnp.bfloat16)
    flush(pay_ref)
    both_ref[:, :768] = low
    both_ref[:, 768:] = attn_ref[...]


def ffn_products_kernel(
    wait, flush, here_ref, core_ref, high_ref, cross_ref, both_ref, sent_ref,
    up_ref, down_ref, two_ref, out_ref,
):
    pieces = (here_ref, core_ref, high_ref, cross_ref)
    lefts = jnp.concatenate([ref[:, :768] for ref in pieces], axis=0)
    for at in range(0, 768, 384):
        rights = jnp.concatenate([ref[:, 768 + at : 1152 + at] for ref in pieces], axis=0)
        out_ref[:, at : at + 384] = lax.dot_general(
            lefts, rights, trans_left, preferred_element_type=jnp.float32
        ).astype(jnp.bfloat16)
    first = lax.axis_index("core") == 0
    both = jnp.concatenate([both_ref[...], sent_ref[...]], axis=0)
    out_ref[:, 768:1024] = lax.dot_general(
        both[:, :768],
        jnp.where(first, both[:, 768:1024], both[:, 896:]),
        trans_left,
        preferred_element_type=jnp.float32,
    ).astype(jnp.bfloat16)
    vec = jnp.concatenate([up_ref[...], down_ref[...], two_ref[...]], axis=1)
    lines = [vec[:, 128 * row : 128 * (row + 1)] for row in range(36)]
    lines = jnp.concatenate(lines + [jnp.zeros((12, 128), jnp.float32)], axis=0).astype(
        jnp.bfloat16
    )
    for plane in range(16):
        out_ref[48 * plane : 48 * plane + 48, 1024:] = lines


def ffn_kernel(wait, flush, hidden_ref, down_ref, out_ref):
    out_ref[...] = jnp.dot(
        hidden_ref[...], down_ref[...], preferred_element_type=jnp.float32
    ).astype(jnp.bfloat16)


def dnormed_kernel(
    wait, flush, got_ref, tokens_ref, q_ref, k_ref, v_ref,
    grads_ref, norm_ref, vec_ref, dn_ref,
):
    wide = lane_ids(HALF, 128) < HALF
    for pair in range(3):
        columns = slice(pair * 128, (pair + 1) * 128)
        key_columns = slice(384 + pair * 128, 512 + pair * 128)
        value_columns = slice(768 + pair * 128, 896 + pair * 128)
        for half in range(2):
            rows = slice(half * HALF, (half + 1) * HALF)
            at = 8 * pair + 2 * half
            even = got_ref[at].astype(jnp.float32) + got_ref[at + 1].astype(jnp.float32)
            odd = got_ref[at + 4].astype(jnp.float32) + got_ref[at + 5].astype(jnp.float32)
            grads_ref[rows, key_columns] = jnp.where(wide, even[:HALF], turn(odd[:HALF])).astype(
                jnp.bfloat16
            )
            grads_ref[rows, value_columns] = jnp.where(
                wide, turn(even[:HALF]), odd[:HALF]
            ).astype(jnp.bfloat16)
            grads_ref[rows, columns] = pairs_low(even[HALF:], odd[HALF:]).astype(jnp.bfloat16)
    for ref in (q_ref, k_ref, v_ref):
        wait(ref)
    dnormed = (
        lax.dot_general(
            grads_ref[:, :384], q_ref[...], trans_right, preferred_element_type=jnp.float32
        )
        + lax.dot_general(
            grads_ref[:, 384:768], k_ref[...], trans_right, preferred_element_type=jnp.float32
        )
        + lax.dot_general(
            grads_ref[:, 768:], v_ref[...], trans_right, preferred_element_type=jnp.float32
        )
    )
    dn_ref[...] = dnormed.astype(jnp.bfloat16)
    _, unit, _ = norm_forward(tokens_ref[...].astype(jnp.float32), 1.0, 0.0)
    total = jnp.sum(grads_ref[...].astype(jnp.float32), axis=0, keepdims=True)
    vec_ref[:, :768] = jnp.sum(dnormed, axis=0, keepdims=True)
    vec_ref[:, 768:1536] = jnp.sum(dnormed * unit, axis=0, keepdims=True)
    vec_ref[:, 1536:1920] = total[:, :384]
    vec_ref[:, 1920:2304] = total[:, 768:]
    norm_ref[...] = vec_ref[:, :1536]


def input_grad_kernel(
    wait, flush, dn_ref, other_ref, tokens_ref, cot_ref, exit_ref, gain_ref, dmid_ref, out_ref
):
    _, unit, inverse = norm_forward(tokens_ref[...].astype(jnp.float32), 1.0, 0.0)
    dnormed = dn_ref[...].astype(jnp.float32) + other_ref[...].astype(jnp.float32)
    active = column((exit_ref[...] > LAYER).astype(jnp.float32))
    out_ref[...] = (
        dmid_ref[...]
        + norm_backward(dnormed, unit, inverse, gain_ref[...])
        + jnp.where(active > 0.0, 0.0, cot_ref[...].astype(jnp.float32))
    )


def output_kernel(
    wait, flush, ffn_ref, other_ref, mid_ref, tokens_ref, exit_ref, bias_ref, out_ref
):
    active = column((exit_ref[...] > LAYER).astype(jnp.float32))
    branch = ffn_ref[...].astype(jnp.float32) + other_ref[...].astype(jnp.float32) + bias_ref[...]
    out_ref[...] = jnp.where(
        active > 0.0, mid_ref[...] + branch, tokens_ref[...].astype(jnp.float32)
    ).astype(jnp.bfloat16)


def merge_kernel(wait, flush, kept_ref, taken_ref, dq_ref, edge_ref, out_ref):
    high = lax.axis_index("zh")
    for block in range(BLOCKS):
        pair = kept_ref[block].astype(jnp.float32) + taken_ref[block].astype(jnp.float32)
        query = dq_ref[block]
        if block == BLOCKS - 1:
            pair = pair + edge_ref[:HALF].astype(jnp.float32)
            query = (query.astype(jnp.float32) + edge_ref[HALF:].astype(jnp.float32)).astype(
                jnp.bfloat16
            )
        out_ref[pl.ds(2 * block + high, 1), :HALF] = pair.astype(jnp.bfloat16)[None]
        out_ref[pl.ds(2 * block + high, 1), HALF:] = query[None]
        pair = kept_ref[BLOCKS + block].astype(jnp.float32) + taken_ref[BLOCKS + block].astype(
            jnp.float32
        )
        out_ref[pl.ds(2 * block + 1 - high, 1), :HALF] = pair.astype(jnp.bfloat16)[None]
        out_ref[pl.ds(2 * block + 1 - high, 1), HALF:] = jnp.zeros((1, 32, 128), jnp.bfloat16)


def qkv_products_kernel(
    wait, flush, keep_ref, sent_ref, grads_ref, grads_sent_ref,
    vec_ref, vec_sent_ref, wa_ref, cross_ref, out_ref,
):
    lefts = jnp.concatenate([keep_ref[...], sent_ref[...]], axis=0)
    vec = vec_ref[...] + vec_sent_ref[...]
    norms = vec[:, :1536] + (wa_ref[...] + cross_ref[...])
    vec = jnp.concatenate([norms, vec[:, 1536:]], axis=1)
    lines = jnp.concatenate(
        [vec[:, :1152], vec[:, 1152:], jnp.zeros((2, 1152), jnp.float32)], axis=0
    )
    for at in range(0, 1152, 384):
        columns = slice(at, at + 384)
        rights = jnp.concatenate([grads_ref[:, columns], grads_sent_ref[:, columns]], axis=0)
        product = lax.dot_general(lefts, rights, trans_left, preferred_element_type=jnp.float32)
        for chip in range(32):
            out_ref[chip, :, columns] = jnp.concatenate(
                [product[16 * chip : 16 * chip + 12], lines[:, columns]], axis=0
            ).astype(jnp.bfloat16)


def finish_kernel(
    wait, flush, got_ref, q_ref, k_ref, v_ref, shift_out, gain_out, q_bias_out, v_bias_out
):
    both = got_ref[0].astype(jnp.float32)
    for source in range(1, 32):
        both = both + got_ref[source].astype(jnp.float32)
    q_ref[...] = both[:12, :384]
    k_ref[...] = both[:12, 384:768]
    v_ref[...] = both[:12, 768:]
    shift_out[...] = both[12:13, :768]
    gain_out[:, :384] = both[12:13, 768:]
    gain_out[:, 384:] = both[13:14, :384]
    q_bias_out[...] = both[13:14, 384:768]
    v_bias_out[...] = both[13:14, 768:]


def ffn_sums_kernel(wait, flush, got_ref, core_ref, high_ref, cross_ref, here_ref):
    total = got_ref[0].astype(jnp.float32)
    for source in range(1, 16):
        total = total + got_ref[source].astype(jnp.float32)
    me = 2 * lax.axis_index("zh") + lax.axis_index("core")
    parts = [total[12 * index : 12 * index + 12, :1024] for index in range(4)]
    vec = jnp.concatenate([total[row : row + 1, 1024:] for row in range(36)], axis=1)
    vec = jnp.concatenate([vec, jnp.zeros((1, 512), jnp.float32)], axis=1)
    lines = [vec[:, 1024 * row : 1024 * (row + 1)] for row in range(5)]
    lines = jnp.concatenate(lines + [jnp.zeros((3, 1024), jnp.float32)], axis=0)

    def part(offset):
        value = parts[offset]
        for index in range(1, 4):
            value = jnp.where(me == index, parts[index ^ offset], value)
        return value

    for ref, offset in ((here_ref, 0), (core_ref, 1), (high_ref, 2), (cross_ref, 3)):
        ref[:12] = part(offset)
        ref[12:16] = jnp.zeros((4, 1024), jnp.float32)
        ref[16:] = lines


def ffn_finish_kernel(
    wait, flush, here_ref, core_ref, high_ref, cross_ref,
    up_ref, down_ref, o_ref, up_bias_out, down_bias_out, gain_out, shift_out, o_bias_out,
):
    first = lax.axis_index("core") == 0
    low = lax.axis_index("zh") == 0
    here, core, high, cross = [
        ref[:12, :768] for ref in (here_ref, core_ref, high_ref, cross_ref)
    ]
    up_ref[:, :768] = jnp.where(first, jnp.where(low, here, high), jnp.where(low, core, cross))
    up_ref[:, 768:] = jnp.where(first, jnp.where(low, high, here), jnp.where(low, cross, core))
    down_ref[:, :768] = jnp.where(first, jnp.where(low, core, cross), jnp.where(low, here, high))
    down_ref[:, 768:] = jnp.where(first, jnp.where(low, cross, core), jnp.where(low, high, here))
    mine = here_ref[:12, 768:] + high_ref[:12, 768:]
    other = core_ref[:12, 768:] + cross_ref[:12, 768:]
    o_ref[:, :256] = jnp.where(first, mine, other)
    o_ref[:, 256:] = jnp.where(first, other[:, 128:], mine[:, 128:])
    vec = (here_ref[16:] + core_ref[16:]) + (high_ref[16:] + cross_ref[16:])
    vec = jnp.concatenate([vec[row : row + 1] for row in range(5)], axis=1)
    begin = 0
    for ref in (up_bias_out, down_bias_out, gain_out, shift_out, o_bias_out):
        ref[...] = vec[:, begin : begin + ref.shape[1]]
        begin += ref.shape[1]


def on_device(
    tokens,
    doc_start,
    exit_layer,
    cotangent,
    ln1_gain,
    ln1_shift,
    q_weight,
    q_bias,
    k_weight,
    v_weight,
    v_bias,
    o_weight,
    o_bias,
    ln2_gain,
    ln2_shift,
    up_weight,
    up_bias,
    down_weight,
    down_bias,
):
    f32 = jnp.float32

    def copied(*arrays):
        return [("d", array) for array in arrays]

    payload, low_one = call(
        project_kernel, "project",
        copied(
            tokens, doc_start, ln1_gain, ln1_shift, q_bias, v_bias, q_weight, k_weight, v_weight
        ),
        [("d", whole(16, HALF + 48, 128)), ("d", whole(128, 768))],
        lazy=(6, 7, 8),
    )
    own = lax.all_to_all(payload, PLANE, 0, 0, tiled=True)
    low_one, o_given = lax.optimization_barrier((low_one, o_weight))
    o_other = lax.ppermute(o_given, "wa", SWAP)
    x_send, x_keep = call(
        prepare_kernel, "prepare",
        copied(low_one),
        [("v", whole(128, 512)), ("d", whole(128, 512))],
    )
    own, x_send, o_other = lax.optimization_barrier((own, x_send, o_other))
    pairs = own[:, :HALF]
    one = lax.ppermute(pairs, "core", SWAP)
    edge = lax.ppermute(own[BLOCKS - 1], "y", ((1, 0), (3, 2)))
    two = lax.ppermute(pairs, "zh", SWAP)
    two, edge = lax.optimization_barrier((two, edge))
    three = lax.ppermute(two, "core", SWAP)
    x_sent = lax.ppermute(x_send, "core", SWAP)
    back, kv, q_rows, start_rows, full_rows = attend(own, one, two, three, edge)
    dhidden, vec_down = call(
        dhidden_kernel, "dhidden",
        copied(cotangent, exit_layer, down_weight),
        [("d", whole(128, 1536, dtype=f32)), ("d", whole(1, 768, dtype=f32))],
    )
    got = lax.all_to_all(back, ("x", "y", "wa"), 0, 0, tiled=True)
    dn_two, ffn_core, ffn_high, ffn_cross, ffn_here, middle, hidden, attn_low, vec_up = call(
        middle_kernel, "middle",
        [("v", got)]
        + copied(
            tokens, cotangent, exit_layer, o_bias, ln2_gain, ln2_shift, up_bias, o_weight, o_other,
            up_weight, dhidden,
        ),
        [
            ("v", whole(128, 768)),
            ("v", whole(128, 1536)),
            ("v", whole(128, 1536)),
            ("v", whole(128, 1536)),
            ("v", whole(128, 1536)),
            ("d", whole(128, 768, dtype=f32)),
            ("d", whole(128, 1536)),
            ("d", whole(128, 384)),
            ("d", whole(1, 1536, dtype=f32)),
        ],
        [pltpu.VMEM((128, 384), jnp.bfloat16), pltpu.VMEM((128, 1536), jnp.bfloat16)],
        lazy=(8, 9, 10, 11),
    )
    dn_two_other = lax.ppermute(dn_two, "wa", SWAP)
    ffn_high = lax.ppermute(ffn_high, "zh", SWAP)
    ffn_cross = lax.ppermute(ffn_cross, ("zh", "core"), CROSS)
    ffn_core = lax.ppermute(ffn_core, "core", SWAP)
    ffn = call(ffn_kernel, "ffn", copied(hidden, down_weight), [("v", whole(128, 768))], cost=0)
    dn_two_other, ffn = lax.optimization_barrier((dn_two_other, ffn))
    dh_payload, dattn_attn, dmiddle, vec_two = call(
        dheads_kernel, "dheads",
        [("v", dn_two), ("v", dn_two_other)]
        + copied(middle, cotangent, exit_layer, ln2_gain, attn_low, o_weight),
        [
            ("d", whole(16, HALF, 128)),
            ("v", whole(128, 1152)),
            ("d", whole(128, 768, dtype=f32)),
            ("d", whole(1, 2304, dtype=f32)),
        ],
        lazy=(7,),
        cost=0,
    )
    dh = lax.all_to_all(dh_payload, PLANE, 0, 0, tiled=True)
    dattn_sent = lax.ppermute(dattn_attn, "core", SWAP)
    ffn_products = call(
        ffn_products_kernel, "ffn_products",
        [("v", ffn_here), ("v", ffn_core), ("v", ffn_high), ("v", ffn_cross)]
        + [("v", dattn_attn), ("v", dattn_sent)]
        + copied(vec_up, vec_down, vec_two),
        [("d", whole(768, 1152))],
    )
    ffn_blocks = lax.all_to_all(ffn_products.reshape(16, 48, 1152), PLANE, 0, 0, tiled=True)
    ffn_other = lax.ppermute(ffn, "wa", SWAP)
    given, kept, dq, edge_grad = attend_grad(kv, q_rows, start_rows, full_rows, dh)
    given, ffn_other = lax.optimization_barrier((given, ffn_other))
    edge_got = lax.ppermute(edge_grad, "y", ((0, 1), (2, 3)))
    taken = lax.ppermute(given, "core", SWAP)
    merged = call(
        merge_kernel, "merge",
        [("v", kept), ("v", taken), ("v", dq), ("v", edge_got)],
        [("d", whole(2 * BLOCKS, 96, 128))],
    )
    merged, ffn_blocks = lax.optimization_barrier((merged, ffn_blocks))
    grads = lax.all_to_all(merged, CHIPS, 0, 0, tiled=True)
    ffn_core, ffn_high, ffn_cross, ffn_here = call(
        ffn_sums_kernel, "ffn_sums", copied(ffn_blocks),
        [("v", whole(24, 1024, dtype=f32)) for _ in range(4)],
        cost=0,
    )
    ffn_core = lax.ppermute(ffn_core, "core", SWAP)
    ffn_high = lax.ppermute(ffn_high, "zh", SWAP)
    ffn_cross = lax.ppermute(ffn_cross, ("zh", "core"), CROSS)
    grads, ffn_core, ffn_high, ffn_cross, x_sent = lax.optimization_barrier(
        (grads, ffn_core, ffn_high, ffn_cross, x_sent)
    )
    grads_rows, norms, vec, dn_one = call(
        dnormed_kernel, "dnormed",
        [("v", grads)] + copied(tokens, q_weight, k_weight, v_weight),
        [
            ("v", whole(128, 1152)),
            ("v", whole(1, 1536, dtype=f32)),
            ("v", whole(1, 2304, dtype=f32)),
            ("v", whole(128, 768)),
        ],
        lazy=(2, 3, 4),
        cost=0,
    )
    dn_one_other = lax.ppermute(dn_one, "wa", SWAP)
    grads_sent = lax.ppermute(grads_rows, "core", SWAP)
    vec_sent = lax.ppermute(vec, "core", SWAP)
    norms_wa = lax.ppermute(norms, "wa", SWAP)
    norms_cross = lax.ppermute(norms, ("core", "wa"), CROSS)
    products = call(
        qkv_products_kernel, "qkv_products",
        copied(x_keep, x_sent)
        + [("v", grads_rows), ("v", grads_sent), ("v", vec), ("v", vec_sent)]
        + [("v", norms_wa), ("v", norms_cross)],
        [("d", whole(32, 16, 1152))],
        cost=0,
    )
    products, dn_one_other = lax.optimization_barrier((products, dn_one_other))
    products = lax.all_to_all(products, CHIPS, 0, 0, tiled=True)
    output = call(
        output_kernel, "output",
        [("v", ffn), ("v", ffn_other)] + copied(middle, tokens, exit_layer, down_bias),
        [("d", whole(128, 768))],
        cost=0,
    )
    (
        up_weight_grad, down_weight_grad_t, o_weight_grad_t,
        up_bias_grad, down_bias_grad, ln2_gain_grad, ln2_shift_grad, o_bias_grad,
    ) = call(
        ffn_finish_kernel, "ffn_finish",
        [("v", ffn_here), ("v", ffn_core), ("v", ffn_high), ("v", ffn_cross)],
        [("d", whole(12, 1536, dtype=f32)) for _ in range(2)]
        + [("d", whole(12, 384, dtype=f32))]
        + [("d", whole(count, dtype=f32)) for count in (1536, 768, 768, 768, 768)],
        cost=0,
    )
    input_grad = call(
        input_grad_kernel, "input_grad",
        [("v", dn_one), ("v", dn_one_other)]
        + copied(tokens, cotangent, exit_layer, ln1_gain, dmiddle),
        [("d", whole(128, 768, dtype=f32))],
        cost=0,
    )
    (
        products, output, input_grad, up_weight_grad, down_weight_grad_t
    ) = lax.optimization_barrier(
        (products, output, input_grad, up_weight_grad, down_weight_grad_t)
    )
    (
        q_weight_grad, k_weight_grad, v_weight_grad,
        ln1_shift_grad, ln1_gain_grad, q_bias_grad, v_bias_grad,
    ) = call(
        finish_kernel, "finish",
        [("v", products)],
        [("d", whole(12, 384, dtype=f32)) for _ in range(3)]
        + [("d", whole(count, dtype=f32)) for count in (768, 768, 384, 384)],
    )
    return (
        output,
        input_grad,
        ln1_gain_grad,
        ln1_shift_grad,
        q_weight_grad,
        q_bias_grad,
        k_weight_grad,
        v_weight_grad,
        v_bias_grad,
        o_weight_grad_t,
        o_bias_grad,
        ln2_gain_grad,
        ln2_shift_grad,
        up_weight_grad,
        up_bias_grad,
        down_weight_grad_t,
        down_bias_grad,
    )


def solution(mesh):
    fine = Mesh(mesh.devices.reshape(4, 4, 2, 2, 2), CTX + ("wa",))
    return jax.shard_map(
        on_device,
        mesh=fine,
        in_specs=(
            P(CTX, None),
            P(CTX),
            P(CTX),
            P(CTX, None),
            P(),
            P(),
            P(None, "wa"),
            P("wa"),
            P(None, "wa"),
            P(None, "wa"),
            P("wa"),
            P("wa", None),
            P(),
            P(),
            P(),
            P(None, "wa"),
            P("wa"),
            P("wa", None),
            P(),
        ),
        out_specs=(
            P(CTX, None),
            P(CTX, None),
            P(),
            P(),
            P(CTX, "wa"),
            P("wa"),
            P(CTX, "wa"),
            P(CTX, "wa"),
            P("wa"),
            P(CTX, "wa"),
            P(),
            P(),
            P(),
            P(CTX, "wa"),
            P("wa"),
            P(CTX, "wa"),
            P(),
        ),
        check_vma=False,
    )
```

```python
import math

import jax
import jax.numpy as jnp
from jax import lax
from jax.experimental import pallas as pl
from jax.experimental.pallas import tpu as pltpu
from jax.sharding import Mesh, PartitionSpec as P

HEAD_DIM = 64
LAYER = 6
CTX = ("x", "y", "zh", "core")
CHIPS = ("x", "y", "zh")
PLANE = ("x", "y")
SWAP = ((0, 1), (1, 0))
CROSS = ((0, 3), (1, 2), (2, 1), (3, 0))
HALF = 64
BLOCKS = 16
GROUP = 256
STREAM = 8192
ROWS = (BLOCKS + 1) * HALF
FF_TILE = 512
FAR = 1e9
SCALING = 1.0 / math.sqrt(HEAD_DIM)
EXP2_SCALE = SCALING / math.log(2.0)
VMEM_BYTES = 64 * 2**20


epsilon = 1e-05
trans_right = (((1,), (1,)), ((), ()))
trans_left = (((0,), (0,)), ((), ()))
cubic_coef = 0.044715


def gelu_pair(values):
    outer = math.sqrt(2.0 / math.pi)
    inner = outer * (values + cubic_coef * values * values * values)
    tangent = jnp.tanh(inner)
    result = 0.5 * values * (1.0 + tangent)
    gelu_slope = 0.5 * (1.0 + tangent) + 0.5 * values * (1.0 - tangent * tangent) * outer * (
        1.0 + 3.0 * cubic_coef * values * values
    )
    return (result, gelu_slope)


def norm_forward(values, gain_vec, shift_vec):
    average = jnp.mean(values, axis=-1, keepdims=True)
    centred = values - average
    inverse_std = lax.rsqrt(jnp.mean(centred * centred, axis=-1, keepdims=True) + epsilon)
    normed = centred * inverse_std
    return (normed * gain_vec + shift_vec, normed, inverse_std)


def norm_backward(grad_out, normed, inverse_std, gain_vec):
    scaled = grad_out * gain_vec
    return inverse_std * (
        scaled
        - jnp.mean(scaled, axis=-1, keepdims=True)
        - normed * jnp.mean(scaled * normed, axis=-1, keepdims=True)
    )


def swap_add(part, axis):
    other = lax.ppermute(part, axis, SWAP)
    return part.astype(jnp.float32) + other.astype(jnp.float32)


def whole(*shape, dtype=jnp.bfloat16):
    return jax.ShapeDtypeStruct(shape, dtype)


def head_place():
    upper = lax.axis_index("y") % 2
    sub = 2 * lax.axis_index("zh") + lax.axis_index("core")
    last = sub == 3
    return (
        upper,
        jnp.where(upper == 1, 3 - sub, sub),
        jnp.where((upper == 0) & last, 1, 0),
        jnp.where((upper == 1) & last, 1, 0),
    )


def call(kernel, name, ins, outs, scratch=(), lazy=(), cost=2):
    copied_in = [at for at, (mode, _) in enumerate(ins) if mode == "d"]
    copied_out = [at for at, (mode, _) in enumerate(outs) if mode == "d"]

    def buffer(array):
        shape = array.shape if len(array.shape) > 1 else (1,) + tuple(array.shape)
        return pltpu.VMEM(shape, array.dtype)

    def body(*refs):
        given, rest = list(refs[: len(ins)]), refs[len(ins) :]
        results, rest = list(rest[: len(outs)]), rest[len(outs) :]
        in_buffers, rest = rest[: len(copied_in)], rest[len(copied_in) :]
        out_buffers, rest = rest[: len(copied_out)], rest[len(copied_out) :]
        in_sems, out_sems, rest = rest[0], rest[1], rest[2:]
        pending, flushing = [], []
        for slot, at in enumerate(copied_in):
            there = in_buffers[slot]
            into = there if len(ins[at][1].shape) > 1 else there.at[0]
            copy = pltpu.make_async_copy(given[at], into, in_sems.at[slot])
            copy.start()
            given[at] = there
            pending.append((there, at, copy))
        targets = []
        for slot, at in enumerate(copied_out):
            made = out_buffers[slot] if len(outs[at][1].shape) > 1 else out_buffers[slot].at[0]
            copy = pltpu.make_async_copy(made, results[at], out_sems.at[slot])
            results[at] = out_buffers[slot]
            targets.append((out_buffers[slot], copy))

        def wait(ref):
            for entry in list(pending):
                if entry[0] is ref:
                    entry[2].wait()
                    pending[:] = [other for other in pending if other is not entry]

        def flush(ref):
            for entry in list(targets):
                if entry[0] is ref:
                    entry[1].start()
                    flushing.append(entry[1])
                    targets[:] = [other for other in targets if other is not entry]

        for entry in list(pending):
            if entry[1] not in lazy:
                wait(entry[0])
        kernel(wait, flush, *given, *results, *rest)
        for entry in list(pending):
            wait(entry[0])
        for entry in list(targets):
            flush(entry[0])
        for copy in flushing:
            copy.wait()

    vmem, anywhere = pl.BlockSpec(memory_space=pltpu.VMEM), pl.BlockSpec(memory_space=pltpu.HBM)
    result = pl.pallas_call(
        body,
        out_shape=tuple(out for _, out in outs),
        in_specs=[anywhere if mode == "d" else vmem for mode, _ in ins],
        out_specs=tuple(anywhere if mode == "d" else vmem for mode, _ in outs),
        scratch_shapes=[buffer(ins[at][1]) for at in copied_in]
        + [buffer(outs[at][1]) for at in copied_out]
        + [
            pltpu.SemaphoreType.DMA((max(1, len(copied_in)),)),
            pltpu.SemaphoreType.DMA((max(1, len(copied_out)),)),
        ]
        + list(scratch),
        compiler_params=pltpu.CompilerParams(vmem_limit_bytes=VMEM_BYTES),
        cost_estimate=pl.CostEstimate(
            flops=cost * 10**9, transcendentals=0, bytes_accessed=0
        ),
        name=name,
    )(*[array for _, array in ins])
    return result[0] if len(outs) == 1 else result


def lane_ids(rows, cols):
    return lax.broadcasted_iota(jnp.int32, (rows, cols), 1)


def row_ids_of(rows, cols):
    return lax.broadcasted_iota(jnp.int32, (rows, cols), 0)


def turn(values):
    return pltpu.roll(values, HALF, 1)


def unpack_low(packed):
    wide = packed.astype(jnp.float32)
    left = lane_ids(32, 128) < HALF
    both = jnp.concatenate([wide, turn(wide)], axis=0)
    return jnp.where(jnp.concatenate([left, left], axis=0), both, 0.0)


def unpack_high(packed):
    wide = packed.astype(jnp.float32)
    right = lane_ids(32, 128) >= HALF
    both = jnp.concatenate([turn(wide), wide], axis=0)
    return jnp.where(jnp.concatenate([right, right], axis=0), both, 0.0)


def pack_from_low(block):
    return jnp.where(lane_ids(32, 128) < HALF, block[:32], turn(block[32:]))


def pack_from_high(block):
    return jnp.where(lane_ids(32, 128) < HALF, turn(block[:32]), block[32:])


def key_places(scal, group):
    lane = lane_ids(8, GROUP)
    sub = (lane >> 6) ^ scal[1]
    return (scal[0] * (STREAM // 2) + GROUP * group + (sub << 6) + (lane & 63)).astype(
        jnp.float32
    )


def edge_places():
    return (STREAM // 2 + lane_ids(8, 128)).astype(jnp.float32)


def query_places(scal, block):
    row = row_ids_of(HALF, 128)
    return (
        scal[0] * (STREAM // 2) + GROUP * block + (scal[1] << 6) + row
    ).astype(jnp.float32)


def spread(rows, width):
    return jnp.concatenate([rows] * (width // 128), axis=1) if width > 128 else rows


def weights_of(scal, queries, starts, keys, places, group):
    scores = lax.dot_general(queries, keys, trans_right, preferred_element_type=jnp.float32)
    count = queries.shape[0]
    own = spread(query_places(scal, group), GROUP)
    limit = jnp.concatenate([own, jnp.full((count - HALF, GROUP), FAR, jnp.float32)], axis=0)
    seen = (spread(starts, GROUP) <= places[:1]) & (places[:1] <= limit)
    return jnp.where(seen, jnp.exp2(scores * EXP2_SCALE), 0.0)


def edge_weights(queries, starts, keys):
    scores = lax.dot_general(queries, keys, trans_right, preferred_element_type=jnp.float32)
    places = edge_places()[:1]
    limit = (STREAM // 2 + row_ids_of(HALF, 128)).astype(jnp.float32)
    return jnp.where(
        (starts <= places) & (places <= limit), jnp.exp2(scores * EXP2_SCALE), 0.0
    )


def attend_kernel(
    wait, flush, own_ref, one_ref, two_ref, three_ref, edge_ref,
    back_ref, kv_ref, q_ref, start_ref, full_ref,
    num_ref, den_ref,
):
    scal = head_place()
    upper = scal[0]
    diag = jnp.where(
        lane_ids(HALF, 128) == row_ids_of(HALF, 128),
        64.0,
        jnp.where(lane_ids(HALF, 128) == row_ids_of(HALF, 128) + HALF, 1.0, 0.0),
    )

    def starts(line, off):
        found = jnp.sum(line.astype(jnp.float32) * diag, axis=1, keepdims=True)
        return jnp.broadcast_to(jnp.where(off, FAR, found), (HALF, 128))

    for block in range(BLOCKS):
        place = jnp.where(upper == 1, BLOCKS - 1 - block, block)
        rows = slice(block * HALF, (block + 1) * HALF)
        mine = own_ref[pl.ds(place, 1)][0]
        kv_ref[block, 0:HALF] = mine[:HALF]
        kv_ref[block, HALF : 2 * HALF] = one_ref[pl.ds(place, 1)][0]
        kv_ref[block, 2 * HALF : 3 * HALF] = two_ref[pl.ds(place, 1)][0]
        kv_ref[block, 3 * HALF :] = three_ref[pl.ds(place, 1)][0]
        q_ref[rows] = unpack_low(mine[HALF : HALF + 32]).astype(jnp.bfloat16)
        off = (scal[3] == 1) if block == 0 else False
        start_ref[rows] = starts(mine[HALF + 32 : HALF + 33], off)
    kv_ref[BLOCKS] = jnp.zeros((GROUP, 128), jnp.bfloat16)
    kv_ref[BLOCKS, :HALF] = edge_ref[:HALF]
    q_ref[BLOCKS * HALF :] = unpack_low(edge_ref[HALF : HALF + 32]).astype(jnp.bfloat16)
    start_ref[BLOCKS * HALF :] = starts(edge_ref[HALF + 32 : HALF + 33], scal[2] == 0)
    flush(kv_ref)
    flush(q_ref)
    flush(start_ref)

    for group in range(BLOCKS + 1):
        rows = slice(group * HALF, ROWS)
        if group < BLOCKS:
            keys = kv_ref[group]
            weights = weights_of(
                scal, q_ref[rows], start_ref[rows], keys, key_places(scal, group), group
            )
            total = weights[:, :128] + weights[:, 128:]
        else:
            keys = kv_ref[group, :128]
            weights = total = edge_weights(q_ref[rows], start_ref[rows], keys)
        product = jnp.dot(weights.astype(jnp.bfloat16), keys, preferred_element_type=jnp.float32)
        if group == 0:
            num_ref[rows] = product
            den_ref[rows] = total
        else:
            num_ref[rows] += product
            den_ref[rows] += total

    for block in range(BLOCKS + 1):
        rows = slice(block * HALF, (block + 1) * HALF)
        den = jnp.sum(den_ref[rows], axis=1, keepdims=True)
        recip = jnp.broadcast_to(1.0 / jnp.where(den == 0.0, 1.0, den), (HALF, 128))
        full = num_ref[rows] * recip
        full_ref[rows] = jnp.where(lane_ids(HALF, 128) < HALF, recip, full)
        packed = pack_from_high(full).astype(jnp.bfloat16)
        if block < BLOCKS:
            place = jnp.where(upper == 1, BLOCKS - 1 - block, block)
            for copy in range(2):
                back_ref[pl.ds(2 * place + copy, 1), :32] = packed[None]
                back_ref[pl.ds(2 * place + copy, 1), 32:] = jnp.zeros((1, 32, 128), jnp.bfloat16)
        else:
            for copy in range(2):
                back_ref[2 * BLOCKS - 2 + copy, 32:] = packed


def attend_grad_kernel(
    wait, flush, kv_ref, q_ref, start_ref, full_ref, dh_in_ref,
    send_ref, keep_ref, dq_ref, edge_ref,
    dhn_ref, dot_ref, dq_acc,
):
    scal = head_place()
    upper = scal[0]
    left = lane_ids(HALF, 128) < HALF
    wait(full_ref)
    for block in range(BLOCKS + 1):
        rows = slice(block * HALF, (block + 1) * HALF)
        if block < BLOCKS:
            place = jnp.where(upper == 1, BLOCKS - 1 - block, block)
            packed = dh_in_ref[pl.ds(place, 1), :32][0]
        else:
            packed = dh_in_ref[BLOCKS - 1, 32:]
        full = full_ref[rows]
        scaled = unpack_high(packed) * jnp.where(left, full, turn(full))
        scaled = scaled.astype(jnp.bfloat16).astype(jnp.float32)
        dhn_ref[rows] = scaled.astype(jnp.bfloat16)
        dot_ref[rows] = jnp.broadcast_to(
            jnp.sum(jnp.where(left, 0.0, scaled * full), axis=1, keepdims=True), (HALF, 128)
        )
    wait(kv_ref)
    wait(q_ref)
    wait(start_ref)
    for group in range(BLOCKS + 1):
        rows = slice(group * HALF, ROWS)
        if group < BLOCKS:
            keys = kv_ref[group]
            weights = weights_of(
                scal, q_ref[rows], start_ref[rows], keys, key_places(scal, group), group
            )
        else:
            keys = kv_ref[group, :128]
            weights = edge_weights(q_ref[rows], start_ref[rows], keys)
        dprob = lax.dot_general(
            dhn_ref[rows], keys, trans_right, preferred_element_type=jnp.float32
        )
        dscore = (weights * (dprob - spread(dot_ref[rows], keys.shape[0]))).astype(jnp.bfloat16)
        dquery = jnp.dot(dscore, keys, preferred_element_type=jnp.float32)
        if group == 0:
            dq_acc[rows] = dquery
        else:
            dq_acc[rows] += dquery
        grads = lax.dot_general(
            dscore, q_ref[rows], trans_left, preferred_element_type=jnp.float32
        ) * SCALING + lax.dot_general(
            weights.astype(jnp.bfloat16),
            dhn_ref[rows],
            trans_left,
            preferred_element_type=jnp.float32,
        )
        low = grads.astype(jnp.bfloat16)
        if group < BLOCKS:
            place = jnp.where(upper == 1, BLOCKS - 1 - group, group)
            for quarter in range(4):
                out = send_ref if quarter % 2 else keep_ref
                out[pl.ds(quarter // 2 * BLOCKS + place, 1)] = low[
                    None, quarter * HALF : (quarter + 1) * HALF
                ]
        else:
            edge_ref[:HALF] = low[:HALF]

    for block in range(BLOCKS + 1):
        rows = slice(block * HALF, (block + 1) * HALF)
        packed = pack_from_low(dq_acc[rows] * SCALING).astype(jnp.bfloat16)
        if block < BLOCKS:
            place = jnp.where(upper == 1, BLOCKS - 1 - block, block)
            dq_ref[pl.ds(place, 1)] = packed[None]
        else:
            edge_ref[HALF:] = packed


def attend(own, one, two, three, edge):
    f32 = jnp.float32
    return call(
        attend_kernel, "attend",
        [("v", own), ("v", one), ("v", two), ("v", three), ("v", edge)],
        [
            ("d", whole(2 * BLOCKS, HALF, 128)),
            ("d", whole(BLOCKS + 1, GROUP, 128)),
            ("d", whole(ROWS, 128)),
            ("d", whole(ROWS, 128, dtype=f32)),
            ("d", whole(ROWS, 128, dtype=f32)),
        ],
        [pltpu.VMEM((ROWS, 128), f32), pltpu.VMEM((ROWS, 128), f32)],
        cost=3,
    )


def attend_grad(kv, q, start, full, dh):
    f32 = jnp.float32
    return call(
        attend_grad_kernel, "attend_grad",
        [("d", kv), ("d", q), ("d", start), ("d", full), ("v", dh)],
        [
            ("v", whole(2 * BLOCKS, HALF, 128)),
            ("v", whole(2 * BLOCKS, HALF, 128)),
            ("v", whole(BLOCKS, 32, 128)),
            ("v", whole(96, 128)),
        ],
        [
            pltpu.VMEM((ROWS, 128), jnp.bfloat16),
            pltpu.VMEM((ROWS, 128), f32),
            pltpu.VMEM((ROWS, 128), f32),
        ],
        lazy=(0, 1, 2, 3),
        cost=40,
    )


def column(line):
    return jnp.sum(
        jnp.where(lane_ids(128, 128) == row_ids_of(128, 128), line, 0.0), axis=1, keepdims=True
    )


def pairs_low(even, odd):
    left = lane_ids(32, 128) < HALF
    return jnp.concatenate(
        [jnp.where(left, even, turn(odd)), jnp.where(left, turn(even), odd)], axis=0
    )


def project_kernel(
    wait, flush,
    tokens_ref, start_ref, gain_ref, shift_ref, q_bias_ref, v_bias_ref, q_ref, k_ref, v_ref,
    pay_ref, low_ref,
):
    normed, _, _ = norm_forward(tokens_ref[...].astype(jnp.float32), gain_ref[...], shift_ref[...])
    low = normed.astype(jnp.bfloat16)
    low_ref[...] = low
    flush(low_ref)
    starts = start_ref[...]
    high_part = (starts >> 6).astype(jnp.float32)
    low_part = (starts & 63).astype(jnp.float32)
    left = lane_ids(1, 128) < HALF
    lines = (
        jnp.where(left, high_part, turn(low_part)),
        jnp.where(left, turn(high_part), low_part),
    )
    lines = [jnp.broadcast_to(line, (16, 128)).astype(jnp.bfloat16) for line in lines]
    wide = lane_ids(HALF, 128) < HALF
    for ref in (q_ref, k_ref, v_ref):
        wait(ref)
    for pair in range(3):
        columns = slice(pair * 128, (pair + 1) * 128)
        queries = (
            jnp.dot(low, q_ref[:, columns], preferred_element_type=jnp.float32)
            + q_bias_ref[:, columns]
        )
        keyset = jnp.dot(low, k_ref[:, columns], preferred_element_type=jnp.float32)
        values = (
            jnp.dot(low, v_ref[:, columns], preferred_element_type=jnp.float32)
            + v_bias_ref[:, columns]
        )
        for half in range(2):
            rows = slice(half * HALF, (half + 1) * HALF)
            for odd in range(2):
                if odd:
                    both = jnp.where(wide, turn(keyset[rows]), values[rows])
                    packed = pack_from_high(queries[rows])
                else:
                    both = jnp.where(wide, keyset[rows], turn(values[rows]))
                    packed = pack_from_low(queries[rows])
                index = 4 * pair + 2 * odd + half
                pay_ref[index, :HALF] = both.astype(jnp.bfloat16)
                pay_ref[index, HALF : HALF + 32] = packed.astype(jnp.bfloat16)
                pay_ref[index, HALF + 32 :] = lines[half]
    pay_ref[12:] = jnp.zeros((4, HALF + 48, 128), jnp.bfloat16)


def prepare_kernel(wait, flush, low_ref, send_ref, keep_ref):
    lane = lane_ids(8, 1024)
    core = lane >> 9
    chip = (lane >> 4) & 31
    rest = lane & 15
    row = 48 * (chip >> 1) + 24 * (chip & 1) + 12 * core + rest
    source = jnp.where(rest < 12, row, -1)[:1]
    order = jnp.where(row_ids_of(768, 1024) == source, 1.0, 0.0).astype(jnp.bfloat16)
    ordered = jnp.dot(low_ref[...], order, preferred_element_type=jnp.float32).astype(jnp.bfloat16)
    first = lax.axis_index("core") == 0
    keep_ref[...] = jnp.where(first, ordered[:, :512], ordered[:, 512:])
    send_ref[...] = jnp.where(first, ordered[:, 512:], ordered[:, :512])


def attn_tile(got_ref, side, pair):
    parts = []
    for half in range(2):
        heads = []
        for odd in range(2):
            index = 4 * pair + 2 * odd
            lower = got_ref[pl.ds(2 * index + side, 1)][0].astype(jnp.float32)
            if half:
                higher = got_ref[pl.ds(2 * index + 2 + side, 1)][0].astype(jnp.float32)
                packed = higher[:32] + lower[32:]
            else:
                packed = lower[:32]
            heads.append(packed)
        parts.append(pairs_low(*heads))
    return jnp.concatenate(parts, axis=0).astype(jnp.bfloat16)


def branch_of(cot_ref, exit_ref):
    active = column((exit_ref[...] > LAYER).astype(jnp.float32))
    return jnp.where(active > 0.0, cot_ref[...].astype(jnp.float32), 0.0)


def dhidden_kernel(wait, flush, cot_ref, exit_ref, down_ref, out_ref, vec_ref):
    branch = branch_of(cot_ref, exit_ref)
    vec_ref[...] = jnp.sum(branch, axis=0, keepdims=True)
    out_ref[...] = lax.dot_general(
        branch.astype(jnp.bfloat16), down_ref[...], trans_right, preferred_element_type=jnp.float32
    )


def middle_kernel(
    wait, flush, got_ref, tokens_ref, cot_ref, exit_ref, o_bias_ref, gain_ref, shift_ref,
    up_bias_ref, o_own_ref, o_other_ref, up_ref, dhidden_ref,
    dn_ref, core_ref, high_ref, cross_ref, here_ref, mid_ref, hidden_ref, attn_ref, vec_ref,
    acc_ref, dpre_ref,
):
    side = lax.axis_index("wa")
    for pair in range(3):
        rows = slice(pair * 128, (pair + 1) * 128)
        attn_ref[:, rows] = attn_tile(got_ref, side, pair)
        acc_ref[:, rows] = attn_tile(got_ref, 1 - side, pair)
    flush(attn_ref)
    wait(o_own_ref)
    wait(o_other_ref)
    total = jnp.dot(
        attn_ref[...], o_own_ref[...], preferred_element_type=jnp.float32
    ) + jnp.dot(acc_ref[...], o_other_ref[...], preferred_element_type=jnp.float32)
    middle = tokens_ref[...].astype(jnp.float32) + (total + o_bias_ref[...])
    mid_ref[...] = middle
    flush(mid_ref)
    normed, _, _ = norm_forward(middle, gain_ref[...], shift_ref[...])
    low = normed.astype(jnp.bfloat16)
    branch_low = branch_of(cot_ref, exit_ref).astype(jnp.bfloat16)
    dnormed = None
    wait(up_ref)
    wait(dhidden_ref)
    for begin in range(0, 1536, FF_TILE):
        columns = slice(begin, begin + FF_TILE)
        pre_act = (
            jnp.dot(low, up_ref[:, columns], preferred_element_type=jnp.float32)
            + up_bias_ref[:, columns]
        )
        hidden_full, slope = gelu_pair(pre_act)
        hidden = hidden_full.astype(jnp.bfloat16)
        hidden_ref[:, columns] = hidden
        dpre = (dhidden_ref[:, columns] * slope).astype(jnp.bfloat16)
        vec_ref[:, columns] = jnp.sum(dpre.astype(jnp.float32), axis=0, keepdims=True)
        dpre_ref[:, columns] = dpre
        dn_term = lax.dot_general(
            dpre, up_ref[:, columns], trans_right, preferred_element_type=jnp.float32
        )
        dnormed = dn_term if dnormed is None else dnormed + dn_term
    dn_ref[...] = dnormed.astype(jnp.bfloat16)
    core, high = lax.axis_index("core"), lax.axis_index("zh")
    for ref, offset in ((core_ref, 1), (high_ref, 2), (cross_ref, 3), (here_ref, 0)):
        up_side = (core ^ (offset & 1)) == 0
        first_half = (high ^ (offset >> 1)) == 0
        ref[:, :768] = jnp.where(up_side, low, branch_low)
        ref[:, 768:] = jnp.where(
            up_side,
            jnp.where(first_half, dpre_ref[:, :768], dpre_ref[:, 768:]),
            jnp.where(first_half, hidden_ref[:, :768], hidden_ref[:, 768:]),
        )


def dheads_kernel(
    wait, flush, dn_ref, other_ref, mid_ref, cot_ref, exit_ref, gain_ref, attn_ref, up_ref, down_ref, o_ref,
    pay_ref, both_ref, dmid_ref, vec_ref,
):
    middle = mid_ref[...]
    _, unit, inverse = norm_forward(middle, gain_ref[...], 0.0)
    dnormed = dn_ref[...].astype(jnp.float32) + other_ref[...].astype(jnp.float32)
    branch = branch_of(cot_ref, exit_ref)
    dmiddle = branch + norm_backward(dnormed, unit, inverse, gain_ref[...])
    dmid_ref[...] = dmiddle
    flush(dmid_ref)
    low = dmiddle.astype(jnp.bfloat16)
    vec_ref[:, :1536] = up_ref[...]
    vec_ref[:, 1536:2304] = down_ref[...]
    vec_ref[:, 2304:3072] = jnp.sum(dnormed * unit, axis=0, keepdims=True)
    vec_ref[:, 3072:3840] = jnp.sum(dnormed, axis=0, keepdims=True)
    vec_ref[:, 3840:] = jnp.sum(low.astype(jnp.float32), axis=0, keepdims=True)
    wait(o_ref)
    for pair in range(3):
        dheads = lax.dot_general(
            low,
            o_ref[pair * 128 : (pair + 1) * 128],
            trans_right,
            preferred_element_type=jnp.float32,
        )
        for odd in range(2):
            pack = pack_from_high if odd else pack_from_low
            lower = pack(dheads[:HALF]).astype(jnp.bfloat16)
            higher = pack(dheads[HALF:]).astype(jnp.bfloat16)
            index = 4 * pair + 2 * odd
            pay_ref[index, :32] = lower
            pay_ref[index, 32:] = higher
            pay_ref[index + 1, :32] = higher
            pay_ref[index + 1, 32:] = higher
    pay_ref[12:] = jnp.zeros((4, HALF, 128), jnp.bfloat16)
    flush(pay_ref)
    both_ref[:, :768] = low
    both_ref[:, 768:] = attn_ref[...]


def ffn_products_kernel(
    wait, flush, here_ref, core_ref, high_ref, cross_ref, both_ref, sent_ref,
    vec_ref, vec_sent_ref, out_ref,
):
    pieces = (here_ref, core_ref, high_ref, cross_ref)
    lefts = jnp.concatenate([ref[:, :768] for ref in pieces], axis=0)
    for at in range(0, 768, 384):
        rights = jnp.concatenate([ref[:, 768 + at : 1152 + at] for ref in pieces], axis=0)
        out_ref[:, at : at + 384] = lax.dot_general(
            lefts, rights, trans_left, preferred_element_type=jnp.float32
        ).astype(jnp.bfloat16)
    first = lax.axis_index("core") == 0
    both = jnp.concatenate([both_ref[...], sent_ref[...]], axis=0)
    product = lax.dot_general(
        both[:, :768],
        jnp.where(first, both[:, 768:1024], both[:, 896:]),
        trans_left,
        preferred_element_type=jnp.float32,
    )
    out_ref[:, 896:] = product[:, 128:].astype(jnp.bfloat16)
    vec = vec_ref[...] + vec_sent_ref[...]
    lines = [vec[:, 128 * row : 128 * (row + 1)] for row in range(36)]
    lines = jnp.concatenate(lines + [jnp.zeros((12, 128), jnp.float32)], axis=0)
    for plane in range(16):
        rows = slice(48 * plane, 48 * plane + 48)
        out_ref[rows, 768:896] = jnp.where(first, product[rows, :128], lines).astype(jnp.bfloat16)


def ffn_kernel(wait, flush, hidden_ref, down_ref, out_ref):
    out_ref[...] = jnp.dot(
        hidden_ref[...], down_ref[...], preferred_element_type=jnp.float32
    ).astype(jnp.bfloat16)


def dnormed_kernel(
    wait, flush, got_ref, tokens_ref, q_ref, k_ref, v_ref,
    grads_ref, norm_ref, vec_ref, dn_ref,
):
    wide = lane_ids(HALF, 128) < HALF
    for pair in range(3):
        columns = slice(pair * 128, (pair + 1) * 128)
        key_columns = slice(384 + pair * 128, 512 + pair * 128)
        value_columns = slice(768 + pair * 128, 896 + pair * 128)
        for half in range(2):
            rows = slice(half * HALF, (half + 1) * HALF)
            at = 8 * pair + 2 * half
            even = got_ref[at].astype(jnp.float32) + got_ref[at + 1].astype(jnp.float32)
            odd = got_ref[at + 4].astype(jnp.float32) + got_ref[at + 5].astype(jnp.float32)
            grads_ref[rows, key_columns] = jnp.where(wide, even[:HALF], turn(odd[:HALF])).astype(
                jnp.bfloat16
            )
            grads_ref[rows, value_columns] = jnp.where(
                wide, turn(even[:HALF]), odd[:HALF]
            ).astype(jnp.bfloat16)
            grads_ref[rows, columns] = pairs_low(even[HALF:], odd[HALF:]).astype(jnp.bfloat16)
    for ref in (q_ref, k_ref, v_ref):
        wait(ref)
    dnormed = (
        lax.dot_general(
            grads_ref[:, :384], q_ref[...], trans_right, preferred_element_type=jnp.float32
        )
        + lax.dot_general(
            grads_ref[:, 384:768], k_ref[...], trans_right, preferred_element_type=jnp.float32
        )
        + lax.dot_general(
            grads_ref[:, 768:], v_ref[...], trans_right, preferred_element_type=jnp.float32
        )
    )
    dn_ref[...] = dnormed.astype(jnp.bfloat16)
    _, unit, _ = norm_forward(tokens_ref[...].astype(jnp.float32), 1.0, 0.0)
    total = jnp.sum(grads_ref[...].astype(jnp.float32), axis=0, keepdims=True)
    vec_ref[:, :768] = jnp.sum(dnormed, axis=0, keepdims=True)
    vec_ref[:, 768:1536] = jnp.sum(dnormed * unit, axis=0, keepdims=True)
    vec_ref[:, 1536:1920] = total[:, :384]
    vec_ref[:, 1920:2304] = total[:, 768:]
    norm_ref[...] = vec_ref[:, :1536]


def input_grad_kernel(
    wait, flush, dn_ref, other_ref, tokens_ref, cot_ref, exit_ref, gain_ref, dmid_ref, out_ref
):
    _, unit, inverse = norm_forward(tokens_ref[...].astype(jnp.float32), 1.0, 0.0)
    dnormed = dn_ref[...].astype(jnp.float32) + other_ref[...].astype(jnp.float32)
    active = column((exit_ref[...] > LAYER).astype(jnp.float32))
    out_ref[...] = (
        dmid_ref[...]
        + norm_backward(dnormed, unit, inverse, gain_ref[...])
        + jnp.where(active > 0.0, 0.0, cot_ref[...].astype(jnp.float32))
    )


def output_kernel(
    wait, flush, ffn_ref, other_ref, mid_ref, tokens_ref, exit_ref, bias_ref, out_ref
):
    active = column((exit_ref[...] > LAYER).astype(jnp.float32))
    branch = ffn_ref[...].astype(jnp.float32) + other_ref[...].astype(jnp.float32) + bias_ref[...]
    out_ref[...] = jnp.where(
        active > 0.0, mid_ref[...] + branch, tokens_ref[...].astype(jnp.float32)
    ).astype(jnp.bfloat16)


def merge_kernel(wait, flush, kept_ref, taken_ref, dq_ref, edge_ref, out_ref):
    high = lax.axis_index("zh")
    for block in range(BLOCKS):
        pair = kept_ref[block].astype(jnp.float32) + taken_ref[block].astype(jnp.float32)
        query = dq_ref[block]
        if block == BLOCKS - 1:
            pair = pair + edge_ref[:HALF].astype(jnp.float32)
            query = (query.astype(jnp.float32) + edge_ref[HALF:].astype(jnp.float32)).astype(
                jnp.bfloat16
            )
        out_ref[pl.ds(2 * block + high, 1), :HALF] = pair.astype(jnp.bfloat16)[None]
        out_ref[pl.ds(2 * block + high, 1), HALF:] = query[None]
        pair = kept_ref[BLOCKS + block].astype(jnp.float32) + taken_ref[BLOCKS + block].astype(
            jnp.float32
        )
        out_ref[pl.ds(2 * block + 1 - high, 1), :HALF] = pair.astype(jnp.bfloat16)[None]
        out_ref[pl.ds(2 * block + 1 - high, 1), HALF:] = jnp.zeros((1, 32, 128), jnp.bfloat16)


def qkv_products_kernel(
    wait, flush, keep_ref, sent_ref, grads_ref, grads_sent_ref,
    vec_ref, vec_sent_ref, wa_ref, cross_ref, out_ref,
):
    lefts = jnp.concatenate([keep_ref[...], sent_ref[...]], axis=0)
    vec = vec_ref[...] + vec_sent_ref[...]
    norms = vec[:, :1536] + (wa_ref[...] + cross_ref[...])
    vec = jnp.concatenate([norms, vec[:, 1536:]], axis=1)
    lines = jnp.concatenate(
        [vec[:, :1152], vec[:, 1152:], jnp.zeros((2, 1152), jnp.float32)], axis=0
    )
    for at in range(0, 1152, 384):
        columns = slice(at, at + 384)
        rights = jnp.concatenate([grads_ref[:, columns], grads_sent_ref[:, columns]], axis=0)
        product = lax.dot_general(lefts, rights, trans_left, preferred_element_type=jnp.float32)
        for chip in range(32):
            out_ref[chip, :, columns] = jnp.concatenate(
                [product[16 * chip : 16 * chip + 12], lines[:, columns]], axis=0
            ).astype(jnp.bfloat16)


def finish_kernel(
    wait, flush, got_ref, q_ref, k_ref, v_ref, shift_out, gain_out, q_bias_out, v_bias_out
):
    both = got_ref[0].astype(jnp.float32)
    for source in range(1, 32):
        both = both + got_ref[source].astype(jnp.float32)
    q_ref[...] = both[:12, :384]
    k_ref[...] = both[:12, 384:768]
    v_ref[...] = both[:12, 768:]
    shift_out[...] = both[12:13, :768]
    gain_out[:, :384] = both[12:13, 768:]
    gain_out[:, 384:] = both[13:14, :384]
    q_bias_out[...] = both[13:14, 384:768]
    v_bias_out[...] = both[13:14, 768:]


def ffn_sums_kernel(wait, flush, got_ref, core_ref, high_ref, cross_ref, here_ref):
    total = got_ref[0].astype(jnp.float32)
    for source in range(1, 16):
        total = total + got_ref[source].astype(jnp.float32)
    me = 2 * lax.axis_index("zh") + lax.axis_index("core")
    parts = [total[12 * index : 12 * index + 12, :1024] for index in range(4)]
    vec = jnp.concatenate([total[row : row + 1, 768:896] for row in range(36)], axis=1)
    vec = jnp.concatenate([vec, jnp.zeros((1, 512), jnp.float32)], axis=1)
    lines = [vec[:, 1024 * row : 1024 * (row + 1)] for row in range(5)]
    lines = jnp.concatenate(lines + [jnp.zeros((3, 1024), jnp.float32)], axis=0)

    def part(offset):
        value = parts[offset]
        for index in range(1, 4):
            value = jnp.where(me == index, parts[index ^ offset], value)
        return value

    for ref, offset in ((here_ref, 0), (core_ref, 1), (high_ref, 2), (cross_ref, 3)):
        ref[...] = jnp.concatenate(
            [part(offset), jnp.zeros((4, 1024), jnp.float32), lines, jnp.zeros((8, 1024), jnp.float32)],
            axis=0,
        ).astype(ref.dtype)


def ffn_finish_kernel(
    wait, flush, here_ref, core_ref, high_ref, cross_ref,
    up_ref, down_ref, o_ref, up_bias_out, down_bias_out, gain_out, shift_out, o_bias_out,
):
    first = lax.axis_index("core") == 0
    low = lax.axis_index("zh") == 0
    alls = [ref[...].astype(jnp.float32) for ref in (here_ref, core_ref, high_ref, cross_ref)]
    here, core, high, cross = [value[:12, :768] for value in alls]
    up_ref[:, :768] = jnp.where(first, jnp.where(low, here, high), jnp.where(low, core, cross))
    up_ref[:, 768:] = jnp.where(first, jnp.where(low, high, here), jnp.where(low, cross, core))
    down_ref[:, :768] = jnp.where(first, jnp.where(low, core, cross), jnp.where(low, here, high))
    down_ref[:, 768:] = jnp.where(first, jnp.where(low, cross, core), jnp.where(low, high, here))
    mine = alls[0][:, 768:] + alls[2][:, 768:]
    other = alls[1][:, 768:] + alls[3][:, 768:]
    o_ref[:, :256] = jnp.where(first, mine, other)[:12]
    o_ref[:, 256:] = jnp.where(first, other[:, 128:], mine[:, 128:])[:12]
    vec = jnp.where(first, alls[1][16:24] + alls[3][16:24], alls[0][16:24] + alls[2][16:24])
    vec = jnp.concatenate([vec[row : row + 1] for row in range(5)], axis=1)
    begin = 0
    for ref in (up_bias_out, down_bias_out, gain_out, shift_out, o_bias_out):
        ref[...] = vec[:, begin : begin + ref.shape[1]]
        begin += ref.shape[1]


def on_device(
    tokens,
    doc_start,
    exit_layer,
    cotangent,
    ln1_gain,
    ln1_shift,
    q_weight,
    q_bias,
    k_weight,
    v_weight,
    v_bias,
    o_weight,
    o_bias,
    ln2_gain,
    ln2_shift,
    up_weight,
    up_bias,
    down_weight,
    down_bias,
):
    f32 = jnp.float32

    def copied(*arrays):
        return [("d", array) for array in arrays]

    payload, low_one = call(
        project_kernel, "project",
        copied(
            tokens, doc_start, ln1_gain, ln1_shift, q_bias, v_bias, q_weight, k_weight, v_weight
        ),
        [("d", whole(16, HALF + 48, 128)), ("d", whole(128, 768))],
        lazy=(6, 7, 8),
    )
    own = lax.all_to_all(payload, PLANE, 0, 0, tiled=True)
    low_one, o_given = lax.optimization_barrier((low_one, o_weight))
    o_other = lax.ppermute(o_given, "wa", SWAP)
    x_send, x_keep = call(
        prepare_kernel, "prepare",
        copied(low_one),
        [("v", whole(128, 512)), ("d", whole(128, 512))],
    )
    own, x_send, o_other = lax.optimization_barrier((own, x_send, o_other))
    pairs = own[:, :HALF]
    one = lax.ppermute(pairs, "core", SWAP)
    edge = lax.ppermute(own[BLOCKS - 1], "y", ((1, 0), (3, 2)))
    two = lax.ppermute(pairs, "zh", SWAP)
    two, edge = lax.optimization_barrier((two, edge))
    three = lax.ppermute(two, "core", SWAP)
    x_sent = lax.ppermute(x_send, "core", SWAP)
    back, kv, q_rows, start_rows, full_rows = attend(own, one, two, three, edge)
    dhidden, vec_down = call(
        dhidden_kernel, "dhidden",
        copied(cotangent, exit_layer, down_weight),
        [("d", whole(128, 1536, dtype=f32)), ("d", whole(1, 768, dtype=f32))],
    )
    got = lax.all_to_all(back, ("x", "y", "wa"), 0, 0, tiled=True)
    dn_two, ffn_core, ffn_high, ffn_cross, ffn_here, middle, hidden, attn_low, vec_up = call(
        middle_kernel, "middle",
        [("v", got)]
        + copied(
            tokens, cotangent, exit_layer, o_bias, ln2_gain, ln2_shift, up_bias, o_weight, o_other,
            up_weight, dhidden,
        ),
        [
            ("v", whole(128, 768)),
            ("v", whole(128, 1536)),
            ("v", whole(128, 1536)),
            ("v", whole(128, 1536)),
            ("v", whole(128, 1536)),
            ("d", whole(128, 768, dtype=f32)),
            ("d", whole(128, 1536)),
            ("d", whole(128, 384)),
            ("d", whole(1, 1536, dtype=f32)),
        ],
        [pltpu.VMEM((128, 384), jnp.bfloat16), pltpu.VMEM((128, 1536), jnp.bfloat16)],
        lazy=(8, 9, 10, 11),
    )
    dn_two_other = lax.ppermute(dn_two, "wa", SWAP)
    ffn_high = lax.ppermute(ffn_high, "zh", SWAP)
    ffn_cross = lax.ppermute(ffn_cross, ("zh", "core"), CROSS)
    ffn_core = lax.ppermute(ffn_core, "core", SWAP)
    ffn = call(ffn_kernel, "ffn", copied(hidden, down_weight), [("v", whole(128, 768))], cost=0)
    dn_two_other, ffn = lax.optimization_barrier((dn_two_other, ffn))
    dh_payload, dattn_attn, dmiddle, vec_two = call(
        dheads_kernel, "dheads",
        [("v", dn_two), ("v", dn_two_other)]
        + copied(middle, cotangent, exit_layer, ln2_gain, attn_low, vec_up, vec_down, o_weight),
        [
            ("d", whole(16, HALF, 128)),
            ("v", whole(128, 1152)),
            ("d", whole(128, 768, dtype=f32)),
            ("v", whole(1, 4608, dtype=f32)),
        ],
        lazy=(9,),
        cost=0,
    )
    dh = lax.all_to_all(dh_payload, PLANE, 0, 0, tiled=True)
    dattn_sent = lax.ppermute(dattn_attn, "core", SWAP)
    vec_two_sent = lax.ppermute(vec_two, "core", SWAP)
    ffn_products = call(
        ffn_products_kernel, "ffn_products",
        [("v", ffn_here), ("v", ffn_core), ("v", ffn_high), ("v", ffn_cross)]
        + [("v", dattn_attn), ("v", dattn_sent), ("v", vec_two), ("v", vec_two_sent)],
        [("d", whole(768, 1024))],
    )
    ffn_blocks = lax.all_to_all(ffn_products.reshape(16, 48, 1024), PLANE, 0, 0, tiled=True)
    ffn_other = lax.ppermute(ffn, "wa", SWAP)
    given, kept, dq, edge_grad = attend_grad(kv, q_rows, start_rows, full_rows, dh)
    given, ffn_other = lax.optimization_barrier((given, ffn_other))
    edge_got = lax.ppermute(edge_grad, "y", ((0, 1), (2, 3)))
    taken = lax.ppermute(given, "core", SWAP)
    merged = call(
        merge_kernel, "merge",
        [("v", kept), ("v", taken), ("v", dq), ("v", edge_got)],
        [("d", whole(2 * BLOCKS, 96, 128))],
    )
    merged, ffn_blocks = lax.optimization_barrier((merged, ffn_blocks))
    grads = lax.all_to_all(merged, CHIPS, 0, 0, tiled=True)
    ffn_core, ffn_high, ffn_cross, ffn_here = call(
        ffn_sums_kernel, "ffn_sums", copied(ffn_blocks),
        [("v", whole(32, 1024)) for _ in range(3)] + [("v", whole(32, 1024, dtype=f32))],
        cost=0,
    )
    ffn_core = lax.ppermute(ffn_core, "core", SWAP)
    ffn_high = lax.ppermute(ffn_high, "zh", SWAP)
    ffn_cross = lax.ppermute(ffn_cross, ("zh", "core"), CROSS)
    grads, ffn_core, ffn_high, ffn_cross, x_sent = lax.optimization_barrier(
        (grads, ffn_core, ffn_high, ffn_cross, x_sent)
    )
    grads_rows, norms, vec, dn_one = call(
        dnormed_kernel, "dnormed",
        [("v", grads)] + copied(tokens, q_weight, k_weight, v_weight),
        [
            ("v", whole(128, 1152)),
            ("v", whole(1, 1536, dtype=f32)),
            ("v", whole(1, 2304, dtype=f32)),
            ("v", whole(128, 768)),
        ],
        lazy=(2, 3, 4),
        cost=0,
    )
    grads_sent = lax.ppermute(grads_rows, "core", SWAP)
    vec_sent = lax.ppermute(vec, "core", SWAP)
    norms_wa = lax.ppermute(norms, "wa", SWAP)
    norms_cross = lax.ppermute(norms, ("core", "wa"), CROSS)
    norms_wa, norms_cross, dn_one = lax.optimization_barrier((norms_wa, norms_cross, dn_one))
    dn_one_other = lax.ppermute(dn_one, "wa", SWAP)
    products = call(
        qkv_products_kernel, "qkv_products",
        copied(x_keep, x_sent)
        + [("v", grads_rows), ("v", grads_sent), ("v", vec), ("v", vec_sent)]
        + [("v", norms_wa), ("v", norms_cross)],
        [("d", whole(32, 16, 1152))],
        cost=0,
    )
    products = lax.all_to_all(products, CHIPS, 0, 0, tiled=True)
    output = call(
        output_kernel, "output",
        [("v", ffn), ("v", ffn_other)] + copied(middle, tokens, exit_layer, down_bias),
        [("d", whole(128, 768))],
        cost=0,
    )
    (
        up_weight_grad, down_weight_grad_t, o_weight_grad_t,
        up_bias_grad, down_bias_grad, ln2_gain_grad, ln2_shift_grad, o_bias_grad,
    ) = call(
        ffn_finish_kernel, "ffn_finish",
        [("v", ffn_here), ("v", ffn_core), ("v", ffn_high), ("v", ffn_cross)],
        [("d", whole(12, 1536, dtype=f32)) for _ in range(2)]
        + [("d", whole(12, 384, dtype=f32))]
        + [("d", whole(count, dtype=f32)) for count in (1536, 768, 768, 768, 768)],
        cost=0,
    )
    input_grad = call(
        input_grad_kernel, "input_grad",
        [("v", dn_one), ("v", dn_one_other)]
        + copied(tokens, cotangent, exit_layer, ln1_gain, dmiddle),
        [("d", whole(128, 768, dtype=f32))],
        cost=0,
    )
    (
        products, output, input_grad, up_weight_grad, down_weight_grad_t
    ) = lax.optimization_barrier(
        (products, output, input_grad, up_weight_grad, down_weight_grad_t)
    )
    (
        q_weight_grad, k_weight_grad, v_weight_grad,
        ln1_shift_grad, ln1_gain_grad, q_bias_grad, v_bias_grad,
    ) = call(
        finish_kernel, "finish",
        [("v", products)],
        [("d", whole(12, 384, dtype=f32)) for _ in range(3)]
        + [("d", whole(count, dtype=f32)) for count in (768, 768, 384, 384)],
    )
    return (
        output,
        input_grad,
        ln1_gain_grad,
        ln1_shift_grad,
        q_weight_grad,
        q_bias_grad,
        k_weight_grad,
        v_weight_grad,
        v_bias_grad,
        o_weight_grad_t,
        o_bias_grad,
        ln2_gain_grad,
        ln2_shift_grad,
        up_weight_grad,
        up_bias_grad,
        down_weight_grad_t,
        down_bias_grad,
    )


def solution(mesh):
    fine = Mesh(mesh.devices.reshape(4, 4, 2, 2, 2), CTX + ("wa",))
    return jax.shard_map(
        on_device,
        mesh=fine,
        in_specs=(
            P(CTX, None),
            P(CTX),
            P(CTX),
            P(CTX, None),
            P(),
            P(),
            P(None, "wa"),
            P("wa"),
            P(None, "wa"),
            P(None, "wa"),
            P("wa"),
            P("wa", None),
            P(),
            P(),
            P(),
            P(None, "wa"),
            P("wa"),
            P("wa", None),
            P(),
        ),
        out_specs=(
            P(CTX, None),
            P(CTX, None),
            P(),
            P(),
            P(CTX, "wa"),
            P("wa"),
            P(CTX, "wa"),
            P(CTX, "wa"),
            P("wa"),
            P(CTX, "wa"),
            P(),
            P(),
            P(),
            P(CTX, "wa"),
            P("wa"),
            P(CTX, "wa"),
            P(),
        ),
        check_vma=False,
    )
```

```python
import math

import jax
import jax.numpy as jnp
from jax import lax
from jax.experimental import pallas as pl
from jax.experimental.pallas import tpu as pltpu
from jax.sharding import Mesh, PartitionSpec as P

HEAD_DIM = 64
LAYER = 6
CTX = ("x", "y", "zh", "core")
CHIPS = ("x", "y", "zh")
PLANE = ("x", "y")
SWAP = ((0, 1), (1, 0))
CROSS = ((0, 3), (1, 2), (2, 1), (3, 0))
HALF = 64
BLOCKS = 16
GROUP = 256
STREAM = 8192
ROWS = (BLOCKS + 1) * HALF
FF_TILE = 512
FAR = 1e9
SCALING = 1.0 / math.sqrt(HEAD_DIM)
EXP2_SCALE = SCALING / math.log(2.0)
VMEM_BYTES = 64 * 2**20


epsilon = 1e-05
trans_right = (((1,), (1,)), ((), ()))
trans_left = (((0,), (0,)), ((), ()))
cubic_coef = 0.044715


def gelu_pair(values):
    outer = math.sqrt(2.0 / math.pi)
    inner = outer * (values + cubic_coef * values * values * values)
    tangent = jnp.tanh(inner)
    result = 0.5 * values * (1.0 + tangent)
    gelu_slope = 0.5 * (1.0 + tangent) + 0.5 * values * (1.0 - tangent * tangent) * outer * (
        1.0 + 3.0 * cubic_coef * values * values
    )
    return (result, gelu_slope)


def norm_forward(values, gain_vec, shift_vec):
    average = jnp.mean(values, axis=-1, keepdims=True)
    centred = values - average
    inverse_std = lax.rsqrt(jnp.mean(centred * centred, axis=-1, keepdims=True) + epsilon)
    normed = centred * inverse_std
    return (normed * gain_vec + shift_vec, normed, inverse_std)


def norm_backward(grad_out, normed, inverse_std, gain_vec):
    scaled = grad_out * gain_vec
    return inverse_std * (
        scaled
        - jnp.mean(scaled, axis=-1, keepdims=True)
        - normed * jnp.mean(scaled * normed, axis=-1, keepdims=True)
    )


def swap_add(part, axis):
    other = lax.ppermute(part, axis, SWAP)
    return part.astype(jnp.float32) + other.astype(jnp.float32)


def whole(*shape, dtype=jnp.bfloat16):
    return jax.ShapeDtypeStruct(shape, dtype)


def head_place():
    upper = lax.axis_index("y") % 2
    sub = 2 * lax.axis_index("zh") + lax.axis_index("core")
    last = sub == 3
    return (
        upper,
        jnp.where(upper == 1, 3 - sub, sub),
        jnp.where((upper == 0) & last, 1, 0),
        jnp.where((upper == 1) & last, 1, 0),
    )


def call(kernel, name, ins, outs, scratch=(), lazy=(), cost=2):
    copied_in = [at for at, (mode, _) in enumerate(ins) if mode == "d"]
    copied_out = [at for at, (mode, _) in enumerate(outs) if mode == "d"]

    def buffer(array):
        shape = array.shape if len(array.shape) > 1 else (1,) + tuple(array.shape)
        return pltpu.VMEM(shape, array.dtype)

    def body(*refs):
        given, rest = list(refs[: len(ins)]), refs[len(ins) :]
        results, rest = list(rest[: len(outs)]), rest[len(outs) :]
        in_buffers, rest = rest[: len(copied_in)], rest[len(copied_in) :]
        out_buffers, rest = rest[: len(copied_out)], rest[len(copied_out) :]
        in_sems, out_sems, rest = rest[0], rest[1], rest[2:]
        pending, flushing = [], []
        for slot, at in enumerate(copied_in):
            there = in_buffers[slot]
            into = there if len(ins[at][1].shape) > 1 else there.at[0]
            copy = pltpu.make_async_copy(given[at], into, in_sems.at[slot])
            copy.start()
            given[at] = there
            pending.append((there, at, copy))
        targets = []
        for slot, at in enumerate(copied_out):
            made = out_buffers[slot] if len(outs[at][1].shape) > 1 else out_buffers[slot].at[0]
            copy = pltpu.make_async_copy(made, results[at], out_sems.at[slot])
            results[at] = out_buffers[slot]
            targets.append((out_buffers[slot], copy))

        def wait(ref):
            for entry in list(pending):
                if entry[0] is ref:
                    entry[2].wait()
                    pending[:] = [other for other in pending if other is not entry]

        def flush(ref):
            for entry in list(targets):
                if entry[0] is ref:
                    entry[1].start()
                    flushing.append(entry[1])
                    targets[:] = [other for other in targets if other is not entry]

        for entry in list(pending):
            if entry[1] not in lazy:
                wait(entry[0])
        kernel(wait, flush, *given, *results, *rest)
        for entry in list(pending):
            wait(entry[0])
        for entry in list(targets):
            flush(entry[0])
        for copy in flushing:
            copy.wait()

    vmem, anywhere = pl.BlockSpec(memory_space=pltpu.VMEM), pl.BlockSpec(memory_space=pltpu.HBM)
    result = pl.pallas_call(
        body,
        out_shape=tuple(out for _, out in outs),
        in_specs=[anywhere if mode == "d" else vmem for mode, _ in ins],
        out_specs=tuple(anywhere if mode == "d" else vmem for mode, _ in outs),
        scratch_shapes=[buffer(ins[at][1]) for at in copied_in]
        + [buffer(outs[at][1]) for at in copied_out]
        + [
            pltpu.SemaphoreType.DMA((max(1, len(copied_in)),)),
            pltpu.SemaphoreType.DMA((max(1, len(copied_out)),)),
        ]
        + list(scratch),
        compiler_params=pltpu.CompilerParams(vmem_limit_bytes=VMEM_BYTES),
        cost_estimate=pl.CostEstimate(
            flops=cost * 10**9, transcendentals=0, bytes_accessed=0
        ),
        name=name,
    )(*[array for _, array in ins])
    return result[0] if len(outs) == 1 else result


def lane_ids(rows, cols):
    return lax.broadcasted_iota(jnp.int32, (rows, cols), 1)


def row_ids_of(rows, cols):
    return lax.broadcasted_iota(jnp.int32, (rows, cols), 0)


def turn(values):
    return pltpu.roll(values, HALF, 1)


def unpack_low(packed):
    wide = packed.astype(jnp.float32)
    left = lane_ids(32, 128) < HALF
    both = jnp.concatenate([wide, turn(wide)], axis=0)
    return jnp.where(jnp.concatenate([left, left], axis=0), both, 0.0)


def unpack_high(packed):
    wide = packed.astype(jnp.float32)
    right = lane_ids(32, 128) >= HALF
    both = jnp.concatenate([turn(wide), wide], axis=0)
    return jnp.where(jnp.concatenate([right, right], axis=0), both, 0.0)


def pack_from_low(block):
    return jnp.where(lane_ids(32, 128) < HALF, block[:32], turn(block[32:]))


def pack_from_high(block):
    return jnp.where(lane_ids(32, 128) < HALF, turn(block[:32]), block[32:])


def key_places(scal, group):
    lane = lane_ids(8, GROUP)
    sub = (lane >> 6) ^ scal[1]
    return (scal[0] * (STREAM // 2) + GROUP * group + (sub << 6) + (lane & 63)).astype(
        jnp.float32
    )


def edge_places():
    return (STREAM // 2 + lane_ids(8, 128)).astype(jnp.float32)


def query_places(scal, block):
    row = row_ids_of(HALF, 128)
    return (
        scal[0] * (STREAM // 2) + GROUP * block + (scal[1] << 6) + row
    ).astype(jnp.float32)


def spread(rows, width):
    return jnp.concatenate([rows] * (width // 128), axis=1) if width > 128 else rows


def weights_of(scal, queries, starts, keys, places, group):
    scores = lax.dot_general(queries, keys, trans_right, preferred_element_type=jnp.float32)
    count = queries.shape[0]
    own = spread(query_places(scal, group), GROUP)
    limit = jnp.concatenate([own, jnp.full((count - HALF, GROUP), FAR, jnp.float32)], axis=0)
    seen = (spread(starts, GROUP) <= places[:1]) & (places[:1] <= limit)
    return jnp.where(seen, jnp.exp2(scores * EXP2_SCALE), 0.0)


def edge_weights(queries, starts, keys):
    scores = lax.dot_general(queries, keys, trans_right, preferred_element_type=jnp.float32)
    places = edge_places()[:1]
    limit = (STREAM // 2 + row_ids_of(HALF, 128)).astype(jnp.float32)
    return jnp.where(
        (starts <= places) & (places <= limit), jnp.exp2(scores * EXP2_SCALE), 0.0
    )


def attend_kernel(
    wait, flush, own_ref, one_ref, two_ref, three_ref, edge_ref,
    back_ref, kv_ref, q_ref, start_ref, full_ref,
    num_ref, den_ref,
):
    scal = head_place()
    upper = scal[0]
    diag = jnp.where(
        lane_ids(HALF, 128) == row_ids_of(HALF, 128),
        64.0,
        jnp.where(lane_ids(HALF, 128) == row_ids_of(HALF, 128) + HALF, 1.0, 0.0),
    )

    def starts(line, off):
        found = jnp.sum(line.astype(jnp.float32) * diag, axis=1, keepdims=True)
        return jnp.broadcast_to(jnp.where(off, FAR, found), (HALF, 128))

    for block in range(BLOCKS):
        place = jnp.where(upper == 1, BLOCKS - 1 - block, block)
        rows = slice(block * HALF, (block + 1) * HALF)
        mine = own_ref[pl.ds(place, 1)][0]
        kv_ref[block, 0:HALF] = mine[:HALF]
        kv_ref[block, HALF : 2 * HALF] = one_ref[pl.ds(place, 1)][0]
        kv_ref[block, 2 * HALF : 3 * HALF] = two_ref[pl.ds(place, 1)][0]
        kv_ref[block, 3 * HALF :] = three_ref[pl.ds(place, 1)][0]
        q_ref[rows] = unpack_low(mine[HALF : HALF + 32]).astype(jnp.bfloat16)
        off = (scal[3] == 1) if block == 0 else False
        start_ref[rows] = starts(mine[HALF + 32 : HALF + 33], off)
    kv_ref[BLOCKS] = jnp.zeros((GROUP, 128), jnp.bfloat16)
    kv_ref[BLOCKS, :HALF] = edge_ref[:HALF]
    q_ref[BLOCKS * HALF :] = unpack_low(edge_ref[HALF : HALF + 32]).astype(jnp.bfloat16)
    start_ref[BLOCKS * HALF :] = starts(edge_ref[HALF + 32 : HALF + 33], scal[2] == 0)
    flush(kv_ref)
    flush(q_ref)
    flush(start_ref)

    for group in range(BLOCKS + 1):
        rows = slice(group * HALF, ROWS)
        if group < BLOCKS:
            keys = kv_ref[group]
            weights = weights_of(
                scal, q_ref[rows], start_ref[rows], keys, key_places(scal, group), group
            )
            total = weights[:, :128] + weights[:, 128:]
        else:
            keys = kv_ref[group, :128]
            weights = total = edge_weights(q_ref[rows], start_ref[rows], keys)
        product = jnp.dot(weights.astype(jnp.bfloat16), keys, preferred_element_type=jnp.float32)
        if group == 0:
            num_ref[rows] = product
            den_ref[rows] = total
        else:
            num_ref[rows] += product
            den_ref[rows] += total

    for block in range(BLOCKS + 1):
        rows = slice(block * HALF, (block + 1) * HALF)
        den = jnp.sum(den_ref[rows], axis=1, keepdims=True)
        recip = jnp.broadcast_to(1.0 / jnp.where(den == 0.0, 1.0, den), (HALF, 128))
        full = num_ref[rows] * recip
        full_ref[rows] = jnp.where(lane_ids(HALF, 128) < HALF, recip, full)
        packed = pack_from_high(full).astype(jnp.bfloat16)
        if block < BLOCKS:
            place = jnp.where(upper == 1, BLOCKS - 1 - block, block)
            for copy in range(2):
                back_ref[pl.ds(2 * place + copy, 1), :32] = packed[None]
                back_ref[pl.ds(2 * place + copy, 1), 32:] = jnp.zeros((1, 32, 128), jnp.bfloat16)
        else:
            for copy in range(2):
                back_ref[2 * BLOCKS - 2 + copy, 32:] = packed


def attend_grad_kernel(
    wait, flush, kv_ref, q_ref, start_ref, full_ref, dh_in_ref,
    send_ref, keep_ref, dq_ref, edge_ref,
    dhn_ref, dot_ref, dq_acc,
):
    scal = head_place()
    upper = scal[0]
    left = lane_ids(HALF, 128) < HALF
    wait(full_ref)
    for block in range(BLOCKS + 1):
        rows = slice(block * HALF, (block + 1) * HALF)
        if block < BLOCKS:
            place = jnp.where(upper == 1, BLOCKS - 1 - block, block)
            packed = dh_in_ref[pl.ds(place, 1), :32][0]
        else:
            packed = dh_in_ref[BLOCKS - 1, 32:]
        full = full_ref[rows]
        scaled = unpack_high(packed) * jnp.where(left, full, turn(full))
        scaled = scaled.astype(jnp.bfloat16).astype(jnp.float32)
        dhn_ref[rows] = scaled.astype(jnp.bfloat16)
        dot_ref[rows] = jnp.broadcast_to(
            jnp.sum(jnp.where(left, 0.0, scaled * full), axis=1, keepdims=True), (HALF, 128)
        )
    wait(kv_ref)
    wait(q_ref)
    wait(start_ref)
    for group in range(BLOCKS + 1):
        rows = slice(group * HALF, ROWS)
        if group < BLOCKS:
            keys = kv_ref[group]
            weights = weights_of(
                scal, q_ref[rows], start_ref[rows], keys, key_places(scal, group), group
            )
        else:
            keys = kv_ref[group, :128]
            weights = edge_weights(q_ref[rows], start_ref[rows], keys)
        dprob = lax.dot_general(
            dhn_ref[rows], keys, trans_right, preferred_element_type=jnp.float32
        )
        dscore = (weights * (dprob - spread(dot_ref[rows], keys.shape[0]))).astype(jnp.bfloat16)
        dquery = jnp.dot(dscore, keys, preferred_element_type=jnp.float32)
        if group == 0:
            dq_acc[rows] = dquery
        else:
            dq_acc[rows] += dquery
        grads = lax.dot_general(
            dscore, q_ref[rows], trans_left, preferred_element_type=jnp.float32
        ) * SCALING + lax.dot_general(
            weights.astype(jnp.bfloat16),
            dhn_ref[rows],
            trans_left,
            preferred_element_type=jnp.float32,
        )
        low = grads.astype(jnp.bfloat16)
        if group < BLOCKS:
            place = jnp.where(upper == 1, BLOCKS - 1 - group, group)
            for quarter in range(4):
                out = send_ref if quarter % 2 else keep_ref
                out[pl.ds(quarter // 2 * BLOCKS + place, 1)] = low[
                    None, quarter * HALF : (quarter + 1) * HALF
                ]
        else:
            edge_ref[:HALF] = low[:HALF]

    for block in range(BLOCKS + 1):
        rows = slice(block * HALF, (block + 1) * HALF)
        packed = pack_from_low(dq_acc[rows] * SCALING).astype(jnp.bfloat16)
        if block < BLOCKS:
            place = jnp.where(upper == 1, BLOCKS - 1 - block, block)
            dq_ref[pl.ds(place, 1)] = packed[None]
        else:
            edge_ref[HALF:] = packed


def attend(own, one, two, three, edge):
    f32 = jnp.float32
    return call(
        attend_kernel, "attend",
        [("v", own), ("v", one), ("v", two), ("v", three), ("v", edge)],
        [
            ("d", whole(2 * BLOCKS, HALF, 128)),
            ("d", whole(BLOCKS + 1, GROUP, 128)),
            ("d", whole(ROWS, 128)),
            ("d", whole(ROWS, 128, dtype=f32)),
            ("d", whole(ROWS, 128, dtype=f32)),
        ],
        [pltpu.VMEM((ROWS, 128), f32), pltpu.VMEM((ROWS, 128), f32)],
        cost=3,
    )


def attend_grad(kv, q, start, full, dh):
    f32 = jnp.float32
    return call(
        attend_grad_kernel, "attend_grad",
        [("d", kv), ("d", q), ("d", start), ("d", full), ("v", dh)],
        [
            ("v", whole(2 * BLOCKS, HALF, 128)),
            ("v", whole(2 * BLOCKS, HALF, 128)),
            ("v", whole(BLOCKS, 32, 128)),
            ("v", whole(96, 128)),
        ],
        [
            pltpu.VMEM((ROWS, 128), jnp.bfloat16),
            pltpu.VMEM((ROWS, 128), f32),
            pltpu.VMEM((ROWS, 128), f32),
        ],
        lazy=(0, 1, 2, 3),
        cost=40,
    )


def column(line):
    return jnp.sum(
        jnp.where(lane_ids(128, 128) == row_ids_of(128, 128), line, 0.0), axis=1, keepdims=True
    )


def pairs_low(even, odd):
    left = lane_ids(32, 128) < HALF
    return jnp.concatenate(
        [jnp.where(left, even, turn(odd)), jnp.where(left, turn(even), odd)], axis=0
    )


def project_kernel(
    wait, flush,
    tokens_ref, start_ref, gain_ref, shift_ref, q_bias_ref, v_bias_ref, q_ref, k_ref, v_ref,
    pay_ref, low_ref,
):
    normed, _, _ = norm_forward(tokens_ref[...].astype(jnp.float32), gain_ref[...], shift_ref[...])
    low = normed.astype(jnp.bfloat16)
    low_ref[...] = low
    flush(low_ref)
    starts = start_ref[...]
    high_part = (starts >> 6).astype(jnp.float32)
    low_part = (starts & 63).astype(jnp.float32)
    left = lane_ids(1, 128) < HALF
    lines = (
        jnp.where(left, high_part, turn(low_part)),
        jnp.where(left, turn(high_part), low_part),
    )
    lines = [jnp.broadcast_to(line, (16, 128)).astype(jnp.bfloat16) for line in lines]
    wide = lane_ids(HALF, 128) < HALF
    for ref in (q_ref, k_ref, v_ref):
        wait(ref)
    for pair in range(3):
        columns = slice(pair * 128, (pair + 1) * 128)
        queries = (
            jnp.dot(low, q_ref[:, columns], preferred_element_type=jnp.float32)
            + q_bias_ref[:, columns]
        )
        keyset = jnp.dot(low, k_ref[:, columns], preferred_element_type=jnp.float32)
        values = (
            jnp.dot(low, v_ref[:, columns], preferred_element_type=jnp.float32)
            + v_bias_ref[:, columns]
        )
        for half in range(2):
            rows = slice(half * HALF, (half + 1) * HALF)
            for odd in range(2):
                if odd:
                    both = jnp.where(wide, turn(keyset[rows]), values[rows])
                    packed = pack_from_high(queries[rows])
                else:
                    both = jnp.where(wide, keyset[rows], turn(values[rows]))
                    packed = pack_from_low(queries[rows])
                index = 4 * pair + 2 * odd + half
                pay_ref[index, :HALF] = both.astype(jnp.bfloat16)
                pay_ref[index, HALF : HALF + 32] = packed.astype(jnp.bfloat16)
                pay_ref[index, HALF + 32 :] = lines[half]
    pay_ref[12:] = jnp.zeros((4, HALF + 48, 128), jnp.bfloat16)


def prepare_kernel(wait, flush, low_ref, send_ref, keep_ref):
    lane = lane_ids(8, 768)
    core = (lane >= 384).astype(jnp.int32)
    within = lane - 384 * core
    chip = (within * 171) >> 11
    source = (24 * chip + 12 * core + (within - 12 * chip))[:1]
    order = jnp.where(row_ids_of(768, 768) == source, 1.0, 0.0).astype(jnp.bfloat16)
    ordered = jnp.dot(low_ref[...], order, preferred_element_type=jnp.float32).astype(jnp.bfloat16)
    first = lax.axis_index("core") == 0
    keep_ref[...] = jnp.where(first, ordered[:, :384], ordered[:, 384:])
    send_ref[...] = jnp.where(first, ordered[:, 384:], ordered[:, :384])


def attn_tile(got_ref, side, pair):
    parts = []
    for half in range(2):
        heads = []
        for odd in range(2):
            index = 4 * pair + 2 * odd
            lower = got_ref[pl.ds(2 * index + side, 1)][0].astype(jnp.float32)
            if half:
                higher = got_ref[pl.ds(2 * index + 2 + side, 1)][0].astype(jnp.float32)
                packed = higher[:32] + lower[32:]
            else:
                packed = lower[:32]
            heads.append(packed)
        parts.append(pairs_low(*heads))
    return jnp.concatenate(parts, axis=0).astype(jnp.bfloat16)


def branch_of(cot_ref, exit_ref):
    active = column((exit_ref[...] > LAYER).astype(jnp.float32))
    return jnp.where(active > 0.0, cot_ref[...].astype(jnp.float32), 0.0)


def dhidden_kernel(wait, flush, cot_ref, exit_ref, down_ref, out_ref, vec_ref):
    branch = branch_of(cot_ref, exit_ref)
    vec_ref[...] = jnp.sum(branch, axis=0, keepdims=True)
    out_ref[...] = lax.dot_general(
        branch.astype(jnp.bfloat16), down_ref[...], trans_right, preferred_element_type=jnp.float32
    )


def middle_kernel(
    wait, flush, got_ref, tokens_ref, cot_ref, exit_ref, o_bias_ref, gain_ref, shift_ref,
    up_bias_ref, o_own_ref, o_other_ref, up_ref, dhidden_ref,
    dn_ref, core_ref, high_ref, cross_ref, here_ref, mid_ref, hidden_ref, attn_ref, vec_ref,
    acc_ref, dpre_ref,
):
    side = lax.axis_index("wa")
    for pair in range(3):
        rows = slice(pair * 128, (pair + 1) * 128)
        attn_ref[:, rows] = attn_tile(got_ref, side, pair)
        acc_ref[:, rows] = attn_tile(got_ref, 1 - side, pair)
    flush(attn_ref)
    wait(o_own_ref)
    wait(o_other_ref)
    total = jnp.dot(
        attn_ref[...], o_own_ref[...], preferred_element_type=jnp.float32
    ) + jnp.dot(acc_ref[...], o_other_ref[...], preferred_element_type=jnp.float32)
    middle = tokens_ref[...].astype(jnp.float32) + (total + o_bias_ref[...])
    mid_ref[...] = middle
    flush(mid_ref)
    normed, _, _ = norm_forward(middle, gain_ref[...], shift_ref[...])
    low = normed.astype(jnp.bfloat16)
    branch_low = branch_of(cot_ref, exit_ref).astype(jnp.bfloat16)
    dnormed = None
    wait(up_ref)
    wait(dhidden_ref)
    for begin in range(0, 1536, FF_TILE):
        columns = slice(begin, begin + FF_TILE)
        pre_act = (
            jnp.dot(low, up_ref[:, columns], preferred_element_type=jnp.float32)
            + up_bias_ref[:, columns]
        )
        hidden_full, slope = gelu_pair(pre_act)
        hidden = hidden_full.astype(jnp.bfloat16)
        hidden_ref[:, columns] = hidden
        dpre = (dhidden_ref[:, columns] * slope).astype(jnp.bfloat16)
        vec_ref[:, columns] = jnp.sum(dpre.astype(jnp.float32), axis=0, keepdims=True)
        dpre_ref[:, columns] = dpre
        dn_term = lax.dot_general(
            dpre, up_ref[:, columns], trans_right, preferred_element_type=jnp.float32
        )
        dnormed = dn_term if dnormed is None else dnormed + dn_term
    dn_ref[...] = dnormed.astype(jnp.bfloat16)
    core, high = lax.axis_index("core"), lax.axis_index("zh")
    for ref, offset in ((core_ref, 1), (high_ref, 2), (cross_ref, 3), (here_ref, 0)):
        up_side = (core ^ (offset & 1)) == 0
        first_half = (high ^ (offset >> 1)) == 0
        ref[:, :768] = jnp.where(up_side, low, branch_low)
        ref[:, 768:] = jnp.where(
            up_side,
            jnp.where(first_half, dpre_ref[:, :768], dpre_ref[:, 768:]),
            jnp.where(first_half, hidden_ref[:, :768], hidden_ref[:, 768:]),
        )


def dheads_kernel(
    wait, flush, dn_ref, other_ref, mid_ref, cot_ref, exit_ref, gain_ref, attn_ref, up_ref, down_ref, o_ref,
    pay_ref, both_ref, dmid_ref, vec_ref,
):
    middle = mid_ref[...]
    _, unit, inverse = norm_forward(middle, gain_ref[...], 0.0)
    dnormed = dn_ref[...].astype(jnp.float32) + other_ref[...].astype(jnp.float32)
    branch = branch_of(cot_ref, exit_ref)
    dmiddle = branch + norm_backward(dnormed, unit, inverse, gain_ref[...])
    dmid_ref[...] = dmiddle
    flush(dmid_ref)
    low = dmiddle.astype(jnp.bfloat16)
    vec_ref[:, :1536] = up_ref[...]
    vec_ref[:, 1536:2304] = down_ref[...]
    vec_ref[:, 2304:3072] = jnp.sum(dnormed * unit, axis=0, keepdims=True)
    vec_ref[:, 3072:3840] = jnp.sum(dnormed, axis=0, keepdims=True)
    vec_ref[:, 3840:] = jnp.sum(low.astype(jnp.float32), axis=0, keepdims=True)
    wait(o_ref)
    for pair in range(3):
        dheads = lax.dot_general(
            low,
            o_ref[pair * 128 : (pair + 1) * 128],
            trans_right,
            preferred_element_type=jnp.float32,
        )
        for odd in range(2):
            pack = pack_from_high if odd else pack_from_low
            lower = pack(dheads[:HALF]).astype(jnp.bfloat16)
            higher = pack(dheads[HALF:]).astype(jnp.bfloat16)
            index = 4 * pair + 2 * odd
            pay_ref[index, :32] = lower
            pay_ref[index, 32:] = higher
            pay_ref[index + 1, :32] = higher
            pay_ref[index + 1, 32:] = higher
    pay_ref[12:] = jnp.zeros((4, HALF, 128), jnp.bfloat16)
    flush(pay_ref)
    both_ref[:, :768] = low
    both_ref[:, 768:] = attn_ref[...]


def ffn_products_kernel(
    wait, flush, here_ref, core_ref, high_ref, cross_ref, both_ref, sent_ref,
    vec_ref, vec_sent_ref, out_ref,
):
    pieces = (here_ref, core_ref, high_ref, cross_ref)
    lefts = jnp.concatenate([ref[:, :768] for ref in pieces], axis=0)
    for at in range(0, 768, 384):
        rights = jnp.concatenate([ref[:, 768 + at : 1152 + at] for ref in pieces], axis=0)
        out_ref[:, at : at + 384] = lax.dot_general(
            lefts, rights, trans_left, preferred_element_type=jnp.float32
        ).astype(jnp.bfloat16)
    first = lax.axis_index("core") == 0
    both = jnp.concatenate([both_ref[...], sent_ref[...]], axis=0)
    product = lax.dot_general(
        both[:, :768],
        jnp.where(first, both[:, 768:1024], both[:, 896:]),
        trans_left,
        preferred_element_type=jnp.float32,
    )
    out_ref[:, 896:] = product[:, 128:].astype(jnp.bfloat16)
    vec = vec_ref[...] + vec_sent_ref[...]
    lines = [vec[:, 128 * row : 128 * (row + 1)] for row in range(36)]
    lines = jnp.concatenate(lines + [jnp.zeros((12, 128), jnp.float32)], axis=0)
    for plane in range(16):
        rows = slice(48 * plane, 48 * plane + 48)
        out_ref[rows, 768:896] = jnp.where(first, product[rows, :128], lines).astype(jnp.bfloat16)


def ffn_kernel(wait, flush, hidden_ref, down_ref, out_ref):
    out_ref[...] = jnp.dot(
        hidden_ref[...], down_ref[...], preferred_element_type=jnp.float32
    ).astype(jnp.bfloat16)


def dnormed_kernel(
    wait, flush, got_ref, tokens_ref, q_ref, k_ref, v_ref,
    grads_ref, norm_ref, vec_ref, dn_ref,
):
    wide = lane_ids(HALF, 128) < HALF
    for pair in range(3):
        columns = slice(pair * 128, (pair + 1) * 128)
        key_columns = slice(384 + pair * 128, 512 + pair * 128)
        value_columns = slice(768 + pair * 128, 896 + pair * 128)
        for half in range(2):
            rows = slice(half * HALF, (half + 1) * HALF)
            at = 8 * pair + 2 * half
            even = got_ref[at].astype(jnp.float32) + got_ref[at + 1].astype(jnp.float32)
            odd = got_ref[at + 4].astype(jnp.float32) + got_ref[at + 5].astype(jnp.float32)
            grads_ref[rows, key_columns] = jnp.where(wide, even[:HALF], turn(odd[:HALF])).astype(
                jnp.bfloat16
            )
            grads_ref[rows, value_columns] = jnp.where(
                wide, turn(even[:HALF]), odd[:HALF]
            ).astype(jnp.bfloat16)
            grads_ref[rows, columns] = pairs_low(even[HALF:], odd[HALF:]).astype(jnp.bfloat16)
    for ref in (q_ref, k_ref, v_ref):
        wait(ref)
    dnormed = (
        lax.dot_general(
            grads_ref[:, :384], q_ref[...], trans_right, preferred_element_type=jnp.float32
        )
        + lax.dot_general(
            grads_ref[:, 384:768], k_ref[...], trans_right, preferred_element_type=jnp.float32
        )
        + lax.dot_general(
            grads_ref[:, 768:], v_ref[...], trans_right, preferred_element_type=jnp.float32
        )
    )
    dn_ref[...] = dnormed.astype(jnp.bfloat16)
    _, unit, _ = norm_forward(tokens_ref[...].astype(jnp.float32), 1.0, 0.0)
    total = jnp.sum(grads_ref[...].astype(jnp.float32), axis=0, keepdims=True)
    vec_ref[:, :768] = jnp.sum(dnormed, axis=0, keepdims=True)
    vec_ref[:, 768:1536] = jnp.sum(dnormed * unit, axis=0, keepdims=True)
    vec_ref[:, 1536:1920] = total[:, :384]
    vec_ref[:, 1920:2304] = total[:, 768:]
    norm_ref[...] = vec_ref[:, :1536]


def input_grad_kernel(
    wait, flush, dn_ref, other_ref, tokens_ref, cot_ref, exit_ref, gain_ref, dmid_ref, out_ref
):
    _, unit, inverse = norm_forward(tokens_ref[...].astype(jnp.float32), 1.0, 0.0)
    dnormed = dn_ref[...].astype(jnp.float32) + other_ref[...].astype(jnp.float32)
    active = column((exit_ref[...] > LAYER).astype(jnp.float32))
    out_ref[...] = (
        dmid_ref[...]
        + norm_backward(dnormed, unit, inverse, gain_ref[...])
        + jnp.where(active > 0.0, 0.0, cot_ref[...].astype(jnp.float32))
    )


def output_kernel(
    wait, flush, ffn_ref, other_ref, mid_ref, tokens_ref, exit_ref, bias_ref, out_ref
):
    active = column((exit_ref[...] > LAYER).astype(jnp.float32))
    branch = ffn_ref[...].astype(jnp.float32) + other_ref[...].astype(jnp.float32) + bias_ref[...]
    out_ref[...] = jnp.where(
        active > 0.0, mid_ref[...] + branch, tokens_ref[...].astype(jnp.float32)
    ).astype(jnp.bfloat16)


def merge_kernel(wait, flush, kept_ref, taken_ref, dq_ref, edge_ref, out_ref):
    high = lax.axis_index("zh")
    for block in range(BLOCKS):
        pair = kept_ref[block].astype(jnp.float32) + taken_ref[block].astype(jnp.float32)
        query = dq_ref[block]
        if block == BLOCKS - 1:
            pair = pair + edge_ref[:HALF].astype(jnp.float32)
            query = (query.astype(jnp.float32) + edge_ref[HALF:].astype(jnp.float32)).astype(
                jnp.bfloat16
            )
        out_ref[pl.ds(2 * block + high, 1), :HALF] = pair.astype(jnp.bfloat16)[None]
        out_ref[pl.ds(2 * block + high, 1), HALF:] = query[None]
        pair = kept_ref[BLOCKS + block].astype(jnp.float32) + taken_ref[BLOCKS + block].astype(
            jnp.float32
        )
        out_ref[pl.ds(2 * block + 1 - high, 1), :HALF] = pair.astype(jnp.bfloat16)[None]
        out_ref[pl.ds(2 * block + 1 - high, 1), HALF:] = jnp.zeros((1, 32, 128), jnp.bfloat16)


def qkv_products_kernel(
    wait, flush, keep_ref, sent_ref, grads_ref, grads_sent_ref,
    vec_ref, vec_sent_ref, wa_ref, cross_ref, out_ref,
    product_ref,
):
    lefts = jnp.concatenate([keep_ref[...], sent_ref[...]], axis=0)
    for at in range(0, 1152, 384):
        columns = slice(at, at + 384)
        rights = jnp.concatenate([grads_ref[:, columns], grads_sent_ref[:, columns]], axis=0)
        product_ref[:, columns] = lax.dot_general(
            lefts, rights, trans_left, preferred_element_type=jnp.float32
        )
    vec = vec_ref[...] + vec_sent_ref[...]
    norms = vec[:, :1536] + (wa_ref[...] + cross_ref[...])
    vec = jnp.concatenate([norms, vec[:, 1536:]], axis=1)
    lines = [vec[:, 128 * row : 128 * (row + 1)] for row in range(18)]
    lines = jnp.concatenate(lines + [jnp.zeros((2, 128), jnp.float32)], axis=0)
    for pair in range(16):
        block = product_ref[24 * pair : 24 * pair + 24]
        for half in range(2):
            rows = slice(12 * half, 12 * half + 12)
            tiles = [block[rows, 128 * tile : 128 * tile + 128] for tile in range(9)]
            out_ref[2 * pair + half] = jnp.concatenate(tiles + [lines], axis=0).astype(jnp.bfloat16)


def finish_kernel(
    wait, flush, got_ref, q_ref, k_ref, v_ref, shift_out, gain_out, q_bias_out, v_bias_out
):
    total = got_ref[0].astype(jnp.float32)
    for source in range(1, 32):
        total = total + got_ref[source].astype(jnp.float32)
    for at, ref in enumerate((q_ref, k_ref, v_ref)):
        for tile in range(3):
            row = 36 * at + 12 * tile
            ref[:, 128 * tile : 128 * tile + 128] = total[row : row + 12]
    row = 108
    for ref in (shift_out, gain_out, q_bias_out, v_bias_out):
        for tile in range(ref.shape[1] // 128):
            ref[:, 128 * tile : 128 * tile + 128] = total[row : row + 1]
            row += 1


def ffn_sums_kernel(wait, flush, got_ref, core_ref, high_ref, cross_ref, here_ref):
    total = got_ref[0].astype(jnp.float32)
    for source in range(1, 16):
        total = total + got_ref[source].astype(jnp.float32)
    me = 2 * lax.axis_index("zh") + lax.axis_index("core")
    parts = [total[12 * index : 12 * index + 12, :1024] for index in range(4)]
    vec = jnp.concatenate([total[row : row + 1, 768:896] for row in range(36)], axis=1)
    vec = jnp.concatenate([vec, jnp.zeros((1, 512), jnp.float32)], axis=1)
    lines = [vec[:, 1024 * row : 1024 * (row + 1)] for row in range(5)]
    lines = jnp.concatenate(lines + [jnp.zeros((3, 1024), jnp.float32)], axis=0)

    def part(offset):
        value = parts[offset]
        for index in range(1, 4):
            value = jnp.where(me == index, parts[index ^ offset], value)
        return value

    for ref, offset in ((here_ref, 0), (core_ref, 1), (high_ref, 2), (cross_ref, 3)):
        ref[...] = jnp.concatenate(
            [part(offset), jnp.zeros((4, 1024), jnp.float32), lines, jnp.zeros((8, 1024), jnp.float32)],
            axis=0,
        ).astype(ref.dtype)


def ffn_finish_kernel(
    wait, flush, here_ref, core_ref, high_ref, cross_ref,
    up_ref, down_ref, o_ref, up_bias_out, down_bias_out, gain_out, shift_out, o_bias_out,
):
    first = lax.axis_index("core") == 0
    low = lax.axis_index("zh") == 0
    alls = [ref[...].astype(jnp.float32) for ref in (here_ref, core_ref, high_ref, cross_ref)]
    here, core, high, cross = [value[:12, :768] for value in alls]
    up_ref[:, :768] = jnp.where(first, jnp.where(low, here, high), jnp.where(low, core, cross))
    up_ref[:, 768:] = jnp.where(first, jnp.where(low, high, here), jnp.where(low, cross, core))
    down_ref[:, :768] = jnp.where(first, jnp.where(low, core, cross), jnp.where(low, here, high))
    down_ref[:, 768:] = jnp.where(first, jnp.where(low, cross, core), jnp.where(low, high, here))
    mine = alls[0][:, 768:] + alls[2][:, 768:]
    other = alls[1][:, 768:] + alls[3][:, 768:]
    o_ref[:, :256] = jnp.where(first, mine, other)[:12]
    o_ref[:, 256:] = jnp.where(first, other[:, 128:], mine[:, 128:])[:12]
    vec = jnp.where(first, alls[1][16:24] + alls[3][16:24], alls[0][16:24] + alls[2][16:24])
    vec = jnp.concatenate([vec[row : row + 1] for row in range(5)], axis=1)
    begin = 0
    for ref in (up_bias_out, down_bias_out, gain_out, shift_out, o_bias_out):
        ref[...] = vec[:, begin : begin + ref.shape[1]]
        begin += ref.shape[1]


def on_device(
    tokens,
    doc_start,
    exit_layer,
    cotangent,
    ln1_gain,
    ln1_shift,
    q_weight,
    q_bias,
    k_weight,
    v_weight,
    v_bias,
    o_weight,
    o_bias,
    ln2_gain,
    ln2_shift,
    up_weight,
    up_bias,
    down_weight,
    down_bias,
):
    f32 = jnp.float32

    def copied(*arrays):
        return [("d", array) for array in arrays]

    payload, low_one = call(
        project_kernel, "project",
        copied(
            tokens, doc_start, ln1_gain, ln1_shift, q_bias, v_bias, q_weight, k_weight, v_weight
        ),
        [("d", whole(16, HALF + 48, 128)), ("d", whole(128, 768))],
        lazy=(6, 7, 8),
    )
    own = lax.all_to_all(payload, PLANE, 0, 0, tiled=True)
    low_one, o_given = lax.optimization_barrier((low_one, o_weight))
    o_other = lax.ppermute(o_given, "wa", SWAP)
    x_send, x_keep = call(
        prepare_kernel, "prepare",
        copied(low_one),
        [("v", whole(128, 384)), ("d", whole(128, 384))],
    )
    own, x_send, o_other = lax.optimization_barrier((own, x_send, o_other))
    pairs = own[:, :HALF]
    one = lax.ppermute(pairs, "core", SWAP)
    edge = lax.ppermute(own[BLOCKS - 1], "y", ((1, 0), (3, 2)))
    two = lax.ppermute(pairs, "zh", SWAP)
    two, edge = lax.optimization_barrier((two, edge))
    three = lax.ppermute(two, "core", SWAP)
    x_sent = lax.ppermute(x_send, "core", SWAP)
    back, kv, q_rows, start_rows, full_rows = attend(own, one, two, three, edge)
    dhidden, vec_down = call(
        dhidden_kernel, "dhidden",
        copied(cotangent, exit_layer, down_weight),
        [("d", whole(128, 1536, dtype=f32)), ("d", whole(1, 768, dtype=f32))],
    )
    got = lax.all_to_all(back, ("x", "y", "wa"), 0, 0, tiled=True)
    dn_two, ffn_core, ffn_high, ffn_cross, ffn_here, middle, hidden, attn_low, vec_up = call(
        middle_kernel, "middle",
        [("v", got)]
        + copied(
            tokens, cotangent, exit_layer, o_bias, ln2_gain, ln2_shift, up_bias, o_weight, o_other,
            up_weight, dhidden,
        ),
        [
            ("v", whole(128, 768)),
            ("v", whole(128, 1536)),
            ("v", whole(128, 1536)),
            ("v", whole(128, 1536)),
            ("v", whole(128, 1536)),
            ("d", whole(128, 768, dtype=f32)),
            ("d", whole(128, 1536)),
            ("d", whole(128, 384)),
            ("d", whole(1, 1536, dtype=f32)),
        ],
        [pltpu.VMEM((128, 384), jnp.bfloat16), pltpu.VMEM((128, 1536), jnp.bfloat16)],
        lazy=(8, 9, 10, 11),
    )
    dn_two_other = lax.ppermute(dn_two, "wa", SWAP)
    ffn_high = lax.ppermute(ffn_high, "zh", SWAP)
    ffn_cross = lax.ppermute(ffn_cross, ("zh", "core"), CROSS)
    ffn_core = lax.ppermute(ffn_core, "core", SWAP)
    ffn = call(ffn_kernel, "ffn", copied(hidden, down_weight), [("v", whole(128, 768))], cost=0)
    dn_two_other, ffn = lax.optimization_barrier((dn_two_other, ffn))
    dh_payload, dattn_attn, dmiddle, vec_two = call(
        dheads_kernel, "dheads",
        [("v", dn_two), ("v", dn_two_other)]
        + copied(middle, cotangent, exit_layer, ln2_gain, attn_low, vec_up, vec_down, o_weight),
        [
            ("d", whole(16, HALF, 128)),
            ("v", whole(128, 1152)),
            ("d", whole(128, 768, dtype=f32)),
            ("v", whole(1, 4608, dtype=f32)),
        ],
        lazy=(9,),
        cost=0,
    )
    dh = lax.all_to_all(dh_payload, PLANE, 0, 0, tiled=True)
    dattn_sent = lax.ppermute(dattn_attn, "core", SWAP)
    vec_two_sent = lax.ppermute(vec_two, "core", SWAP)
    ffn_products = call(
        ffn_products_kernel, "ffn_products",
        [("v", ffn_here), ("v", ffn_core), ("v", ffn_high), ("v", ffn_cross)]
        + [("v", dattn_attn), ("v", dattn_sent), ("v", vec_two), ("v", vec_two_sent)],
        [("d", whole(768, 1024))],
    )
    ffn_blocks = lax.all_to_all(ffn_products.reshape(16, 48, 1024), PLANE, 0, 0, tiled=True)
    ffn_other = lax.ppermute(ffn, "wa", SWAP)
    given, kept, dq, edge_grad = attend_grad(kv, q_rows, start_rows, full_rows, dh)
    given, ffn_other = lax.optimization_barrier((given, ffn_other))
    edge_got = lax.ppermute(edge_grad, "y", ((0, 1), (2, 3)))
    taken = lax.ppermute(given, "core", SWAP)
    merged = call(
        merge_kernel, "merge",
        [("v", kept), ("v", taken), ("v", dq), ("v", edge_got)],
        [("d", whole(2 * BLOCKS, 96, 128))],
    )
    merged, ffn_blocks = lax.optimization_barrier((merged, ffn_blocks))
    grads = lax.all_to_all(merged, CHIPS, 0, 0, tiled=True)
    ffn_core, ffn_high, ffn_cross, ffn_here = call(
        ffn_sums_kernel, "ffn_sums", copied(ffn_blocks),
        [("v", whole(32, 1024)) for _ in range(3)] + [("v", whole(32, 1024, dtype=f32))],
        cost=0,
    )
    ffn_core = lax.ppermute(ffn_core, "core", SWAP)
    ffn_high = lax.ppermute(ffn_high, "zh", SWAP)
    ffn_cross = lax.ppermute(ffn_cross, ("zh", "core"), CROSS)
    grads, ffn_core, ffn_high, ffn_cross, x_sent = lax.optimization_barrier(
        (grads, ffn_core, ffn_high, ffn_cross, x_sent)
    )
    grads_rows, norms, vec, dn_one = call(
        dnormed_kernel, "dnormed",
        [("v", grads)] + copied(tokens, q_weight, k_weight, v_weight),
        [
            ("v", whole(128, 1152)),
            ("v", whole(1, 1536, dtype=f32)),
            ("v", whole(1, 2304, dtype=f32)),
            ("v", whole(128, 768)),
        ],
        lazy=(2, 3, 4),
        cost=0,
    )
    grads_sent = lax.ppermute(grads_rows, "core", SWAP)
    vec_sent = lax.ppermute(vec, "core", SWAP)
    norms_wa = lax.ppermute(norms, "wa", SWAP)
    norms_cross = lax.ppermute(norms, ("core", "wa"), CROSS)
    norms_wa, norms_cross, dn_one = lax.optimization_barrier((norms_wa, norms_cross, dn_one))
    dn_one_other = lax.ppermute(dn_one, "wa", SWAP)
    products = call(
        qkv_products_kernel, "qkv_products",
        copied(x_keep, x_sent)
        + [("v", grads_rows), ("v", grads_sent), ("v", vec), ("v", vec_sent)]
        + [("v", norms_wa), ("v", norms_cross)],
        [("d", whole(32, 128, 128))],
        [pltpu.VMEM((384, 1152), f32)],
        cost=0,
    )
    products = lax.all_to_all(products, CHIPS, 0, 0, tiled=True)
    output = call(
        output_kernel, "output",
        [("v", ffn), ("v", ffn_other)] + copied(middle, tokens, exit_layer, down_bias),
        [("d", whole(128, 768))],
        cost=0,
    )
    (
        up_weight_grad, down_weight_grad_t, o_weight_grad_t,
        up_bias_grad, down_bias_grad, ln2_gain_grad, ln2_shift_grad, o_bias_grad,
    ) = call(
        ffn_finish_kernel, "ffn_finish",
        [("v", ffn_here), ("v", ffn_core), ("v", ffn_high), ("v", ffn_cross)],
        [("d", whole(12, 1536, dtype=f32)) for _ in range(2)]
        + [("d", whole(12, 384, dtype=f32))]
        + [("d", whole(count, dtype=f32)) for count in (1536, 768, 768, 768, 768)],
        cost=0,
    )
    input_grad = call(
        input_grad_kernel, "input_grad",
        [("v", dn_one), ("v", dn_one_other)]
        + copied(tokens, cotangent, exit_layer, ln1_gain, dmiddle),
        [("d", whole(128, 768, dtype=f32))],
        cost=0,
    )
    (
        products, output, input_grad, up_weight_grad, down_weight_grad_t
    ) = lax.optimization_barrier(
        (products, output, input_grad, up_weight_grad, down_weight_grad_t)
    )
    (
        q_weight_grad, k_weight_grad, v_weight_grad,
        ln1_shift_grad, ln1_gain_grad, q_bias_grad, v_bias_grad,
    ) = call(
        finish_kernel, "finish",
        [("v", products)],
        [("d", whole(12, 384, dtype=f32)) for _ in range(3)]
        + [("d", whole(count, dtype=f32)) for count in (768, 768, 384, 384)],
    )
    return (
        output,
        input_grad,
        ln1_gain_grad,
        ln1_shift_grad,
        q_weight_grad,
        q_bias_grad,
        k_weight_grad,
        v_weight_grad,
        v_bias_grad,
        o_weight_grad_t,
        o_bias_grad,
        ln2_gain_grad,
        ln2_shift_grad,
        up_weight_grad,
        up_bias_grad,
        down_weight_grad_t,
        down_bias_grad,
    )


def solution(mesh):
    fine = Mesh(mesh.devices.reshape(4, 4, 2, 2, 2), CTX + ("wa",))
    return jax.shard_map(
        on_device,
        mesh=fine,
        in_specs=(
            P(CTX, None),
            P(CTX),
            P(CTX),
            P(CTX, None),
            P(),
            P(),
            P(None, "wa"),
            P("wa"),
            P(None, "wa"),
            P(None, "wa"),
            P("wa"),
            P("wa", None),
            P(),
            P(),
            P(),
            P(None, "wa"),
            P("wa"),
            P("wa", None),
            P(),
        ),
        out_specs=(
            P(CTX, None),
            P(CTX, None),
            P(),
            P(),
            P(CTX, "wa"),
            P("wa"),
            P(CTX, "wa"),
            P(CTX, "wa"),
            P("wa"),
            P(CTX, "wa"),
            P(),
            P(),
            P(),
            P(CTX, "wa"),
            P("wa"),
            P(CTX, "wa"),
            P(),
        ),
        check_vma=False,
    )
```

```python
import math

import jax
import jax.numpy as jnp
from jax import lax
from jax.experimental import pallas as pl
from jax.experimental.pallas import tpu as pltpu
from jax.sharding import Mesh, PartitionSpec as P

HEAD_DIM = 64
LAYER = 6
CTX = ("x", "y", "zh", "core")
CHIPS = ("x", "y", "zh")
PLANE = ("x", "y")
EDGE = ("y", "zh", "core")
SWAP = ((0, 1), (1, 0))
CROSS = ((0, 3), (1, 2), (2, 1), (3, 0))
HALF = 64
BLOCKS = 16
GROUP = 256
STREAM = 8192
ROWS = (BLOCKS + 1) * HALF
FF_TILE = 768
FAR = 1e9
SCALING = 1.0 / math.sqrt(HEAD_DIM)
EXP2_SCALE = SCALING / math.log(2.0)
VMEM_BYTES = 64 * 2**20


epsilon = 1e-05
trans_right = (((1,), (1,)), ((), ()))
trans_left = (((0,), (0,)), ((), ()))
cubic_coef = 0.044715


def gelu_pair(values):
    outer = math.sqrt(2.0 / math.pi)
    inner = outer * (values + cubic_coef * values * values * values)
    tangent = jnp.tanh(inner)
    result = 0.5 * values * (1.0 + tangent)
    gelu_slope = 0.5 * (1.0 + tangent) + 0.5 * values * (1.0 - tangent * tangent) * outer * (
        1.0 + 3.0 * cubic_coef * values * values
    )
    return (result, gelu_slope)


def norm_forward(values, gain_vec, shift_vec):
    average = jnp.mean(values, axis=-1, keepdims=True)
    centred = values - average
    inverse_std = lax.rsqrt(jnp.mean(centred * centred, axis=-1, keepdims=True) + epsilon)
    normed = centred * inverse_std
    return (normed * gain_vec + shift_vec, normed, inverse_std)


def norm_backward(grad_out, normed, inverse_std, gain_vec):
    scaled = grad_out * gain_vec
    return inverse_std * (
        scaled
        - jnp.mean(scaled, axis=-1, keepdims=True)
        - normed * jnp.mean(scaled * normed, axis=-1, keepdims=True)
    )


def swap_add(part, axis):
    other = lax.ppermute(part, axis, SWAP)
    return part.astype(jnp.float32) + other.astype(jnp.float32)


def whole(*shape, dtype=jnp.bfloat16):
    return jax.ShapeDtypeStruct(shape, dtype)


def head_place():
    upper = lax.axis_index("y") % 2
    sub = 2 * lax.axis_index("zh") + lax.axis_index("core")
    last = sub == 3
    return (
        upper,
        jnp.where(upper == 1, 3 - sub, sub),
        jnp.where((upper == 0) & last, 1, 0),
        jnp.where((upper == 1) & last, 1, 0),
    )


def call(kernel, name, ins, outs, scratch=(), lazy=(), cost=2):
    copied_in = [at for at, (mode, _) in enumerate(ins) if mode == "d"]
    copied_out = [at for at, (mode, _) in enumerate(outs) if mode == "d"]

    def buffer(array):
        shape = array.shape if len(array.shape) > 1 else (1,) + tuple(array.shape)
        return pltpu.VMEM(shape, array.dtype)

    def body(*refs):
        given, rest = list(refs[: len(ins)]), refs[len(ins) :]
        results, rest = list(rest[: len(outs)]), rest[len(outs) :]
        in_buffers, rest = rest[: len(copied_in)], rest[len(copied_in) :]
        out_buffers, rest = rest[: len(copied_out)], rest[len(copied_out) :]
        in_sems, out_sems, rest = rest[0], rest[1], rest[2:]
        pending, flushing = [], []
        for slot, at in enumerate(copied_in):
            there = in_buffers[slot]
            into = there if len(ins[at][1].shape) > 1 else there.at[0]
            copy = pltpu.make_async_copy(given[at], into, in_sems.at[slot])
            copy.start()
            given[at] = there
            pending.append((there, at, copy))
        targets, extra, begun = [], [], []
        for slot, at in enumerate(copied_out):
            made = out_buffers[slot] if len(outs[at][1].shape) > 1 else out_buffers[slot].at[0]
            targets.append((out_buffers[slot], made, results[at], out_sems.at[slot]))
            results[at] = out_buffers[slot]

        def wait(ref):
            for entry in list(pending):
                if entry[0] is ref:
                    entry[2].wait()
                    pending[:] = [other for other in pending if other is not entry]

        def flush(ref, begin=None, end=None):
            for buffer_ref, made, there, sem in targets:
                if buffer_ref is not ref:
                    continue
                if begin is not None:
                    sem = out_sems.at[len(copied_out) + len(extra)]
                    extra.append(sem)
                    made, there = made.at[begin:end], there.at[begin:end]
                copy = pltpu.make_async_copy(made, there, sem)
                copy.start()
                flushing.append(copy)
                begun.append(ref)

        for entry in list(pending):
            if entry[1] not in lazy:
                wait(entry[0])
        kernel(wait, flush, *given, *results, *rest)
        for entry in list(pending):
            wait(entry[0])
        for entry in targets:
            if not any(ref is entry[0] for ref in begun):
                flush(entry[0])
        for copy in flushing:
            copy.wait()

    vmem, anywhere = pl.BlockSpec(memory_space=pltpu.VMEM), pl.BlockSpec(memory_space=pltpu.HBM)
    result = pl.pallas_call(
        body,
        out_shape=tuple(out for _, out in outs),
        in_specs=[anywhere if mode == "d" else vmem for mode, _ in ins],
        out_specs=tuple(anywhere if mode == "d" else vmem for mode, _ in outs),
        scratch_shapes=[buffer(ins[at][1]) for at in copied_in]
        + [buffer(outs[at][1]) for at in copied_out]
        + [
            pltpu.SemaphoreType.DMA((max(1, len(copied_in)),)),
            pltpu.SemaphoreType.DMA((len(copied_out) + 4,)),
        ]
        + list(scratch),
        compiler_params=pltpu.CompilerParams(vmem_limit_bytes=VMEM_BYTES),
        cost_estimate=pl.CostEstimate(
            flops=cost * 10**9, transcendentals=0, bytes_accessed=0
        ),
        name=name,
    )(*[array for _, array in ins])
    return result[0] if len(outs) == 1 else result


def lane_ids(rows, cols):
    return lax.broadcasted_iota(jnp.int32, (rows, cols), 1)


def row_ids_of(rows, cols):
    return lax.broadcasted_iota(jnp.int32, (rows, cols), 0)


def turn(values):
    return pltpu.roll(values, HALF, 1)


def unpack_low(packed):
    wide = packed.astype(jnp.float32)
    left = lane_ids(32, 128) < HALF
    both = jnp.concatenate([wide, turn(wide)], axis=0)
    return jnp.where(jnp.concatenate([left, left], axis=0), both, 0.0)


def unpack_high(packed):
    wide = packed.astype(jnp.float32)
    right = lane_ids(32, 128) >= HALF
    both = jnp.concatenate([turn(wide), wide], axis=0)
    return jnp.where(jnp.concatenate([right, right], axis=0), both, 0.0)


def pack_from_low(block):
    return jnp.where(lane_ids(32, 128) < HALF, block[:32], turn(block[32:]))


def pack_from_high(block):
    return jnp.where(lane_ids(32, 128) < HALF, turn(block[:32]), block[32:])


def key_places(scal, group):
    lane = lane_ids(8, GROUP)
    sub = (lane >> 6) ^ scal[1]
    return (scal[0] * (STREAM // 2) + GROUP * group + (sub << 6) + (lane & 63)).astype(
        jnp.float32
    )


def edge_places():
    return (STREAM // 2 + lane_ids(8, 128)).astype(jnp.float32)


def query_places(scal, block):
    row = row_ids_of(HALF, 128)
    return (
        scal[0] * (STREAM // 2) + GROUP * block + (scal[1] << 6) + row
    ).astype(jnp.float32)


def spread(rows, width):
    return jnp.concatenate([rows] * (width // 128), axis=1) if width > 128 else rows


def weights_of(scal, queries, starts, keys, places, group):
    scores = lax.dot_general(queries, keys, trans_right, preferred_element_type=jnp.float32)
    count = queries.shape[0]
    own = spread(query_places(scal, group), GROUP)
    limit = jnp.concatenate([own, jnp.full((count - HALF, GROUP), FAR, jnp.float32)], axis=0)
    seen = (spread(starts, GROUP) <= places[:1]) & (places[:1] <= limit)
    return jnp.where(seen, jnp.exp2(scores * EXP2_SCALE), 0.0)


def edge_weights(queries, starts, keys):
    scores = lax.dot_general(queries, keys, trans_right, preferred_element_type=jnp.float32)
    places = edge_places()[:1]
    limit = (STREAM // 2 + row_ids_of(HALF, 128)).astype(jnp.float32)
    return jnp.where(
        (starts <= places) & (places <= limit), jnp.exp2(scores * EXP2_SCALE), 0.0
    )


def attend_kernel(
    wait, flush, own_ref, one_ref, two_ref, three_ref, edge_ref,
    back_ref, kv_ref, q_ref, start_ref, full_ref,
    num_ref, den_ref,
):
    scal = head_place()
    upper = scal[0]
    diag = jnp.where(
        lane_ids(HALF, 128) == row_ids_of(HALF, 128),
        64.0,
        jnp.where(lane_ids(HALF, 128) == row_ids_of(HALF, 128) + HALF, 1.0, 0.0),
    )

    def starts(line, off):
        found = jnp.sum(line.astype(jnp.float32) * diag, axis=1, keepdims=True)
        return jnp.broadcast_to(jnp.where(off, FAR, found), (HALF, 128))

    for block in range(BLOCKS):
        place = jnp.where(upper == 1, BLOCKS - 1 - block, block)
        rows = slice(block * HALF, (block + 1) * HALF)
        mine = own_ref[pl.ds(place, 1)][0]
        kv_ref[block, 0:HALF] = mine[:HALF]
        kv_ref[block, HALF : 2 * HALF] = one_ref[pl.ds(place, 1)][0]
        kv_ref[block, 2 * HALF : 3 * HALF] = two_ref[pl.ds(place, 1)][0]
        kv_ref[block, 3 * HALF :] = three_ref[pl.ds(place, 1)][0]
        q_ref[rows] = unpack_low(mine[HALF : HALF + 32]).astype(jnp.bfloat16)
        off = (scal[3] == 1) if block == 0 else False
        start_ref[rows] = starts(mine[HALF + 32 : HALF + 33], off)
    kv_ref[BLOCKS] = jnp.zeros((GROUP, 128), jnp.bfloat16)
    kv_ref[BLOCKS, :HALF] = edge_ref[:HALF]
    q_ref[BLOCKS * HALF :] = unpack_low(edge_ref[HALF : HALF + 32]).astype(jnp.bfloat16)
    start_ref[BLOCKS * HALF :] = starts(edge_ref[HALF + 32 : HALF + 33], scal[2] == 0)
    flush(kv_ref)
    flush(q_ref)
    flush(start_ref)

    for group in range(BLOCKS + 1):
        rows = slice(group * HALF, ROWS)
        if group < BLOCKS:
            keys = kv_ref[group]
            weights = weights_of(
                scal, q_ref[rows], start_ref[rows], keys, key_places(scal, group), group
            )
            total = weights[:, :128] + weights[:, 128:]
        else:
            keys = kv_ref[group, :128]
            weights = total = edge_weights(q_ref[rows], start_ref[rows], keys)
        product = jnp.dot(weights.astype(jnp.bfloat16), keys, preferred_element_type=jnp.float32)
        if group == 0:
            num_ref[rows] = product
            den_ref[rows] = total
        else:
            num_ref[rows] += product
            den_ref[rows] += total

    for block in range(BLOCKS + 1):
        rows = slice(block * HALF, (block + 1) * HALF)
        den = jnp.sum(den_ref[rows], axis=1, keepdims=True)
        recip = jnp.broadcast_to(1.0 / jnp.where(den == 0.0, 1.0, den), (HALF, 128))
        full = num_ref[rows] * recip
        full_ref[rows] = jnp.where(lane_ids(HALF, 128) < HALF, recip, full)
    flush(full_ref)
    for place in range(BLOCKS):
        block = jnp.where(upper == 1, BLOCKS - 1 - place, place)
        rows = pl.ds(pl.multiple_of(block * HALF, HALF), HALF)
        packed = pack_from_high(full_ref[rows]).astype(jnp.bfloat16)
        if place < BLOCKS - 1:
            edge = jnp.zeros((32, 128), jnp.bfloat16)
        else:
            edge = pack_from_high(full_ref[BLOCKS * HALF :]).astype(jnp.bfloat16)
        for copy in range(2):
            back_ref[2 * place + copy, :32] = packed
            back_ref[2 * place + copy, 32:] = edge
        if place == BLOCKS // 2 - 1:
            flush(back_ref, 0, BLOCKS)
    flush(back_ref, BLOCKS, 2 * BLOCKS)


def attend_grad_kernel(
    wait, flush, kv_ref, q_ref, start_ref, full_ref, dh_in_ref,
    send_ref, keep_ref, dq_ref, edge_ref,
    dhn_ref, dot_ref, dq_acc,
):
    scal = head_place()
    upper = scal[0]
    left = lane_ids(HALF, 128) < HALF
    wait(full_ref)
    for block in range(BLOCKS + 1):
        rows = slice(block * HALF, (block + 1) * HALF)
        if block < BLOCKS:
            place = jnp.where(upper == 1, BLOCKS - 1 - block, block)
            packed = dh_in_ref[pl.ds(place, 1), :32][0]
        else:
            packed = dh_in_ref[BLOCKS - 1, 32:]
        full = full_ref[rows]
        scaled = unpack_high(packed) * jnp.where(left, full, turn(full))
        scaled = scaled.astype(jnp.bfloat16).astype(jnp.float32)
        dhn_ref[rows] = scaled.astype(jnp.bfloat16)
        dot_ref[rows] = jnp.broadcast_to(
            jnp.sum(jnp.where(left, 0.0, scaled * full), axis=1, keepdims=True), (HALF, 128)
        )
    wait(kv_ref)
    wait(q_ref)
    wait(start_ref)
    for group in range(BLOCKS + 1):
        rows = slice(group * HALF, ROWS)
        if group < BLOCKS:
            keys = kv_ref[group]
            weights = weights_of(
                scal, q_ref[rows], start_ref[rows], keys, key_places(scal, group), group
            )
        else:
            keys = kv_ref[group, :128]
            weights = edge_weights(q_ref[rows], start_ref[rows], keys)
        dprob = lax.dot_general(
            dhn_ref[rows], keys, trans_right, preferred_element_type=jnp.float32
        )
        dscore = (weights * (dprob - spread(dot_ref[rows], keys.shape[0]))).astype(jnp.bfloat16)
        dquery = jnp.dot(dscore, keys, preferred_element_type=jnp.float32)
        if group == 0:
            dq_acc[rows] = dquery
        else:
            dq_acc[rows] += dquery
        grads = lax.dot_general(
            dscore, q_ref[rows], trans_left, preferred_element_type=jnp.float32
        ) * SCALING + lax.dot_general(
            weights.astype(jnp.bfloat16),
            dhn_ref[rows],
            trans_left,
            preferred_element_type=jnp.float32,
        )
        low = grads.astype(jnp.bfloat16)
        if group < BLOCKS:
            place = jnp.where(upper == 1, BLOCKS - 1 - group, group)
            for quarter in range(4):
                out = send_ref if quarter % 2 else keep_ref
                out[pl.ds(quarter // 2 * BLOCKS + place, 1)] = low[
                    None, quarter * HALF : (quarter + 1) * HALF
                ]
        else:
            edge_ref[:HALF] = low[:HALF]

    for block in range(BLOCKS + 1):
        rows = slice(block * HALF, (block + 1) * HALF)
        packed = pack_from_low(dq_acc[rows] * SCALING).astype(jnp.bfloat16)
        if block < BLOCKS:
            place = jnp.where(upper == 1, BLOCKS - 1 - block, block)
            dq_ref[pl.ds(place, 1)] = packed[None]
        else:
            edge_ref[HALF:] = packed


def attend(own, one, two, three, edge):
    f32 = jnp.float32
    return call(
        attend_kernel, "attend",
        [("v", own), ("v", one), ("v", two), ("v", three), ("v", edge)],
        [
            ("d", whole(2 * BLOCKS, HALF, 128)),
            ("d", whole(BLOCKS + 1, GROUP, 128)),
            ("d", whole(ROWS, 128)),
            ("d", whole(ROWS, 128, dtype=f32)),
            ("d", whole(ROWS, 128, dtype=f32)),
        ],
        [pltpu.VMEM((ROWS, 128), f32), pltpu.VMEM((ROWS, 128), f32)],
        cost=3,
    )


def attend_grad(kv, q, start, full, dh):
    f32 = jnp.float32
    return call(
        attend_grad_kernel, "attend_grad",
        [("d", kv), ("d", q), ("d", start), ("d", full), ("v", dh)],
        [
            ("v", whole(2 * BLOCKS, HALF, 128)),
            ("v", whole(2 * BLOCKS, HALF, 128)),
            ("v", whole(BLOCKS, 32, 128)),
            ("v", whole(96, 128)),
        ],
        [
            pltpu.VMEM((ROWS, 128), jnp.bfloat16),
            pltpu.VMEM((ROWS, 128), f32),
            pltpu.VMEM((ROWS, 128), f32),
        ],
        lazy=(0, 1, 2, 3),
        cost=40,
    )


def column(line):
    return jnp.sum(
        jnp.where(lane_ids(128, 128) == row_ids_of(128, 128), line, 0.0), axis=1, keepdims=True
    )


def pairs_low(even, odd):
    left = lane_ids(32, 128) < HALF
    return jnp.concatenate(
        [jnp.where(left, even, turn(odd)), jnp.where(left, turn(even), odd)], axis=0
    )


def project_kernel(
    wait, flush,
    tokens_ref, start_ref, gain_ref, shift_ref, q_bias_ref, v_bias_ref, q_ref, k_ref, v_ref,
    pay_ref, low_ref,
):
    normed, _, _ = norm_forward(tokens_ref[...].astype(jnp.float32), gain_ref[...], shift_ref[...])
    low = normed.astype(jnp.bfloat16)
    low_ref[...] = low
    flush(low_ref)
    starts = start_ref[...]
    high_part = (starts >> 6).astype(jnp.float32)
    low_part = (starts & 63).astype(jnp.float32)
    left = lane_ids(1, 128) < HALF
    lines = (
        jnp.where(left, high_part, turn(low_part)),
        jnp.where(left, turn(high_part), low_part),
    )
    lines = [jnp.broadcast_to(line, (16, 128)).astype(jnp.bfloat16) for line in lines]
    wide = lane_ids(HALF, 128) < HALF
    for ref in (q_ref, k_ref, v_ref):
        wait(ref)
    pay_ref[12:] = jnp.zeros((4, HALF + 48, 128), jnp.bfloat16)
    flush(pay_ref, 12, 16)
    all_queries = jnp.dot(low, q_ref[...], preferred_element_type=jnp.float32) + q_bias_ref[...]
    all_keys = jnp.dot(low, k_ref[...], preferred_element_type=jnp.float32)
    all_values = jnp.dot(low, v_ref[...], preferred_element_type=jnp.float32) + v_bias_ref[...]
    for pair in range(3):
        columns = slice(pair * 128, (pair + 1) * 128)
        queries, keyset, values = all_queries[:, columns], all_keys[:, columns], all_values[:, columns]
        for half in range(2):
            rows = slice(half * HALF, (half + 1) * HALF)
            for odd in range(2):
                if odd:
                    both = jnp.where(wide, turn(keyset[rows]), values[rows])
                    packed = pack_from_high(queries[rows])
                else:
                    both = jnp.where(wide, keyset[rows], turn(values[rows]))
                    packed = pack_from_low(queries[rows])
                index = 4 * pair + 2 * odd + half
                pay_ref[index, :HALF] = both.astype(jnp.bfloat16)
                pay_ref[index, HALF : HALF + 32] = packed.astype(jnp.bfloat16)
                pay_ref[index, HALF + 32 :] = lines[half]
        flush(pay_ref, 4 * pair, 4 * pair + 4)


def prepare_kernel(wait, flush, low_ref, send_ref, keep_ref):
    lane = lane_ids(8, 768)
    core = (lane >= 384).astype(jnp.int32)
    within = lane - 384 * core
    chip = (within * 171) >> 11
    source = (24 * chip + 12 * core + (within - 12 * chip))[:1]
    order = jnp.where(row_ids_of(768, 768) == source, 1.0, 0.0).astype(jnp.bfloat16)
    ordered = jnp.dot(low_ref[...], order, preferred_element_type=jnp.float32).astype(jnp.bfloat16)
    first = lax.axis_index("core") == 0
    keep_ref[...] = jnp.where(first, ordered[:, :384], ordered[:, 384:])
    send_ref[...] = jnp.where(first, ordered[:, 384:], ordered[:, :384])


def attn_tile(got_ref, side, pair):
    parts = []
    for half in range(2):
        heads = []
        for odd in range(2):
            index = 4 * pair + 2 * odd
            lower = got_ref[pl.ds(2 * index + side, 1)][0].astype(jnp.float32)
            if half:
                higher = got_ref[pl.ds(2 * index + 2 + side, 1)][0].astype(jnp.float32)
                packed = higher[:32] + lower[32:]
            else:
                packed = lower[:32]
            heads.append(packed)
        parts.append(pairs_low(*heads))
    return jnp.concatenate(parts, axis=0).astype(jnp.bfloat16)


def branch_of(cot_ref, exit_ref):
    active = column((exit_ref[...] > LAYER).astype(jnp.float32))
    return jnp.where(active > 0.0, cot_ref[...].astype(jnp.float32), 0.0)


def dhidden_kernel(wait, flush, cot_ref, exit_ref, down_ref, out_ref, vec_ref):
    branch = branch_of(cot_ref, exit_ref)
    vec_ref[...] = jnp.sum(branch, axis=0, keepdims=True)
    out_ref[...] = lax.dot_general(
        branch.astype(jnp.bfloat16), down_ref[...], trans_right, preferred_element_type=jnp.float32
    )


def middle_kernel(
    wait, flush, got_ref, tokens_ref, cot_ref, exit_ref, o_bias_ref, gain_ref, shift_ref,
    up_bias_ref, o_own_ref, o_other_ref, up_ref, dhidden_ref,
    dn_ref, core_ref, high_ref, cross_ref, here_ref, mid_ref, hidden_ref, attn_ref, vec_ref,
    acc_ref, dpre_ref,
):
    side = lax.axis_index("wa")
    for pair in range(3):
        rows = slice(pair * 128, (pair + 1) * 128)
        attn_ref[:, rows] = attn_tile(got_ref, side, pair)
        acc_ref[:, rows] = attn_tile(got_ref, 1 - side, pair)
    flush(attn_ref)
    wait(o_own_ref)
    wait(o_other_ref)
    total = jnp.dot(
        attn_ref[...], o_own_ref[...], preferred_element_type=jnp.float32
    ) + jnp.dot(acc_ref[...], o_other_ref[...], preferred_element_type=jnp.float32)
    middle = tokens_ref[...].astype(jnp.float32) + (total + o_bias_ref[...])
    mid_ref[...] = middle
    flush(mid_ref)
    normed, _, _ = norm_forward(middle, gain_ref[...], shift_ref[...])
    low = normed.astype(jnp.bfloat16)
    branch_low = branch_of(cot_ref, exit_ref).astype(jnp.bfloat16)
    dnormed = None
    wait(up_ref)
    wait(dhidden_ref)
    for begin in range(0, 1536, FF_TILE):
        columns = slice(begin, begin + FF_TILE)
        pre_act = (
            jnp.dot(low, up_ref[:, columns], preferred_element_type=jnp.float32)
            + up_bias_ref[:, columns]
        )
        hidden_full, slope = gelu_pair(pre_act)
        hidden = hidden_full.astype(jnp.bfloat16)
        hidden_ref[:, columns] = hidden
        dpre = (dhidden_ref[:, columns] * slope).astype(jnp.bfloat16)
        vec_ref[:, columns] = jnp.sum(dpre.astype(jnp.float32), axis=0, keepdims=True)
        dpre_ref[:, columns] = dpre
        dn_term = lax.dot_general(
            dpre, up_ref[:, columns], trans_right, preferred_element_type=jnp.float32
        )
        dnormed = dn_term if dnormed is None else dnormed + dn_term
    dn_ref[...] = dnormed.astype(jnp.bfloat16)
    core, high = lax.axis_index("core"), lax.axis_index("zh")
    for ref, offset in ((core_ref, 1), (high_ref, 2), (cross_ref, 3), (here_ref, 0)):
        up_side = (core ^ (offset & 1)) == 0
        first_half = (high ^ (offset >> 1)) == 0
        ref[:, :768] = jnp.where(up_side, low, branch_low)
        ref[:, 768:] = jnp.where(
            up_side,
            jnp.where(first_half, dpre_ref[:, :768], dpre_ref[:, 768:]),
            jnp.where(first_half, hidden_ref[:, :768], hidden_ref[:, 768:]),
        )


def dheads_kernel(
    wait, flush, dn_ref, other_ref, mid_ref, cot_ref, exit_ref, gain_ref, attn_ref, up_ref, down_ref, o_ref,
    pay_ref, both_ref, dmid_ref, vec_ref,
):
    middle = mid_ref[...]
    _, unit, inverse = norm_forward(middle, gain_ref[...], 0.0)
    dnormed = dn_ref[...].astype(jnp.float32) + other_ref[...].astype(jnp.float32)
    branch = branch_of(cot_ref, exit_ref)
    dmiddle = branch + norm_backward(dnormed, unit, inverse, gain_ref[...])
    dmid_ref[...] = dmiddle
    flush(dmid_ref)
    low = dmiddle.astype(jnp.bfloat16)
    vec_ref[:, :1536] = up_ref[...]
    vec_ref[:, 1536:2304] = down_ref[...]
    vec_ref[:, 2304:3072] = jnp.sum(dnormed * unit, axis=0, keepdims=True)
    vec_ref[:, 3072:3840] = jnp.sum(dnormed, axis=0, keepdims=True)
    vec_ref[:, 3840:] = jnp.sum(low.astype(jnp.float32), axis=0, keepdims=True)
    pay_ref[12:] = jnp.zeros((4, HALF, 128), jnp.bfloat16)
    flush(pay_ref, 12, 16)
    wait(o_ref)
    all_heads = lax.dot_general(low, o_ref[...], trans_right, preferred_element_type=jnp.float32)
    for pair in range(3):
        dheads = all_heads[:, pair * 128 : (pair + 1) * 128]
        for odd in range(2):
            pack = pack_from_high if odd else pack_from_low
            lower = pack(dheads[:HALF]).astype(jnp.bfloat16)
            higher = pack(dheads[HALF:]).astype(jnp.bfloat16)
            index = 4 * pair + 2 * odd
            pay_ref[index, :32] = lower
            pay_ref[index, 32:] = higher
            pay_ref[index + 1, :32] = higher
            pay_ref[index + 1, 32:] = higher
        flush(pay_ref, 4 * pair, 4 * pair + 4)
    both_ref[:, :768] = low
    both_ref[:, 768:] = attn_ref[...]


def ffn_products_kernel(
    wait, flush, here_ref, core_ref, high_ref, cross_ref, both_ref, sent_ref,
    vec_ref, vec_sent_ref, out_ref,
):
    pieces = (here_ref, core_ref, high_ref, cross_ref)
    lefts = jnp.concatenate([ref[:, :768] for ref in pieces], axis=0)
    for at in range(0, 768, 384):
        rights = jnp.concatenate([ref[:, 768 + at : 1152 + at] for ref in pieces], axis=0)
        out_ref[:, at : at + 384] = lax.dot_general(
            lefts, rights, trans_left, preferred_element_type=jnp.float32
        ).astype(jnp.bfloat16)
    first = lax.axis_index("core") == 0
    both = jnp.concatenate([both_ref[...], sent_ref[...]], axis=0)
    product = lax.dot_general(
        both[:, :768],
        jnp.where(first, both[:, 768:1024], both[:, 896:]),
        trans_left,
        preferred_element_type=jnp.float32,
    )
    out_ref[:, 896:] = product[:, 128:].astype(jnp.bfloat16)
    vec = vec_ref[...] + vec_sent_ref[...]
    lines = [vec[:, 128 * row : 128 * (row + 1)] for row in range(36)]
    lines = jnp.concatenate(lines + [jnp.zeros((12, 128), jnp.float32)], axis=0)
    for plane in range(16):
        rows = slice(48 * plane, 48 * plane + 48)
        out_ref[rows, 768:896] = jnp.where(first, product[rows, :128], lines).astype(jnp.bfloat16)


def ffn_kernel(wait, flush, hidden_ref, down_ref, out_ref):
    out_ref[...] = jnp.dot(
        hidden_ref[...], down_ref[...], preferred_element_type=jnp.float32
    ).astype(jnp.bfloat16)


def dnormed_kernel(
    wait, flush, got_ref, tokens_ref, q_ref, k_ref, v_ref,
    grads_ref, norm_ref, vec_ref, dn_ref,
):
    wide = lane_ids(HALF, 128) < HALF
    for pair in range(3):
        columns = slice(pair * 128, (pair + 1) * 128)
        key_columns = slice(384 + pair * 128, 512 + pair * 128)
        value_columns = slice(768 + pair * 128, 896 + pair * 128)
        for half in range(2):
            rows = slice(half * HALF, (half + 1) * HALF)
            at = 8 * pair + 2 * half
            even = got_ref[at].astype(jnp.float32) + got_ref[at + 1].astype(jnp.float32)
            odd = got_ref[at + 4].astype(jnp.float32) + got_ref[at + 5].astype(jnp.float32)
            grads_ref[rows, key_columns] = jnp.where(wide, even[:HALF], turn(odd[:HALF])).astype(
                jnp.bfloat16
            )
            grads_ref[rows, value_columns] = jnp.where(
                wide, turn(even[:HALF]), odd[:HALF]
            ).astype(jnp.bfloat16)
            grads_ref[rows, columns] = pairs_low(even[HALF:], odd[HALF:]).astype(jnp.bfloat16)
    for ref in (q_ref, k_ref, v_ref):
        wait(ref)
    dnormed = (
        lax.dot_general(
            grads_ref[:, :384], q_ref[...], trans_right, preferred_element_type=jnp.float32
        )
        + lax.dot_general(
            grads_ref[:, 384:768], k_ref[...], trans_right, preferred_element_type=jnp.float32
        )
        + lax.dot_general(
            grads_ref[:, 768:], v_ref[...], trans_right, preferred_element_type=jnp.float32
        )
    )
    dn_ref[...] = dnormed.astype(jnp.bfloat16)
    _, unit, _ = norm_forward(tokens_ref[...].astype(jnp.float32), 1.0, 0.0)
    total = jnp.sum(grads_ref[...].astype(jnp.float32), axis=0, keepdims=True)
    vec_ref[:, :768] = jnp.sum(dnormed, axis=0, keepdims=True)
    vec_ref[:, 768:1536] = jnp.sum(dnormed * unit, axis=0, keepdims=True)
    vec_ref[:, 1536:1920] = total[:, :384]
    vec_ref[:, 1920:2304] = total[:, 768:]
    norm_ref[...] = vec_ref[:, :1536]


def input_grad_kernel(
    wait, flush, dn_ref, other_ref, tokens_ref, cot_ref, exit_ref, gain_ref, dmid_ref, out_ref
):
    _, unit, inverse = norm_forward(tokens_ref[...].astype(jnp.float32), 1.0, 0.0)
    dnormed = dn_ref[...].astype(jnp.float32) + other_ref[...].astype(jnp.float32)
    active = column((exit_ref[...] > LAYER).astype(jnp.float32))
    out_ref[...] = (
        dmid_ref[...]
        + norm_backward(dnormed, unit, inverse, gain_ref[...])
        + jnp.where(active > 0.0, 0.0, cot_ref[...].astype(jnp.float32))
    )


def output_kernel(
    wait, flush, ffn_ref, other_ref, mid_ref, tokens_ref, exit_ref, bias_ref, out_ref
):
    active = column((exit_ref[...] > LAYER).astype(jnp.float32))
    branch = ffn_ref[...].astype(jnp.float32) + other_ref[...].astype(jnp.float32) + bias_ref[...]
    out_ref[...] = jnp.where(
        active > 0.0, mid_ref[...] + branch, tokens_ref[...].astype(jnp.float32)
    ).astype(jnp.bfloat16)


def merge_kernel(wait, flush, kept_ref, taken_ref, dq_ref, edge_ref, out_ref):
    high = lax.axis_index("zh")
    for block in range(BLOCKS):
        pair = kept_ref[block].astype(jnp.float32) + taken_ref[block].astype(jnp.float32)
        query = dq_ref[block]
        if block == BLOCKS - 1:
            pair = pair + edge_ref[:HALF].astype(jnp.float32)
            query = (query.astype(jnp.float32) + edge_ref[HALF:].astype(jnp.float32)).astype(
                jnp.bfloat16
            )
        out_ref[pl.ds(2 * block + high, 1), :HALF] = pair.astype(jnp.bfloat16)[None]
        out_ref[pl.ds(2 * block + high, 1), HALF:] = query[None]
        pair = kept_ref[BLOCKS + block].astype(jnp.float32) + taken_ref[BLOCKS + block].astype(
            jnp.float32
        )
        out_ref[pl.ds(2 * block + 1 - high, 1), :HALF] = pair.astype(jnp.bfloat16)[None]
        out_ref[pl.ds(2 * block + 1 - high, 1), HALF:] = jnp.zeros((1, 32, 128), jnp.bfloat16)
        if block % 8 == 7:
            flush(out_ref, 2 * block - 14, 2 * block + 2)


def qkv_products_kernel(
    wait, flush, keep_ref, sent_ref, grads_ref, grads_sent_ref,
    vec_ref, vec_sent_ref, wa_ref, cross_ref, out_ref,
    product_ref,
):
    lefts = jnp.concatenate([keep_ref[...], sent_ref[...]], axis=0)
    for at in range(0, 1152, 384):
        columns = slice(at, at + 384)
        rights = jnp.concatenate([grads_ref[:, columns], grads_sent_ref[:, columns]], axis=0)
        product_ref[:, columns] = lax.dot_general(
            lefts, rights, trans_left, preferred_element_type=jnp.float32
        )
    vec = vec_ref[...] + vec_sent_ref[...]
    norms = vec[:, :1536] + (wa_ref[...] + cross_ref[...])
    vec = jnp.concatenate([norms, vec[:, 1536:]], axis=1)
    lines = [vec[:, 128 * row : 128 * (row + 1)] for row in range(18)]
    lines = jnp.concatenate(lines + [jnp.zeros((2, 128), jnp.float32)], axis=0)
    for pair in range(16):
        block = product_ref[24 * pair : 24 * pair + 24]
        for half in range(2):
            rows = slice(12 * half, 12 * half + 12)
            tiles = [block[rows, 128 * tile : 128 * tile + 128] for tile in range(9)]
            out_ref[2 * pair + half] = jnp.concatenate(tiles + [lines], axis=0).astype(jnp.bfloat16)
        if pair % 8 == 7:
            flush(out_ref, 2 * pair - 14, 2 * pair + 2)


def finish_kernel(
    wait, flush, got_ref, q_ref, k_ref, v_ref, shift_out, gain_out, q_bias_out, v_bias_out
):
    total = got_ref[0].astype(jnp.float32)
    for source in range(1, 32):
        total = total + got_ref[source].astype(jnp.float32)
    for at, ref in enumerate((q_ref, k_ref, v_ref)):
        for tile in range(3):
            row = 36 * at + 12 * tile
            ref[:, 128 * tile : 128 * tile + 128] = total[row : row + 12]
    row = 108
    for ref in (shift_out, gain_out, q_bias_out, v_bias_out):
        for tile in range(ref.shape[1] // 128):
            ref[:, 128 * tile : 128 * tile + 128] = total[row : row + 1]
            row += 1


def ffn_sums_kernel(wait, flush, got_ref, core_ref, high_ref, cross_ref, here_ref):
    total = got_ref[0].astype(jnp.float32)
    for source in range(1, 16):
        total = total + got_ref[source].astype(jnp.float32)
    me = 2 * lax.axis_index("zh") + lax.axis_index("core")
    parts = [total[12 * index : 12 * index + 12, :1024] for index in range(4)]
    vec = jnp.concatenate([total[row : row + 1, 768:896] for row in range(36)], axis=1)
    lines = jnp.concatenate([vec[:, 1152 * row : 1152 * (row + 1)] for row in range(4)], axis=0)
    spare = jnp.zeros((12, 128), jnp.float32)

    def part(offset):
        value = parts[offset]
        for index in range(1, 4):
            value = jnp.where(me == index, parts[index ^ offset], value)
        return value

    for ref, offset in ((here_ref, 0), (core_ref, 1), (high_ref, 2), (cross_ref, 3)):
        both = jnp.concatenate([part(offset), spare], axis=1)
        ref[...] = jnp.concatenate([both, lines], axis=0).astype(ref.dtype)


def ffn_finish_kernel(
    wait, flush, here_ref, core_ref, high_ref, cross_ref,
    up_ref, down_ref, o_ref, up_bias_out, down_bias_out, gain_out, shift_out, o_bias_out,
):
    first = lax.axis_index("core") == 0
    low = lax.axis_index("zh") == 0
    alls = [ref[...].astype(jnp.float32) for ref in (here_ref, core_ref, high_ref, cross_ref)]
    here, core, high, cross = [value[:12, :768] for value in alls]
    up_ref[:, :768] = jnp.where(first, jnp.where(low, here, high), jnp.where(low, core, cross))
    up_ref[:, 768:] = jnp.where(first, jnp.where(low, high, here), jnp.where(low, cross, core))
    down_ref[:, :768] = jnp.where(first, jnp.where(low, core, cross), jnp.where(low, here, high))
    down_ref[:, 768:] = jnp.where(first, jnp.where(low, cross, core), jnp.where(low, high, here))
    mine = alls[0][:, 768:1024] + alls[2][:, 768:1024]
    other = alls[1][:, 768:1024] + alls[3][:, 768:1024]
    o_ref[:, :256] = jnp.where(first, mine, other)[:12]
    o_ref[:, 256:] = jnp.where(first, other[:, 128:], mine[:, 128:])[:12]
    vec = jnp.where(first, alls[1][12:] + alls[3][12:], alls[0][12:] + alls[2][12:])
    vec = jnp.concatenate([vec[row : row + 1] for row in range(4)], axis=1)
    begin = 0
    for ref in (up_bias_out, down_bias_out, gain_out, shift_out, o_bias_out):
        ref[...] = vec[:, begin : begin + ref.shape[1]]
        begin += ref.shape[1]


def on_device(
    tokens,
    doc_start,
    exit_layer,
    cotangent,
    ln1_gain,
    ln1_shift,
    q_weight,
    q_bias,
    k_weight,
    v_weight,
    v_bias,
    o_weight,
    o_bias,
    ln2_gain,
    ln2_shift,
    up_weight,
    up_bias,
    down_weight,
    down_bias,
):
    f32 = jnp.float32

    def copied(*arrays):
        return [("d", array) for array in arrays]

    payload, low_one = call(
        project_kernel, "project",
        copied(
            tokens, doc_start, ln1_gain, ln1_shift, q_bias, v_bias, q_weight, k_weight, v_weight
        ),
        [("d", whole(16, HALF + 48, 128)), ("d", whole(128, 768))],
        lazy=(6, 7, 8),
    )
    own = lax.all_to_all(payload, PLANE, 0, 0, tiled=True)
    low_one, o_given = lax.optimization_barrier((low_one, o_weight))
    o_other = lax.ppermute(o_given, "wa", SWAP)
    x_send, x_keep = call(
        prepare_kernel, "prepare",
        copied(low_one),
        [("v", whole(128, 384)), ("d", whole(128, 384))],
    )
    own, x_send, o_other = lax.optimization_barrier((own, x_send, o_other))
    pairs = own[:, :HALF]
    one = lax.ppermute(pairs, "core", SWAP)
    edge = lax.ppermute(own[BLOCKS - 1], EDGE, ((7, 3), (15, 11)))
    two = lax.ppermute(pairs, "zh", SWAP)
    two, edge = lax.optimization_barrier((two, edge))
    three = lax.ppermute(two, "core", SWAP)
    x_sent = lax.ppermute(x_send, "core", SWAP)
    back, kv, q_rows, start_rows, full_rows = attend(own, one, two, three, edge)
    dhidden, vec_down = call(
        dhidden_kernel, "dhidden",
        copied(cotangent, exit_layer, down_weight),
        [("d", whole(128, 1536, dtype=f32)), ("d", whole(1, 768, dtype=f32))],
    )
    got = lax.all_to_all(back, ("x", "y", "wa"), 0, 0, tiled=True)
    dn_two, ffn_core, ffn_high, ffn_cross, ffn_here, middle, hidden, attn_low, vec_up = call(
        middle_kernel, "middle",
        [("v", got)]
        + copied(
            tokens, cotangent, exit_layer, o_bias, ln2_gain, ln2_shift, up_bias, o_weight, o_other,
            up_weight, dhidden,
        ),
        [
            ("v", whole(128, 768)),
            ("v", whole(128, 1536)),
            ("v", whole(128, 1536)),
            ("v", whole(128, 1536)),
            ("v", whole(128, 1536)),
            ("d", whole(128, 768, dtype=f32)),
            ("d", whole(128, 1536)),
            ("d", whole(128, 384)),
            ("d", whole(1, 1536, dtype=f32)),
        ],
        [pltpu.VMEM((128, 384), jnp.bfloat16), pltpu.VMEM((128, 1536), jnp.bfloat16)],
        lazy=(8, 9, 10, 11),
    )
    dn_two_other = lax.ppermute(dn_two, "wa", SWAP)
    ffn_high = lax.ppermute(ffn_high, "zh", SWAP)
    ffn_cross = lax.ppermute(ffn_cross, ("zh", "core"), CROSS)
    ffn_core = lax.ppermute(ffn_core, "core", SWAP)
    ffn = call(ffn_kernel, "ffn", copied(hidden, down_weight), [("v", whole(128, 768))], cost=0)
    dn_two_other, ffn = lax.optimization_barrier((dn_two_other, ffn))
    dh_payload, dattn_attn, dmiddle, vec_two = call(
        dheads_kernel, "dheads",
        [("v", dn_two), ("v", dn_two_other)]
        + copied(middle, cotangent, exit_layer, ln2_gain, attn_low, vec_up, vec_down, o_weight),
        [
            ("d", whole(16, HALF, 128)),
            ("v", whole(128, 1152)),
            ("d", whole(128, 768, dtype=f32)),
            ("v", whole(1, 4608, dtype=f32)),
        ],
        lazy=(9,),
        cost=0,
    )
    dh = lax.all_to_all(dh_payload, PLANE, 0, 0, tiled=True)
    dattn_sent = lax.ppermute(dattn_attn, "core", SWAP)
    vec_two_sent = lax.ppermute(vec_two, "core", SWAP)
    ffn_products = call(
        ffn_products_kernel, "ffn_products",
        [("v", ffn_here), ("v", ffn_core), ("v", ffn_high), ("v", ffn_cross)]
        + [("v", dattn_attn), ("v", dattn_sent), ("v", vec_two), ("v", vec_two_sent)],
        [("d", whole(768, 1024))],
    )
    ffn_blocks = lax.all_to_all(ffn_products.reshape(16, 48, 1024), PLANE, 0, 0, tiled=True)
    ffn_other = lax.ppermute(ffn, "wa", SWAP)
    given, kept, dq, edge_grad = attend_grad(kv, q_rows, start_rows, full_rows, dh)
    given, ffn_other = lax.optimization_barrier((given, ffn_other))
    edge_got = lax.ppermute(edge_grad, EDGE, ((3, 7), (11, 15)))
    taken = lax.ppermute(given, "core", SWAP)
    merged = call(
        merge_kernel, "merge",
        [("v", kept), ("v", taken), ("v", dq), ("v", edge_got)],
        [("d", whole(2 * BLOCKS, 96, 128))],
    )
    merged, ffn_blocks = lax.optimization_barrier((merged, ffn_blocks))
    grads = lax.all_to_all(merged, CHIPS, 0, 0, tiled=True)
    ffn_core, ffn_high, ffn_cross, ffn_here = call(
        ffn_sums_kernel, "ffn_sums", copied(ffn_blocks),
        [("v", whole(16, 1152)) for _ in range(3)] + [("v", whole(16, 1152, dtype=f32))],
        cost=0,
    )
    ffn_core = lax.ppermute(ffn_core, "core", SWAP)
    ffn_high = lax.ppermute(ffn_high, "zh", SWAP)
    ffn_cross = lax.ppermute(ffn_cross, ("zh", "core"), CROSS)
    grads, ffn_core, ffn_high, ffn_cross, x_sent = lax.optimization_barrier(
        (grads, ffn_core, ffn_high, ffn_cross, x_sent)
    )
    grads_rows, norms, vec, dn_one = call(
        dnormed_kernel, "dnormed",
        [("v", grads)] + copied(tokens, q_weight, k_weight, v_weight),
        [
            ("v", whole(128, 1152)),
            ("v", whole(1, 1536, dtype=f32)),
            ("v", whole(1, 2304, dtype=f32)),
            ("v", whole(128, 768)),
        ],
        lazy=(2, 3, 4),
        cost=0,
    )
    grads_sent = lax.ppermute(grads_rows, "core", SWAP)
    vec_sent = lax.ppermute(vec, "core", SWAP)
    norms_wa = lax.ppermute(norms, "wa", SWAP)
    norms_cross = lax.ppermute(norms, ("core", "wa"), CROSS)
    norms_wa, norms_cross, dn_one = lax.optimization_barrier((norms_wa, norms_cross, dn_one))
    dn_one_other = lax.ppermute(dn_one, "wa", SWAP)
    products = call(
        qkv_products_kernel, "qkv_products",
        copied(x_keep, x_sent)
        + [("v", grads_rows), ("v", grads_sent), ("v", vec), ("v", vec_sent)]
        + [("v", norms_wa), ("v", norms_cross)],
        [("d", whole(32, 128, 128))],
        [pltpu.VMEM((384, 1152), f32)],
        cost=0,
    )
    products = lax.all_to_all(products, CHIPS, 0, 0, tiled=True)
    output = call(
        output_kernel, "output",
        [("v", ffn), ("v", ffn_other)] + copied(middle, tokens, exit_layer, down_bias),
        [("d", whole(128, 768))],
        cost=0,
    )
    (
        up_weight_grad, down_weight_grad_t, o_weight_grad_t,
        up_bias_grad, down_bias_grad, ln2_gain_grad, ln2_shift_grad, o_bias_grad,
    ) = call(
        ffn_finish_kernel, "ffn_finish",
        [("v", ffn_here), ("v", ffn_core), ("v", ffn_high), ("v", ffn_cross)],
        [("d", whole(12, 1536, dtype=f32)) for _ in range(2)]
        + [("d", whole(12, 384, dtype=f32))]
        + [("d", whole(count, dtype=f32)) for count in (1536, 768, 768, 768, 768)],
        cost=0,
    )
    input_grad = call(
        input_grad_kernel, "input_grad",
        [("v", dn_one), ("v", dn_one_other)]
        + copied(tokens, cotangent, exit_layer, ln1_gain, dmiddle),
        [("d", whole(128, 768, dtype=f32))],
        cost=0,
    )
    (
        products, output, input_grad, up_weight_grad, down_weight_grad_t
    ) = lax.optimization_barrier(
        (products, output, input_grad, up_weight_grad, down_weight_grad_t)
    )
    (
        q_weight_grad, k_weight_grad, v_weight_grad,
        ln1_shift_grad, ln1_gain_grad, q_bias_grad, v_bias_grad,
    ) = call(
        finish_kernel, "finish",
        [("v", products)],
        [("d", whole(12, 384, dtype=f32)) for _ in range(3)]
        + [("d", whole(count, dtype=f32)) for count in (768, 768, 384, 384)],
    )
    return (
        output,
        input_grad,
        ln1_gain_grad,
        ln1_shift_grad,
        q_weight_grad,
        q_bias_grad,
        k_weight_grad,
        v_weight_grad,
        v_bias_grad,
        o_weight_grad_t,
        o_bias_grad,
        ln2_gain_grad,
        ln2_shift_grad,
        up_weight_grad,
        up_bias_grad,
        down_weight_grad_t,
        down_bias_grad,
    )


def solution(mesh):
    fine = Mesh(mesh.devices.reshape(4, 4, 2, 2, 2), CTX + ("wa",))
    return jax.shard_map(
        on_device,
        mesh=fine,
        in_specs=(
            P(CTX, None),
            P(CTX),
            P(CTX),
            P(CTX, None),
            P(),
            P(),
            P(None, "wa"),
            P("wa"),
            P(None, "wa"),
            P(None, "wa"),
            P("wa"),
            P("wa", None),
            P(),
            P(),
            P(),
            P(None, "wa"),
            P("wa"),
            P("wa", None),
            P(),
        ),
        out_specs=(
            P(CTX, None),
            P(CTX, None),
            P(),
            P(),
            P(CTX, "wa"),
            P("wa"),
            P(CTX, "wa"),
            P(CTX, "wa"),
            P("wa"),
            P(CTX, "wa"),
            P(),
            P(),
            P(),
            P(CTX, "wa"),
            P("wa"),
            P(CTX, "wa"),
            P(),
        ),
        check_vma=False,
    )
```

```python
import math

import jax
import jax.numpy as jnp
from jax import lax
from jax.experimental import pallas as pl
from jax.experimental.pallas import tpu as pltpu
from jax.sharding import Mesh, PartitionSpec as P

HEAD_DIM = 64
LAYER = 6
CTX = ("x", "y", "zh", "core")
CHIPS = ("x", "y", "zh")
PLANE = ("x", "y")
EDGE = ("y", "zh", "core")
SWAP = ((0, 1), (1, 0))
CROSS = ((0, 3), (1, 2), (2, 1), (3, 0))
HALF = 64
BLOCKS = 16
GROUP = 256
STREAM = 8192
ROWS = (BLOCKS + 1) * HALF
FF_TILE = 768
FAR = 1e9
SCALING = 1.0 / math.sqrt(HEAD_DIM)
EXP2_SCALE = SCALING / math.log(2.0)
VMEM_BYTES = 64 * 2**20


epsilon = 1e-05
trans_right = (((1,), (1,)), ((), ()))
trans_left = (((0,), (0,)), ((), ()))
cubic_coef = 0.044715


def gelu_pair(values):
    outer = math.sqrt(2.0 / math.pi)
    inner = outer * (values + cubic_coef * values * values * values)
    tangent = jnp.tanh(inner)
    result = 0.5 * values * (1.0 + tangent)
    gelu_slope = 0.5 * (1.0 + tangent) + 0.5 * values * (1.0 - tangent * tangent) * outer * (
        1.0 + 3.0 * cubic_coef * values * values
    )
    return (result, gelu_slope)


def norm_forward(values, gain_vec, shift_vec):
    average = jnp.mean(values, axis=-1, keepdims=True)
    centred = values - average
    inverse_std = lax.rsqrt(jnp.mean(centred * centred, axis=-1, keepdims=True) + epsilon)
    normed = centred * inverse_std
    return (normed * gain_vec + shift_vec, normed, inverse_std)


def norm_backward(grad_out, normed, inverse_std, gain_vec):
    scaled = grad_out * gain_vec
    return inverse_std * (
        scaled
        - jnp.mean(scaled, axis=-1, keepdims=True)
        - normed * jnp.mean(scaled * normed, axis=-1, keepdims=True)
    )


def swap_add(part, axis):
    other = lax.ppermute(part, axis, SWAP)
    return part.astype(jnp.float32) + other.astype(jnp.float32)


def whole(*shape, dtype=jnp.bfloat16):
    return jax.ShapeDtypeStruct(shape, dtype)


def head_place():
    upper = lax.axis_index("y") % 2
    sub = 2 * lax.axis_index("zh") + lax.axis_index("core")
    last = sub == 3
    return (
        upper,
        jnp.where(upper == 1, 3 - sub, sub),
        jnp.where((upper == 0) & last, 1, 0),
        jnp.where((upper == 1) & last, 1, 0),
    )


def call(kernel, name, ins, outs, scratch=(), lazy=(), cost=2):
    copied_in = [at for at, (mode, _) in enumerate(ins) if mode == "d"]
    copied_out = [at for at, (mode, _) in enumerate(outs) if mode == "d"]

    def buffer(array):
        shape = array.shape if len(array.shape) > 1 else (1,) + tuple(array.shape)
        return pltpu.VMEM(shape, array.dtype)

    def body(*refs):
        given, rest = list(refs[: len(ins)]), refs[len(ins) :]
        results, rest = list(rest[: len(outs)]), rest[len(outs) :]
        in_buffers, rest = rest[: len(copied_in)], rest[len(copied_in) :]
        out_buffers, rest = rest[: len(copied_out)], rest[len(copied_out) :]
        in_sems, out_sems, rest = rest[0], rest[1], rest[2:]
        pending, flushing = [], []
        for slot, at in enumerate(copied_in):
            there = in_buffers[slot]
            into = there if len(ins[at][1].shape) > 1 else there.at[0]
            copy = pltpu.make_async_copy(given[at], into, in_sems.at[slot])
            copy.start()
            given[at] = there
            pending.append((there, at, copy))
        targets, extra, begun = [], [], []
        for slot, at in enumerate(copied_out):
            made = out_buffers[slot] if len(outs[at][1].shape) > 1 else out_buffers[slot].at[0]
            targets.append((out_buffers[slot], made, results[at], out_sems.at[slot]))
            results[at] = out_buffers[slot]

        def wait(ref):
            for entry in list(pending):
                if entry[0] is ref:
                    entry[2].wait()
                    pending[:] = [other for other in pending if other is not entry]

        def flush(ref, begin=None, end=None):
            for buffer_ref, made, there, sem in targets:
                if buffer_ref is not ref:
                    continue
                if begin is not None:
                    sem = out_sems.at[len(copied_out) + len(extra)]
                    extra.append(sem)
                    made, there = made.at[begin:end], there.at[begin:end]
                copy = pltpu.make_async_copy(made, there, sem)
                copy.start()
                flushing.append(copy)
                begun.append(ref)

        for entry in list(pending):
            if entry[1] not in lazy:
                wait(entry[0])
        kernel(wait, flush, *given, *results, *rest)
        for entry in list(pending):
            wait(entry[0])
        for entry in targets:
            if not any(ref is entry[0] for ref in begun):
                flush(entry[0])
        for copy in flushing:
            copy.wait()

    vmem, anywhere = pl.BlockSpec(memory_space=pltpu.VMEM), pl.BlockSpec(memory_space=pltpu.HBM)
    result = pl.pallas_call(
        body,
        out_shape=tuple(out for _, out in outs),
        in_specs=[anywhere if mode == "d" else vmem for mode, _ in ins],
        out_specs=tuple(anywhere if mode == "d" else vmem for mode, _ in outs),
        scratch_shapes=[buffer(ins[at][1]) for at in copied_in]
        + [buffer(outs[at][1]) for at in copied_out]
        + [
            pltpu.SemaphoreType.DMA((max(1, len(copied_in)),)),
            pltpu.SemaphoreType.DMA((len(copied_out) + 4,)),
        ]
        + list(scratch),
        compiler_params=pltpu.CompilerParams(vmem_limit_bytes=VMEM_BYTES),
        cost_estimate=pl.CostEstimate(
            flops=cost * 10**9, transcendentals=0, bytes_accessed=0
        ),
        name=name,
    )(*[array for _, array in ins])
    return result[0] if len(outs) == 1 else result


def lane_ids(rows, cols):
    return lax.broadcasted_iota(jnp.int32, (rows, cols), 1)


def row_ids_of(rows, cols):
    return lax.broadcasted_iota(jnp.int32, (rows, cols), 0)


def turn(values):
    return pltpu.roll(values, HALF, 1)


def unpack_low(packed):
    wide = packed.astype(jnp.float32)
    left = lane_ids(32, 128) < HALF
    both = jnp.concatenate([wide, turn(wide)], axis=0)
    return jnp.where(jnp.concatenate([left, left], axis=0), both, 0.0)


def unpack_high(packed):
    wide = packed.astype(jnp.float32)
    right = lane_ids(32, 128) >= HALF
    both = jnp.concatenate([turn(wide), wide], axis=0)
    return jnp.where(jnp.concatenate([right, right], axis=0), both, 0.0)


def pack_from_low(block):
    return jnp.where(lane_ids(32, 128) < HALF, block[:32], turn(block[32:]))


def pack_from_high(block):
    return jnp.where(lane_ids(32, 128) < HALF, turn(block[:32]), block[32:])


def key_places(scal, group):
    lane = lane_ids(8, GROUP)
    sub = (lane >> 6) ^ scal[1]
    return (scal[0] * (STREAM // 2) + GROUP * group + (sub << 6) + (lane & 63)).astype(
        jnp.float32
    )


def edge_places():
    return (STREAM // 2 + lane_ids(8, 128)).astype(jnp.float32)


def query_places(scal, block):
    row = row_ids_of(HALF, 128)
    return (
        scal[0] * (STREAM // 2) + GROUP * block + (scal[1] << 6) + row
    ).astype(jnp.float32)


def spread(rows, width):
    return jnp.concatenate([rows] * (width // 128), axis=1) if width > 128 else rows


def weights_of(scal, queries, starts, keys, places, group):
    scores = lax.dot_general(queries, keys, trans_right, preferred_element_type=jnp.float32)
    count = queries.shape[0]
    own = spread(query_places(scal, group), GROUP)
    limit = jnp.concatenate([own, jnp.full((count - HALF, GROUP), FAR, jnp.float32)], axis=0)
    seen = (spread(starts, GROUP) <= places[:1]) & (places[:1] <= limit)
    return jnp.where(seen, jnp.exp2(scores * EXP2_SCALE), 0.0)


def edge_weights(queries, starts, keys):
    scores = lax.dot_general(queries, keys, trans_right, preferred_element_type=jnp.float32)
    places = edge_places()[:1]
    limit = (STREAM // 2 + row_ids_of(HALF, 128)).astype(jnp.float32)
    return jnp.where(
        (starts <= places) & (places <= limit), jnp.exp2(scores * EXP2_SCALE), 0.0
    )


def attend_kernel(
    wait, flush, own_ref, one_ref, two_ref, three_ref, edge_ref,
    back_ref, kv_ref, q_ref, start_ref, full_ref,
    num_ref, den_ref,
):
    scal = head_place()
    upper = scal[0]
    diag = jnp.where(
        lane_ids(HALF, 128) == row_ids_of(HALF, 128),
        64.0,
        jnp.where(lane_ids(HALF, 128) == row_ids_of(HALF, 128) + HALF, 1.0, 0.0),
    )

    def starts(line, off):
        found = jnp.sum(line.astype(jnp.float32) * diag, axis=1, keepdims=True)
        return jnp.broadcast_to(jnp.where(off, FAR, found), (HALF, 128))

    for block in range(BLOCKS):
        place = jnp.where(upper == 1, BLOCKS - 1 - block, block)
        rows = slice(block * HALF, (block + 1) * HALF)
        mine = own_ref[pl.ds(place, 1)][0]
        kv_ref[block, 0:HALF] = mine[:HALF]
        kv_ref[block, HALF : 2 * HALF] = one_ref[pl.ds(place, 1)][0]
        kv_ref[block, 2 * HALF : 3 * HALF] = two_ref[pl.ds(place, 1)][0]
        kv_ref[block, 3 * HALF :] = three_ref[pl.ds(place, 1)][0]
        q_ref[rows] = unpack_low(mine[HALF : HALF + 32]).astype(jnp.bfloat16)
        off = (scal[3] == 1) if block == 0 else False
        start_ref[rows] = starts(mine[HALF + 32 : HALF + 33], off)
    kv_ref[BLOCKS] = jnp.zeros((GROUP, 128), jnp.bfloat16)
    kv_ref[BLOCKS, :HALF] = edge_ref[:HALF]
    q_ref[BLOCKS * HALF :] = unpack_low(edge_ref[HALF : HALF + 32]).astype(jnp.bfloat16)
    start_ref[BLOCKS * HALF :] = starts(edge_ref[HALF + 32 : HALF + 33], scal[2] == 0)
    flush(kv_ref)
    flush(q_ref)
    flush(start_ref)

    for group in range(BLOCKS + 1):
        rows = slice(group * HALF, ROWS)
        if group < BLOCKS:
            keys = kv_ref[group]
            weights = weights_of(
                scal, q_ref[rows], start_ref[rows], keys, key_places(scal, group), group
            )
            total = weights[:, :128] + weights[:, 128:]
        else:
            keys = kv_ref[group, :128]
            weights = total = edge_weights(q_ref[rows], start_ref[rows], keys)
        product = jnp.dot(weights.astype(jnp.bfloat16), keys, preferred_element_type=jnp.float32)
        if group == 0:
            num_ref[rows] = product
            den_ref[rows] = total
        else:
            num_ref[rows] += product
            den_ref[rows] += total

    for block in range(BLOCKS + 1):
        rows = slice(block * HALF, (block + 1) * HALF)
        den = jnp.sum(den_ref[rows], axis=1, keepdims=True)
        recip = jnp.broadcast_to(1.0 / jnp.where(den == 0.0, 1.0, den), (HALF, 128))
        full = num_ref[rows] * recip
        full_ref[rows] = jnp.where(lane_ids(HALF, 128) < HALF, recip, full)
    flush(full_ref)
    for place in range(BLOCKS):
        block = jnp.where(upper == 1, BLOCKS - 1 - place, place)
        rows = pl.ds(pl.multiple_of(block * HALF, HALF), HALF)
        packed = pack_from_high(full_ref[rows]).astype(jnp.bfloat16)
        if place < BLOCKS - 1:
            edge = jnp.zeros((32, 128), jnp.bfloat16)
        else:
            edge = pack_from_high(full_ref[BLOCKS * HALF :]).astype(jnp.bfloat16)
        for copy in range(2):
            back_ref[2 * place + copy, :32] = packed
            back_ref[2 * place + copy, 32:] = edge
        if place == BLOCKS // 2 - 1:
            flush(back_ref, 0, BLOCKS)
    flush(back_ref, BLOCKS, 2 * BLOCKS)


def attend_grad_kernel(
    wait, flush, kv_ref, q_ref, start_ref, full_ref, dh_in_ref,
    send_ref, keep_ref, dq_ref, edge_ref,
    dhn_ref, dot_ref, dq_acc,
):
    scal = head_place()
    upper = scal[0]
    left = lane_ids(HALF, 128) < HALF
    wait(full_ref)
    for block in range(BLOCKS + 1):
        rows = slice(block * HALF, (block + 1) * HALF)
        if block < BLOCKS:
            place = jnp.where(upper == 1, BLOCKS - 1 - block, block)
            packed = dh_in_ref[pl.ds(place, 1), :32][0]
        else:
            packed = dh_in_ref[BLOCKS - 1, 32:]
        full = full_ref[rows]
        scaled = unpack_high(packed) * jnp.where(left, full, turn(full))
        scaled = scaled.astype(jnp.bfloat16).astype(jnp.float32)
        dhn_ref[rows] = scaled.astype(jnp.bfloat16)
        dot_ref[rows] = jnp.broadcast_to(
            jnp.sum(jnp.where(left, 0.0, scaled * full), axis=1, keepdims=True), (HALF, 128)
        )
    wait(kv_ref)
    wait(q_ref)
    wait(start_ref)
    for group in range(BLOCKS + 1):
        rows = slice(group * HALF, ROWS)
        if group < BLOCKS:
            keys = kv_ref[group]
            weights = weights_of(
                scal, q_ref[rows], start_ref[rows], keys, key_places(scal, group), group
            )
        else:
            keys = kv_ref[group, :128]
            weights = edge_weights(q_ref[rows], start_ref[rows], keys)
        dprob = lax.dot_general(
            dhn_ref[rows], keys, trans_right, preferred_element_type=jnp.float32
        )
        dscore = (weights * (dprob - spread(dot_ref[rows], keys.shape[0]))).astype(jnp.bfloat16)
        dquery = jnp.dot(dscore, keys, preferred_element_type=jnp.float32)
        if group == 0:
            dq_acc[rows] = dquery
        else:
            dq_acc[rows] += dquery
        grads = lax.dot_general(
            dscore, q_ref[rows], trans_left, preferred_element_type=jnp.float32
        ) * SCALING + lax.dot_general(
            weights.astype(jnp.bfloat16),
            dhn_ref[rows],
            trans_left,
            preferred_element_type=jnp.float32,
        )
        low = grads.astype(jnp.bfloat16)
        if group < BLOCKS:
            place = jnp.where(upper == 1, BLOCKS - 1 - group, group)
            for quarter in range(4):
                out = send_ref if quarter % 2 else keep_ref
                out[pl.ds(quarter // 2 * BLOCKS + place, 1)] = low[
                    None, quarter * HALF : (quarter + 1) * HALF
                ]
        else:
            edge_ref[:HALF] = low[:HALF]

    for block in range(BLOCKS + 1):
        rows = slice(block * HALF, (block + 1) * HALF)
        packed = pack_from_low(dq_acc[rows] * SCALING).astype(jnp.bfloat16)
        if block < BLOCKS:
            place = jnp.where(upper == 1, BLOCKS - 1 - block, block)
            dq_ref[pl.ds(place, 1)] = packed[None]
        else:
            edge_ref[HALF:] = packed


def attend(own, one, two, three, edge):
    f32 = jnp.float32
    return call(
        attend_kernel, "attend",
        [("v", own), ("v", one), ("v", two), ("v", three), ("v", edge)],
        [
            ("d", whole(2 * BLOCKS, HALF, 128)),
            ("d", whole(BLOCKS + 1, GROUP, 128)),
            ("d", whole(ROWS, 128)),
            ("d", whole(ROWS, 128, dtype=f32)),
            ("d", whole(ROWS, 128, dtype=f32)),
        ],
        [pltpu.VMEM((ROWS, 128), f32), pltpu.VMEM((ROWS, 128), f32)],
        cost=3,
    )


def attend_grad(kv, q, start, full, dh):
    f32 = jnp.float32
    return call(
        attend_grad_kernel, "attend_grad",
        [("d", kv), ("d", q), ("d", start), ("d", full), ("v", dh)],
        [
            ("v", whole(2 * BLOCKS, HALF, 128)),
            ("v", whole(2 * BLOCKS, HALF, 128)),
            ("v", whole(BLOCKS, 32, 128)),
            ("v", whole(96, 128)),
        ],
        [
            pltpu.VMEM((ROWS, 128), jnp.bfloat16),
            pltpu.VMEM((ROWS, 128), f32),
            pltpu.VMEM((ROWS, 128), f32),
        ],
        lazy=(0, 1, 2, 3),
        cost=40,
    )


def column(line):
    return jnp.sum(
        jnp.where(lane_ids(128, 128) == row_ids_of(128, 128), line, 0.0), axis=1, keepdims=True
    )


def pairs_low(even, odd):
    left = lane_ids(32, 128) < HALF
    return jnp.concatenate(
        [jnp.where(left, even, turn(odd)), jnp.where(left, turn(even), odd)], axis=0
    )


def project_kernel(
    wait, flush,
    tokens_ref, start_ref, gain_ref, shift_ref, q_bias_ref, v_bias_ref, q_ref, k_ref, v_ref,
    pay_ref, low_ref,
):
    normed, _, _ = norm_forward(tokens_ref[...].astype(jnp.float32), gain_ref[...], shift_ref[...])
    low = normed.astype(jnp.bfloat16)
    low_ref[...] = low
    flush(low_ref)
    starts = start_ref[...]
    high_part = (starts >> 6).astype(jnp.float32)
    low_part = (starts & 63).astype(jnp.float32)
    left = lane_ids(1, 128) < HALF
    lines = (
        jnp.where(left, high_part, turn(low_part)),
        jnp.where(left, turn(high_part), low_part),
    )
    lines = [jnp.broadcast_to(line, (16, 128)).astype(jnp.bfloat16) for line in lines]
    wide = lane_ids(HALF, 128) < HALF
    for ref in (q_ref, k_ref, v_ref):
        wait(ref)
    pay_ref[12:] = jnp.zeros((4, HALF + 48, 128), jnp.bfloat16)
    flush(pay_ref, 12, 16)
    all_queries = jnp.dot(low, q_ref[...], preferred_element_type=jnp.float32) + q_bias_ref[...]
    all_keys = jnp.dot(low, k_ref[...], preferred_element_type=jnp.float32)
    all_values = jnp.dot(low, v_ref[...], preferred_element_type=jnp.float32) + v_bias_ref[...]
    for pair in range(3):
        columns = slice(pair * 128, (pair + 1) * 128)
        queries, keyset, values = all_queries[:, columns], all_keys[:, columns], all_values[:, columns]
        for half in range(2):
            rows = slice(half * HALF, (half + 1) * HALF)
            for odd in range(2):
                if odd:
                    both = jnp.where(wide, turn(keyset[rows]), values[rows])
                    packed = pack_from_high(queries[rows])
                else:
                    both = jnp.where(wide, keyset[rows], turn(values[rows]))
                    packed = pack_from_low(queries[rows])
                index = 4 * pair + 2 * odd + half
                pay_ref[index, :HALF] = both.astype(jnp.bfloat16)
                pay_ref[index, HALF : HALF + 32] = packed.astype(jnp.bfloat16)
                pay_ref[index, HALF + 32 :] = lines[half]
        flush(pay_ref, 4 * pair, 4 * pair + 4)


def prepare_kernel(wait, flush, low_ref, send_ref, keep_ref):
    lane = lane_ids(8, 768)
    core = (lane >= 384).astype(jnp.int32)
    within = lane - 384 * core
    chip = (within * 171) >> 11
    source = (24 * chip + 12 * core + (within - 12 * chip))[:1]
    order = jnp.where(row_ids_of(768, 768) == source, 1.0, 0.0).astype(jnp.bfloat16)
    ordered = jnp.dot(low_ref[...], order, preferred_element_type=jnp.float32).astype(jnp.bfloat16)
    first = lax.axis_index("core") == 0
    keep_ref[...] = jnp.where(first, ordered[:, :384], ordered[:, 384:])
    send_ref[...] = jnp.where(first, ordered[:, 384:], ordered[:, :384])


def attn_tile(got_ref, side, pair):
    parts = []
    for half in range(2):
        heads = []
        for odd in range(2):
            index = 4 * pair + 2 * odd
            lower = got_ref[pl.ds(2 * index + side, 1)][0].astype(jnp.float32)
            if half:
                higher = got_ref[pl.ds(2 * index + 2 + side, 1)][0].astype(jnp.float32)
                packed = higher[:32] + lower[32:]
            else:
                packed = lower[:32]
            heads.append(packed)
        parts.append(pairs_low(*heads))
    return jnp.concatenate(parts, axis=0).astype(jnp.bfloat16)


def branch_of(cot_ref, exit_ref):
    active = column((exit_ref[...] > LAYER).astype(jnp.float32))
    return jnp.where(active > 0.0, cot_ref[...].astype(jnp.float32), 0.0)


def dhidden_kernel(wait, flush, cot_ref, exit_ref, down_ref, out_ref, vec_ref):
    branch = branch_of(cot_ref, exit_ref)
    vec_ref[...] = jnp.sum(branch, axis=0, keepdims=True)
    out_ref[...] = lax.dot_general(
        branch.astype(jnp.bfloat16), down_ref[...], trans_right, preferred_element_type=jnp.float32
    )


def middle_kernel(
    wait, flush, got_ref, tokens_ref, cot_ref, exit_ref, o_bias_ref, gain_ref, shift_ref,
    up_bias_ref, o_own_ref, o_other_ref, up_ref, dhidden_ref,
    dn_ref, core_ref, high_ref, cross_ref, here_ref, mid_ref, hidden_ref, attn_ref, vec_ref,
    acc_ref, dpre_ref,
):
    side = lax.axis_index("wa")
    for pair in range(3):
        rows = slice(pair * 128, (pair + 1) * 128)
        attn_ref[:, rows] = attn_tile(got_ref, side, pair)
        acc_ref[:, rows] = attn_tile(got_ref, 1 - side, pair)
    flush(attn_ref)
    wait(o_own_ref)
    wait(o_other_ref)
    total = jnp.dot(
        attn_ref[...], o_own_ref[...], preferred_element_type=jnp.float32
    ) + jnp.dot(acc_ref[...], o_other_ref[...], preferred_element_type=jnp.float32)
    middle = tokens_ref[...].astype(jnp.float32) + (total + o_bias_ref[...])
    mid_ref[...] = middle
    flush(mid_ref)
    normed, _, _ = norm_forward(middle, gain_ref[...], shift_ref[...])
    low = normed.astype(jnp.bfloat16)
    branch_low = branch_of(cot_ref, exit_ref).astype(jnp.bfloat16)
    dnormed = None
    wait(up_ref)
    wait(dhidden_ref)
    for begin in range(0, 1536, FF_TILE):
        columns = slice(begin, begin + FF_TILE)
        pre_act = (
            jnp.dot(low, up_ref[:, columns], preferred_element_type=jnp.float32)
            + up_bias_ref[:, columns]
        )
        hidden_full, slope = gelu_pair(pre_act)
        hidden = hidden_full.astype(jnp.bfloat16)
        hidden_ref[:, columns] = hidden
        dpre = (dhidden_ref[:, columns] * slope).astype(jnp.bfloat16)
        vec_ref[:, columns] = jnp.sum(dpre.astype(jnp.float32), axis=0, keepdims=True)
        dpre_ref[:, columns] = dpre
        dn_term = lax.dot_general(
            dpre, up_ref[:, columns], trans_right, preferred_element_type=jnp.float32
        )
        dnormed = dn_term if dnormed is None else dnormed + dn_term
    dn_ref[...] = dnormed.astype(jnp.bfloat16)
    core, high = lax.axis_index("core"), lax.axis_index("zh")
    for ref, offset in ((core_ref, 1), (high_ref, 2), (cross_ref, 3), (here_ref, 0)):
        up_side = (core ^ (offset & 1)) == 0
        first_half = (high ^ (offset >> 1)) == 0
        ref[:, :768] = jnp.where(up_side, low, branch_low)
        ref[:, 768:] = jnp.where(
            up_side,
            jnp.where(first_half, dpre_ref[:, :768], dpre_ref[:, 768:]),
            jnp.where(first_half, hidden_ref[:, :768], hidden_ref[:, 768:]),
        )


def dheads_kernel(
    wait, flush, dn_ref, other_ref, mid_ref, cot_ref, exit_ref, gain_ref, attn_ref, up_ref, down_ref, o_ref,
    pay_ref, both_ref, dmid_ref, vec_ref,
):
    middle = mid_ref[...]
    _, unit, inverse = norm_forward(middle, gain_ref[...], 0.0)
    dnormed = dn_ref[...].astype(jnp.float32) + other_ref[...].astype(jnp.float32)
    branch = branch_of(cot_ref, exit_ref)
    dmiddle = branch + norm_backward(dnormed, unit, inverse, gain_ref[...])
    dmid_ref[...] = dmiddle
    flush(dmid_ref)
    low = dmiddle.astype(jnp.bfloat16)
    vec_ref[:, :1536] = up_ref[...]
    vec_ref[:, 1536:2304] = down_ref[...]
    vec_ref[:, 2304:3072] = jnp.sum(dnormed * unit, axis=0, keepdims=True)
    vec_ref[:, 3072:3840] = jnp.sum(dnormed, axis=0, keepdims=True)
    vec_ref[:, 3840:] = jnp.sum(low.astype(jnp.float32), axis=0, keepdims=True)
    pay_ref[12:] = jnp.zeros((4, HALF, 128), jnp.bfloat16)
    flush(pay_ref, 12, 16)
    wait(o_ref)
    all_heads = lax.dot_general(low, o_ref[...], trans_right, preferred_element_type=jnp.float32)
    for pair in range(3):
        dheads = all_heads[:, pair * 128 : (pair + 1) * 128]
        for odd in range(2):
            pack = pack_from_high if odd else pack_from_low
            lower = pack(dheads[:HALF]).astype(jnp.bfloat16)
            higher = pack(dheads[HALF:]).astype(jnp.bfloat16)
            index = 4 * pair + 2 * odd
            pay_ref[index, :32] = lower
            pay_ref[index, 32:] = higher
            pay_ref[index + 1, :32] = higher
            pay_ref[index + 1, 32:] = higher
        flush(pay_ref, 4 * pair, 4 * pair + 4)
    both_ref[:, :768] = low
    both_ref[:, 768:] = attn_ref[...]


def ffn_products_kernel(
    wait, flush, here_ref, core_ref, high_ref, cross_ref, both_ref, sent_ref,
    vec_ref, vec_sent_ref, out_ref,
):
    pieces = (here_ref, core_ref, high_ref, cross_ref)
    first = lax.axis_index("core") == 0
    vec = vec_ref[...] + vec_sent_ref[...]
    lines = [vec[:, 128 * row : 128 * (row + 1)] for row in range(36)]
    lines = jnp.concatenate(lines + [jnp.zeros((12, 128), jnp.float32)], axis=0)
    rights = jnp.concatenate([ref[:, 768:] for ref in pieces], axis=0)
    both = jnp.concatenate([both_ref[...], sent_ref[...]], axis=0)
    attn = jnp.where(first, both[:, 768:1024], both[:, 896:])
    for half in range(2):
        rows = slice(384 * half, 384 * half + 384)
        product = lax.dot_general(
            both[:, rows], attn, trans_left, preferred_element_type=jnp.float32
        )
        out_ref[rows, 896:] = product[:, 128:].astype(jnp.bfloat16)
        for plane in range(8):
            at = slice(48 * plane, 48 * plane + 48)
            out_ref[384 * half + 48 * plane : 384 * half + 48 * plane + 48, 768:896] = jnp.where(
                first, product[at, :128], lines
            ).astype(jnp.bfloat16)
        lefts = jnp.concatenate([ref[:, rows] for ref in pieces], axis=0)
        out_ref[rows, :768] = lax.dot_general(
            lefts, rights, trans_left, preferred_element_type=jnp.float32
        ).astype(jnp.bfloat16)
        flush(out_ref, 384 * half, 384 * half + 384)


def ffn_kernel(wait, flush, hidden_ref, down_ref, out_ref):
    out_ref[...] = jnp.dot(
        hidden_ref[...], down_ref[...], preferred_element_type=jnp.float32
    ).astype(jnp.bfloat16)


def dnormed_kernel(
    wait, flush, got_ref, tokens_ref, q_ref, k_ref, v_ref,
    grads_ref, norm_ref, vec_ref, dn_ref,
):
    wide = lane_ids(HALF, 128) < HALF
    for pair in range(3):
        columns = slice(pair * 128, (pair + 1) * 128)
        key_columns = slice(384 + pair * 128, 512 + pair * 128)
        value_columns = slice(768 + pair * 128, 896 + pair * 128)
        for half in range(2):
            rows = slice(half * HALF, (half + 1) * HALF)
            at = 8 * pair + 2 * half
            even = got_ref[at].astype(jnp.float32) + got_ref[at + 1].astype(jnp.float32)
            odd = got_ref[at + 4].astype(jnp.float32) + got_ref[at + 5].astype(jnp.float32)
            grads_ref[rows, key_columns] = jnp.where(wide, even[:HALF], turn(odd[:HALF])).astype(
                jnp.bfloat16
            )
            grads_ref[rows, value_columns] = jnp.where(
                wide, turn(even[:HALF]), odd[:HALF]
            ).astype(jnp.bfloat16)
            grads_ref[rows, columns] = pairs_low(even[HALF:], odd[HALF:]).astype(jnp.bfloat16)
    for ref in (q_ref, k_ref, v_ref):
        wait(ref)
    dnormed = (
        lax.dot_general(
            grads_ref[:, :384], q_ref[...], trans_right, preferred_element_type=jnp.float32
        )
        + lax.dot_general(
            grads_ref[:, 384:768], k_ref[...], trans_right, preferred_element_type=jnp.float32
        )
        + lax.dot_general(
            grads_ref[:, 768:], v_ref[...], trans_right, preferred_element_type=jnp.float32
        )
    )
    dn_ref[...] = dnormed.astype(jnp.bfloat16)
    _, unit, _ = norm_forward(tokens_ref[...].astype(jnp.float32), 1.0, 0.0)
    total = jnp.sum(grads_ref[...].astype(jnp.float32), axis=0, keepdims=True)
    vec_ref[:, :768] = jnp.sum(dnormed, axis=0, keepdims=True)
    vec_ref[:, 768:1536] = jnp.sum(dnormed * unit, axis=0, keepdims=True)
    vec_ref[:, 1536:1920] = total[:, :384]
    vec_ref[:, 1920:2304] = total[:, 768:]
    norm_ref[...] = vec_ref[:, :1536]


def input_grad_kernel(
    wait, flush, dn_ref, other_ref, tokens_ref, cot_ref, exit_ref, gain_ref, dmid_ref, out_ref
):
    _, unit, inverse = norm_forward(tokens_ref[...].astype(jnp.float32), 1.0, 0.0)
    dnormed = dn_ref[...].astype(jnp.float32) + other_ref[...].astype(jnp.float32)
    active = column((exit_ref[...] > LAYER).astype(jnp.float32))
    out_ref[...] = (
        dmid_ref[...]
        + norm_backward(dnormed, unit, inverse, gain_ref[...])
        + jnp.where(active > 0.0, 0.0, cot_ref[...].astype(jnp.float32))
    )


def output_kernel(
    wait, flush, ffn_ref, other_ref, mid_ref, tokens_ref, exit_ref, bias_ref, out_ref
):
    active = column((exit_ref[...] > LAYER).astype(jnp.float32))
    branch = ffn_ref[...].astype(jnp.float32) + other_ref[...].astype(jnp.float32) + bias_ref[...]
    out_ref[...] = jnp.where(
        active > 0.0, mid_ref[...] + branch, tokens_ref[...].astype(jnp.float32)
    ).astype(jnp.bfloat16)


def merge_kernel(wait, flush, kept_ref, taken_ref, dq_ref, edge_ref, out_ref):
    high = lax.axis_index("zh")
    for block in range(BLOCKS):
        pair = kept_ref[block].astype(jnp.float32) + taken_ref[block].astype(jnp.float32)
        query = dq_ref[block]
        if block == BLOCKS - 1:
            pair = pair + edge_ref[:HALF].astype(jnp.float32)
            query = (query.astype(jnp.float32) + edge_ref[HALF:].astype(jnp.float32)).astype(
                jnp.bfloat16
            )
        out_ref[pl.ds(2 * block + high, 1), :HALF] = pair.astype(jnp.bfloat16)[None]
        out_ref[pl.ds(2 * block + high, 1), HALF:] = query[None]
        pair = kept_ref[BLOCKS + block].astype(jnp.float32) + taken_ref[BLOCKS + block].astype(
            jnp.float32
        )
        out_ref[pl.ds(2 * block + 1 - high, 1), :HALF] = pair.astype(jnp.bfloat16)[None]
        out_ref[pl.ds(2 * block + 1 - high, 1), HALF:] = jnp.zeros((1, 32, 128), jnp.bfloat16)
        if block % 8 == 7:
            flush(out_ref, 2 * block - 14, 2 * block + 2)


def qkv_products_kernel(
    wait, flush, keep_ref, sent_ref, grads_ref, grads_sent_ref,
    vec_ref, vec_sent_ref, wa_ref, cross_ref, out_ref,
    product_ref,
):
    lefts = jnp.concatenate([keep_ref[...], sent_ref[...]], axis=0)
    for at in range(0, 1152, 384):
        columns = slice(at, at + 384)
        rights = jnp.concatenate([grads_ref[:, columns], grads_sent_ref[:, columns]], axis=0)
        product_ref[:, columns] = lax.dot_general(
            lefts, rights, trans_left, preferred_element_type=jnp.float32
        )
    vec = vec_ref[...] + vec_sent_ref[...]
    norms = vec[:, :1536] + (wa_ref[...] + cross_ref[...])
    vec = jnp.concatenate([norms, vec[:, 1536:]], axis=1)
    lines = [vec[:, 128 * row : 128 * (row + 1)] for row in range(18)]
    lines = jnp.concatenate(lines + [jnp.zeros((2, 128), jnp.float32)], axis=0)
    for pair in range(16):
        block = product_ref[24 * pair : 24 * pair + 24]
        for half in range(2):
            rows = slice(12 * half, 12 * half + 12)
            tiles = [block[rows, 128 * tile : 128 * tile + 128] for tile in range(9)]
            out_ref[2 * pair + half] = jnp.concatenate(tiles + [lines], axis=0).astype(jnp.bfloat16)
        if pair % 8 == 7:
            flush(out_ref, 2 * pair - 14, 2 * pair + 2)


def finish_kernel(
    wait, flush, got_ref, q_ref, k_ref, v_ref, shift_out, gain_out, q_bias_out, v_bias_out
):
    total = got_ref[0].astype(jnp.float32)
    for source in range(1, 32):
        total = total + got_ref[source].astype(jnp.float32)
    for at, ref in enumerate((q_ref, k_ref, v_ref)):
        for tile in range(3):
            row = 36 * at + 12 * tile
            ref[:, 128 * tile : 128 * tile + 128] = total[row : row + 12]
    row = 108
    for ref in (shift_out, gain_out, q_bias_out, v_bias_out):
        for tile in range(ref.shape[1] // 128):
            ref[:, 128 * tile : 128 * tile + 128] = total[row : row + 1]
            row += 1


def ffn_sums_kernel(wait, flush, got_ref, core_ref, high_ref, cross_ref, here_ref):
    total = got_ref[0].astype(jnp.float32)
    for source in range(1, 16):
        total = total + got_ref[source].astype(jnp.float32)
    me = 2 * lax.axis_index("zh") + lax.axis_index("core")
    parts = [total[12 * index : 12 * index + 12, :1024] for index in range(4)]
    vec = jnp.concatenate([total[row : row + 1, 768:896] for row in range(36)], axis=1)
    lines = jnp.concatenate([vec[:, 1152 * row : 1152 * (row + 1)] for row in range(4)], axis=0)
    spare = jnp.zeros((12, 128), jnp.float32)

    def part(offset):
        value = parts[offset]
        for index in range(1, 4):
            value = jnp.where(me == index, parts[index ^ offset], value)
        return value

    for ref, offset in ((here_ref, 0), (core_ref, 1), (high_ref, 2), (cross_ref, 3)):
        both = jnp.concatenate([part(offset), spare], axis=1)
        ref[...] = jnp.concatenate([both, lines], axis=0).astype(ref.dtype)


def ffn_finish_kernel(
    wait, flush, here_ref, core_ref, high_ref, cross_ref,
    up_ref, down_ref, o_ref, up_bias_out, down_bias_out, gain_out, shift_out, o_bias_out,
):
    first = lax.axis_index("core") == 0
    low = lax.axis_index("zh") == 0
    alls = [ref[...].astype(jnp.float32) for ref in (here_ref, core_ref, high_ref, cross_ref)]
    here, core, high, cross = [value[:12, :768] for value in alls]
    up_ref[:, :768] = jnp.where(first, jnp.where(low, here, high), jnp.where(low, core, cross))
    up_ref[:, 768:] = jnp.where(first, jnp.where(low, high, here), jnp.where(low, cross, core))
    down_ref[:, :768] = jnp.where(first, jnp.where(low, core, cross), jnp.where(low, here, high))
    down_ref[:, 768:] = jnp.where(first, jnp.where(low, cross, core), jnp.where(low, high, here))
    mine = alls[0][:, 768:1024] + alls[2][:, 768:1024]
    other = alls[1][:, 768:1024] + alls[3][:, 768:1024]
    o_ref[:, :256] = jnp.where(first, mine, other)[:12]
    o_ref[:, 256:] = jnp.where(first, other[:, 128:], mine[:, 128:])[:12]
    vec = jnp.where(first, alls[1][12:] + alls[3][12:], alls[0][12:] + alls[2][12:])
    vec = jnp.concatenate([vec[row : row + 1] for row in range(4)], axis=1)
    begin = 0
    for ref in (up_bias_out, down_bias_out, gain_out, shift_out, o_bias_out):
        ref[...] = vec[:, begin : begin + ref.shape[1]]
        begin += ref.shape[1]


def on_device(
    tokens,
    doc_start,
    exit_layer,
    cotangent,
    ln1_gain,
    ln1_shift,
    q_weight,
    q_bias,
    k_weight,
    v_weight,
    v_bias,
    o_weight,
    o_bias,
    ln2_gain,
    ln2_shift,
    up_weight,
    up_bias,
    down_weight,
    down_bias,
):
    f32 = jnp.float32

    def copied(*arrays):
        return [("d", array) for array in arrays]

    payload, low_one = call(
        project_kernel, "project",
        copied(
            tokens, doc_start, ln1_gain, ln1_shift, q_bias, v_bias, q_weight, k_weight, v_weight
        ),
        [("d", whole(16, HALF + 48, 128)), ("d", whole(128, 768))],
        lazy=(6, 7, 8),
    )
    own = lax.all_to_all(payload, PLANE, 0, 0, tiled=True)
    low_one, o_given = lax.optimization_barrier((low_one, o_weight))
    o_other = lax.ppermute(o_given, "wa", SWAP)
    x_send, x_keep = call(
        prepare_kernel, "prepare",
        copied(low_one),
        [("v", whole(128, 384)), ("d", whole(128, 384))],
    )
    own, x_send, o_other = lax.optimization_barrier((own, x_send, o_other))
    pairs = own[:, :HALF]
    one = lax.ppermute(pairs, "core", SWAP)
    edge = lax.ppermute(own[BLOCKS - 1], EDGE, ((7, 3), (15, 11)))
    two = lax.ppermute(pairs, "zh", SWAP)
    two, edge = lax.optimization_barrier((two, edge))
    three = lax.ppermute(two, "core", SWAP)
    x_sent = lax.ppermute(x_send, "core", SWAP)
    back, kv, q_rows, start_rows, full_rows = attend(own, one, two, three, edge)
    dhidden, vec_down = call(
        dhidden_kernel, "dhidden",
        copied(cotangent, exit_layer, down_weight),
        [("d", whole(128, 1536, dtype=f32)), ("d", whole(1, 768, dtype=f32))],
    )
    got = lax.all_to_all(back, ("x", "y", "wa"), 0, 0, tiled=True)
    dn_two, ffn_core, ffn_high, ffn_cross, ffn_here, middle, hidden, attn_low, vec_up = call(
        middle_kernel, "middle",
        [("v", got)]
        + copied(
            tokens, cotangent, exit_layer, o_bias, ln2_gain, ln2_shift, up_bias, o_weight, o_other,
            up_weight, dhidden,
        ),
        [
            ("v", whole(128, 768)),
            ("v", whole(128, 1536)),
            ("v", whole(128, 1536)),
            ("v", whole(128, 1536)),
            ("v", whole(128, 1536)),
            ("d", whole(128, 768, dtype=f32)),
            ("d", whole(128, 1536)),
            ("d", whole(128, 384)),
            ("d", whole(1, 1536, dtype=f32)),
        ],
        [pltpu.VMEM((128, 384), jnp.bfloat16), pltpu.VMEM((128, 1536), jnp.bfloat16)],
        lazy=(8, 9, 10, 11),
    )
    dn_two_other = lax.ppermute(dn_two, "wa", SWAP)
    ffn_high = lax.ppermute(ffn_high, "zh", SWAP)
    ffn_cross = lax.ppermute(ffn_cross, ("zh", "core"), CROSS)
    ffn_core = lax.ppermute(ffn_core, "core", SWAP)
    ffn = call(ffn_kernel, "ffn", copied(hidden, down_weight), [("v", whole(128, 768))], cost=0)
    dn_two_other, ffn = lax.optimization_barrier((dn_two_other, ffn))
    dh_payload, dattn_attn, dmiddle, vec_two = call(
        dheads_kernel, "dheads",
        [("v", dn_two), ("v", dn_two_other)]
        + copied(middle, cotangent, exit_layer, ln2_gain, attn_low, vec_up, vec_down, o_weight),
        [
            ("d", whole(16, HALF, 128)),
            ("v", whole(128, 1152)),
            ("d", whole(128, 768, dtype=f32)),
            ("v", whole(1, 4608, dtype=f32)),
        ],
        lazy=(9,),
        cost=0,
    )
    dh = lax.all_to_all(dh_payload, PLANE, 0, 0, tiled=True)
    dattn_sent = lax.ppermute(dattn_attn, "core", SWAP)
    vec_two_sent = lax.ppermute(vec_two, "core", SWAP)
    ffn_products = call(
        ffn_products_kernel, "ffn_products",
        [("v", ffn_here), ("v", ffn_core), ("v", ffn_high), ("v", ffn_cross)]
        + [("v", dattn_attn), ("v", dattn_sent), ("v", vec_two), ("v", vec_two_sent)],
        [("d", whole(768, 1024))],
    )
    ffn_blocks = lax.all_to_all(ffn_products.reshape(16, 48, 1024), PLANE, 0, 0, tiled=True)
    ffn_other = lax.ppermute(ffn, "wa", SWAP)
    given, kept, dq, edge_grad = attend_grad(kv, q_rows, start_rows, full_rows, dh)
    given, ffn_other = lax.optimization_barrier((given, ffn_other))
    edge_got = lax.ppermute(edge_grad, EDGE, ((3, 7), (11, 15)))
    taken = lax.ppermute(given, "core", SWAP)
    merged = call(
        merge_kernel, "merge",
        [("v", kept), ("v", taken), ("v", dq), ("v", edge_got)],
        [("d", whole(2 * BLOCKS, 96, 128))],
    )
    merged, ffn_blocks = lax.optimization_barrier((merged, ffn_blocks))
    grads = lax.all_to_all(merged, CHIPS, 0, 0, tiled=True)
    ffn_core, ffn_high, ffn_cross, ffn_here = call(
        ffn_sums_kernel, "ffn_sums", copied(ffn_blocks),
        [("v", whole(16, 1152)) for _ in range(3)] + [("v", whole(16, 1152, dtype=f32))],
        cost=0,
    )
    ffn_core = lax.ppermute(ffn_core, "core", SWAP)
    ffn_high = lax.ppermute(ffn_high, "zh", SWAP)
    ffn_cross = lax.ppermute(ffn_cross, ("zh", "core"), CROSS)
    grads, ffn_core, ffn_high, ffn_cross, x_sent = lax.optimization_barrier(
        (grads, ffn_core, ffn_high, ffn_cross, x_sent)
    )
    grads_rows, norms, vec, dn_one = call(
        dnormed_kernel, "dnormed",
        [("v", grads)] + copied(tokens, q_weight, k_weight, v_weight),
        [
            ("v", whole(128, 1152)),
            ("v", whole(1, 1536, dtype=f32)),
            ("v", whole(1, 2304, dtype=f32)),
            ("v", whole(128, 768)),
        ],
        lazy=(2, 3, 4),
        cost=0,
    )
    grads_sent = lax.ppermute(grads_rows, "core", SWAP)
    vec_sent = lax.ppermute(vec, "core", SWAP)
    norms_wa = lax.ppermute(norms, "wa", SWAP)
    norms_cross = lax.ppermute(norms, ("core", "wa"), CROSS)
    norms_wa, norms_cross, dn_one = lax.optimization_barrier((norms_wa, norms_cross, dn_one))
    dn_one_other = lax.ppermute(dn_one, "wa", SWAP)
    products = call(
        qkv_products_kernel, "qkv_products",
        copied(x_keep, x_sent)
        + [("v", grads_rows), ("v", grads_sent), ("v", vec), ("v", vec_sent)]
        + [("v", norms_wa), ("v", norms_cross)],
        [("d", whole(32, 128, 128))],
        [pltpu.VMEM((384, 1152), f32)],
        cost=0,
    )
    products = lax.all_to_all(products, CHIPS, 0, 0, tiled=True)
    output = call(
        output_kernel, "output",
        [("v", ffn), ("v", ffn_other)] + copied(middle, tokens, exit_layer, down_bias),
        [("d", whole(128, 768))],
        cost=0,
    )
    (
        up_weight_grad, down_weight_grad_t, o_weight_grad_t,
        up_bias_grad, down_bias_grad, ln2_gain_grad, ln2_shift_grad, o_bias_grad,
    ) = call(
        ffn_finish_kernel, "ffn_finish",
        [("v", ffn_here), ("v", ffn_core), ("v", ffn_high), ("v", ffn_cross)],
        [("d", whole(12, 1536, dtype=f32)) for _ in range(2)]
        + [("d", whole(12, 384, dtype=f32))]
        + [("d", whole(count, dtype=f32)) for count in (1536, 768, 768, 768, 768)],
        cost=0,
    )
    input_grad = call(
        input_grad_kernel, "input_grad",
        [("v", dn_one), ("v", dn_one_other)]
        + copied(tokens, cotangent, exit_layer, ln1_gain, dmiddle),
        [("d", whole(128, 768, dtype=f32))],
        cost=0,
    )
    (
        products, output, input_grad, up_weight_grad, down_weight_grad_t
    ) = lax.optimization_barrier(
        (products, output, input_grad, up_weight_grad, down_weight_grad_t)
    )
    (
        q_weight_grad, k_weight_grad, v_weight_grad,
        ln1_shift_grad, ln1_gain_grad, q_bias_grad, v_bias_grad,
    ) = call(
        finish_kernel, "finish",
        [("v", products)],
        [("d", whole(12, 384, dtype=f32)) for _ in range(3)]
        + [("d", whole(count, dtype=f32)) for count in (768, 768, 384, 384)],
    )
    return (
        output,
        input_grad,
        ln1_gain_grad,
        ln1_shift_grad,
        q_weight_grad,
        q_bias_grad,
        k_weight_grad,
        v_weight_grad,
        v_bias_grad,
        o_weight_grad_t,
        o_bias_grad,
        ln2_gain_grad,
        ln2_shift_grad,
        up_weight_grad,
        up_bias_grad,
        down_weight_grad_t,
        down_bias_grad,
    )


def solution(mesh):
    fine = Mesh(mesh.devices.reshape(4, 4, 2, 2, 2), CTX + ("wa",))
    return jax.shard_map(
        on_device,
        mesh=fine,
        in_specs=(
            P(CTX, None),
            P(CTX),
            P(CTX),
            P(CTX, None),
            P(),
            P(),
            P(None, "wa"),
            P("wa"),
            P(None, "wa"),
            P(None, "wa"),
            P("wa"),
            P("wa", None),
            P(),
            P(),
            P(),
            P(None, "wa"),
            P("wa"),
            P("wa", None),
            P(),
        ),
        out_specs=(
            P(CTX, None),
            P(CTX, None),
            P(),
            P(),
            P(CTX, "wa"),
            P("wa"),
            P(CTX, "wa"),
            P(CTX, "wa"),
            P("wa"),
            P(CTX, "wa"),
            P(),
            P(),
            P(),
            P(CTX, "wa"),
            P("wa"),
            P(CTX, "wa"),
            P(),
        ),
        check_vma=False,
    )
```

```python
import math

import jax
import jax.numpy as jnp
from jax import lax
from jax.experimental import pallas as pl
from jax.experimental.pallas import tpu as pltpu
from jax.sharding import Mesh, PartitionSpec as P

HEAD_DIM = 64
LAYER = 6
CTX = ("x", "y", "zh", "core")
CHIPS = ("x", "y", "zh")
PLANE = ("x", "y")
EDGE = ("y", "zh", "core")
SWAP = ((0, 1), (1, 0))
CROSS = ((0, 3), (1, 2), (2, 1), (3, 0))
HALF = 64
BLOCKS = 16
GROUP = 256
STREAM = 8192
ROWS = (BLOCKS + 1) * HALF
FF_TILE = 768
FAR = 1e9
SCALING = 1.0 / math.sqrt(HEAD_DIM)
EXP2_SCALE = SCALING / math.log(2.0)
VMEM_BYTES = 64 * 2**20


epsilon = 1e-05
trans_right = (((1,), (1,)), ((), ()))
trans_left = (((0,), (0,)), ((), ()))
cubic_coef = 0.044715


def gelu_pair(values):
    outer = math.sqrt(2.0 / math.pi)
    inner = outer * (values + cubic_coef * values * values * values)
    tangent = jnp.tanh(inner)
    result = 0.5 * values * (1.0 + tangent)
    gelu_slope = 0.5 * (1.0 + tangent) + 0.5 * values * (1.0 - tangent * tangent) * outer * (
        1.0 + 3.0 * cubic_coef * values * values
    )
    return (result, gelu_slope)


def norm_forward(values, gain_vec, shift_vec):
    average = jnp.mean(values, axis=-1, keepdims=True)
    centred = values - average
    inverse_std = lax.rsqrt(jnp.mean(centred * centred, axis=-1, keepdims=True) + epsilon)
    normed = centred * inverse_std
    return (normed * gain_vec + shift_vec, normed, inverse_std)


def norm_backward(grad_out, normed, inverse_std, gain_vec):
    scaled = grad_out * gain_vec
    return inverse_std * (
        scaled
        - jnp.mean(scaled, axis=-1, keepdims=True)
        - normed * jnp.mean(scaled * normed, axis=-1, keepdims=True)
    )


def swap_add(part, axis):
    other = lax.ppermute(part, axis, SWAP)
    return part.astype(jnp.float32) + other.astype(jnp.float32)


def whole(*shape, dtype=jnp.bfloat16):
    return jax.ShapeDtypeStruct(shape, dtype)


def head_place():
    upper = lax.axis_index("y") % 2
    sub = 2 * lax.axis_index("zh") + lax.axis_index("core")
    last = sub == 3
    return (
        upper,
        jnp.where(upper == 1, 3 - sub, sub),
        jnp.where((upper == 0) & last, 1, 0),
        jnp.where((upper == 1) & last, 1, 0),
    )


def call(kernel, name, ins, outs, scratch=(), lazy=(), cost=2):
    copied_in = [at for at, (mode, _) in enumerate(ins) if mode == "d"]
    copied_out = [at for at, (mode, _) in enumerate(outs) if mode == "d"]

    def buffer(array):
        shape = array.shape if len(array.shape) > 1 else (1,) + tuple(array.shape)
        return pltpu.VMEM(shape, array.dtype)

    def body(*refs):
        given, rest = list(refs[: len(ins)]), refs[len(ins) :]
        results, rest = list(rest[: len(outs)]), rest[len(outs) :]
        in_buffers, rest = rest[: len(copied_in)], rest[len(copied_in) :]
        out_buffers, rest = rest[: len(copied_out)], rest[len(copied_out) :]
        in_sems, out_sems, rest = rest[0], rest[1], rest[2:]
        pending, flushing = [], []
        for slot, at in enumerate(copied_in):
            there = in_buffers[slot]
            into = there if len(ins[at][1].shape) > 1 else there.at[0]
            copy = pltpu.make_async_copy(given[at], into, in_sems.at[slot])
            copy.start()
            given[at] = there
            pending.append((there, at, copy))
        targets, extra, begun = [], [], []
        for slot, at in enumerate(copied_out):
            made = out_buffers[slot] if len(outs[at][1].shape) > 1 else out_buffers[slot].at[0]
            targets.append((out_buffers[slot], made, results[at], out_sems.at[slot]))
            results[at] = out_buffers[slot]

        def wait(ref):
            for entry in list(pending):
                if entry[0] is ref:
                    entry[2].wait()
                    pending[:] = [other for other in pending if other is not entry]

        def flush(ref, begin=None, end=None):
            for buffer_ref, made, there, sem in targets:
                if buffer_ref is not ref:
                    continue
                if begin is not None:
                    sem = out_sems.at[len(copied_out) + len(extra)]
                    extra.append(sem)
                    made, there = made.at[begin:end], there.at[begin:end]
                copy = pltpu.make_async_copy(made, there, sem)
                copy.start()
                flushing.append(copy)
                begun.append(ref)

        for entry in list(pending):
            if entry[1] not in lazy:
                wait(entry[0])
        kernel(wait, flush, *given, *results, *rest)
        for entry in list(pending):
            wait(entry[0])
        for entry in targets:
            if not any(ref is entry[0] for ref in begun):
                flush(entry[0])
        for copy in flushing:
            copy.wait()

    vmem, anywhere = pl.BlockSpec(memory_space=pltpu.VMEM), pl.BlockSpec(memory_space=pltpu.HBM)
    result = pl.pallas_call(
        body,
        out_shape=tuple(out for _, out in outs),
        in_specs=[anywhere if mode == "d" else vmem for mode, _ in ins],
        out_specs=tuple(anywhere if mode == "d" else vmem for mode, _ in outs),
        scratch_shapes=[buffer(ins[at][1]) for at in copied_in]
        + [buffer(outs[at][1]) for at in copied_out]
        + [
            pltpu.SemaphoreType.DMA((max(1, len(copied_in)),)),
            pltpu.SemaphoreType.DMA((len(copied_out) + 4,)),
        ]
        + list(scratch),
        compiler_params=pltpu.CompilerParams(vmem_limit_bytes=VMEM_BYTES),
        cost_estimate=pl.CostEstimate(
            flops=cost * 10**9, transcendentals=0, bytes_accessed=0
        ),
        name=name,
    )(*[array for _, array in ins])
    return result[0] if len(outs) == 1 else result


def lane_ids(rows, cols):
    return lax.broadcasted_iota(jnp.int32, (rows, cols), 1)


def row_ids_of(rows, cols):
    return lax.broadcasted_iota(jnp.int32, (rows, cols), 0)


def turn(values):
    return pltpu.roll(values, HALF, 1)


def unpack_low(packed):
    wide = packed.astype(jnp.float32)
    left = lane_ids(32, 128) < HALF
    both = jnp.concatenate([wide, turn(wide)], axis=0)
    return jnp.where(jnp.concatenate([left, left], axis=0), both, 0.0)


def unpack_high(packed):
    wide = packed.astype(jnp.float32)
    right = lane_ids(32, 128) >= HALF
    both = jnp.concatenate([turn(wide), wide], axis=0)
    return jnp.where(jnp.concatenate([right, right], axis=0), both, 0.0)


def pack_from_low(block):
    return jnp.where(lane_ids(32, 128) < HALF, block[:32], turn(block[32:]))


def pack_from_high(block):
    return jnp.where(lane_ids(32, 128) < HALF, turn(block[:32]), block[32:])


def key_places(scal, group):
    lane = lane_ids(8, GROUP)
    sub = (lane >> 6) ^ scal[1]
    return (scal[0] * (STREAM // 2) + GROUP * group + (sub << 6) + (lane & 63)).astype(
        jnp.float32
    )


def edge_places():
    return (STREAM // 2 + lane_ids(8, 128)).astype(jnp.float32)


def query_places(scal, block):
    row = row_ids_of(HALF, 128)
    return (
        scal[0] * (STREAM // 2) + GROUP * block + (scal[1] << 6) + row
    ).astype(jnp.float32)


def spread(rows, width):
    return jnp.concatenate([rows] * (width // 128), axis=1) if width > 128 else rows


def weights_of(scal, queries, starts, keys, places, group):
    scores = lax.dot_general(queries, keys, trans_right, preferred_element_type=jnp.float32)
    count = queries.shape[0]
    own = spread(query_places(scal, group), GROUP)
    limit = jnp.concatenate([own, jnp.full((count - HALF, GROUP), FAR, jnp.float32)], axis=0)
    seen = (spread(starts, GROUP) <= places[:1]) & (places[:1] <= limit)
    return jnp.where(seen, jnp.exp2(scores * EXP2_SCALE), 0.0)


def edge_weights(queries, starts, keys):
    scores = lax.dot_general(queries, keys, trans_right, preferred_element_type=jnp.float32)
    places = edge_places()[:1]
    limit = (STREAM // 2 + row_ids_of(HALF, 128)).astype(jnp.float32)
    return jnp.where(
        (starts <= places) & (places <= limit), jnp.exp2(scores * EXP2_SCALE), 0.0
    )


def attend_kernel(
    wait, flush, own_ref, one_ref, two_ref, three_ref, edge_ref,
    back_ref, kv_ref, q_ref, start_ref, full_ref,
    num_ref, den_ref,
):
    scal = head_place()
    upper = scal[0]
    diag = jnp.where(
        lane_ids(HALF, 128) == row_ids_of(HALF, 128),
        64.0,
        jnp.where(lane_ids(HALF, 128) == row_ids_of(HALF, 128) + HALF, 1.0, 0.0),
    )

    def starts(line, off):
        found = jnp.sum(line.astype(jnp.float32) * diag, axis=1, keepdims=True)
        return jnp.broadcast_to(jnp.where(off, FAR, found), (HALF, 128))

    for block in range(BLOCKS):
        place = jnp.where(upper == 1, BLOCKS - 1 - block, block)
        rows = slice(block * HALF, (block + 1) * HALF)
        mine = own_ref[pl.ds(place, 1)][0]
        kv_ref[block, 0:HALF] = mine[:HALF]
        kv_ref[block, HALF : 2 * HALF] = one_ref[pl.ds(place, 1)][0]
        kv_ref[block, 2 * HALF : 3 * HALF] = two_ref[pl.ds(place, 1)][0]
        kv_ref[block, 3 * HALF :] = three_ref[pl.ds(place, 1)][0]
        q_ref[rows] = unpack_low(mine[HALF : HALF + 32]).astype(jnp.bfloat16)
        off = (scal[3] == 1) if block == 0 else False
        start_ref[rows] = starts(mine[HALF + 32 : HALF + 33], off)
    kv_ref[BLOCKS] = jnp.zeros((GROUP, 128), jnp.bfloat16)
    kv_ref[BLOCKS, :HALF] = edge_ref[:HALF]
    q_ref[BLOCKS * HALF :] = unpack_low(edge_ref[HALF : HALF + 32]).astype(jnp.bfloat16)
    start_ref[BLOCKS * HALF :] = starts(edge_ref[HALF + 32 : HALF + 33], scal[2] == 0)
    flush(kv_ref)
    flush(q_ref)
    flush(start_ref)

    for group in range(BLOCKS + 1):
        rows = slice(group * HALF, ROWS)
        if group < BLOCKS:
            keys = kv_ref[group]
            weights = weights_of(
                scal, q_ref[rows], start_ref[rows], keys, key_places(scal, group), group
            )
            total = weights[:, :128] + weights[:, 128:]
        else:
            keys = kv_ref[group, :128]
            weights = total = edge_weights(q_ref[rows], start_ref[rows], keys)
        product = jnp.dot(weights.astype(jnp.bfloat16), keys, preferred_element_type=jnp.float32)
        if group == 0:
            num_ref[rows] = product
            den_ref[rows] = total
        else:
            num_ref[rows] += product
            den_ref[rows] += total

    for block in range(BLOCKS + 1):
        rows = slice(block * HALF, (block + 1) * HALF)
        den = jnp.sum(den_ref[rows], axis=1, keepdims=True)
        recip = jnp.broadcast_to(1.0 / jnp.where(den == 0.0, 1.0, den), (HALF, 128))
        full = num_ref[rows] * recip
        full_ref[rows] = jnp.where(lane_ids(HALF, 128) < HALF, recip, full)
    flush(full_ref)
    for place in range(BLOCKS):
        block = jnp.where(upper == 1, BLOCKS - 1 - place, place)
        rows = pl.ds(pl.multiple_of(block * HALF, HALF), HALF)
        packed = pack_from_high(full_ref[rows]).astype(jnp.bfloat16)
        if place < BLOCKS - 1:
            edge = jnp.zeros((32, 128), jnp.bfloat16)
        else:
            edge = pack_from_high(full_ref[BLOCKS * HALF :]).astype(jnp.bfloat16)
        for copy in range(2):
            back_ref[2 * place + copy, :32] = packed
            back_ref[2 * place + copy, 32:] = edge
        if place == BLOCKS // 2 - 1:
            flush(back_ref, 0, BLOCKS)
    flush(back_ref, BLOCKS, 2 * BLOCKS)


def attend_grad_kernel(
    wait, flush, kv_ref, q_ref, start_ref, full_ref, dh_in_ref,
    send_ref, keep_ref, dq_ref, edge_ref,
    dhn_ref, dot_ref, dq_acc,
):
    scal = head_place()
    upper = scal[0]
    left = lane_ids(HALF, 128) < HALF
    wait(full_ref)
    for block in range(BLOCKS + 1):
        rows = slice(block * HALF, (block + 1) * HALF)
        if block < BLOCKS:
            place = jnp.where(upper == 1, BLOCKS - 1 - block, block)
            packed = dh_in_ref[pl.ds(place, 1), :32][0]
        else:
            packed = dh_in_ref[BLOCKS - 1, 32:]
        full = full_ref[rows]
        scaled = unpack_high(packed) * jnp.where(left, full, turn(full))
        scaled = scaled.astype(jnp.bfloat16).astype(jnp.float32)
        dhn_ref[rows] = scaled.astype(jnp.bfloat16)
        dot_ref[rows] = jnp.broadcast_to(
            jnp.sum(jnp.where(left, 0.0, scaled * full), axis=1, keepdims=True), (HALF, 128)
        )
    wait(kv_ref)
    wait(q_ref)
    wait(start_ref)
    for group in range(BLOCKS + 1):
        rows = slice(group * HALF, ROWS)
        if group < BLOCKS:
            keys = kv_ref[group]
            weights = weights_of(
                scal, q_ref[rows], start_ref[rows], keys, key_places(scal, group), group
            )
        else:
            keys = kv_ref[group, :128]
            weights = edge_weights(q_ref[rows], start_ref[rows], keys)
        dprob = lax.dot_general(
            dhn_ref[rows], keys, trans_right, preferred_element_type=jnp.float32
        )
        dscore = (weights * (dprob - spread(dot_ref[rows], keys.shape[0]))).astype(jnp.bfloat16)
        dquery = jnp.dot(dscore, keys, preferred_element_type=jnp.float32)
        if group == 0:
            dq_acc[rows] = dquery
        else:
            dq_acc[rows] += dquery
        grads = lax.dot_general(
            dscore, q_ref[rows], trans_left, preferred_element_type=jnp.float32
        ) * SCALING + lax.dot_general(
            weights.astype(jnp.bfloat16),
            dhn_ref[rows],
            trans_left,
            preferred_element_type=jnp.float32,
        )
        low = grads.astype(jnp.bfloat16)
        if group < BLOCKS:
            place = jnp.where(upper == 1, BLOCKS - 1 - group, group)
            for quarter in range(4):
                out = send_ref if quarter % 2 else keep_ref
                out[pl.ds(quarter // 2 * BLOCKS + place, 1)] = low[
                    None, quarter * HALF : (quarter + 1) * HALF
                ]
        else:
            edge_ref[:HALF] = low[:HALF]

    for block in range(BLOCKS + 1):
        rows = slice(block * HALF, (block + 1) * HALF)
        packed = pack_from_low(dq_acc[rows] * SCALING).astype(jnp.bfloat16)
        if block < BLOCKS:
            place = jnp.where(upper == 1, BLOCKS - 1 - block, block)
            dq_ref[pl.ds(place, 1)] = packed[None]
        else:
            edge_ref[HALF:] = packed


def attend(own, one, two, three, edge):
    f32 = jnp.float32
    return call(
        attend_kernel, "attend",
        [("v", own), ("v", one), ("v", two), ("v", three), ("v", edge)],
        [
            ("d", whole(2 * BLOCKS, HALF, 128)),
            ("d", whole(BLOCKS + 1, GROUP, 128)),
            ("d", whole(ROWS, 128)),
            ("d", whole(ROWS, 128, dtype=f32)),
            ("d", whole(ROWS, 128, dtype=f32)),
        ],
        [pltpu.VMEM((ROWS, 128), f32), pltpu.VMEM((ROWS, 128), f32)],
        cost=3,
    )


def attend_grad(kv, q, start, full, dh):
    f32 = jnp.float32
    return call(
        attend_grad_kernel, "attend_grad",
        [("d", kv), ("d", q), ("d", start), ("d", full), ("v", dh)],
        [
            ("v", whole(2 * BLOCKS, HALF, 128)),
            ("v", whole(2 * BLOCKS, HALF, 128)),
            ("v", whole(BLOCKS, 32, 128)),
            ("v", whole(96, 128)),
        ],
        [
            pltpu.VMEM((ROWS, 128), jnp.bfloat16),
            pltpu.VMEM((ROWS, 128), f32),
            pltpu.VMEM((ROWS, 128), f32),
        ],
        lazy=(0, 1, 2, 3),
        cost=40,
    )


def column(line):
    return jnp.sum(
        jnp.where(lane_ids(128, 128) == row_ids_of(128, 128), line, 0.0), axis=1, keepdims=True
    )


def pairs_low(even, odd):
    left = lane_ids(32, 128) < HALF
    return jnp.concatenate(
        [jnp.where(left, even, turn(odd)), jnp.where(left, turn(even), odd)], axis=0
    )


def project_kernel(
    wait, flush,
    tokens_ref, start_ref, gain_ref, shift_ref, q_bias_ref, v_bias_ref, q_ref, k_ref, v_ref,
    pay_ref, low_ref,
):
    normed, _, _ = norm_forward(tokens_ref[...].astype(jnp.float32), gain_ref[...], shift_ref[...])
    low = normed.astype(jnp.bfloat16)
    low_ref[...] = low
    flush(low_ref)
    starts = start_ref[...]
    high_part = (starts >> 6).astype(jnp.float32)
    low_part = (starts & 63).astype(jnp.float32)
    left = lane_ids(1, 128) < HALF
    lines = (
        jnp.where(left, high_part, turn(low_part)),
        jnp.where(left, turn(high_part), low_part),
    )
    lines = [jnp.broadcast_to(line, (16, 128)).astype(jnp.bfloat16) for line in lines]
    wide = lane_ids(HALF, 128) < HALF
    for ref in (q_ref, k_ref, v_ref):
        wait(ref)
    pay_ref[12:] = jnp.zeros((4, HALF + 48, 128), jnp.bfloat16)
    flush(pay_ref, 12, 16)
    all_queries = jnp.dot(low, q_ref[...], preferred_element_type=jnp.float32) + q_bias_ref[...]
    all_keys = jnp.dot(low, k_ref[...], preferred_element_type=jnp.float32)
    all_values = jnp.dot(low, v_ref[...], preferred_element_type=jnp.float32) + v_bias_ref[...]
    for pair in range(3):
        columns = slice(pair * 128, (pair + 1) * 128)
        queries, keyset, values = all_queries[:, columns], all_keys[:, columns], all_values[:, columns]
        for half in range(2):
            rows = slice(half * HALF, (half + 1) * HALF)
            for odd in range(2):
                if odd:
                    both = jnp.where(wide, turn(keyset[rows]), values[rows])
                    packed = pack_from_high(queries[rows])
                else:
                    both = jnp.where(wide, keyset[rows], turn(values[rows]))
                    packed = pack_from_low(queries[rows])
                index = 4 * pair + 2 * odd + half
                pay_ref[index, :HALF] = both.astype(jnp.bfloat16)
                pay_ref[index, HALF : HALF + 32] = packed.astype(jnp.bfloat16)
                pay_ref[index, HALF + 32 :] = lines[half]
        flush(pay_ref, 4 * pair, 4 * pair + 4)


def prepare_kernel(wait, flush, low_ref, send_ref, keep_ref):
    lane = lane_ids(8, 768)
    core = (lane >= 384).astype(jnp.int32)
    within = lane - 384 * core
    chip = (within * 171) >> 11
    source = (24 * chip + 12 * core + (within - 12 * chip))[:1]
    order = jnp.where(row_ids_of(768, 768) == source, 1.0, 0.0).astype(jnp.bfloat16)
    ordered = jnp.dot(low_ref[...], order, preferred_element_type=jnp.float32).astype(jnp.bfloat16)
    first = lax.axis_index("core") == 0
    keep_ref[...] = jnp.where(first, ordered[:, :384], ordered[:, 384:])
    send_ref[...] = jnp.where(first, ordered[:, 384:], ordered[:, :384])


def attn_tile(got_ref, side, pair):
    parts = []
    for half in range(2):
        heads = []
        for odd in range(2):
            index = 4 * pair + 2 * odd
            lower = got_ref[pl.ds(2 * index + side, 1)][0].astype(jnp.float32)
            if half:
                higher = got_ref[pl.ds(2 * index + 2 + side, 1)][0].astype(jnp.float32)
                packed = higher[:32] + lower[32:]
            else:
                packed = lower[:32]
            heads.append(packed)
        parts.append(pairs_low(*heads))
    return jnp.concatenate(parts, axis=0).astype(jnp.bfloat16)


def branch_of(cot_ref, exit_ref):
    active = column((exit_ref[...] > LAYER).astype(jnp.float32))
    return jnp.where(active > 0.0, cot_ref[...].astype(jnp.float32), 0.0)


def dhidden_kernel(wait, flush, cot_ref, exit_ref, down_ref, out_ref, vec_ref):
    branch = branch_of(cot_ref, exit_ref)
    vec_ref[...] = jnp.sum(branch, axis=0, keepdims=True)
    out_ref[...] = lax.dot_general(
        branch.astype(jnp.bfloat16), down_ref[...], trans_right, preferred_element_type=jnp.float32
    )


def middle_kernel(
    wait, flush, got_ref, tokens_ref, cot_ref, exit_ref, o_bias_ref, gain_ref, shift_ref,
    up_bias_ref, o_own_ref, o_other_ref, up_ref, dhidden_ref,
    dn_ref, core_ref, high_ref, cross_ref, here_ref, mid_ref, hidden_ref, attn_ref, vec_ref,
    acc_ref, dpre_ref,
):
    side = lax.axis_index("wa")
    for pair in range(3):
        rows = slice(pair * 128, (pair + 1) * 128)
        attn_ref[:, rows] = attn_tile(got_ref, side, pair)
        acc_ref[:, rows] = attn_tile(got_ref, 1 - side, pair)
    flush(attn_ref)
    wait(o_own_ref)
    wait(o_other_ref)
    total = jnp.dot(
        attn_ref[...], o_own_ref[...], preferred_element_type=jnp.float32
    ) + jnp.dot(acc_ref[...], o_other_ref[...], preferred_element_type=jnp.float32)
    middle = tokens_ref[...].astype(jnp.float32) + (total + o_bias_ref[...])
    mid_ref[...] = middle
    flush(mid_ref)
    normed, _, _ = norm_forward(middle, gain_ref[...], shift_ref[...])
    low = normed.astype(jnp.bfloat16)
    branch_low = branch_of(cot_ref, exit_ref).astype(jnp.bfloat16)
    dnormed = None
    wait(up_ref)
    wait(dhidden_ref)
    for begin in range(0, 1536, FF_TILE):
        columns = slice(begin, begin + FF_TILE)
        pre_act = (
            jnp.dot(low, up_ref[:, columns], preferred_element_type=jnp.float32)
            + up_bias_ref[:, columns]
        )
        hidden_full, slope = gelu_pair(pre_act)
        hidden = hidden_full.astype(jnp.bfloat16)
        hidden_ref[:, columns] = hidden
        dpre = (dhidden_ref[:, columns] * slope).astype(jnp.bfloat16)
        vec_ref[:, columns] = jnp.sum(dpre.astype(jnp.float32), axis=0, keepdims=True)
        dpre_ref[:, columns] = dpre
        dn_term = lax.dot_general(
            dpre, up_ref[:, columns], trans_right, preferred_element_type=jnp.float32
        )
        dnormed = dn_term if dnormed is None else dnormed + dn_term
    dn_ref[...] = dnormed.astype(jnp.bfloat16)
    core, high = lax.axis_index("core"), lax.axis_index("zh")
    for ref, offset in ((core_ref, 1), (high_ref, 2), (cross_ref, 3), (here_ref, 0)):
        up_side = (core ^ (offset & 1)) == 0
        first_half = (high ^ (offset >> 1)) == 0
        ref[:, :768] = jnp.where(up_side, low, branch_low)
        ref[:, 768:] = jnp.where(
            up_side,
            jnp.where(first_half, dpre_ref[:, :768], dpre_ref[:, 768:]),
            jnp.where(first_half, hidden_ref[:, :768], hidden_ref[:, 768:]),
        )


def dheads_kernel(
    wait, flush, dn_ref, other_ref, mid_ref, cot_ref, exit_ref, gain_ref, attn_ref, up_ref, down_ref, o_ref,
    pay_ref, both_ref, dmid_ref, vec_ref,
):
    middle = mid_ref[...]
    _, unit, inverse = norm_forward(middle, gain_ref[...], 0.0)
    dnormed = dn_ref[...].astype(jnp.float32) + other_ref[...].astype(jnp.float32)
    branch = branch_of(cot_ref, exit_ref)
    dmiddle = branch + norm_backward(dnormed, unit, inverse, gain_ref[...])
    dmid_ref[...] = dmiddle
    flush(dmid_ref)
    low = dmiddle.astype(jnp.bfloat16)
    pay_ref[12:] = jnp.zeros((4, HALF, 128), jnp.bfloat16)
    flush(pay_ref, 12, 16)
    wait(o_ref)
    all_heads = lax.dot_general(low, o_ref[...], trans_right, preferred_element_type=jnp.float32)
    for pair in range(3):
        dheads = all_heads[:, pair * 128 : (pair + 1) * 128]
        for odd in range(2):
            pack = pack_from_high if odd else pack_from_low
            lower = pack(dheads[:HALF]).astype(jnp.bfloat16)
            higher = pack(dheads[HALF:]).astype(jnp.bfloat16)
            index = 4 * pair + 2 * odd
            pay_ref[index, :32] = lower
            pay_ref[index, 32:] = higher
            pay_ref[index + 1, :32] = higher
            pay_ref[index + 1, 32:] = higher
        flush(pay_ref, 4 * pair, 4 * pair + 4)
    vec_ref[:, :1536] = up_ref[...]
    vec_ref[:, 1536:2304] = down_ref[...]
    vec_ref[:, 2304:3072] = jnp.sum(dnormed * unit, axis=0, keepdims=True)
    vec_ref[:, 3072:3840] = jnp.sum(dnormed, axis=0, keepdims=True)
    vec_ref[:, 3840:] = jnp.sum(low.astype(jnp.float32), axis=0, keepdims=True)
    both_ref[:, :768] = low
    both_ref[:, 768:] = attn_ref[...]


def ffn_products_kernel(
    wait, flush, here_ref, core_ref, high_ref, cross_ref, both_ref, sent_ref,
    vec_ref, vec_sent_ref, out_ref,
):
    pieces = (here_ref, core_ref, high_ref, cross_ref)
    first = lax.axis_index("core") == 0
    vec = vec_ref[...] + vec_sent_ref[...]
    lines = [vec[:, 128 * row : 128 * (row + 1)] for row in range(36)]
    lines = jnp.concatenate(lines + [jnp.zeros((12, 128), jnp.float32)], axis=0)
    rights = jnp.concatenate([ref[:, 768:] for ref in pieces], axis=0)
    both = jnp.concatenate([both_ref[...], sent_ref[...]], axis=0)
    attn = jnp.where(first, both[:, 768:1024], both[:, 896:])
    for half in range(2):
        rows = slice(384 * half, 384 * half + 384)
        product = lax.dot_general(
            both[:, rows], attn, trans_left, preferred_element_type=jnp.float32
        )
        out_ref[rows, 896:] = product[:, 128:].astype(jnp.bfloat16)
        for plane in range(8):
            at = slice(48 * plane, 48 * plane + 48)
            out_ref[384 * half + 48 * plane : 384 * half + 48 * plane + 48, 768:896] = jnp.where(
                first, product[at, :128], lines
            ).astype(jnp.bfloat16)
        lefts = jnp.concatenate([ref[:, rows] for ref in pieces], axis=0)
        out_ref[rows, :768] = lax.dot_general(
            lefts, rights, trans_left, preferred_element_type=jnp.float32
        ).astype(jnp.bfloat16)
        flush(out_ref, 384 * half, 384 * half + 384)


def ffn_kernel(wait, flush, hidden_ref, down_ref, out_ref):
    out_ref[...] = jnp.dot(
        hidden_ref[...], down_ref[...], preferred_element_type=jnp.float32
    ).astype(jnp.bfloat16)


def dnormed_kernel(
    wait, flush, got_ref, tokens_ref, q_ref, k_ref, v_ref,
    grads_ref, norm_ref, vec_ref, dn_ref,
):
    wide = lane_ids(HALF, 128) < HALF
    for pair in range(3):
        columns = slice(pair * 128, (pair + 1) * 128)
        key_columns = slice(384 + pair * 128, 512 + pair * 128)
        value_columns = slice(768 + pair * 128, 896 + pair * 128)
        for half in range(2):
            rows = slice(half * HALF, (half + 1) * HALF)
            at = 8 * pair + 2 * half
            even = got_ref[at].astype(jnp.float32) + got_ref[at + 1].astype(jnp.float32)
            odd = got_ref[at + 4].astype(jnp.float32) + got_ref[at + 5].astype(jnp.float32)
            grads_ref[rows, key_columns] = jnp.where(wide, even[:HALF], turn(odd[:HALF])).astype(
                jnp.bfloat16
            )
            grads_ref[rows, value_columns] = jnp.where(
                wide, turn(even[:HALF]), odd[:HALF]
            ).astype(jnp.bfloat16)
            grads_ref[rows, columns] = pairs_low(even[HALF:], odd[HALF:]).astype(jnp.bfloat16)
    for ref in (q_ref, k_ref, v_ref):
        wait(ref)
    dnormed = (
        lax.dot_general(
            grads_ref[:, :384], q_ref[...], trans_right, preferred_element_type=jnp.float32
        )
        + lax.dot_general(
            grads_ref[:, 384:768], k_ref[...], trans_right, preferred_element_type=jnp.float32
        )
        + lax.dot_general(
            grads_ref[:, 768:], v_ref[...], trans_right, preferred_element_type=jnp.float32
        )
    )
    dn_ref[...] = dnormed.astype(jnp.bfloat16)
    _, unit, _ = norm_forward(tokens_ref[...].astype(jnp.float32), 1.0, 0.0)
    total = jnp.sum(grads_ref[...].astype(jnp.float32), axis=0, keepdims=True)
    vec_ref[:, :768] = jnp.sum(dnormed, axis=0, keepdims=True)
    vec_ref[:, 768:1536] = jnp.sum(dnormed * unit, axis=0, keepdims=True)
    vec_ref[:, 1536:1920] = total[:, :384]
    vec_ref[:, 1920:2304] = total[:, 768:]
    norm_ref[...] = vec_ref[:, :1536]


def input_grad_kernel(
    wait, flush, dn_ref, other_ref, tokens_ref, cot_ref, exit_ref, gain_ref, dmid_ref, out_ref
):
    _, unit, inverse = norm_forward(tokens_ref[...].astype(jnp.float32), 1.0, 0.0)
    dnormed = dn_ref[...].astype(jnp.float32) + other_ref[...].astype(jnp.float32)
    active = column((exit_ref[...] > LAYER).astype(jnp.float32))
    out_ref[...] = (
        dmid_ref[...]
        + norm_backward(dnormed, unit, inverse, gain_ref[...])
        + jnp.where(active > 0.0, 0.0, cot_ref[...].astype(jnp.float32))
    )


def output_kernel(
    wait, flush, ffn_ref, other_ref, mid_ref, tokens_ref, exit_ref, bias_ref, out_ref
):
    active = column((exit_ref[...] > LAYER).astype(jnp.float32))
    branch = ffn_ref[...].astype(jnp.float32) + other_ref[...].astype(jnp.float32) + bias_ref[...]
    out_ref[...] = jnp.where(
        active > 0.0, mid_ref[...] + branch, tokens_ref[...].astype(jnp.float32)
    ).astype(jnp.bfloat16)


def merge_kernel(wait, flush, kept_ref, taken_ref, dq_ref, edge_ref, out_ref):
    high = lax.axis_index("zh")
    for block in range(BLOCKS):
        pair = kept_ref[block].astype(jnp.float32) + taken_ref[block].astype(jnp.float32)
        query = dq_ref[block]
        if block == BLOCKS - 1:
            pair = pair + edge_ref[:HALF].astype(jnp.float32)
            query = (query.astype(jnp.float32) + edge_ref[HALF:].astype(jnp.float32)).astype(
                jnp.bfloat16
            )
        out_ref[pl.ds(2 * block + high, 1), :HALF] = pair.astype(jnp.bfloat16)[None]
        out_ref[pl.ds(2 * block + high, 1), HALF:] = query[None]
        pair = kept_ref[BLOCKS + block].astype(jnp.float32) + taken_ref[BLOCKS + block].astype(
            jnp.float32
        )
        out_ref[pl.ds(2 * block + 1 - high, 1), :HALF] = pair.astype(jnp.bfloat16)[None]
        out_ref[pl.ds(2 * block + 1 - high, 1), HALF:] = jnp.zeros((1, 32, 128), jnp.bfloat16)
        if block % 8 == 7:
            flush(out_ref, 2 * block - 14, 2 * block + 2)


def qkv_products_kernel(
    wait, flush, keep_ref, sent_ref, grads_ref, grads_sent_ref,
    vec_ref, vec_sent_ref, wa_ref, cross_ref, out_ref,
    product_ref,
):
    vec = vec_ref[...] + vec_sent_ref[...]
    norms = vec[:, :1536] + (wa_ref[...] + cross_ref[...])
    vec = jnp.concatenate([norms, vec[:, 1536:]], axis=1)
    lines = [vec[:, 128 * row : 128 * (row + 1)] for row in range(18)]
    lines = jnp.concatenate(lines + [jnp.zeros((2, 128), jnp.float32)], axis=0)
    rights = jnp.concatenate([grads_ref[...], grads_sent_ref[...]], axis=0)
    for pair in range(16):
        if pair % 8 == 0:
            features = slice(24 * pair, 24 * pair + 192)
            lefts = jnp.concatenate([keep_ref[:, features], sent_ref[:, features]], axis=0)
            product_ref[features] = lax.dot_general(
                lefts, rights, trans_left, preferred_element_type=jnp.float32
            )
        block = product_ref[24 * pair : 24 * pair + 24]
        for half in range(2):
            rows = slice(12 * half, 12 * half + 12)
            tiles = [block[rows, 128 * tile : 128 * tile + 128] for tile in range(9)]
            out_ref[2 * pair + half] = jnp.concatenate(tiles + [lines], axis=0).astype(jnp.bfloat16)
        if pair % 8 == 7:
            flush(out_ref, 2 * pair - 14, 2 * pair + 2)


def finish_kernel(
    wait, flush, got_ref, q_ref, k_ref, v_ref, shift_out, gain_out, q_bias_out, v_bias_out
):
    total = got_ref[0].astype(jnp.float32)
    for source in range(1, 32):
        total = total + got_ref[source].astype(jnp.float32)
    for at, ref in enumerate((q_ref, k_ref, v_ref)):
        for tile in range(3):
            row = 36 * at + 12 * tile
            ref[:, 128 * tile : 128 * tile + 128] = total[row : row + 12]
    row = 108
    for ref in (shift_out, gain_out, q_bias_out, v_bias_out):
        for tile in range(ref.shape[1] // 128):
            ref[:, 128 * tile : 128 * tile + 128] = total[row : row + 1]
            row += 1


def ffn_sums_kernel(wait, flush, got_ref, core_ref, high_ref, cross_ref, here_ref):
    total = got_ref[0].astype(jnp.float32)
    for source in range(1, 16):
        total = total + got_ref[source].astype(jnp.float32)
    me = 2 * lax.axis_index("zh") + lax.axis_index("core")
    parts = [total[12 * index : 12 * index + 12, :1024] for index in range(4)]
    vec = jnp.concatenate([total[row : row + 1, 768:896] for row in range(36)], axis=1)
    lines = jnp.concatenate([vec[:, 1152 * row : 1152 * (row + 1)] for row in range(4)], axis=0)
    spare = jnp.zeros((12, 128), jnp.float32)

    def part(offset):
        value = parts[offset]
        for index in range(1, 4):
            value = jnp.where(me == index, parts[index ^ offset], value)
        return value

    for ref, offset in ((here_ref, 0), (core_ref, 1), (high_ref, 2), (cross_ref, 3)):
        both = jnp.concatenate([part(offset), spare], axis=1)
        ref[...] = jnp.concatenate([both, lines], axis=0).astype(ref.dtype)


def ffn_finish_kernel(
    wait, flush, here_ref, core_ref, high_ref, cross_ref,
    up_ref, down_ref, o_ref, up_bias_out, down_bias_out, gain_out, shift_out, o_bias_out,
):
    first = lax.axis_index("core") == 0
    low = lax.axis_index("zh") == 0
    alls = [ref[...].astype(jnp.float32) for ref in (here_ref, core_ref, high_ref, cross_ref)]
    here, core, high, cross = [value[:12, :768] for value in alls]
    up_ref[:, :768] = jnp.where(first, jnp.where(low, here, high), jnp.where(low, core, cross))
    up_ref[:, 768:] = jnp.where(first, jnp.where(low, high, here), jnp.where(low, cross, core))
    down_ref[:, :768] = jnp.where(first, jnp.where(low, core, cross), jnp.where(low, here, high))
    down_ref[:, 768:] = jnp.where(first, jnp.where(low, cross, core), jnp.where(low, high, here))
    mine = alls[0][:, 768:1024] + alls[2][:, 768:1024]
    other = alls[1][:, 768:1024] + alls[3][:, 768:1024]
    o_ref[:, :256] = jnp.where(first, mine, other)[:12]
    o_ref[:, 256:] = jnp.where(first, other[:, 128:], mine[:, 128:])[:12]
    vec = jnp.where(first, alls[1][12:] + alls[3][12:], alls[0][12:] + alls[2][12:])
    vec = jnp.concatenate([vec[row : row + 1] for row in range(4)], axis=1)
    begin = 0
    for ref in (up_bias_out, down_bias_out, gain_out, shift_out, o_bias_out):
        ref[...] = vec[:, begin : begin + ref.shape[1]]
        begin += ref.shape[1]


def on_device(
    tokens,
    doc_start,
    exit_layer,
    cotangent,
    ln1_gain,
    ln1_shift,
    q_weight,
    q_bias,
    k_weight,
    v_weight,
    v_bias,
    o_weight,
    o_bias,
    ln2_gain,
    ln2_shift,
    up_weight,
    up_bias,
    down_weight,
    down_bias,
):
    f32 = jnp.float32

    def copied(*arrays):
        return [("d", array) for array in arrays]

    payload, low_one = call(
        project_kernel, "project",
        copied(
            tokens, doc_start, ln1_gain, ln1_shift, q_bias, v_bias, q_weight, k_weight, v_weight
        ),
        [("d", whole(16, HALF + 48, 128)), ("d", whole(128, 768))],
        lazy=(6, 7, 8),
    )
    own = lax.all_to_all(payload, PLANE, 0, 0, tiled=True)
    low_one, o_given = lax.optimization_barrier((low_one, o_weight))
    o_other = lax.ppermute(o_given, "wa", SWAP)
    x_send, x_keep = call(
        prepare_kernel, "prepare",
        copied(low_one),
        [("v", whole(128, 384)), ("d", whole(128, 384))],
    )
    own, x_send, o_other = lax.optimization_barrier((own, x_send, o_other))
    pairs = own[:, :HALF]
    one = lax.ppermute(pairs, "core", SWAP)
    edge = lax.ppermute(own[BLOCKS - 1], EDGE, ((7, 3), (15, 11)))
    two = lax.ppermute(pairs, "zh", SWAP)
    two, edge = lax.optimization_barrier((two, edge))
    three = lax.ppermute(two, "core", SWAP)
    x_sent = lax.ppermute(x_send, "core", SWAP)
    back, kv, q_rows, start_rows, full_rows = attend(own, one, two, three, edge)
    dhidden, vec_down = call(
        dhidden_kernel, "dhidden",
        copied(cotangent, exit_layer, down_weight),
        [("d", whole(128, 1536, dtype=f32)), ("d", whole(1, 768, dtype=f32))],
    )
    got = lax.all_to_all(back, ("x", "y", "wa"), 0, 0, tiled=True)
    dn_two, ffn_core, ffn_high, ffn_cross, ffn_here, middle, hidden, attn_low, vec_up = call(
        middle_kernel, "middle",
        [("v", got)]
        + copied(
            tokens, cotangent, exit_layer, o_bias, ln2_gain, ln2_shift, up_bias, o_weight, o_other,
            up_weight, dhidden,
        ),
        [
            ("v", whole(128, 768)),
            ("v", whole(128, 1536)),
            ("v", whole(128, 1536)),
            ("v", whole(128, 1536)),
            ("v", whole(128, 1536)),
            ("d", whole(128, 768, dtype=f32)),
            ("d", whole(128, 1536)),
            ("d", whole(128, 384)),
            ("d", whole(1, 1536, dtype=f32)),
        ],
        [pltpu.VMEM((128, 384), jnp.bfloat16), pltpu.VMEM((128, 1536), jnp.bfloat16)],
        lazy=(8, 9, 10, 11),
    )
    dn_two_other = lax.ppermute(dn_two, "wa", SWAP)
    ffn_high = lax.ppermute(ffn_high, "zh", SWAP)
    ffn_cross = lax.ppermute(ffn_cross, ("zh", "core"), CROSS)
    ffn_core = lax.ppermute(ffn_core, "core", SWAP)
    ffn = call(ffn_kernel, "ffn", copied(hidden, down_weight), [("v", whole(128, 768))], cost=0)
    dn_two_other, ffn = lax.optimization_barrier((dn_two_other, ffn))
    dh_payload, dattn_attn, dmiddle, vec_two = call(
        dheads_kernel, "dheads",
        [("v", dn_two), ("v", dn_two_other)]
        + copied(middle, cotangent, exit_layer, ln2_gain, attn_low, vec_up, vec_down, o_weight),
        [
            ("d", whole(16, HALF, 128)),
            ("v", whole(128, 1152)),
            ("d", whole(128, 768, dtype=f32)),
            ("v", whole(1, 4608, dtype=f32)),
        ],
        lazy=(9,),
        cost=0,
    )
    dh = lax.all_to_all(dh_payload, PLANE, 0, 0, tiled=True)
    dattn_sent = lax.ppermute(dattn_attn, "core", SWAP)
    vec_two_sent = lax.ppermute(vec_two, "core", SWAP)
    ffn_products = call(
        ffn_products_kernel, "ffn_products",
        [("v", ffn_here), ("v", ffn_core), ("v", ffn_high), ("v", ffn_cross)]
        + [("v", dattn_attn), ("v", dattn_sent), ("v", vec_two), ("v", vec_two_sent)],
        [("d", whole(768, 1024))],
    )
    ffn_blocks = lax.all_to_all(ffn_products.reshape(16, 48, 1024), PLANE, 0, 0, tiled=True)
    ffn_other = lax.ppermute(ffn, "wa", SWAP)
    given, kept, dq, edge_grad = attend_grad(kv, q_rows, start_rows, full_rows, dh)
    given, ffn_other = lax.optimization_barrier((given, ffn_other))
    edge_got = lax.ppermute(edge_grad, EDGE, ((3, 7), (11, 15)))
    taken = lax.ppermute(given, "core", SWAP)
    merged = call(
        merge_kernel, "merge",
        [("v", kept), ("v", taken), ("v", dq), ("v", edge_got)],
        [("d", whole(2 * BLOCKS, 96, 128))],
    )
    merged, ffn_blocks = lax.optimization_barrier((merged, ffn_blocks))
    grads = lax.all_to_all(merged, CHIPS, 0, 0, tiled=True)
    ffn_core, ffn_high, ffn_cross, ffn_here = call(
        ffn_sums_kernel, "ffn_sums", copied(ffn_blocks),
        [("v", whole(16, 1152)) for _ in range(3)] + [("v", whole(16, 1152, dtype=f32))],
        cost=0,
    )
    ffn_core = lax.ppermute(ffn_core, "core", SWAP)
    ffn_high = lax.ppermute(ffn_high, "zh", SWAP)
    ffn_cross = lax.ppermute(ffn_cross, ("zh", "core"), CROSS)
    grads, ffn_core, ffn_high, ffn_cross, x_sent = lax.optimization_barrier(
        (grads, ffn_core, ffn_high, ffn_cross, x_sent)
    )
    grads_rows, norms, vec, dn_one = call(
        dnormed_kernel, "dnormed",
        [("v", grads)] + copied(tokens, q_weight, k_weight, v_weight),
        [
            ("v", whole(128, 1152)),
            ("v", whole(1, 1536, dtype=f32)),
            ("v", whole(1, 2304, dtype=f32)),
            ("v", whole(128, 768)),
        ],
        lazy=(2, 3, 4),
        cost=0,
    )
    grads_sent = lax.ppermute(grads_rows, "core", SWAP)
    vec_sent = lax.ppermute(vec, "core", SWAP)
    norms_wa = lax.ppermute(norms, "wa", SWAP)
    norms_cross = lax.ppermute(norms, ("core", "wa"), CROSS)
    norms_wa, norms_cross, dn_one = lax.optimization_barrier((norms_wa, norms_cross, dn_one))
    dn_one_other = lax.ppermute(dn_one, "wa", SWAP)
    products = call(
        qkv_products_kernel, "qkv_products",
        copied(x_keep, x_sent)
        + [("v", grads_rows), ("v", grads_sent), ("v", vec), ("v", vec_sent)]
        + [("v", norms_wa), ("v", norms_cross)],
        [("d", whole(32, 128, 128))],
        [pltpu.VMEM((384, 1152), f32)],
        cost=0,
    )
    products = lax.all_to_all(products, CHIPS, 0, 0, tiled=True)
    output = call(
        output_kernel, "output",
        [("v", ffn), ("v", ffn_other)] + copied(middle, tokens, exit_layer, down_bias),
        [("d", whole(128, 768))],
        cost=0,
    )
    (
        up_weight_grad, down_weight_grad_t, o_weight_grad_t,
        up_bias_grad, down_bias_grad, ln2_gain_grad, ln2_shift_grad, o_bias_grad,
    ) = call(
        ffn_finish_kernel, "ffn_finish",
        [("v", ffn_here), ("v", ffn_core), ("v", ffn_high), ("v", ffn_cross)],
        [("d", whole(12, 1536, dtype=f32)) for _ in range(2)]
        + [("d", whole(12, 384, dtype=f32))]
        + [("d", whole(count, dtype=f32)) for count in (1536, 768, 768, 768, 768)],
        cost=0,
    )
    input_grad = call(
        input_grad_kernel, "input_grad",
        [("v", dn_one), ("v", dn_one_other)]
        + copied(tokens, cotangent, exit_layer, ln1_gain, dmiddle),
        [("d", whole(128, 768, dtype=f32))],
        cost=0,
    )
    (
        products, output, input_grad, up_weight_grad, down_weight_grad_t
    ) = lax.optimization_barrier(
        (products, output, input_grad, up_weight_grad, down_weight_grad_t)
    )
    (
        q_weight_grad, k_weight_grad, v_weight_grad,
        ln1_shift_grad, ln1_gain_grad, q_bias_grad, v_bias_grad,
    ) = call(
        finish_kernel, "finish",
        [("v", products)],
        [("d", whole(12, 384, dtype=f32)) for _ in range(3)]
        + [("d", whole(count, dtype=f32)) for count in (768, 768, 384, 384)],
    )
    return (
        output,
        input_grad,
        ln1_gain_grad,
        ln1_shift_grad,
        q_weight_grad,
        q_bias_grad,
        k_weight_grad,
        v_weight_grad,
        v_bias_grad,
        o_weight_grad_t,
        o_bias_grad,
        ln2_gain_grad,
        ln2_shift_grad,
        up_weight_grad,
        up_bias_grad,
        down_weight_grad_t,
        down_bias_grad,
    )


def solution(mesh):
    fine = Mesh(mesh.devices.reshape(4, 4, 2, 2, 2), CTX + ("wa",))
    return jax.shard_map(
        on_device,
        mesh=fine,
        in_specs=(
            P(CTX, None),
            P(CTX),
            P(CTX),
            P(CTX, None),
            P(),
            P(),
            P(None, "wa"),
            P("wa"),
            P(None, "wa"),
            P(None, "wa"),
            P("wa"),
            P("wa", None),
            P(),
            P(),
            P(),
            P(None, "wa"),
            P("wa"),
            P("wa", None),
            P(),
        ),
        out_specs=(
            P(CTX, None),
            P(CTX, None),
            P(),
            P(),
            P(CTX, "wa"),
            P("wa"),
            P(CTX, "wa"),
            P(CTX, "wa"),
            P("wa"),
            P(CTX, "wa"),
            P(),
            P(),
            P(),
            P(CTX, "wa"),
            P("wa"),
            P(CTX, "wa"),
            P(),
        ),
        check_vma=False,
    )
```
